32 devices in a mesh: dp: 8 (over z, y), chan: 4 (over x, core).
Axes of the slice: x: 2, y: 2, z: 4, core: 2. Of those that a mesh axis runs over, the one named last changes fastest.
Arguments:
- noisy: bfloat16 [16, 32, 32, 512], P('dp', None, None, 'chan'), may hold values from -6 to 6
- noise: float32 [16, 32, 32, 512], P('dp', None, None, 'chan'), may hold values from -6 to 6
- timesteps: int32 [16], P('dp'), may hold values from 0 to 999
- classes: int32 [16], P('dp'), may hold values from 0 to 999
- sample_weight: float32 [16], P('dp'), may hold values from 0.5 to 7.5
- conv_in: float32 [3, 4608, 512], P(None, 'dp', 'chan'), may hold values from -0.09375 to 0.09375
- conv_out: float32 [2, 4608, 512], P(None, 'dp', 'chan'), may hold values from -0.09375 to 0.09375
- emb_proj: float32 [2, 1024, 1024], P(None, 'dp', 'chan'), may hold values from -0.09375 to 0.09375
- attn_weight: float32 [512, 2048], P('dp', 'chan'), may hold values from -1.41421356 to 1.41421356
- time_in: float32 [256, 1024], P('dp', 'chan'), may hold values from -0.375 to 0.375
- emb_out: float32 [1024, 2024], P('dp', 'chan'), may hold values from -4 to 4
- norms: float32 [6, 2, 512], P(None, None, 'chan'), may hold values from -0.4 to 1.75
- conv_in_rows: float32 [3, 4608], P(None, 'dp'), may hold values from 9.313226e-11 to 1.3969839e-09
- conv_in_cols: float32 [3, 512], P(None, 'chan'), may hold values from 9.313226e-11 to 1.3969839e-09
- conv_out_rows: float32 [2, 4608], P(None, 'dp'), may hold values from 9.313226e-11 to 1.3969839e-09
- conv_out_cols: float32 [2, 512], P(None, 'chan'), may hold values from 9.313226e-11 to 1.3969839e-09
- emb_proj_rows: float32 [2, 1024], P(None, 'dp'), may hold values from 9.313226e-11 to 1.3969839e-09
- emb_proj_cols: float32 [2, 1024], P(None, 'chan'), may hold values from 9.313226e-11 to 1.3969839e-09
- attn_rows: float32 [512], P('dp'), may hold values from 5.820766e-08 to 2.3283064e-07
- attn_cols: float32 [2048], P('chan'), may hold values from 9.313226e-11 to 1.3969839e-09
- time_rows: float32 [256], P('dp'), may hold values from 9.313226e-11 to 1.3969839e-09
- time_cols: float32 [1024], P('chan'), may hold values from 9.313226e-11 to 1.3969839e-09
- embout_rows: float32 [1024], P('dp'), may hold values from 9.313226e-11 to 1.3969839e-09
- embout_cols: float32 [2024], P('chan'), may hold values from 9.313226e-11 to 1.3969839e-09
- norm_second: float32 [6, 2, 512], P(None, None, 'chan'), may hold values from 9.536743e-07 to 3.8146973e-06
Outputs:
- loss: float32 [], replicated
- conv_in_grad: float32 [3, 4608, 512], P(None, 'dp', 'chan')
- conv_in_rows_new: float32 [3, 4608], P(None, 'dp')
- conv_in_cols_new: float32 [3, 512], P(None, 'chan')
- conv_in_new: float32 [3, 4608, 512], P(None, 'dp', 'chan')
- conv_out_grad: float32 [2, 4608, 512], P(None, 'dp', 'chan')
- conv_out_rows_new: float32 [2, 4608], P(None, 'dp')
- conv_out_cols_new: float32 [2, 512], P(None, 'chan')
- conv_out_new: float32 [2, 4608, 512], P(None, 'dp', 'chan')
- emb_proj_grad: float32 [2, 1024, 1024], P(None, 'dp', 'chan')
- emb_proj_rows_new: float32 [2, 1024], P(None, 'dp')
- emb_proj_cols_new: float32 [2, 1024], P(None, 'chan')
- emb_proj_new: float32 [2, 1024, 1024], P(None, 'dp', 'chan')
- attn_grad: float32 [512, 2048], P('dp', 'chan')
- attn_rows_new: float32 [512], P('dp')
- attn_cols_new: float32 [2048], P('chan')
- attn_new: float32 [512, 2048], P('dp', 'chan')
- time_grad: float32 [256, 1024], P('dp', 'chan')
- time_rows_new: float32 [256], P('dp')
- time_cols_new: float32 [1024], P('chan')
- time_new: float32 [256, 1024], P('dp', 'chan')
- embout_grad: float32 [1024, 2024], P('dp', 'chan')
- embout_rows_new: float32 [1024], P('dp')
- embout_cols_new: float32 [2024], P('chan')
- embout_new: float32 [1024, 2024], P('dp', 'chan')
- norm_grad: float32 [6, 2, 512], P(None, None, 'chan')
- norm_second_new: float32 [6, 2, 512], P(None, None, 'chan')
- norms_new: float32 [6, 2, 512], P(None, None, 'chan')
The draws below stay inside these ranges and needn't reach their ends.
All inputs are finite; a program needn't handle non-finite values.
Results may differ from the reference program's by a relative error of at most 0.02.
Values may be sent and summed in bfloat16 or wider, within the bound.
A program may use at most 192 MiB of HBM per device.

```python
import math
import jax
import jax.numpy as jnp
import numpy as np
from jax import lax

C = 512
HEADS = 8
GROUPS = 32
E = 1024
TF = 256
K = 1000
S = 32
STEP = 10
PIX = 1024
QB = 512
IMAGES = 16
N_CHAN = 4


def draw_noise(key, part):
    key = jax.random.fold_in(key, 11)
    position = jnp.arange(C, dtype=jnp.float32) / (C - 1)
    sampled = jax.random.truncated_normal(key, -4.0, 4.0, (IMAGES, S, S, C), jnp.float32)
    channel_ramp = 0.7 + 0.7 * position
    return sampled * channel_ramp


def draw_sample_weight(key, part):
    key = jax.random.fold_in(key, 12)
    position = jnp.arange(IMAGES, dtype=jnp.float32) / max(IMAGES - 1, 1)
    return (1.0 + 2.0 * position) * jax.random.uniform(key, (IMAGES,), jnp.float32, 0.7, 1.3)


def draw_attn_weight(key, part):
    key = jax.random.fold_in(key, 13)
    sampled = jax.random.truncated_normal(key, -4.0, 4.0, (C, 4 * C), jnp.float32)
    local_col = jnp.arange(4 * C) % (4 * C // N_CHAN)
    col_scale = jnp.where(local_col >= 3 * C // N_CHAN, 8.0, 1.0) / jnp.sqrt(jnp.float32(C))
    return sampled * col_scale[None, :]


def draw_emb_out(key, part):
    key = jax.random.fold_in(key, 14)
    sampled = jax.random.truncated_normal(key, -4.0, 4.0, (E, E + K), jnp.float32)
    local_col = jnp.arange(E + K) % ((E + K) // N_CHAN)
    col_scale = jnp.where(local_col >= E // N_CHAN, 1.0, 1.0 / jnp.sqrt(jnp.float32(E)))
    return sampled * col_scale[None, :]


def draw_norms(key, part):
    key = jax.random.fold_in(key, 15)
    first_key, second_key = jax.random.split(key)
    position = jnp.arange(C, dtype=jnp.float32) / (C - 1)
    gain_rows = (0.7 + 0.8 * position)[None, :] * jax.random.uniform(first_key, (6, C), jnp.float32, 0.85, 1.15)
    biases = 0.1 * jax.random.truncated_normal(second_key, -4.0, 4.0, (6, C), jnp.float32)
    return jnp.stack([gain_rows, biases], 1)


def touch_ends(drawn, rng, least, high):
    longest = drawn.shape.index(max(drawn.shape))
    spots = []
    for shift in (0, 1):
        where = [jax.random.randint(jax.random.fold_in(rng, axis), (), 0, length) for axis, length in enumerate(drawn.shape)]
        where[longest] = (where[longest] + shift) % drawn.shape[longest]
        spots.append(tuple(where))
    return drawn.at[spots[0]].set(least).at[spots[1]].set(high)


def shard_levels(own_key, extent, cuts, smallest, top_value):
    level = 1.0
    for axis_at, parts in cuts:
        draws = jax.random.uniform(jax.random.fold_in(jax.random.fold_in(own_key, 6), axis_at), (parts,), jnp.float32, smallest / len(cuts), top_value / len(cuts))
        level = level * jnp.repeat(jnp.exp(draws), extent[axis_at] // parts).reshape((-1,) + (1,) * (len(extent) - 1 - axis_at))
    return level


def rank_bounds(number_of, slope):
    loads = [(1 << 20) // math.isqrt(grade ** slope) + 1 for grade in range(1, number_of + 1)]
    deviation = 1 + sum(loads) // (1 << 30)
    return np.cumsum(np.array([max(1, weight // deviation) for weight in loads]))


def ranked_ids(rng, shape, count, lean):
    grid = rank_bounds(count, lean)
    lot = jax.random.randint(jax.random.fold_in(rng, 1), shape, 0, int(grid[count - 1]))
    standing = jnp.searchsorted(jnp.asarray(grid, jnp.int32), lot, side="right")
    return jax.random.permutation(jax.random.fold_in(rng, 2), count)[standing].astype(jnp.int32)


def centred(own_key, shape, scale, most, shards=(), kind=jnp.bfloat16):
    array = scale * jax.random.normal(own_key, shape, jnp.float32)
    if shards:
        array = array * shard_levels(own_key, shape, shards, -0.22, 0.18)
    return jnp.clip(array, -most, most).astype(kind)


def setup_inputs(seed: int = 0) -> dict:
    arg_keys = jax.random.split(jax.random.key(seed), 26)
    return {
        "noisy": centred(arg_keys[0], (IMAGES, S, S, C), 1.0, 6.0, ((0, 8), (3, 4))),
        "noise": draw_noise(jax.random.fold_in(arg_keys[25], 71), 0),
        "timesteps": touch_ends(jax.random.randint(arg_keys[2], (IMAGES,), 0, 1000), jax.random.fold_in(arg_keys[2], 1), 0, 999).astype(jnp.int32),
        "classes": touch_ends(ranked_ids(arg_keys[3], (IMAGES,), K, 2), jax.random.fold_in(arg_keys[3], 3), 0, K - 1).astype(jnp.int32),
        "sample_weight": draw_sample_weight(jax.random.fold_in(arg_keys[25], 71), 0),
        "conv_in": centred(arg_keys[5], (3, 9 * C, C), (9 * C) ** -0.5, 0.09375, ((1, 8), (2, 4)), jnp.float32),
        "conv_out": centred(arg_keys[6], (2, 9 * C, C), (9 * C) ** -0.5, 0.09375, ((1, 8), (2, 4)), jnp.float32),
        "emb_proj": centred(arg_keys[7], (2, E, 2 * C), (4 * E) ** -0.5, 0.09375, ((1, 8), (2, 4)), jnp.float32),
        "attn_weight": draw_attn_weight(jax.random.fold_in(arg_keys[25], 71), 0),
        "time_in": centred(arg_keys[9], (TF, E), TF ** -0.5, 0.375, ((0, 8), (1, 4)), jnp.float32),
        "emb_out": draw_emb_out(jax.random.fold_in(arg_keys[25], 71), 0),
        "norms": draw_norms(jax.random.fold_in(arg_keys[25], 71), 0),
        "conv_in_rows": jnp.clip(jnp.exp(math.log(1.3969838619232178e-09) - 2.7080502 * jax.random.uniform(arg_keys[12], (3, 9 * C), jnp.float32) ** shard_levels(arg_keys[12], (3, 9 * C), ((1, 8),), -0.2, 0.2)), 9.313225884932663e-11, 1.3969838619232178e-09),
        "conv_in_cols": jnp.clip(jnp.exp(math.log(1.3969838619232178e-09) - 2.7080502 * jax.random.uniform(arg_keys[13], (3, C), jnp.float32) ** shard_levels(arg_keys[13], (3, C), ((1, 4),), -0.2, 0.2)), 9.313225884932663e-11, 1.3969838619232178e-09),
        "conv_out_rows": jnp.clip(jnp.exp(math.log(1.3969838619232178e-09) - 2.7080502 * jax.random.uniform(arg_keys[14], (2, 9 * C), jnp.float32) ** shard_levels(arg_keys[14], (2, 9 * C), ((1, 8),), -0.2, 0.2)), 9.313225884932663e-11, 1.3969838619232178e-09),
        "conv_out_cols": jnp.clip(jnp.exp(math.log(1.3969838619232178e-09) - 2.7080502 * jax.random.uniform(arg_keys[15], (2, C), jnp.float32) ** shard_levels(arg_keys[15], (2, C), ((1, 4),), -0.2, 0.2)), 9.313225884932663e-11, 1.3969838619232178e-09),
        "emb_proj_rows": jnp.clip(jnp.exp(math.log(1.3969838619232178e-09) - 2.7080502 * jax.random.uniform(arg_keys[16], (2, E), jnp.float32) ** shard_levels(arg_keys[16], (2, E), ((1, 8),), -0.2, 0.2)), 9.313225884932663e-11, 1.3969838619232178e-09),
        "emb_proj_cols": jnp.clip(jnp.exp(math.log(1.3969838619232178e-09) - 2.7080502 * jax.random.uniform(arg_keys[17], (2, 2 * C), jnp.float32) ** shard_levels(arg_keys[17], (2, 2 * C), ((1, 4),), -0.2, 0.2)), 9.313225884932663e-11, 1.3969838619232178e-09),
        "attn_rows": jnp.clip(jnp.exp(math.log(2.3283064365386963e-07) - 1.3862944 * jax.random.uniform(arg_keys[18], (C,), jnp.float32) ** shard_levels(arg_keys[18], (C,), ((0, 8),), -0.2, 0.2)), 5.820766091346741e-08, 2.3283064365386963e-07),
        "attn_cols": jnp.clip(jnp.exp(math.log(1.3969838619232178e-09) - 2.7080502 * jax.random.uniform(arg_keys[19], (4 * C,), jnp.float32) ** shard_levels(arg_keys[19], (4 * C,), ((0, 4),), -0.2, 0.2)), 9.313225884932663e-11, 1.3969838619232178e-09),
        "time_rows": jnp.clip(jnp.exp(math.log(1.3969838619232178e-09) - 2.7080502 * jax.random.uniform(arg_keys[20], (TF,), jnp.float32) ** shard_levels(arg_keys[20], (TF,), ((0, 8),), -0.2, 0.2)), 9.313225884932663e-11, 1.3969838619232178e-09),
        "time_cols": jnp.clip(jnp.exp(math.log(1.3969838619232178e-09) - 2.7080502 * jax.random.uniform(arg_keys[21], (E,), jnp.float32) ** shard_levels(arg_keys[21], (E,), ((0, 4),), -0.2, 0.2)), 9.313225884932663e-11, 1.3969838619232178e-09),
        "embout_rows": jnp.clip(jnp.exp(math.log(1.3969838619232178e-09) - 2.7080502 * jax.random.uniform(arg_keys[22], (E,), jnp.float32) ** shard_levels(arg_keys[22], (E,), ((0, 8),), -0.2, 0.2)), 9.313225884932663e-11, 1.3969838619232178e-09),
        "embout_cols": jnp.clip(jnp.exp(math.log(1.3969838619232178e-09) - 2.7080502 * jax.random.uniform(arg_keys[23], (E + K,), jnp.float32) ** shard_levels(arg_keys[23], (E + K,), ((0, 4),), -0.2, 0.2)), 9.313225884932663e-11, 1.3969838619232178e-09),
        "norm_second": jnp.clip(jnp.exp(math.log(3.814697265625e-06) - 1.3862944 * jax.random.uniform(arg_keys[24], (6, 2, C), jnp.float32) ** shard_levels(arg_keys[24], (6, 2, C), ((2, 4),), -0.2, 0.2)), 9.5367431640625e-07, 3.814697265625e-06),
    }


@jax.custom_vjp
def low(v):
    return lax.optimization_barrier(v.astype(jnp.bfloat16)).astype(jnp.float32)

@jax.custom_vjp
def low_back(v):
    return v

def low_keep(v):
    return (low(v), None)

def low_pass(kept, grad):
    return (grad,)

def back_keep(v):
    return (v, None)

def back_low(kept, grad):
    return (low(grad),)
low.defvjp(low_keep, low_pass)
low_back.defvjp(back_keep, back_low)
highest = lax.Precision.HIGHEST
step_rate = 0.5
floor_scale = 0.001
tiny_square = 1e-30
norm_eps = 1e-05

def shifted_view(values, shift_y, shift_x):
    padded = jnp.pad(values, ((0, 0), (1, 1), (1, 1), (0, 0)))
    height, across = (values.shape[1], values.shape[2])
    return padded[:, 1 + shift_y:1 + shift_y + height, 1 + shift_x:1 + shift_x + across, :]

def convolve(values, kernel):
    summed = jnp.zeros(values.shape[:3] + (kernel.shape[2],), jnp.float32)
    for tap_index in range(9):
        moved = shifted_view(values, tap_index // 3 - 1, tap_index % 3 - 1)
        summed = summed + jnp.einsum('bhwi,io->bhwo', moved, kernel[tap_index], precision=highest)
    return summed

def group_norm(values, gain_vec, bias_vec):
    images, height, across, channels = values.shape
    grouped = values.reshape(images, height * across, GROUPS, channels // GROUPS)
    center = grouped - lax.optimization_barrier(jnp.mean(grouped, (1, 3), keepdims=True))
    variance = lax.optimization_barrier(jnp.mean(center * center, (1, 3), keepdims=True))
    return (center * lax.rsqrt(variance + norm_eps)).reshape(values.shape) * gain_vec + bias_vec

def split_weights(params):
    conv_in, conv_out, emb_proj, attn_weight, time_in, emb_out, norms = params
    kernels_in = low(conv_in).reshape(3, 9, C, C)
    kernels_out = jnp.swapaxes(low(conv_out).reshape(2, 9, C, C), 2, 3)
    attn_low = low(attn_weight).reshape(C, N_CHAN, 4 * C // N_CHAN)
    boundary = 3 * C // N_CHAN
    qkv_weight = attn_low[:, :, :boundary].reshape(C, HEADS, 3, C // HEADS)
    proj_weight = attn_low[:, :, boundary:].reshape(C, C)
    out_low = low(emb_out).reshape(E, N_CHAN, (E + K) // N_CHAN)
    hidden_weight = out_low[:, :, :E // N_CHAN].reshape(E, E)
    class_table = out_low[:, :, E // N_CHAN:].reshape(E, K)
    return (kernels_in, kernels_out, low(emb_proj), qkv_weight, proj_weight, low(time_in), hidden_weight, class_table)

def embed_forward(timesteps, classes, time_weight, hidden_weight, class_table):
    half_count = TF // 2
    frequency = jnp.exp(-math.log(10000.0) * jnp.arange(half_count, dtype=jnp.float32) / half_count)
    angles = timesteps.astype(jnp.float32)[:, None] * frequency[None, :]
    sinusoid = low(jnp.concatenate([jnp.cos(angles), jnp.sin(angles)], 1))
    time_pre = low_back(jnp.dot(sinusoid, time_weight, precision=highest))
    hidden = low(jax.nn.silu(time_pre))
    onehot = (classes[:, None] == jnp.arange(K)[None, :]).astype(jnp.float32)
    embedding = low_back(jnp.dot(hidden, hidden_weight.T, precision=highest) + jnp.dot(onehot, class_table.T, precision=highest))
    return low(jax.nn.silu(embedding))

def residual_block(stream, kernel_in, kernel_out, modulator, norm_pair, context):
    entry_act = low(jax.nn.silu(group_norm(stream, norm_pair[0, 0], norm_pair[0, 1])))
    inner_act = low_back(convolve(entry_act, kernel_in))
    modulate = low_back(jnp.dot(context, modulator, precision=highest)).reshape(-1, C, 2)
    mixed = group_norm(inner_act, norm_pair[1, 0], norm_pair[1, 1]) * (1.0 + modulate[:, None, None, :, 0]) + modulate[:, None, None, :, 1]
    hidden = low(jax.nn.silu(mixed))
    return stream + low_back(convolve(hidden, kernel_out))

def attention_block(stream, qkv_weight, proj_weight, norm_one):
    images, height, across, channels = stream.shape
    pixels = height * across
    head_size = C // HEADS
    scale_factor = head_size ** (-0.5)
    entry_act = low(group_norm(stream, norm_one[0], norm_one[1])).reshape(images, pixels, C)
    qkv_low = low(low_back(jnp.einsum('bpc,cnkd->bpnkd', entry_act, qkv_weight, precision=highest)))
    queries, keys_low, values_low = (qkv_low[:, :, :, 0], qkv_low[:, :, :, 1], qkv_low[:, :, :, 2])

    def score_block(query_block):
        scores = low_back(jnp.einsum('bqhd,bkhd->bhqk', query_block, keys_low, precision=highest)) * scale_factor
        weights = jax.nn.softmax(scores, axis=-1)
        return jnp.einsum('bhqk,bkhd->bqhd', low(weights), values_low, precision=highest)
    stacked = jnp.moveaxis(queries.reshape(images, pixels // QB, QB, HEADS, head_size), 1, 0)
    attended = lax.map(jax.checkpoint(score_block), stacked)
    attended = jnp.moveaxis(attended, 0, 1).reshape(images, pixels, C)
    attended = low(low_back(attended))
    branch = low_back(jnp.einsum('bpi,oi->bpo', attended, proj_weight, precision=highest))
    return stream + branch.reshape(stream.shape)

def loss_head(stream, kernel, norm_one, noise, sample_weight):
    entry_act = low(jax.nn.silu(group_norm(stream, norm_one[0], norm_one[1])))
    predicted = low_back(convolve(entry_act, kernel))
    residual_error = predicted - noise
    return jnp.sum(sample_weight[:, None, None, None] * residual_error * residual_error) / (IMAGES * PIX * C)

def forward(params, noisy, noise, timesteps, classes, sample_weight):
    kernels_in, kernels_out, modulators, qkv_weight, proj_weight, time_weight, hidden_weight, class_table = split_weights(params)
    norms = params[6]
    context = embed_forward(timesteps, classes, time_weight, hidden_weight, class_table)
    stream = noisy.astype(jnp.float32)
    stream = residual_block(stream, kernels_in[0], kernels_out[0], modulators[0], norms[0:2], context)
    stream = attention_block(stream, qkv_weight, proj_weight, norms[2])
    stream = residual_block(stream, kernels_in[1], kernels_out[1], modulators[1], norms[3:5], context)
    return loss_head(stream, kernels_in[2], norms[5], noise, sample_weight)

def factored(gradient, weight, row_stats, col_stats, decay_rate):
    squared = gradient * gradient + tiny_square
    rows_new = decay_rate * row_stats + (1.0 - decay_rate) * lax.optimization_barrier(jnp.mean(squared, 2))
    cols_new = decay_rate * col_stats + (1.0 - decay_rate) * lax.optimization_barrier(jnp.mean(squared, 1))
    row_mean = lax.optimization_barrier(jnp.mean(rows_new, 1, keepdims=True))
    update = gradient * lax.rsqrt(rows_new / row_mean)[:, :, None] * lax.rsqrt(cols_new)[:, None, :]
    clip_factor = jnp.maximum(1.0, jnp.sqrt(lax.optimization_barrier(jnp.mean(update * update, (1, 2)))))
    scale_factor = jnp.maximum(floor_scale, jnp.sqrt(lax.optimization_barrier(jnp.mean(weight * weight, (1, 2)))))
    weight_new = weight - (step_rate * scale_factor / clip_factor)[:, None, None] * update
    return (rows_new, cols_new, weight_new)

def reference(noisy, noise, timesteps, classes, sample_weight, conv_in, conv_out, emb_proj, attn_weight, time_in, emb_out, norms, conv_in_rows, conv_in_cols, conv_out_rows, conv_out_cols, emb_proj_rows, emb_proj_cols, attn_rows, attn_cols, time_rows, time_cols, embout_rows, embout_cols, norm_second):
    params = (conv_in, conv_out, emb_proj, attn_weight, time_in, emb_out, norms)
    group_size = math.gcd(IMAGES, 4)
    group_count = IMAGES // group_size

    def regroup(values):
        return values.reshape((group_count, group_size) + values.shape[1:])
    batches = (regroup(noisy), regroup(noise), regroup(timesteps), regroup(classes), regroup(sample_weight))

    def accumulate(carried, batch_items):
        loss_total, grads_total = carried
        loss_value, pullback = jax.vjp(lambda params_in: forward(params_in, *batch_items), params)
        grad_step, = pullback(jnp.ones((), jnp.float32))
        return ((loss_total + loss_value, jax.tree.map(jnp.add, grads_total, grad_step)), None)
    start_carry = (jnp.zeros((), jnp.float32), jax.tree.map(jnp.zeros_like, params))
    (loss, grads), _ = lax.scan(accumulate, start_carry, batches)
    decay_rate = 1.0 - STEP ** (-0.8)
    stats = [(conv_in_rows, conv_in_cols), (conv_out_rows, conv_out_cols), (emb_proj_rows, emb_proj_cols), (attn_rows, attn_cols), (time_rows, time_cols), (embout_rows, embout_cols)]
    results = [loss]
    for position in range(6):
        weight = params[position]
        gradient = grads[position]
        row_stats, col_stats = stats[position]
        if weight.ndim == 2:
            rows_new, cols_new, weight_new = factored(gradient[None], weight[None], row_stats[None], col_stats[None], decay_rate)
            results += [gradient, rows_new[0], cols_new[0], weight_new[0]]
        else:
            rows_new, cols_new, weight_new = factored(gradient, weight, row_stats, col_stats, decay_rate)
            results += [gradient, rows_new, cols_new, weight_new]
    norm_grad = grads[6]
    second_new = decay_rate * norm_second + (1.0 - decay_rate) * (norm_grad * norm_grad + tiny_square)
    update = norm_grad * lax.rsqrt(second_new)
    clip_factor = jnp.maximum(1.0, jnp.sqrt(lax.optimization_barrier(jnp.mean(update * update, 2, keepdims=True))))
    scale_factor = jnp.maximum(floor_scale, jnp.sqrt(lax.optimization_barrier(jnp.mean(norms * norms, 2, keepdims=True))))
    norms_new = norms - step_rate * scale_factor / clip_factor * update
    results += [norm_grad, second_new, norms_new]
    return (results[0], results[1], results[2], results[3], results[4], results[5], results[6], results[7], results[8], results[9], results[10], results[11], results[12], results[13], results[14], results[15], results[16], results[17], results[18], results[19], results[20], results[21], results[22], results[23], results[24], results[25], results[26], results[27])
```

```python
import functools
import math

import jax
import jax.numpy as jnp
from jax import lax
from jax.experimental import pallas as pl
from jax.experimental.pallas import tpu as pltpu
from jax.sharding import Mesh
from jax.sharding import PartitionSpec as P

C = 512
HEADS = 8
GROUPS = 32
TF = 256
STEP = 10
SIDE = 32
PIX = 1024
HALF = 256
BLOCK = 128
PAD = SIDE
ROWS = PIX + 2 * PAD
CHUNK = 256

single = jnp.float32
narrow = jnp.bfloat16
step_rate = 0.5
floor_scale = 0.001
tiny_square = 1e-30
norm_eps = 1e-05

TAPS = [(t // 3 - 1, t % 3 - 1) for t in range(9)]


def dot(a, b):
    return jnp.dot(a, b, preferred_element_type=single)


def dot_t(a, b):
    return lax.dot_general(a, b, (((1,), (1,)), ((), ())), preferred_element_type=single)


def group_sum(row):
    lane = lax.broadcasted_iota(jnp.int32, (HALF, HALF), 0)
    other = lax.broadcasted_iota(jnp.int32, (HALF, HALF), 1)
    size = C // GROUPS
    ones = jnp.where(lane // size == other // size, 1.0, 0.0).astype(single)
    tall = jnp.broadcast_to(row, (8, HALF))
    return jnp.dot(tall, ones, precision=lax.Precision.HIGHEST, preferred_element_type=single)[0:1]


def loop_sum(count, make):
    zeros = make(None)

    def body(i, carried):
        return [old + new for old, new in zip(carried, make(i))]

    return lax.fori_loop(0, count, body, [jnp.zeros((1, HALF), single)] * zeros)


def rows_of(i, size=CHUNK, offset=0):
    return pl.ds(pl.multiple_of(offset + i * size, 32), size)


def stats(x_ref):
    members = float(PIX * (C // GROUPS))

    def first(i):
        if i is None:
            return 1
        return [jnp.sum(x_ref[rows_of(i), :], 0, keepdims=True)]

    (total,) = loop_sum(PIX // CHUNK, first)
    mean = group_sum(total) / members

    def second(i):
        if i is None:
            return 1
        center = x_ref[rows_of(i), :] - mean
        return [jnp.sum(center * center, 0, keepdims=True)]

    (square,) = loop_sum(PIX // CHUNK, second)
    rstd = lax.rsqrt(group_sum(square) / members + norm_eps)
    return mean, rstd


def sigmoid(v):
    return 1.0 / (1.0 + jnp.exp(-v))


def norm_forward(x_ref, gain, bias, act, store):
    mean, rstd = stats(x_ref)

    @pl.loop(0, PIX // CHUNK)
    def _(i):
        value = (x_ref[rows_of(i), :] - mean) * rstd * gain + bias
        if act:
            value = value * sigmoid(value)
        store(i, value.astype(narrow))


def norm_backward(x_ref, load_grad, gain, bias, act, tmp_ref, store):
    mean, rstd = stats(x_ref)
    members = float(PIX * (C // GROUPS))

    def first(i):
        if i is None:
            return 2
        hat = (x_ref[rows_of(i), :] - mean) * rstd
        grad = load_grad(i)
        if act:
            mixed = hat * gain + bias
            gate = sigmoid(mixed)
            grad = grad * gate * (1.0 + mixed * (1.0 - gate))
        tmp_ref[rows_of(i), :] = grad
        return [jnp.sum(grad, 0, keepdims=True), jnp.sum(grad * hat, 0, keepdims=True)]

    total, along = loop_sum(PIX // CHUNK, first)
    mean_grad = group_sum(gain * total) / members
    mean_along = group_sum(gain * along) / members

    @pl.loop(0, PIX // CHUNK)
    def _(i):
        hat = (x_ref[rows_of(i), :] - mean) * rstd
        store(i, rstd * (tmp_ref[rows_of(i), :] * gain - mean_grad - hat * mean_along))

    return total, along


def shifts(load, s_ref, width):
    for b in range(3):
        s_ref[b, 0:PAD, 0:width] = jnp.zeros((PAD, width), narrow)
        s_ref[b, PAD + PIX : ROWS, 0:width] = jnp.zeros((PAD, width), narrow)
    size = 128

    @pl.loop(0, PIX // size)
    def _(i):
        value = load(i, size)
        wide = value.astype(single)
        across = lax.broadcasted_iota(jnp.int32, wide.shape, 0) % SIDE
        left = jnp.where(across > 0, pltpu.roll(wide, 1, 0), 0.0)
        right = jnp.where(across < SIDE - 1, pltpu.roll(wide, size - 1, 0), 0.0)
        at = rows_of(i, size, PAD)
        s_ref[0, at, 0:width] = left.astype(narrow)
        s_ref[1, at, 0:width] = value
        s_ref[2, at, 0:width] = right.astype(narrow)


def tap_rows(s_ref, t, sign, i, size, width):
    a, b = TAPS[t]
    return s_ref[sign * b + 1, rows_of(i, size, PAD + sign * a * SIDE), 0:width]


def split_core(value):
    core = lax.axis_index("lo")
    b0, b1, b2, b3 = [value[:, k * BLOCK : (k + 1) * BLOCK] for k in range(4)]
    even, odd = jnp.concatenate([b0, b2], 1), jnp.concatenate([b1, b3], 1)
    first = core == 0
    return jnp.where(first, even, odd), jnp.where(first, odd, even)


def join_core(own_ref, peer_ref, full_ref):
    core = lax.axis_index("lo")

    @pl.loop(0, PIX // CHUNK)
    def _(i):
        at = rows_of(i)
        own, peer = own_ref[at, :].astype(single), peer_ref[at, :].astype(single)
        even = jnp.where(core == 0, own, peer).astype(narrow)
        odd = jnp.where(core == 0, peer, own).astype(narrow)
        full_ref[at, 0:BLOCK] = even[:, 0:BLOCK]
        full_ref[at, BLOCK : 2 * BLOCK] = odd[:, 0:BLOCK]
        full_ref[at, 2 * BLOCK : 3 * BLOCK] = even[:, BLOCK:]
        full_ref[at, 3 * BLOCK :] = odd[:, BLOCK:]


def conv_wide(s_ref, w_ref, store):
    @pl.loop(0, PIX // CHUNK)
    def _(i):
        total = None
        for t in range(9):
            part = dot(tap_rows(s_ref, t, 1, i, CHUNK, C), w_ref[t * C : (t + 1) * C, :])
            total = part if total is None else total + part
        store(i, total)


def conv_tall(s_ref, w_ref, sign, store):
    @pl.loop(0, PIX // CHUNK)
    def _(i):
        total = None
        for t in range(9):
            part = dot_t(tap_rows(s_ref, t, sign, i, CHUNK, HALF), w_ref[t * C : (t + 1) * C, :])
            total = part if total is None else total + part
        store(i, total)


def conv_back(s_ref, w_ref, store):
    @pl.loop(0, PIX // CHUNK)
    def _(i):
        total = None
        for t in range(9):
            part = dot(tap_rows(s_ref, t, -1, i, CHUNK, C), w_ref[t * C : (t + 1) * C, :])
            total = part if total is None else total + part
        store(i, total)


def transpose_into(load, t_ref):
    for i in range(PIX // CHUNK):
        t_ref[:, i * CHUNK : (i + 1) * CHUNK] = jnp.transpose(load(i).astype(single)).astype(narrow)


def kernel_grad(t_ref, s_ref, sign, store):
    for t in range(9):
        a, b = TAPS[t]
        start = PAD + sign * a * SIDE
        store(t, dot(t_ref[...], s_ref[sign * b + 1, start : start + PIX, 0:HALF]))


def low_lanes(shape):
    return lax.broadcasted_iota(jnp.int32, shape, 1) < BLOCK // 2


def swap_halves(value):
    half = BLOCK // 2
    return jnp.concatenate([value[:, half:], value[:, :half]], 1)


def mask_half(value, upper):
    low = low_lanes(value.shape)
    return jnp.where(low != upper, value.astype(single), 0.0).astype(narrow)


def head_parts(qkv_ref, s, h):
    base = 3 * BLOCK * s
    b0, b1, b2 = [slice(base + k * BLOCK, base + (k + 1) * BLOCK) for k in range(3)]
    return (b0, b0, b1) if h == 0 else (b1, b2, b2)


SCALE = (C // HEADS) ** (-0.5)


def attend(qkv_ref, k_ref, vt_ref, log_ref, out_ref):
    for s in range(2):
        for h in range(2):
            q_at, k_at, v_at = head_parts(qkv_ref, s, h)
            k_ref[...] = swap_halves(qkv_ref[:, k_at])
            vt_ref[...] = jnp.transpose(qkv_ref[:, v_at].astype(single)).astype(narrow)

            @pl.loop(0, PIX // CHUNK)
            def _(i):
                query = mask_half(qkv_ref[rows_of(i), q_at], h == 1)
                scores = dot_t(k_ref[...], query) * SCALE
                top = jnp.max(scores, 0, keepdims=True)
                exponent = jnp.exp(scores - top)
                total = jnp.sum(exponent, 0, keepdims=True)
                mixed = dot(vt_ref[...], exponent.astype(narrow)) / total
                log_ref[2 * s + h, i] = top + jnp.log(total)
                turned = jnp.transpose(mixed)
                at = rows_of(i)
                lanes = slice(s * BLOCK, (s + 1) * BLOCK)
                if h == 0:
                    out_ref[at, lanes] = turned.astype(narrow)
                else:
                    kept = out_ref[at, lanes].astype(single)
                    out_ref[at, lanes] = jnp.where(low_lanes(turned.shape), kept, turned).astype(narrow)


def attend_back(qkv_ref, log_ref, grad_ref, k_ref, kt_ref, dk_ref, dv_ref, dqkv):
    for s in range(2):
        lanes = slice(s * BLOCK, (s + 1) * BLOCK)
        for h in range(2):
            q_at, k_at, v_at = head_parts(qkv_ref, s, h)
            q_to, k_to, v_to = head_parts(None, 0, h)
            grad_to = dqkv[s]
            k_ref[...] = swap_halves(qkv_ref[:, k_at])
            kt_ref[...] = jnp.transpose(k_ref[...].astype(single)).astype(narrow)
            dk_ref[...] = jnp.zeros_like(dk_ref)
            dv_ref[...] = jnp.zeros_like(dv_ref)

            @pl.loop(0, PIX // CHUNK)
            def _(i):
                at = rows_of(i)
                query = mask_half(qkv_ref[at, q_at], h == 1)
                grad = mask_half(grad_ref[at, lanes], h == 1)
                weights = jnp.exp(dot_t(k_ref[...], query) * SCALE - log_ref[2 * s + h, i])
                dv_ref[...] += dot(weights.astype(narrow), grad)
                dweights = dot_t(qkv_ref[:, v_at], grad)
                inner = jnp.sum(weights * dweights, 0, keepdims=True)
                dscores = (weights * (dweights - inner) * SCALE).astype(narrow)
                dk_ref[...] += dot(dscores, query)
                turned = jnp.transpose(dot(kt_ref[...], dscores))
                kept = grad_to[at, q_to].astype(single)
                low = low_lanes(turned.shape)
                if h == 0:
                    grad_to[at, q_to] = turned.astype(narrow)
                else:
                    grad_to[at, q_to] = jnp.where(low, kept, turned).astype(narrow)

            low = low_lanes((PIX, BLOCK))
            dk = swap_halves(dk_ref[...])
            if h == 0:
                grad_to[:, k_to] = jnp.where(low, grad_to[:, k_to].astype(single), dk).astype(narrow)
                grad_to[:, v_to] = dv_ref[...].astype(narrow)
            else:
                grad_to[:, k_to] = jnp.where(low, dk, dv_ref[...]).astype(narrow)


VMEM = pl.BlockSpec(memory_space=pltpu.VMEM)


def call(body, outs, scratch, args, name):
    return pl.pallas_call(
        body,
        out_shape=outs,
        in_specs=[VMEM] * len(args),
        out_specs=[VMEM] * len(outs),
        scratch_shapes=scratch,
        compiler_params=pltpu.CompilerParams(vmem_limit_bytes=56 * 2**20),
        name=name,
    )(*args)


def struct(shape, dtype=single):
    return jax.ShapeDtypeStruct(shape, dtype)


def entry_kernel(act, x_ref, own_ref, recv_ref, norm_ref, stream_ref, entry_ref):
    @pl.loop(0, PIX // CHUNK)
    def _(i):
        at = rows_of(i)
        stream_ref[at, :] = x_ref[at, :] + (own_ref[at, :] + recv_ref[at, :].astype(single))

    def store(i, value):
        entry_ref[rows_of(i), :] = value

    norm_forward(stream_ref, norm_ref[0:1, :], norm_ref[1:2, :], act, store)


def first_kernel(x_ref, norm_ref, stream_ref, entry_ref):
    @pl.loop(0, PIX // CHUNK)
    def _(i):
        at = rows_of(i)
        stream_ref[at, :] = x_ref[at, :].astype(single)

    def store(i, value):
        entry_ref[rows_of(i), :] = value

    norm_forward(stream_ref, norm_ref[0:1, :], norm_ref[1:2, :], True, store)


def mid_rows(norm_ref, mod_ref):
    gain, bias = norm_ref[0:1, :], norm_ref[1:2, :]
    scale, shift = 1.0 + mod_ref[0:1, :], mod_ref[1:2, :]
    return gain, bias, scale, shift


def put_split(own_ref, peer_ref):
    def store(i, value):
        own, peer = split_core(value)
        own_ref[rows_of(i), :] = own
        peer_ref[rows_of(i), :] = peer.astype(narrow)

    return store


def shift_full(full_ref, s_ref, width):
    shifts(lambda i, size: full_ref[rows_of(i, size), :], s_ref, width)


def res_kernel(own_ref, peer_ref, win_ref, wout_ref, norm_ref, mod_ref, inner_ref, hidden_ref, part_ref, send_ref, full_ref, s_ref):
    join_core(own_ref, peer_ref, full_ref)
    shift_full(full_ref, s_ref, C)

    def put(i, value):
        inner_ref[rows_of(i), :] = value

    conv_wide(s_ref, win_ref, put)
    gain, bias, scale, shift = mid_rows(norm_ref, mod_ref)

    def store(i, value):
        hidden_ref[rows_of(i), :] = value

    norm_forward(inner_ref, gain * scale, bias * scale + shift, True, store)
    shift_full(hidden_ref, s_ref, HALF)
    conv_tall(s_ref, wout_ref, 1, put_split(part_ref, send_ref))


def attn_kernel(own_ref, peer_ref, w_ref, qkv_ref, log_ref, out_ref, part_ref, send_ref, full_ref, k_ref, vt_ref):
    join_core(own_ref, peer_ref, full_ref)

    @pl.loop(0, PIX // CHUNK)
    def _(i):
        at = rows_of(i)
        for s in range(2):
            value = dot(full_ref[at, :], w_ref[:, s * C : s * C + 3 * BLOCK])
            qkv_ref[at, s * 3 * BLOCK : (s + 1) * 3 * BLOCK] = value.astype(narrow)

    attend(qkv_ref, k_ref, vt_ref, log_ref, out_ref)
    store = put_split(part_ref, send_ref)

    @pl.loop(0, PIX // CHUNK)
    def _(i):
        at = rows_of(i)
        value = dot_t(out_ref[at, 0:BLOCK], w_ref[:, 3 * BLOCK : C])
        store(i, value + dot_t(out_ref[at, BLOCK:], w_ref[:, C + 3 * BLOCK :]))


def load_rows(ref):
    return lambda i: ref[rows_of(i), :]


def head_kernel(total, own_ref, peer_ref, w_ref, noise_ref, weight_ref, loss_ref, dw_ref, part_ref, send_ref, full_ref, s_ref, t_ref, grad_ref):
    join_core(own_ref, peer_ref, full_ref)
    shift_full(full_ref, s_ref, C)
    loss_ref[...] = jnp.zeros_like(loss_ref)

    def store(i, value):
        error = value - noise_ref[rows_of(i), :]
        weight = weight_ref[0:1, :]
        loss_ref[...] += jnp.sum(weight * error * error, 0, keepdims=True)
        grad_ref[rows_of(i), :] = (2.0 * weight * error / total).astype(narrow)

    conv_wide(s_ref, w_ref, store)
    wide_back(full_ref, w_ref, grad_ref, dw_ref, part_ref, send_ref, s_ref, t_ref)


def wide_back(full_ref, w_ref, grad_ref, dw_ref, part_ref, send_ref, s_ref, t_ref):
    shift_full(grad_ref, s_ref, HALF)
    transpose_into(load_rows(full_ref), t_ref)

    def keep(t, value):
        dw_ref[t * C : (t + 1) * C, :] = value.astype(narrow)

    kernel_grad(t_ref, s_ref, -1, keep)
    conv_tall(s_ref, w_ref, -1, put_split(part_ref, send_ref))


def normback_kernel(act, x_ref, part_ref, recv_ref, up_ref, norm_ref, dx_ref, low_ref, sums_ref, tmp_ref):
    def load(i):
        return part_ref[rows_of(i), :] + recv_ref[rows_of(i), :].astype(single)

    def store(i, value):
        value = value + up_ref[rows_of(i), :]
        dx_ref[rows_of(i), :] = value
        low_ref[rows_of(i), :] = value.astype(narrow)

    total, along = norm_backward(x_ref, load, norm_ref[0:1, :], norm_ref[1:2, :], act, tmp_ref, store)
    sums_ref[0:1, :] = along
    sums_ref[1:2, :] = total


def resback_kernel(
    gown_ref, gpeer_ref, hidden_ref, inner_ref, norm_ref, mod_ref, wout_ref, own_ref, peer_ref, win_ref,
    dout_ref, din_ref, part_ref, send_ref, sums_ref, dmod_ref,
    full_ref, s_ref, t_ref, dh_ref, tmp_ref, grad_ref,
):
    join_core(gown_ref, gpeer_ref, full_ref)
    transpose_into(load_rows(full_ref), t_ref)
    shift_full(hidden_ref, s_ref, HALF)

    def keep(t, value):
        dout_ref[t * C : (t + 1) * C, :] = value.astype(narrow)

    kernel_grad(t_ref, s_ref, 1, keep)
    shift_full(full_ref, s_ref, C)

    def put(i, value):
        dh_ref[rows_of(i), :] = value

    conv_back(s_ref, wout_ref, put)
    gain, bias, scale, shift = mid_rows(norm_ref, mod_ref)

    def store(i, value):
        grad_ref[rows_of(i), :] = value.astype(narrow)

    total, along = norm_backward(
        inner_ref, load_rows(dh_ref), gain * scale, bias * scale + shift, True, tmp_ref, store
    )
    sums_ref[0:1, :] = scale * along
    sums_ref[1:2, :] = scale * total
    dmod_ref[0:1, :] = gain * along + bias * total
    dmod_ref[1:2, :] = total
    join_core(own_ref, peer_ref, full_ref)
    wide_back(full_ref, win_ref, grad_ref, din_ref, part_ref, send_ref, s_ref, t_ref)


def attnback_kernel(
    gown_ref, gpeer_ref, qkv_ref, log_ref, out_ref, w_ref, own_ref, peer_ref,
    dw_ref, part_ref, send_ref,
    full_ref, t_ref, grad_ref, k_ref, kt_ref, dk_ref, dv_ref, dqkv_ref,
):
    join_core(gown_ref, gpeer_ref, full_ref)
    transpose_into(load_rows(full_ref), t_ref)
    for s in range(2):
        lanes = slice(s * BLOCK, (s + 1) * BLOCK)
        dw_ref[:, s * C + 3 * BLOCK : (s + 1) * C] = dot(t_ref[...], out_ref[:, lanes]).astype(narrow)

        @pl.loop(0, PIX // CHUNK)
        def _(i):
            at = rows_of(i)
            value = dot(full_ref[at, :], w_ref[:, s * C + 3 * BLOCK : (s + 1) * C])
            grad_ref[at, lanes] = value.astype(narrow)

    dqkv = [dqkv_ref.at[:, s * 3 * BLOCK : (s + 1) * 3 * BLOCK] for s in range(2)]
    attend_back(qkv_ref, log_ref, grad_ref, k_ref, kt_ref, dk_ref, dv_ref, dqkv)
    join_core(own_ref, peer_ref, full_ref)
    transpose_into(load_rows(full_ref), t_ref)
    for s in range(2):
        lanes = slice(s * 3 * BLOCK, (s + 1) * 3 * BLOCK)
        dw_ref[:, s * C : s * C + 3 * BLOCK] = dot(t_ref[...], dqkv_ref[:, lanes]).astype(narrow)
    store = put_split(part_ref, send_ref)

    @pl.loop(0, PIX // CHUNK)
    def _(i):
        at = rows_of(i)
        value = dot_t(dqkv_ref[at, 0 : 3 * BLOCK], w_ref[:, 0 : 3 * BLOCK])
        store(i, value + dot_t(dqkv_ref[at, 3 * BLOCK :], w_ref[:, C : C + 3 * BLOCK]))


HALF_F32 = struct((PIX, HALF))
HALF_LOW = struct((PIX, HALF), narrow)
FULL_LOW = pltpu.VMEM((PIX, C), narrow)
SHIFTED = pltpu.VMEM((3, ROWS, C), narrow)
TURNED = pltpu.VMEM((C, PIX), narrow)
SWAP = [(0, 1), (1, 0)]


def core_swap(value):
    return lax.ppermute(value, "lo", SWAP)


def image_swap(value):
    return lax.ppermute(value, "hi", SWAP)


DP = ("dz", "dy")


def pick_image(value):
    hi = lax.axis_index("hi")
    kept = jnp.where(hi == 0, value[0], value[1])
    came = image_swap(jnp.where(hi == 0, value[1], value[0]))
    return jnp.where(hi == 0, jnp.concatenate([kept, came], 1), jnp.concatenate([came, kept], 1))


def join_image(value, axis):
    hi = lax.axis_index("hi")
    came = image_swap(value)
    return jnp.where(
        hi == 0, jnp.concatenate([value, came], axis), jnp.concatenate([came, value], axis)
    )


def gather_weight(shard):
    rows = lax.all_gather(shard, DP, axis=0, tiled=True)
    return lax.all_gather(rows, "hi", axis=1, tiled=True)


def scatter_grad(value):
    cols = lax.psum_scatter(value, "hi", scatter_dimension=1, tiled=True)
    return lax.psum_scatter(cols, DP, scatter_dimension=0, tiled=True).astype(single)


def chan_index():
    return lax.axis_index("hi") * 2 + lax.axis_index("lo")


def sinusoid_of(timesteps):
    half_count = TF // 2
    frequency = jnp.exp(-math.log(10000.0) * jnp.arange(half_count, dtype=single) / half_count)
    angles = timesteps.astype(single)[:, None] * frequency[None, :]
    return jnp.concatenate([jnp.cos(angles), jnp.sin(angles)], 1).astype(narrow)


def embed_forward(timesteps, classes, time_in, emb_out, emb_proj):
    times = lax.all_gather(timesteps, DP, axis=0, tiled=True)
    labels = lax.all_gather(classes, DP, axis=0, tiled=True)
    rows = time_in.shape[0]
    place = lax.axis_index(DP) * rows
    sinusoid = lax.dynamic_slice_in_dim(sinusoid_of(times), place, rows, 1)
    pre = lax.psum(dot(sinusoid, time_in), DP)
    hidden = jax.nn.silu(pre).astype(narrow)
    class_here = emb_out.shape[1] - hidden.shape[1]
    numbers = chan_index() * class_here + jnp.arange(class_here)
    onehot = (labels[:, None] == numbers[None, :]).astype(narrow)
    joined = jnp.concatenate([hidden, onehot], 1)
    embedding = lax.psum(dot_t(joined, emb_out), ("hi", "lo"))
    context = jax.nn.silu(embedding).astype(narrow)
    parts = jnp.einsum("be,lej->blj", context, emb_proj, preferred_element_type=single)
    mine = lax.psum_scatter(parts, DP, scatter_dimension=0, tiled=True)
    hi = lax.axis_index("hi")
    kept = jnp.where(hi == 0, mine[0], mine[1])
    came = image_swap(jnp.where(hi == 0, mine[1], mine[0]))
    wide = jnp.where(hi == 0, jnp.concatenate([kept, came], 1), jnp.concatenate([came, kept], 1))
    modulate = jnp.swapaxes(wide.reshape(2, HALF, 2), 1, 2)
    return modulate, (sinusoid, pre, joined, embedding, context)


def embed_backward(saved, dmod, emb_proj, emb_out):
    sinusoid, pre, joined, embedding, context = saved
    flat = jnp.swapaxes(dmod, 1, 2).reshape(2, 2 * HALF).astype(narrow)
    hi = lax.axis_index("hi")
    width = flat.shape[1] // 2
    kept = jnp.where(hi == 0, flat[:, :width], flat[:, width:])
    came = image_swap(jnp.where(hi == 0, flat[:, width:], flat[:, :width]))
    both = jnp.where(hi == 0, jnp.stack([kept, came]), jnp.stack([came, kept]))
    grads = lax.all_gather(both, DP, axis=0, tiled=True)
    proj_grad = jnp.einsum("be,blj->lej", context, grads, preferred_element_type=single)
    part = jnp.einsum("blj,lej->be", grads, emb_proj, preferred_element_type=single)
    context_grad = lax.psum(part, ("hi", "lo"))
    _, pullback = jax.vjp(jax.nn.silu, embedding)
    (embed_grad,) = pullback(context_grad)
    embed_low = embed_grad.astype(narrow)
    out_grad = jnp.einsum("be,bj->ej", embed_low, joined, preferred_element_type=single)
    joined_grad = lax.psum(dot(embed_low, emb_out[:, : pre.shape[1]]), DP)
    _, pullback = jax.vjp(jax.nn.silu, pre)
    (pre_grad,) = pullback(joined_grad)
    time_grad = jnp.einsum("bt,be->te", sinusoid, pre_grad.astype(narrow), preferred_element_type=single)
    return proj_grad, time_grad, out_grad


def res_forward(own, peer, win, wout, norm, mod):
    outs = [HALF_F32, HALF_LOW, HALF_F32, HALF_LOW]
    return call(res_kernel, outs, [FULL_LOW, SHIFTED], [own, peer, win, wout, norm, mod], "res_forward")


def res_backward(gown, gpeer, hidden, inner, norm, mod, wout, own, peer, win):
    taps = struct((9 * C, HALF), narrow)
    outs = [taps, taps, HALF_F32, HALF_LOW, struct((2, HALF)), struct((2, HALF))]
    scratch = [FULL_LOW, SHIFTED, TURNED, pltpu.VMEM((PIX, HALF), single), pltpu.VMEM((PIX, HALF), single), pltpu.VMEM((PIX, HALF), narrow)]
    return call(resback_kernel, outs, scratch, [gown, gpeer, hidden, inner, norm, mod, wout, own, peer, win], "res_backward")


def norm_step(act, x, part, recv, up, norm):
    outs = [HALF_F32, HALF_LOW, struct((2, HALF))]
    body = functools.partial(normback_kernel, act)
    return call(body, outs, [pltpu.VMEM((PIX, HALF), single)], [x, part, recv, up, norm], "norm_backward")


def entry_step(act, x, part, recv, norm):
    return call(functools.partial(entry_kernel, act), [HALF_F32, HALF_LOW], [], [x, part, recv, norm], "entry")


def network(noisy, noise, sample_weight, kernels_in, kernels_out, attn, norms, modulate):
    images = noisy.shape[0] * lax.axis_size("dz") * lax.axis_size("dy")
    total = float(images * PIX * C)
    x0 = pick_image(noisy.reshape(2, PIX, BLOCK))
    target = pick_image(noise.reshape(2, PIX, BLOCK))
    weight = jnp.where(lax.axis_index("hi") == 0, sample_weight[0], sample_weight[1])
    weight = jnp.broadcast_to(weight, (8, HALF))
    stream0, entry0 = call(first_kernel, [HALF_F32, HALF_LOW], [], [x0, norms[0]], "entry")
    peer0 = core_swap(entry0)
    inner0, hidden0, part, send = res_forward(entry0, peer0, kernels_in[0], kernels_out[0], norms[1], modulate[0])
    stream1, entry1 = entry_step(False, stream0, part, core_swap(send), norms[2])
    peer1 = core_swap(entry1)
    outs = [struct((PIX, 6 * BLOCK), narrow), struct((4, PIX // CHUNK, 1, CHUNK)), HALF_LOW, HALF_F32, HALF_LOW]
    scratch = [FULL_LOW, pltpu.VMEM((PIX, BLOCK), narrow), pltpu.VMEM((BLOCK, PIX), narrow)]
    qkv, log, attended, part, send = call(attn_kernel, outs, scratch, [entry1, peer1, attn], "attention")
    stream2, entry2 = entry_step(True, stream1, part, core_swap(send), norms[3])
    peer2 = core_swap(entry2)
    inner2, hidden2, part, send = res_forward(entry2, peer2, kernels_in[1], kernels_out[1], norms[4], modulate[1])
    stream3, entry3 = entry_step(True, stream2, part, core_swap(send), norms[5])
    peer3 = core_swap(entry3)
    taps = struct((9 * C, HALF), narrow)
    outs = [struct((1, HALF)), taps, HALF_F32, HALF_LOW]
    scratch = [FULL_LOW, SHIFTED, TURNED, pltpu.VMEM((PIX, HALF), narrow)]
    args = [entry3, peer3, kernels_in[2], target, weight]
    loss, din2, part, send = call(functools.partial(head_kernel, total), outs, scratch, args, "head")
    zero = jnp.zeros((PIX, HALF), single)
    grad3, low3, sums5 = norm_step(True, stream3, part, core_swap(send), zero, norms[5])
    dout1, din1, part, send, sums4, dmod1 = res_backward(
        low3, core_swap(low3), hidden2, inner2, norms[4], modulate[1], kernels_out[1], entry2, peer2, kernels_in[1]
    )
    grad2, low2, sums3 = norm_step(True, stream2, part, core_swap(send), grad3, norms[3])
    outs = [struct((C, 2 * C), narrow), HALF_F32, HALF_LOW]
    scratch = [
        FULL_LOW, TURNED, pltpu.VMEM((PIX, HALF), narrow), pltpu.VMEM((PIX, BLOCK), narrow), pltpu.VMEM((BLOCK, PIX), narrow),
        pltpu.VMEM((PIX, BLOCK), single), pltpu.VMEM((PIX, BLOCK), single), pltpu.VMEM((PIX, 6 * BLOCK), narrow),
    ]
    args = [low2, core_swap(low2), qkv, log, attended, attn, entry1, peer1]
    dattn, part, send = call(attnback_kernel, outs, scratch, args, "attention_backward")
    grad1, low1, sums2 = norm_step(False, stream1, part, core_swap(send), grad2, norms[2])
    dout0, din0, part, send, sums1, dmod0 = res_backward(
        low1, core_swap(low1), hidden0, inner0, norms[1], modulate[0], kernels_out[0], entry0, peer0, kernels_in[0]
    )
    _, _, sums0 = norm_step(True, stream0, part, core_swap(send), grad1, norms[0])
    sums = jnp.stack([sums0, sums1, sums2, sums3, sums4, sums5])
    return jnp.sum(loss) / total, (din0, din1, din2), (dout0, dout1), dattn, sums, jnp.stack([dmod0, dmod1])


MESH = pl.DeviceIdType.MESH
ANY = pl.BlockSpec(memory_space=pl.ANY)
LAYERS = 6
STEPS = 10


def remote(src, dst, send, recv, **where):
    return pltpu.make_async_remote_copy(
        src_ref=src, dst_ref=dst, send_sem=send, recv_sem=recv, device_id=where, device_id_type=MESH
    )


def place():
    return lax.axis_index("dz"), lax.axis_index("dy"), lax.axis_index("hi")


def greet(others):
    barrier = pltpu.get_barrier_semaphore()
    for where in others:
        pl.semaphore_signal(barrier, inc=1, device_id=where, device_id_type=MESH)
    pl.semaphore_wait(barrier, len(others))


def neighbours():
    z, y, x = place()
    others = [{"dz": (z + k) % 4} for k in (1, 2, 3)]
    return others + [{"dy": 1 - y}, {"hi": 1 - x}, {"lo": 1 - lax.axis_index("lo")}]


class Layout:
    def __init__(self, rows, lanes):
        self.rows, self.lanes = rows, lanes

    def block(self, zz, yy):
        return pl.ds(pl.multiple_of((zz * 2 + yy) * self.rows, 32), self.rows)

    def cols(self, xx):
        return pl.ds(pl.multiple_of(xx * self.lanes, 128), self.lanes)


class Gather:
    def __init__(self, layer, shard, full, send, recv, local):
        z, y, x = place()
        rows, lanes = shard.shape
        at = Layout(rows, lanes)
        mine = full.at[at.block(z, y), at.cols(x)]
        self.local = pltpu.make_async_copy(shard, mine, local.at[layer])

        def copy(j, src, dst, **where):
            return remote(src, dst, send.at[layer, j], recv.at[layer, j], **where)

        self.along_z = [copy(k - 1, shard, mine, dz=(z + k) % 4) for k in (1, 2, 3)]
        self.first, self.second = [], []
        for n in range(2):
            part = full.at[at.block(n, y), at.cols(x)]
            self.first.append(copy(3 + n, part, part, dy=1 - y))
            part = full.at[at.block(2 + n, y), at.cols(x)]
            self.first.append(copy(5 + n, part, part, hi=1 - x))
        part = full.at[0 : 4 * rows, at.cols(x)]
        self.second.append(copy(7, part, part, hi=1 - x))
        for n in range(2):
            part = full.at[at.block(2 + n, y), :]
            self.second.append(copy(8 + n, part, part, dy=1 - y))

    def start(self):
        self.local.start()
        for copy in self.along_z:
            copy.start()

    def turn(self):
        self.local.wait()
        for copy in self.along_z:
            copy.wait_recv()
        for copy in self.first:
            copy.start()

    def spread(self):
        for copy in self.first:
            copy.wait_recv()
        for copy in self.second:
            copy.start()

    def ready(self):
        for copy in self.second:
            copy.wait_recv()

    def drain(self):
        for copy in self.along_z + self.first + self.second:
            copy.wait_send()


def add_rows(count, lanes, into, other):
    size = 64 if lanes > 128 else 192

    @pl.loop(0, count // size)
    def _(i):
        at = pl.ds(pl.multiple_of(i * size, 32), size)
        total = into.at[at, :][...].astype(single) + other.at[at, :][...].astype(single)
        into.at[at, :][...] = total.astype(narrow)


class Reduce:
    def __init__(self, layer, grad, bufs, out, send, recv):
        z, y, x = place()
        ra, rb, rc, rd, rz = bufs
        rows, lanes = out.shape
        at = Layout(rows, lanes)
        self.rows, self.lanes, self.out, self.grad, self.bufs = rows, lanes, out, grad, bufs
        self.at, self.here = at, (z, y, x)

        def copy(j, src, dst, **where):
            return remote(src, dst, send.at[layer, j], recv.at[layer, j], **where)

        self.first = [copy(0, grad.at[0 : 4 * rows, at.cols(1 - x)], ra, hi=1 - x)]
        self.second, self.third = [], []
        for n in range(2):
            self.first.append(copy(1 + n, grad.at[at.block(2 + n, 1 - y), :], rb.at[n], dy=1 - y))
        for n in range(2):
            part = grad.at[at.block(n, 1 - y), at.cols(x)]
            self.second.append(copy(3 + n, part, rc.at[n], dy=1 - y))
        for n in range(2):
            part = grad.at[at.block(2 + n, y), at.cols(1 - x)]
            self.second.append(copy(5 + n, part, rd.at[n], hi=1 - x))
        for k in (1, 2, 3):
            zz = (z + k) % 4
            part = grad.at[at.block(zz, y), at.cols(x)]
            self.third.append(copy(6 + k, part, rz.at[k - 1], dz=zz))

    def start(self):
        for copy in self.first:
            copy.start()

    def turn(self):
        (z, y, x), at, (ra, rb, rc, rd, rz) = self.here, self.at, self.bufs
        self.first[0].wait_recv()
        add_rows(4 * self.rows, self.lanes, self.grad.at[0 : 4 * self.rows, at.cols(x)], ra)
        for copy in self.second[:2]:
            copy.start()
        for n in range(2):
            self.first[1 + n].wait_recv()
            add_rows(self.rows, 2 * self.lanes, self.grad.at[at.block(2 + n, y), :], rb.at[n])
            self.second[2 + n].start()

    def spread(self):
        (z, y, x), at, (ra, rb, rc, rd, rz) = self.here, self.at, self.bufs
        for n in range(2):
            self.second[n].wait_recv()
            add_rows(self.rows, self.lanes, self.grad.at[at.block(n, y), at.cols(x)], rc.at[n])
        for n in range(2):
            self.second[2 + n].wait_recv()
            add_rows(self.rows, self.lanes, self.grad.at[at.block(2 + n, y), at.cols(x)], rd.at[n])
        for copy in self.third:
            copy.start()

    def finish(self):
        (z, y, x), at, (ra, rb, rc, rd, rz) = self.here, self.at, self.bufs
        for copy in self.third:
            copy.wait_recv()
        size = 64
        mine = self.grad.at[at.block(z, y), at.cols(x)]

        @pl.loop(0, self.rows // size)
        def _(i):
            part = pl.ds(pl.multiple_of(i * size, 32), size)
            total = mine.at[part, :][...].astype(single)
            for k in range(3):
                total = total + rz.at[k, part, :][...].astype(single)
            self.out.at[part, :][...] = total

    def drain(self):
        for copy in self.first + self.second + self.third:
            copy.wait_send()


class Core:
    def __init__(self, send, recv):
        self.send, self.recv, self.used = send, recv, 0
        self.core = lax.axis_index("lo")

    def take(self, count):
        base = self.used
        self.used += count
        return base

    def copy(self, index, src, dst):
        return remote(src, dst, self.send.at[index], self.recv.at[index], lo=1 - self.core)

    def lanes(self, j):
        return pl.ds(pl.multiple_of((2 * j + self.core) * BLOCK, 128), BLOCK)

    def share(self, full):
        base = self.take(2 * (PIX // CHUNK))

        def copies(i):
            parts = [full.at[rows_of(i), self.lanes(j)] for j in range(2)]
            return [self.copy(base + 2 * i + j, part, part) for j, part in enumerate(parts)]

        def store(i, value):
            for j in range(2):
                full[rows_of(i), self.lanes(j)] = value[:, j * BLOCK : (j + 1) * BLOCK]
            for copy in copies(i):
                copy.start()

        def wait():
            @pl.loop(0, PIX // CHUNK)
            def _(i):
                for copy in copies(i):
                    copy.wait()

        return store, wait

    def combine(self, part, send, recv):
        base = self.take(PIX // CHUNK)

        def one(i):
            return self.copy(base + i, send.at[rows_of(i), :], recv.at[rows_of(i), :])

        def store(i, value):
            own, peer = split_core(value)
            part[rows_of(i), :] = own
            send[rows_of(i), :] = peer.astype(narrow)
            one(i).start()

        def wait():
            @pl.loop(0, PIX // CHUNK)
            def _(i):
                one(i).wait()

        def load(i):
            return part[rows_of(i), :] + recv[rows_of(i), :].astype(single)

        return store, wait, load


class Spill:
    def __init__(self, sems):
        self.sems, self.used, self.open = sems, 0, []

    def start(self, src, dst):
        copy = pltpu.make_async_copy(src, dst, self.sems.at[self.used])
        self.used += 1
        copy.start()
        self.open.append(copy)
        return copy

    def finish(self, copy):
        copy.wait()
        self.open = [other for other in self.open if other is not copy]

    def drain(self):
        for copy in self.open:
            copy.wait()


def forward_kernel(
    total,
    x0_ref, noise_hbm, weight_ref, norms_ref, mod_ref, s0, s1, s2, s3, s4, s5,
    w0_out, w1_out, w2_out, w3_out, w4_out, w5_out,
    full0_out, full1_out, full2_out, full3_out, x1_out, x2_out, x3_out,
    inner0_out, inner2_out, hidden0_out, hidden2_out, qkv_out, att_out, pg_out, log_ref, loss_ref,
    w0, w1, w2, w3, w4, w5,
    full0, full1, full2, full3, x1, x2, x3, inner0, inner2, hidden0, hidden2, qkv, att, pg, noise_ref,
    shifted, part, send0, send1, send2, recv0, recv1, recv2, k_ref, vt_ref,
    gsend, grecv, glocal, csend, crecv, lsem,
):
    greet(neighbours())
    gathers = [
        Gather(n, shard, full, gsend, grecv, glocal)
        for n, (shard, full) in enumerate(zip((s0, s1, s2, s3, s4, s5), (w0, w1, w2, w3, w4, w5)))
    ]
    for gather in gathers:
        gather.start()
    spill, core = Spill(lsem), Core(csend, crecv)
    noise_here = spill.start(noise_hbm, noise_ref)

    def norm_row(n):
        return norms_ref[n, 0:1, :], norms_ref[n, 1:2, :]

    class First:
        def __getitem__(self, at):
            return x0_ref[at].astype(single)

    def entry(x, n, act, full):
        gain, bias = norm_row(n)
        store, wait = core.share(full)
        norm_forward(x, gain, bias, act, store)
        return wait

    def residual(full, w_in, w_out, ready, n, layer, inner, hidden, send, recv):
        shift_full(full, shifted, C)

        def put(i, value):
            inner[rows_of(i), :] = value

        conv_wide(shifted, w_in, put)
        gain, bias = norm_row(n)
        scale, shift = 1.0 + mod_ref[layer, 0:1, :], mod_ref[layer, 1:2, :]

        def keep(i, value):
            hidden[rows_of(i), :] = value

        norm_forward(inner, gain * scale, bias * scale + shift, True, keep)
        shift_full(hidden, shifted, HALF)
        ready()
        store, wait, load = core.combine(part, send, recv)
        conv_tall(shifted, w_out, 1, store)
        return wait, load

    def advance(x_old, load, x_new):
        @pl.loop(0, PIX // CHUNK)
        def _(i):
            x_new[rows_of(i), :] = x_old[rows_of(i), :] + load(i)

    def after(n, copies):
        gathers[n].ready()
        spill.start(copies[0], copies[1])

    wait = entry(First(), 0, True, full0)
    gathers[0].turn()
    gathers[1].turn()
    gathers[0].spread()
    gathers[2].turn()
    gathers[1].spread()
    wait()
    spill.start(full0, full0_out)
    after(0, (w0, w0_out))

    def ready1():
        gathers[3].turn()
        gathers[2].spread()
        after(1, (w1, w1_out))

    wait, load = residual(full0, w0, w1, ready1, 1, 0, inner0, hidden0, send0, recv0)
    spill.start(inner0, inner0_out)
    spill.start(hidden0, hidden0_out)
    wait()
    advance(First(), load, x1)
    spill.start(x1, x1_out)
    wait = entry(x1, 2, False, full1)
    gathers[4].turn()
    gathers[3].spread()
    after(2, (w2, w2_out))
    wait()
    spill.start(full1, full1_out)

    @pl.loop(0, PIX // CHUNK)
    def _(i):
        at = rows_of(i)
        for s in range(2):
            value = dot(full1[at, :], w2[:, s * C : s * C + 3 * BLOCK])
            qkv[at, s * 3 * BLOCK : (s + 1) * 3 * BLOCK] = value.astype(narrow)

    spill.start(qkv, qkv_out)
    attend(qkv, k_ref, vt_ref, log_ref, att)
    spill.start(att, att_out)
    gathers[5].turn()
    gathers[4].spread()
    store, wait, load = core.combine(part, send1, recv1)

    @pl.loop(0, PIX // CHUNK)
    def _(i):
        at = rows_of(i)
        value = dot_t(att[at, 0:BLOCK], w2[:, 3 * BLOCK : C])
        store(i, value + dot_t(att[at, BLOCK:], w2[:, C + 3 * BLOCK :]))

    wait()
    advance(x1, load, x2)
    spill.start(x2, x2_out)
    wait = entry(x2, 3, True, full2)
    after(3, (w3, w3_out))
    wait()
    spill.start(full2, full2_out)

    def ready4():
        gathers[5].spread()
        after(4, (w4, w4_out))

    wait, load = residual(full2, w3, w4, ready4, 4, 1, inner2, hidden2, send2, recv2)
    spill.start(inner2, inner2_out)
    spill.start(hidden2, hidden2_out)
    wait()
    advance(x2, load, x3)
    spill.start(x3, x3_out)
    wait = entry(x3, 5, True, full3)
    after(5, (w5, w5_out))
    wait()
    spill.start(full3, full3_out)
    shift_full(full3, shifted, C)
    spill.finish(noise_here)
    loss_ref[...] = jnp.zeros_like(loss_ref)

    def store(i, value):
        error = value - noise_ref[rows_of(i), :]
        weight = weight_ref[0:1, :]
        loss_ref[...] += jnp.sum(weight * error * error, 0, keepdims=True)
        pg[rows_of(i), :] = (2.0 * weight * error / total).astype(narrow)

    conv_wide(shifted, w5, store)
    spill.start(pg, pg_out)
    for gather in gathers:
        gather.drain()
    spill.drain()


def backward_kernel(
    norms_ref, mod_ref, log_ref,
    x0_hbm, w0_hbm, w1_hbm, w2_hbm, w3_hbm, w4_hbm, w5_hbm,
    full0_hbm, full1_hbm, full2_hbm, full3_hbm, x1_hbm, x2_hbm, x3_hbm,
    inner0_hbm, inner2_hbm, hidden0_hbm, hidden2_hbm, qkv_hbm, att_hbm, pg_hbm,
    g0, g1, g2, g3, g4, g5, sums_ref, dmod_ref,
    wa, wb, wattn, d0, d1, d2, d3, d4, d5,
    ra, rb, rc, rd, rz, qa, qb, qc, qd, qz,
    gfull3, gfull2, gfull1, entry, x_ref, x0_ref, inner, hidden, qkv, att, pg,
    shifted, turned, tmp, dh, part, up, send, recv0, recv1, recv2, recv3,
    k_ref, kt_ref, dk_ref, dv_ref,
    rsend, rrecv, csend, crecv, lsem,
):
    spill, core = Spill(lsem), Core(csend, crecv)
    load_w5 = spill.start(w5_hbm, wa)
    load_w4 = spill.start(w4_hbm, wb)
    load_pg = spill.start(pg_hbm, pg)
    load_entry = spill.start(full3_hbm, entry)
    load_x = spill.start(x3_hbm, x_ref)
    load_hidden = spill.start(hidden2_hbm, hidden)
    load_inner = spill.start(inner2_hbm, inner)
    load_qkv = spill.start(qkv_hbm, qkv)
    load_att = spill.start(att_hbm, att)
    load_attn = spill.start(w2_hbm, wattn)
    load_x0 = spill.start(x0_hbm, x0_ref)
    greet(neighbours())
    grads = [d0, d1, d2, d3, d4, d5]
    outs = [g0, g1, g2, g3, g4, g5]
    slots = {0: 0, 1: 1, 3: 2, 4: 3, 5: 4}
    reduces = []
    for n in range(LAYERS):
        bufs = (qa, qb, qc, qd, qz) if n == 2 else tuple(buf.at[slots[n]] for buf in (ra, rb, rc, rd, rz))
        reduces.append(Reduce(n, grads[n], bufs, outs[n], rsend, rrecv))

    def norm_row(n):
        return norms_ref[n, 0:1, :], norms_ref[n, 1:2, :]

    def keep_taps(grad):
        def keep(t, value):
            grad[t * C : (t + 1) * C, :] = value.astype(narrow)

        return keep

    def wide(w, grad, n, recv):
        shift_full(pg, shifted, HALF)
        transpose_into(load_rows(entry), turned)
        kernel_grad(turned, shifted, -1, keep_taps(grad))
        reduces[n].start()
        store, wait, load = core.combine(part, send, recv)
        conv_tall(shifted, w, -1, store)
        return wait, load

    def through_norm(x, load, n, act, first, gfull):
        gain, bias = norm_row(n)
        if gfull is not None:
            share, wait = core.share(gfull)
        else:
            share, wait = None, None

        def store(i, value):
            if share is None:
                return
            if not first:
                value = value + up[rows_of(i), :]
            up[rows_of(i), :] = value
            share(i, value.astype(narrow))

        summed, along = norm_backward(x, load, gain, bias, act, tmp, store)
        sums_ref[n, 0:1, :] = along
        sums_ref[n, 1:2, :] = summed
        return wait

    def residual(gfull, w_out, n_out, n_norm, layer):
        transpose_into(load_rows(gfull), turned)
        shift_full(hidden, shifted, HALF)
        kernel_grad(turned, shifted, 1, keep_taps(grads[n_out]))
        reduces[n_out].start()
        shift_full(gfull, shifted, C)

        def put(i, value):
            dh[rows_of(i), :] = value

        conv_back(shifted, w_out, put)
        gain, bias = norm_row(n_norm)
        scale, shift = 1.0 + mod_ref[layer, 0:1, :], mod_ref[layer, 1:2, :]

        def store(i, value):
            pg[rows_of(i), :] = value.astype(narrow)

        summed, along = norm_backward(inner, load_rows(dh), gain * scale, bias * scale + shift, True, tmp, store)
        sums_ref[n_norm, 0:1, :] = scale * along
        sums_ref[n_norm, 1:2, :] = scale * summed
        dmod_ref[layer, 0:1, :] = gain * along + bias * summed
        dmod_ref[layer, 1:2, :] = summed

    done = spill.finish
    done(load_pg)
    done(load_entry)
    done(load_w5)
    wait, load = wide(wa, d5, 5, recv0)
    load_w3 = spill.start(w3_hbm, wa)
    load_entry = spill.start(full2_hbm, entry)
    done(load_x)
    wait()
    wait = through_norm(x_ref, load, 5, True, True, gfull3)
    load_x = spill.start(x2_hbm, x_ref)
    reduces[5].turn()
    wait()
    done(load_hidden)
    done(load_inner)
    done(load_w4)
    residual(gfull3, wb, 4, 4, 1)
    load_hidden = spill.start(hidden0_hbm, hidden)
    load_inner = spill.start(inner0_hbm, inner)
    load_w1 = spill.start(w1_hbm, wb)
    reduces[5].spread()
    done(load_entry)
    done(load_w3)
    wait, load = wide(wa, d3, 3, recv1)
    load_w0 = spill.start(w0_hbm, wa)
    load_entry = spill.start(full1_hbm, entry)
    reduces[4].turn()
    done(load_x)
    wait()
    wait = through_norm(x_ref, load, 3, True, False, gfull2)
    load_x = spill.start(x1_hbm, x_ref)
    reduces[3].turn()
    reduces[4].spread()
    reduces[5].finish()
    wait()
    done(load_qkv)
    done(load_att)
    done(load_attn)
    transpose_into(load_rows(gfull2), turned)
    for s in range(2):
        lanes = slice(s * BLOCK, (s + 1) * BLOCK)
        d2[:, s * C + 3 * BLOCK : (s + 1) * C] = dot(turned[...], att[:, lanes]).astype(narrow)

        @pl.loop(0, PIX // CHUNK)
        def _(i):
            at = rows_of(i)
            value = dot(gfull2[at, :], wattn[:, s * C + 3 * BLOCK : (s + 1) * C])
            pg[at, lanes] = value.astype(narrow)

    dqkv = [shifted.at[s, 0:PIX, 0 : 3 * BLOCK] for s in range(2)]
    attend_back(qkv, log_ref, pg, k_ref, kt_ref, dk_ref, dv_ref, dqkv)
    done(load_entry)
    transpose_into(load_rows(entry), turned)
    for s in range(2):
        d2[:, s * C : s * C + 3 * BLOCK] = dot(turned[...], dqkv[s][...]).astype(narrow)
    reduces[2].start()
    store, wait, load = core.combine(part, send, recv2)

    @pl.loop(0, PIX // CHUNK)
    def _(i):
        at = rows_of(i)
        value = dot_t(dqkv[0].at[at, :][...], wattn[:, 0 : 3 * BLOCK])
        store(i, value + dot_t(dqkv[1].at[at, :][...], wattn[:, C : C + 3 * BLOCK]))

    load_entry = spill.start(full0_hbm, entry)
    done(load_x)
    wait()
    wait = through_norm(x_ref, load, 2, False, False, gfull1)
    reduces[3].spread()
    reduces[2].turn()
    reduces[4].finish()
    wait()
    done(load_hidden)
    done(load_inner)
    done(load_w1)
    residual(gfull1, wb, 1, 1, 0)
    reduces[2].spread()
    reduces[3].finish()
    done(load_entry)
    done(load_w0)
    wait, load = wide(wa, d0, 0, recv3)
    reduces[1].turn()
    reduces[2].finish()
    wait()
    done(load_x0)

    class First:
        def __getitem__(self, at):
            return x0_ref[at].astype(single)

    through_norm(First(), load, 0, True, False, None)
    reduces[0].turn()
    reduces[1].spread()
    reduces[0].spread()
    reduces[1].finish()
    reduces[0].finish()
    for reduce in reduces:
        reduce.drain()
    spill.drain()


def vmem(shape, dtype=single):
    return pltpu.VMEM(shape, dtype)


def semaphores(*shape):
    return pltpu.SemaphoreType.DMA(shape)


TAPS_SHAPE = (9 * C, HALF)
ATTN_SHAPE = (C, 2 * C)
FULL = (PIX, C)
OWN = (PIX, HALF)
QKV = (PIX, 6 * BLOCK)
LOGS = (4, PIX // CHUNK, 1, CHUNK)
WEIGHTS = [TAPS_SHAPE, TAPS_SHAPE, ATTN_SHAPE, TAPS_SHAPE, TAPS_SHAPE, TAPS_SHAPE]


def fused(body, outs, out_specs, in_specs, scratch, args, number, limit, name):
    return pl.pallas_call(
        body,
        out_shape=outs,
        in_specs=in_specs,
        out_specs=out_specs,
        scratch_shapes=scratch,
        compiler_params=pltpu.CompilerParams(
            vmem_limit_bytes=limit * 2**20, collective_id=number, has_side_effects=True
        ),
        name=name,
    )(*args)


def fused_network(noisy, noise, sample_weight, shards, norms, modulate):
    images = noisy.shape[0] * lax.axis_size("dz") * lax.axis_size("dy")
    total = float(images * PIX * C)
    x0 = pick_image(noisy.reshape(2, PIX, BLOCK))
    target = pick_image(noise.reshape(2, PIX, BLOCK))
    weight = jnp.where(lax.axis_index("hi") == 0, sample_weight[0], sample_weight[1])
    weight = jnp.broadcast_to(weight, (8, HALF))
    low_shapes = WEIGHTS + [FULL] * 4
    kept = [struct(s, narrow) for s in low_shapes] + [struct(OWN)] * 5
    kept += [struct(OWN, narrow)] * 2 + [struct(QKV, narrow)] + [struct(OWN, narrow)] * 2
    outs = kept + [struct(LOGS), struct((1, HALF))]
    scratch = [vmem(s, narrow) for s in low_shapes] + [vmem(OWN)] * 5
    scratch += [vmem(OWN, narrow)] * 2 + [vmem(QKV, narrow)] + [vmem(OWN, narrow)] * 2 + [vmem(OWN)]
    scratch += [vmem((3, ROWS, C), narrow), vmem(OWN)] + [vmem(OWN, narrow)] * 6
    scratch += [vmem((PIX, BLOCK), narrow), vmem((BLOCK, PIX), narrow)]
    scratch += [semaphores(LAYERS, STEPS)] * 2 + [semaphores(LAYERS), semaphores(48), semaphores(48), semaphores(32)]
    args = [x0, target, weight, norms, modulate, *shards]
    in_specs = [VMEM, ANY, VMEM, VMEM, VMEM] + [ANY] * 6
    body = functools.partial(forward_kernel, total)
    out_specs = [ANY] * len(kept) + [VMEM] * 2
    results = fused(body, outs, out_specs, in_specs, scratch, args, 1, 56, "forward")
    w0, w1, w2, w3, w4, w5, *acts, log, loss = results
    outs = [struct(shard.shape) for shard in shards] + [struct((6, 2, HALF)), struct((2, 2, HALF))]
    scratch = [vmem(TAPS_SHAPE, narrow)] * 2 + [vmem(ATTN_SHAPE, narrow)] + [vmem(s, narrow) for s in WEIGHTS]
    for lead, (rows, lanes) in ((5, shards[0].shape), (None, shards[2].shape)):
        shapes = [(4 * rows, lanes), (2, rows, 2 * lanes), (2, rows, lanes), (2, rows, lanes), (3, rows, lanes)]
        scratch += [vmem(s if lead is None else (lead, *s), narrow) for s in shapes]
    scratch += [vmem(FULL, narrow)] * 4 + [vmem(OWN), vmem(OWN, narrow), vmem(OWN), vmem(OWN, narrow)]
    scratch += [vmem(QKV, narrow), vmem(OWN, narrow), vmem(OWN, narrow)]
    scratch += [vmem((3, ROWS, C), narrow), vmem((C, PIX), narrow)] + [vmem(OWN)] * 4 + [vmem(OWN, narrow)] * 5
    scratch += [vmem((PIX, BLOCK), narrow), vmem((BLOCK, PIX), narrow)] + [vmem((PIX, BLOCK))] * 2
    scratch += [semaphores(LAYERS, STEPS)] * 2 + [semaphores(48), semaphores(48), semaphores(32)]
    args = [norms, modulate, log, x0, w0, w1, w2, w3, w4, w5, *acts]
    in_specs = [VMEM] * 3 + [ANY] * (len(args) - 3)
    *grads, sums, dmod = fused(
        backward_kernel, outs, [VMEM] * len(outs), in_specs, scratch, args, 2, 62, "backward"
    )
    return jnp.sum(loss) / total, grads, sums, dmod


def pack_flat(members):
    return jnp.concatenate([member.reshape(-1) for member in members])


def unpack_flat(vector, shape_list):
    pieces = []
    offset = 0
    for array_shape in shape_list:
        extent = math.prod(array_shape)
        pieces.append(vector[offset : offset + extent].reshape(array_shape))
        offset += extent
    return pieces


def per_device(
    noisy,
    noise,
    timesteps,
    classes,
    sample_weight,
    conv_in,
    conv_out,
    emb_proj,
    attn_weight,
    time_in,
    emb_out,
    norms,
    conv_in_rows,
    conv_in_cols,
    conv_out_rows,
    conv_out_cols,
    emb_proj_rows,
    emb_proj_cols,
    attn_rows,
    attn_cols,
    time_rows,
    time_cols,
    embout_rows,
    embout_cols,
    norm_second,
):
    masters = [conv_in, conv_out, emb_proj, attn_weight[None], time_in[None], emb_out[None]]
    lowered = [master.astype(narrow) for master in masters]
    modulate, saved = embed_forward(timesteps, classes, lowered[4][0], lowered[5][0], lowered[2])
    norms_wide = join_image(norms, 2)
    shards = [lowered[0][0], lowered[1][0], lowered[3][0], lowered[0][1], lowered[1][1], lowered[0][2]]
    if lax.axis_size("dz") == 4 and shards[0].shape[0] % 64 == 0 and shards[2].shape[0] % 64 == 0:
        loss_part, reduced_parts, sums, dmod = fused_network(
            noisy, noise, sample_weight, shards, norms_wide, modulate
        )
    else:
        full = [gather_weight(shard) for shard in shards]
        loss_part, din, dout, dattn, sums, dmod = network(
            noisy, noise, sample_weight, (full[0], full[3], full[5]), (full[1], full[4]), full[2], norms_wide, modulate
        )
        reduced_parts = [scatter_grad(part) for part in (din[0], dout[0], dattn, din[1], dout[1], din[2])]
    in0_grad, out0_grad, attn_grad, in1_grad, out1_grad, head_grad = reduced_parts
    proj_grad, time_grad, embout_grad = embed_backward(saved, dmod, lowered[2], lowered[5][0])
    norm_local = lax.psum_scatter(sums, "hi", scatter_dimension=2, tiled=True)
    reduced = [
        jnp.stack([in0_grad, in1_grad, head_grad]),
        jnp.stack([out0_grad, out1_grad]),
        proj_grad,
        attn_grad[None],
        time_grad[None],
        embout_grad[None],
    ]
    decay_rate = 1.0 - STEP ** (-0.8)
    dp_count = lax.axis_size("dz") * lax.axis_size("dy")
    chan_count = lax.axis_size("hi") * lax.axis_size("lo")
    rows_old = [
        conv_in_rows,
        conv_out_rows,
        emb_proj_rows,
        attn_rows[None],
        time_rows[None],
        embout_rows[None],
    ]
    cols_old = [
        conv_in_cols,
        conv_out_cols,
        emb_proj_cols,
        attn_cols[None],
        time_cols[None],
        embout_cols[None],
    ]
    squares = [gradient * gradient + tiny_square for gradient in reduced]
    full_rows = [squared.shape[1] * dp_count for squared in squares]
    full_cols = [squared.shape[2] * chan_count for squared in squares]
    row_parts = [jnp.sum(squared, 2) for squared in squares]
    col_parts = [jnp.sum(squared, 1) for squared in squares]
    row_shapes = [member.shape for member in row_parts]
    col_shapes = [member.shape for member in col_parts]
    norm_width = norm_local.shape[2]
    row_totals = unpack_flat(lax.psum(pack_flat(row_parts), ("hi", "lo")), row_shapes)
    rows_new = [
        decay_rate * rows_old[position]
        + (1.0 - decay_rate) * row_totals[position] / full_cols[position]
        for position in range(6)
    ]
    row_sums_local = [jnp.sum(member, 1) for member in rows_new]
    col_vector, norm_total = lax.psum((pack_flat(col_parts + row_sums_local), norm_local), DP)
    col_pieces = unpack_flat(col_vector, col_shapes + [(member.shape[0],) for member in rows_new])
    col_totals = col_pieces[:6]
    row_means = [col_pieces[6 + position] / full_rows[position] for position in range(6)]
    cols_new = [
        decay_rate * cols_old[position]
        + (1.0 - decay_rate) * col_totals[position] / full_rows[position]
        for position in range(6)
    ]
    updates = [
        reduced[position]
        * lax.rsqrt(rows_new[position] / row_means[position][:, None])[:, :, None]
        * lax.rsqrt(cols_new[position])[:, None, :]
        for position in range(6)
    ]
    second_new = decay_rate * norm_second + (1.0 - decay_rate) * (
        norm_total * norm_total + tiny_square
    )
    norm_update = norm_total * lax.rsqrt(second_new)
    update_squares = pack_flat([jnp.sum(member * member, (1, 2)) for member in updates])
    weight_squares = pack_flat([jnp.sum(master * master, (1, 2)) for master in masters])
    norm_update_sq = jnp.sum(norm_update * norm_update, 2) / dp_count
    norm_weight_sq = jnp.sum(norms * norms, 2) / dp_count
    update_total, weight_total, norm_update_total, norm_weight_total, loss = lax.psum(
        (update_squares, weight_squares, norm_update_sq, norm_weight_sq, loss_part), ("dz", "dy", "hi", "lo")
    )
    layer_shapes = [(member.shape[0],) for member in masters]
    update_sums = unpack_flat(update_total, layer_shapes)
    weight_sums = unpack_flat(weight_total, layer_shapes)
    results = [loss]
    for position in range(6):
        entries = float(full_rows[position] * full_cols[position])
        clip_factor = jnp.maximum(1.0, jnp.sqrt(update_sums[position] / entries))
        scale_factor = jnp.maximum(floor_scale, jnp.sqrt(weight_sums[position] / entries))
        weight_new = (
            masters[position]
            - (step_rate * scale_factor / clip_factor)[:, None, None] * updates[position]
        )
        if position >= 3:
            results += [
                reduced[position][0],
                rows_new[position][0],
                cols_new[position][0],
                weight_new[0],
            ]
        else:
            results += [reduced[position], rows_new[position], cols_new[position], weight_new]
    norm_entries = float(norm_width * chan_count)
    norm_clip = jnp.maximum(1.0, jnp.sqrt(norm_update_total / norm_entries))
    norm_scale = jnp.maximum(floor_scale, jnp.sqrt(norm_weight_total / norm_entries))
    norms_new = norms - (step_rate * norm_scale / norm_clip)[:, :, None] * norm_update
    results += [norm_total, second_new, norms_new]
    return (
        results[0],
        results[1],
        results[2],
        results[3],
        results[4],
        results[5],
        results[6],
        results[7],
        results[8],
        results[9],
        results[10],
        results[11],
        results[12],
        results[13],
        results[14],
        results[15],
        results[16],
        results[17],
        results[18],
        results[19],
        results[20],
        results[21],
        results[22],
        results[23],
        results[24],
        results[25],
        results[26],
        results[27],
    )


CHAN = ("hi", "lo")


def solution(mesh):
    dp, chan = mesh.shape["dp"], mesh.shape["chan"]
    mesh = Mesh(mesh.devices.reshape(dp // 2, 2, 2, chan // 2), DP + CHAN)
    in_specs = (
        P(DP, None, None, CHAN),
        P(DP, None, None, CHAN),
        P(DP),
        P(DP),
        P(DP),
        P(None, DP, CHAN),
        P(None, DP, CHAN),
        P(None, DP, CHAN),
        P(DP, CHAN),
        P(DP, CHAN),
        P(DP, CHAN),
        P(None, None, CHAN),
        P(None, DP),
        P(None, CHAN),
        P(None, DP),
        P(None, CHAN),
        P(None, DP),
        P(None, CHAN),
        P(DP),
        P(CHAN),
        P(DP),
        P(CHAN),
        P(DP),
        P(CHAN),
        P(None, None, CHAN),
    )
    out_specs = (
        P(),
        P(None, DP, CHAN),
        P(None, DP),
        P(None, CHAN),
        P(None, DP, CHAN),
        P(None, DP, CHAN),
        P(None, DP),
        P(None, CHAN),
        P(None, DP, CHAN),
        P(None, DP, CHAN),
        P(None, DP),
        P(None, CHAN),
        P(None, DP, CHAN),
        P(DP, CHAN),
        P(DP),
        P(CHAN),
        P(DP, CHAN),
        P(DP, CHAN),
        P(DP),
        P(CHAN),
        P(DP, CHAN),
        P(DP, CHAN),
        P(DP),
        P(CHAN),
        P(DP, CHAN),
        P(None, None, CHAN),
        P(None, None, CHAN),
        P(None, None, CHAN),
    )
    return jax.shard_map(
        per_device, mesh=mesh, in_specs=in_specs, out_specs=out_specs, check_vma=False
    )
```

```python
import functools
import math

import jax
import jax.numpy as jnp
from jax import lax
from jax.experimental import pallas as pl
from jax.experimental.pallas import tpu as pltpu
from jax.sharding import Mesh
from jax.sharding import PartitionSpec as P

C = 512
HEADS = 8
GROUPS = 32
TF = 256
STEP = 10
SIDE = 32
PIX = 1024
HALF = 256
BLOCK = 128
PAD = SIDE
ROWS = PIX + 2 * PAD
CHUNK = 256

single = jnp.float32
narrow = jnp.bfloat16
step_rate = 0.5
floor_scale = 0.001
tiny_square = 1e-30
norm_eps = 1e-05

TAPS = [(t // 3 - 1, t % 3 - 1) for t in range(9)]


def dot(a, b):
    return jnp.dot(a, b, preferred_element_type=single)


def dot_t(a, b):
    return lax.dot_general(a, b, (((1,), (1,)), ((), ())), preferred_element_type=single)


def group_sum(row):
    lane = lax.broadcasted_iota(jnp.int32, (HALF, HALF), 0)
    other = lax.broadcasted_iota(jnp.int32, (HALF, HALF), 1)
    size = C // GROUPS
    ones = jnp.where(lane // size == other // size, 1.0, 0.0).astype(single)
    tall = jnp.broadcast_to(row, (8, HALF))
    return jnp.dot(tall, ones, precision=lax.Precision.HIGHEST, preferred_element_type=single)[0:1]


def loop_sum(count, make):
    zeros = make(None)

    def body(i, carried):
        return [old + new for old, new in zip(carried, make(i))]

    return lax.fori_loop(0, count, body, [jnp.zeros((1, HALF), single)] * zeros)


def rows_of(i, size=CHUNK, offset=0):
    return pl.ds(pl.multiple_of(offset + i * size, 32), size)


def stats(x_ref):
    members = float(PIX * (C // GROUPS))

    def first(i):
        if i is None:
            return 1
        return [jnp.sum(x_ref[rows_of(i), :], 0, keepdims=True)]

    (total,) = loop_sum(PIX // CHUNK, first)
    mean = group_sum(total) / members

    def second(i):
        if i is None:
            return 1
        center = x_ref[rows_of(i), :] - mean
        return [jnp.sum(center * center, 0, keepdims=True)]

    (square,) = loop_sum(PIX // CHUNK, second)
    rstd = lax.rsqrt(group_sum(square) / members + norm_eps)
    return mean, rstd


def sigmoid(v):
    return 1.0 / (1.0 + jnp.exp(-v))


def norm_forward(x_ref, gain, bias, act, store):
    mean, rstd = stats(x_ref)

    @pl.loop(0, PIX // CHUNK)
    def _(i):
        value = (x_ref[rows_of(i), :] - mean) * rstd * gain + bias
        if act:
            value = value * sigmoid(value)
        store(i, value.astype(narrow))


def norm_backward(x_ref, load_grad, gain, bias, act, tmp_ref, store):
    mean, rstd = stats(x_ref)
    members = float(PIX * (C // GROUPS))

    def first(i):
        if i is None:
            return 2
        hat = (x_ref[rows_of(i), :] - mean) * rstd
        grad = load_grad(i)
        if act:
            mixed = hat * gain + bias
            gate = sigmoid(mixed)
            grad = grad * gate * (1.0 + mixed * (1.0 - gate))
        tmp_ref[rows_of(i), :] = grad
        return [jnp.sum(grad, 0, keepdims=True), jnp.sum(grad * hat, 0, keepdims=True)]

    total, along = loop_sum(PIX // CHUNK, first)
    mean_grad = group_sum(gain * total) / members
    mean_along = group_sum(gain * along) / members

    @pl.loop(0, PIX // CHUNK)
    def _(i):
        hat = (x_ref[rows_of(i), :] - mean) * rstd
        store(i, rstd * (tmp_ref[rows_of(i), :] * gain - mean_grad - hat * mean_along))

    return total, along


def shifts(load, s_ref, width):
    for b in range(3):
        s_ref[b, 0:PAD, 0:width] = jnp.zeros((PAD, width), narrow)
        s_ref[b, PAD + PIX : ROWS, 0:width] = jnp.zeros((PAD, width), narrow)
    size = 128

    @pl.loop(0, PIX // size)
    def _(i):
        value = load(i, size)
        wide = value.astype(single)
        across = lax.broadcasted_iota(jnp.int32, wide.shape, 0) % SIDE
        left = jnp.where(across > 0, pltpu.roll(wide, 1, 0), 0.0)
        right = jnp.where(across < SIDE - 1, pltpu.roll(wide, size - 1, 0), 0.0)
        at = rows_of(i, size, PAD)
        s_ref[0, at, 0:width] = left.astype(narrow)
        s_ref[1, at, 0:width] = value
        s_ref[2, at, 0:width] = right.astype(narrow)


def tap_rows(s_ref, t, sign, i, size, width):
    a, b = TAPS[t]
    return s_ref[sign * b + 1, rows_of(i, size, PAD + sign * a * SIDE), 0:width]


def split_core(value):
    core = lax.axis_index("lo")
    b0, b1, b2, b3 = [value[:, k * BLOCK : (k + 1) * BLOCK] for k in range(4)]
    even, odd = jnp.concatenate([b0, b2], 1), jnp.concatenate([b1, b3], 1)
    first = core == 0
    return jnp.where(first, even, odd), jnp.where(first, odd, even)


def join_core(own_ref, peer_ref, full_ref):
    core = lax.axis_index("lo")

    @pl.loop(0, PIX // CHUNK)
    def _(i):
        at = rows_of(i)
        own, peer = own_ref[at, :].astype(single), peer_ref[at, :].astype(single)
        even = jnp.where(core == 0, own, peer).astype(narrow)
        odd = jnp.where(core == 0, peer, own).astype(narrow)
        full_ref[at, 0:BLOCK] = even[:, 0:BLOCK]
        full_ref[at, BLOCK : 2 * BLOCK] = odd[:, 0:BLOCK]
        full_ref[at, 2 * BLOCK : 3 * BLOCK] = even[:, BLOCK:]
        full_ref[at, 3 * BLOCK :] = odd[:, BLOCK:]


def conv_wide(s_ref, w_ref, store):
    @pl.loop(0, PIX // CHUNK)
    def _(i):
        total = None
        for t in range(9):
            part = dot(tap_rows(s_ref, t, 1, i, CHUNK, C), w_ref[t * C : (t + 1) * C, :])
            total = part if total is None else total + part
        store(i, total)


def conv_tall(s_ref, w_ref, sign, store):
    @pl.loop(0, PIX // CHUNK)
    def _(i):
        total = None
        for t in range(9):
            part = dot_t(tap_rows(s_ref, t, sign, i, CHUNK, HALF), w_ref[t * C : (t + 1) * C, :])
            total = part if total is None else total + part
        store(i, total)


def conv_back(s_ref, w_ref, store):
    @pl.loop(0, PIX // CHUNK)
    def _(i):
        total = None
        for t in range(9):
            part = dot(tap_rows(s_ref, t, -1, i, CHUNK, C), w_ref[t * C : (t + 1) * C, :])
            total = part if total is None else total + part
        store(i, total)


def transpose_into(load, t_ref):
    for i in range(PIX // CHUNK):
        t_ref[:, i * CHUNK : (i + 1) * CHUNK] = jnp.transpose(load(i).astype(single)).astype(narrow)


def kernel_grad(t_ref, s_ref, sign, store):
    for t in range(9):
        a, b = TAPS[t]
        start = PAD + sign * a * SIDE
        store(t, dot(t_ref[...], s_ref[sign * b + 1, start : start + PIX, 0:HALF]))


def low_lanes(shape):
    return lax.broadcasted_iota(jnp.int32, shape, 1) < BLOCK // 2


def swap_halves(value):
    half = BLOCK // 2
    return jnp.concatenate([value[:, half:], value[:, :half]], 1)


def mask_half(value, upper):
    low = low_lanes(value.shape)
    return jnp.where(low != upper, value.astype(single), 0.0).astype(narrow)


def head_parts(qkv_ref, s, h):
    base = 3 * BLOCK * s
    b0, b1, b2 = [slice(base + k * BLOCK, base + (k + 1) * BLOCK) for k in range(3)]
    return (b0, b0, b1) if h == 0 else (b1, b2, b2)


SCALE = (C // HEADS) ** (-0.5)


def attend(qkv_ref, k_ref, vt_ref, log_ref, out_ref):
    for s in range(2):
        for h in range(2):
            q_at, k_at, v_at = head_parts(qkv_ref, s, h)
            k_ref[...] = swap_halves(qkv_ref[:, k_at])
            vt_ref[...] = jnp.transpose(qkv_ref[:, v_at].astype(single)).astype(narrow)

            @pl.loop(0, PIX // CHUNK)
            def _(i):
                query = mask_half(qkv_ref[rows_of(i), q_at], h == 1)
                scores = dot_t(k_ref[...], query) * SCALE
                top = jnp.max(scores, 0, keepdims=True)
                exponent = jnp.exp(scores - top)
                total = jnp.sum(exponent, 0, keepdims=True)
                mixed = dot(vt_ref[...], exponent.astype(narrow)) / total
                log_ref[2 * s + h, i] = top + jnp.log(total)
                turned = jnp.transpose(mixed)
                at = rows_of(i)
                lanes = slice(s * BLOCK, (s + 1) * BLOCK)
                if h == 0:
                    out_ref[at, lanes] = turned.astype(narrow)
                else:
                    kept = out_ref[at, lanes].astype(single)
                    out_ref[at, lanes] = jnp.where(low_lanes(turned.shape), kept, turned).astype(narrow)


def attend_back(qkv_ref, log_ref, grad_ref, k_ref, kt_ref, dk_ref, dv_ref, dqkv):
    for s in range(2):
        lanes = slice(s * BLOCK, (s + 1) * BLOCK)
        for h in range(2):
            q_at, k_at, v_at = head_parts(qkv_ref, s, h)
            q_to, k_to, v_to = head_parts(None, 0, h)
            grad_to = dqkv[s]
            k_ref[...] = swap_halves(qkv_ref[:, k_at])
            kt_ref[...] = jnp.transpose(k_ref[...].astype(single)).astype(narrow)
            dk_ref[...] = jnp.zeros_like(dk_ref)
            dv_ref[...] = jnp.zeros_like(dv_ref)

            @pl.loop(0, PIX // CHUNK)
            def _(i):
                at = rows_of(i)
                query = mask_half(qkv_ref[at, q_at], h == 1)
                grad = mask_half(grad_ref[at, lanes], h == 1)
                weights = jnp.exp(dot_t(k_ref[...], query) * SCALE - log_ref[2 * s + h, i])
                dv_ref[...] += dot(weights.astype(narrow), grad)
                dweights = dot_t(qkv_ref[:, v_at], grad)
                inner = jnp.sum(weights * dweights, 0, keepdims=True)
                dscores = (weights * (dweights - inner) * SCALE).astype(narrow)
                dk_ref[...] += dot(dscores, query)
                turned = jnp.transpose(dot(kt_ref[...], dscores))
                kept = grad_to[at, q_to].astype(single)
                low = low_lanes(turned.shape)
                if h == 0:
                    grad_to[at, q_to] = turned.astype(narrow)
                else:
                    grad_to[at, q_to] = jnp.where(low, kept, turned).astype(narrow)

            low = low_lanes((PIX, BLOCK))
            dk = swap_halves(dk_ref[...])
            if h == 0:
                grad_to[:, k_to] = jnp.where(low, grad_to[:, k_to].astype(single), dk).astype(narrow)
                grad_to[:, v_to] = dv_ref[...].astype(narrow)
            else:
                grad_to[:, k_to] = jnp.where(low, dk, dv_ref[...]).astype(narrow)


VMEM = pl.BlockSpec(memory_space=pltpu.VMEM)


def call(body, outs, scratch, args, name):
    return pl.pallas_call(
        body,
        out_shape=outs,
        in_specs=[VMEM] * len(args),
        out_specs=[VMEM] * len(outs),
        scratch_shapes=scratch,
        compiler_params=pltpu.CompilerParams(vmem_limit_bytes=56 * 2**20),
        name=name,
    )(*args)


def struct(shape, dtype=single):
    return jax.ShapeDtypeStruct(shape, dtype)


def entry_kernel(act, x_ref, own_ref, recv_ref, norm_ref, stream_ref, entry_ref):
    @pl.loop(0, PIX // CHUNK)
    def _(i):
        at = rows_of(i)
        stream_ref[at, :] = x_ref[at, :] + (own_ref[at, :] + recv_ref[at, :].astype(single))

    def store(i, value):
        entry_ref[rows_of(i), :] = value

    norm_forward(stream_ref, norm_ref[0:1, :], norm_ref[1:2, :], act, store)


def first_kernel(x_ref, norm_ref, stream_ref, entry_ref):
    @pl.loop(0, PIX // CHUNK)
    def _(i):
        at = rows_of(i)
        stream_ref[at, :] = x_ref[at, :].astype(single)

    def store(i, value):
        entry_ref[rows_of(i), :] = value

    norm_forward(stream_ref, norm_ref[0:1, :], norm_ref[1:2, :], True, store)


def mid_rows(norm_ref, mod_ref):
    gain, bias = norm_ref[0:1, :], norm_ref[1:2, :]
    scale, shift = 1.0 + mod_ref[0:1, :], mod_ref[1:2, :]
    return gain, bias, scale, shift


def put_split(own_ref, peer_ref):
    def store(i, value):
        own, peer = split_core(value)
        own_ref[rows_of(i), :] = own
        peer_ref[rows_of(i), :] = peer.astype(narrow)

    return store


def shift_full(full_ref, s_ref, width):
    shifts(lambda i, size: full_ref[rows_of(i, size), :], s_ref, width)


def res_kernel(own_ref, peer_ref, win_ref, wout_ref, norm_ref, mod_ref, inner_ref, hidden_ref, part_ref, send_ref, full_ref, s_ref):
    join_core(own_ref, peer_ref, full_ref)
    shift_full(full_ref, s_ref, C)

    def put(i, value):
        inner_ref[rows_of(i), :] = value

    conv_wide(s_ref, win_ref, put)
    gain, bias, scale, shift = mid_rows(norm_ref, mod_ref)

    def store(i, value):
        hidden_ref[rows_of(i), :] = value

    norm_forward(inner_ref, gain * scale, bias * scale + shift, True, store)
    shift_full(hidden_ref, s_ref, HALF)
    conv_tall(s_ref, wout_ref, 1, put_split(part_ref, send_ref))


def attn_kernel(own_ref, peer_ref, w_ref, qkv_ref, log_ref, out_ref, part_ref, send_ref, full_ref, k_ref, vt_ref):
    join_core(own_ref, peer_ref, full_ref)

    @pl.loop(0, PIX // CHUNK)
    def _(i):
        at = rows_of(i)
        for s in range(2):
            value = dot(full_ref[at, :], w_ref[:, s * C : s * C + 3 * BLOCK])
            qkv_ref[at, s * 3 * BLOCK : (s + 1) * 3 * BLOCK] = value.astype(narrow)

    attend(qkv_ref, k_ref, vt_ref, log_ref, out_ref)
    store = put_split(part_ref, send_ref)

    @pl.loop(0, PIX // CHUNK)
    def _(i):
        at = rows_of(i)
        value = dot_t(out_ref[at, 0:BLOCK], w_ref[:, 3 * BLOCK : C])
        store(i, value + dot_t(out_ref[at, BLOCK:], w_ref[:, C + 3 * BLOCK :]))


def load_rows(ref):
    return lambda i: ref[rows_of(i), :]


def head_kernel(total, own_ref, peer_ref, w_ref, noise_ref, weight_ref, loss_ref, dw_ref, part_ref, send_ref, full_ref, s_ref, t_ref, grad_ref):
    join_core(own_ref, peer_ref, full_ref)
    shift_full(full_ref, s_ref, C)
    loss_ref[...] = jnp.zeros_like(loss_ref)

    def store(i, value):
        error = value - noise_ref[rows_of(i), :]
        weight = weight_ref[0:1, :]
        loss_ref[...] += jnp.sum(weight * error * error, 0, keepdims=True)
        grad_ref[rows_of(i), :] = (2.0 * weight * error / total).astype(narrow)

    conv_wide(s_ref, w_ref, store)
    wide_back(full_ref, w_ref, grad_ref, dw_ref, part_ref, send_ref, s_ref, t_ref)


def wide_back(full_ref, w_ref, grad_ref, dw_ref, part_ref, send_ref, s_ref, t_ref):
    shift_full(grad_ref, s_ref, HALF)
    transpose_into(load_rows(full_ref), t_ref)

    def keep(t, value):
        dw_ref[t * C : (t + 1) * C, :] = value.astype(narrow)

    kernel_grad(t_ref, s_ref, -1, keep)
    conv_tall(s_ref, w_ref, -1, put_split(part_ref, send_ref))


def normback_kernel(act, x_ref, part_ref, recv_ref, up_ref, norm_ref, dx_ref, low_ref, sums_ref, tmp_ref):
    def load(i):
        return part_ref[rows_of(i), :] + recv_ref[rows_of(i), :].astype(single)

    def store(i, value):
        value = value + up_ref[rows_of(i), :]
        dx_ref[rows_of(i), :] = value
        low_ref[rows_of(i), :] = value.astype(narrow)

    total, along = norm_backward(x_ref, load, norm_ref[0:1, :], norm_ref[1:2, :], act, tmp_ref, store)
    sums_ref[0:1, :] = along
    sums_ref[1:2, :] = total


def resback_kernel(
    gown_ref, gpeer_ref, hidden_ref, inner_ref, norm_ref, mod_ref, wout_ref, own_ref, peer_ref, win_ref,
    dout_ref, din_ref, part_ref, send_ref, sums_ref, dmod_ref,
    full_ref, s_ref, t_ref, dh_ref, tmp_ref, grad_ref,
):
    join_core(gown_ref, gpeer_ref, full_ref)
    transpose_into(load_rows(full_ref), t_ref)
    shift_full(hidden_ref, s_ref, HALF)

    def keep(t, value):
        dout_ref[t * C : (t + 1) * C, :] = value.astype(narrow)

    kernel_grad(t_ref, s_ref, 1, keep)
    shift_full(full_ref, s_ref, C)

    def put(i, value):
        dh_ref[rows_of(i), :] = value

    conv_back(s_ref, wout_ref, put)
    gain, bias, scale, shift = mid_rows(norm_ref, mod_ref)

    def store(i, value):
        grad_ref[rows_of(i), :] = value.astype(narrow)

    total, along = norm_backward(
        inner_ref, load_rows(dh_ref), gain * scale, bias * scale + shift, True, tmp_ref, store
    )
    sums_ref[0:1, :] = scale * along
    sums_ref[1:2, :] = scale * total
    dmod_ref[0:1, :] = gain * along + bias * total
    dmod_ref[1:2, :] = total
    join_core(own_ref, peer_ref, full_ref)
    wide_back(full_ref, win_ref, grad_ref, din_ref, part_ref, send_ref, s_ref, t_ref)


def attnback_kernel(
    gown_ref, gpeer_ref, qkv_ref, log_ref, out_ref, w_ref, own_ref, peer_ref,
    dw_ref, part_ref, send_ref,
    full_ref, t_ref, grad_ref, k_ref, kt_ref, dk_ref, dv_ref, dqkv_ref,
):
    join_core(gown_ref, gpeer_ref, full_ref)
    transpose_into(load_rows(full_ref), t_ref)
    for s in range(2):
        lanes = slice(s * BLOCK, (s + 1) * BLOCK)
        dw_ref[:, s * C + 3 * BLOCK : (s + 1) * C] = dot(t_ref[...], out_ref[:, lanes]).astype(narrow)

        @pl.loop(0, PIX // CHUNK)
        def _(i):
            at = rows_of(i)
            value = dot(full_ref[at, :], w_ref[:, s * C + 3 * BLOCK : (s + 1) * C])
            grad_ref[at, lanes] = value.astype(narrow)

    dqkv = [dqkv_ref.at[:, s * 3 * BLOCK : (s + 1) * 3 * BLOCK] for s in range(2)]
    attend_back(qkv_ref, log_ref, grad_ref, k_ref, kt_ref, dk_ref, dv_ref, dqkv)
    join_core(own_ref, peer_ref, full_ref)
    transpose_into(load_rows(full_ref), t_ref)
    for s in range(2):
        lanes = slice(s * 3 * BLOCK, (s + 1) * 3 * BLOCK)
        dw_ref[:, s * C : s * C + 3 * BLOCK] = dot(t_ref[...], dqkv_ref[:, lanes]).astype(narrow)
    store = put_split(part_ref, send_ref)

    @pl.loop(0, PIX // CHUNK)
    def _(i):
        at = rows_of(i)
        value = dot_t(dqkv_ref[at, 0 : 3 * BLOCK], w_ref[:, 0 : 3 * BLOCK])
        store(i, value + dot_t(dqkv_ref[at, 3 * BLOCK :], w_ref[:, C : C + 3 * BLOCK]))


HALF_F32 = struct((PIX, HALF))
HALF_LOW = struct((PIX, HALF), narrow)
FULL_LOW = pltpu.VMEM((PIX, C), narrow)
SHIFTED = pltpu.VMEM((3, ROWS, C), narrow)
TURNED = pltpu.VMEM((C, PIX), narrow)
SWAP = [(0, 1), (1, 0)]


def core_swap(value):
    return lax.ppermute(value, "lo", SWAP)


def image_swap(value):
    return lax.ppermute(value, "hi", SWAP)


DP = ("dz", "dy")


def pick_image(value):
    hi = lax.axis_index("hi")
    kept = jnp.where(hi == 0, value[0], value[1])
    came = image_swap(jnp.where(hi == 0, value[1], value[0]))
    return jnp.where(hi == 0, jnp.concatenate([kept, came], 1), jnp.concatenate([came, kept], 1))


def join_image(value, axis):
    hi = lax.axis_index("hi")
    came = image_swap(value)
    return jnp.where(
        hi == 0, jnp.concatenate([value, came], axis), jnp.concatenate([came, value], axis)
    )


def gather_weight(shard):
    rows = lax.all_gather(shard, DP, axis=0, tiled=True)
    return lax.all_gather(rows, "hi", axis=1, tiled=True)


def scatter_grad(value):
    cols = lax.psum_scatter(value, "hi", scatter_dimension=1, tiled=True)
    return lax.psum_scatter(cols, DP, scatter_dimension=0, tiled=True).astype(single)


def chan_index():
    return lax.axis_index("hi") * 2 + lax.axis_index("lo")


def sinusoid_of(timesteps):
    half_count = TF // 2
    frequency = jnp.exp(-math.log(10000.0) * jnp.arange(half_count, dtype=single) / half_count)
    angles = timesteps.astype(single)[:, None] * frequency[None, :]
    return jnp.concatenate([jnp.cos(angles), jnp.sin(angles)], 1).astype(narrow)


def embed_forward(timesteps, classes, time_in, emb_out, emb_proj):
    times = lax.all_gather(timesteps, DP, axis=0, tiled=True)
    labels = lax.all_gather(classes, DP, axis=0, tiled=True)
    rows = time_in.shape[0]
    place = lax.axis_index(DP) * rows
    sinusoid = lax.dynamic_slice_in_dim(sinusoid_of(times), place, rows, 1)
    pre = lax.psum(dot(sinusoid, time_in), DP)
    hidden = jax.nn.silu(pre).astype(narrow)
    class_here = emb_out.shape[1] - hidden.shape[1]
    numbers = chan_index() * class_here + jnp.arange(class_here)
    onehot = (labels[:, None] == numbers[None, :]).astype(narrow)
    joined = jnp.concatenate([hidden, onehot], 1)
    embedding = lax.psum(dot_t(joined, emb_out), ("hi", "lo"))
    context = jax.nn.silu(embedding).astype(narrow)
    parts = jnp.einsum("be,lej->blj", context, emb_proj, preferred_element_type=single)
    mine = lax.psum_scatter(parts, DP, scatter_dimension=0, tiled=True)
    hi = lax.axis_index("hi")
    kept = jnp.where(hi == 0, mine[0], mine[1])
    came = image_swap(jnp.where(hi == 0, mine[1], mine[0]))
    wide = jnp.where(hi == 0, jnp.concatenate([kept, came], 1), jnp.concatenate([came, kept], 1))
    modulate = jnp.swapaxes(wide.reshape(2, HALF, 2), 1, 2)
    return modulate, (sinusoid, pre, joined, embedding, context)


def embed_backward(saved, dmod, emb_proj, emb_out):
    sinusoid, pre, joined, embedding, context = saved
    flat = jnp.swapaxes(dmod, 1, 2).reshape(2, 2 * HALF).astype(narrow)
    hi = lax.axis_index("hi")
    width = flat.shape[1] // 2
    kept = jnp.where(hi == 0, flat[:, :width], flat[:, width:])
    came = image_swap(jnp.where(hi == 0, flat[:, width:], flat[:, :width]))
    both = jnp.where(hi == 0, jnp.stack([kept, came]), jnp.stack([came, kept]))
    grads = lax.all_gather(both, DP, axis=0, tiled=True)
    proj_grad = jnp.einsum("be,blj->lej", context, grads, preferred_element_type=single)
    part = jnp.einsum("blj,lej->be", grads, emb_proj, preferred_element_type=single)
    context_grad = lax.psum(part, ("hi", "lo"))
    _, pullback = jax.vjp(jax.nn.silu, embedding)
    (embed_grad,) = pullback(context_grad)
    embed_low = embed_grad.astype(narrow)
    out_grad = jnp.einsum("be,bj->ej", embed_low, joined, preferred_element_type=single)
    joined_grad = lax.psum(dot(embed_low, emb_out[:, : pre.shape[1]]), DP)
    _, pullback = jax.vjp(jax.nn.silu, pre)
    (pre_grad,) = pullback(joined_grad)
    time_grad = jnp.einsum("bt,be->te", sinusoid, pre_grad.astype(narrow), preferred_element_type=single)
    return proj_grad, time_grad, out_grad


def res_forward(own, peer, win, wout, norm, mod):
    outs = [HALF_F32, HALF_LOW, HALF_F32, HALF_LOW]
    return call(res_kernel, outs, [FULL_LOW, SHIFTED], [own, peer, win, wout, norm, mod], "res_forward")


def res_backward(gown, gpeer, hidden, inner, norm, mod, wout, own, peer, win):
    taps = struct((9 * C, HALF), narrow)
    outs = [taps, taps, HALF_F32, HALF_LOW, struct((2, HALF)), struct((2, HALF))]
    scratch = [FULL_LOW, SHIFTED, TURNED, pltpu.VMEM((PIX, HALF), single), pltpu.VMEM((PIX, HALF), single), pltpu.VMEM((PIX, HALF), narrow)]
    return call(resback_kernel, outs, scratch, [gown, gpeer, hidden, inner, norm, mod, wout, own, peer, win], "res_backward")


def norm_step(act, x, part, recv, up, norm):
    outs = [HALF_F32, HALF_LOW, struct((2, HALF))]
    body = functools.partial(normback_kernel, act)
    return call(body, outs, [pltpu.VMEM((PIX, HALF), single)], [x, part, recv, up, norm], "norm_backward")


def entry_step(act, x, part, recv, norm):
    return call(functools.partial(entry_kernel, act), [HALF_F32, HALF_LOW], [], [x, part, recv, norm], "entry")


def network(noisy, noise, sample_weight, kernels_in, kernels_out, attn, norms, modulate):
    images = noisy.shape[0] * lax.axis_size("dz") * lax.axis_size("dy")
    total = float(images * PIX * C)
    x0 = pick_image(noisy.reshape(2, PIX, BLOCK))
    target = pick_image(noise.reshape(2, PIX, BLOCK))
    weight = jnp.where(lax.axis_index("hi") == 0, sample_weight[0], sample_weight[1])
    weight = jnp.broadcast_to(weight, (8, HALF))
    stream0, entry0 = call(first_kernel, [HALF_F32, HALF_LOW], [], [x0, norms[0]], "entry")
    peer0 = core_swap(entry0)
    inner0, hidden0, part, send = res_forward(entry0, peer0, kernels_in[0], kernels_out[0], norms[1], modulate[0])
    stream1, entry1 = entry_step(False, stream0, part, core_swap(send), norms[2])
    peer1 = core_swap(entry1)
    outs = [struct((PIX, 6 * BLOCK), narrow), struct((4, PIX // CHUNK, 1, CHUNK)), HALF_LOW, HALF_F32, HALF_LOW]
    scratch = [FULL_LOW, pltpu.VMEM((PIX, BLOCK), narrow), pltpu.VMEM((BLOCK, PIX), narrow)]
    qkv, log, attended, part, send = call(attn_kernel, outs, scratch, [entry1, peer1, attn], "attention")
    stream2, entry2 = entry_step(True, stream1, part, core_swap(send), norms[3])
    peer2 = core_swap(entry2)
    inner2, hidden2, part, send = res_forward(entry2, peer2, kernels_in[1], kernels_out[1], norms[4], modulate[1])
    stream3, entry3 = entry_step(True, stream2, part, core_swap(send), norms[5])
    peer3 = core_swap(entry3)
    taps = struct((9 * C, HALF), narrow)
    outs = [struct((1, HALF)), taps, HALF_F32, HALF_LOW]
    scratch = [FULL_LOW, SHIFTED, TURNED, pltpu.VMEM((PIX, HALF), narrow)]
    args = [entry3, peer3, kernels_in[2], target, weight]
    loss, din2, part, send = call(functools.partial(head_kernel, total), outs, scratch, args, "head")
    zero = jnp.zeros((PIX, HALF), single)
    grad3, low3, sums5 = norm_step(True, stream3, part, core_swap(send), zero, norms[5])
    dout1, din1, part, send, sums4, dmod1 = res_backward(
        low3, core_swap(low3), hidden2, inner2, norms[4], modulate[1], kernels_out[1], entry2, peer2, kernels_in[1]
    )
    grad2, low2, sums3 = norm_step(True, stream2, part, core_swap(send), grad3, norms[3])
    outs = [struct((C, 2 * C), narrow), HALF_F32, HALF_LOW]
    scratch = [
        FULL_LOW, TURNED, pltpu.VMEM((PIX, HALF), narrow), pltpu.VMEM((PIX, BLOCK), narrow), pltpu.VMEM((BLOCK, PIX), narrow),
        pltpu.VMEM((PIX, BLOCK), single), pltpu.VMEM((PIX, BLOCK), single), pltpu.VMEM((PIX, 6 * BLOCK), narrow),
    ]
    args = [low2, core_swap(low2), qkv, log, attended, attn, entry1, peer1]
    dattn, part, send = call(attnback_kernel, outs, scratch, args, "attention_backward")
    grad1, low1, sums2 = norm_step(False, stream1, part, core_swap(send), grad2, norms[2])
    dout0, din0, part, send, sums1, dmod0 = res_backward(
        low1, core_swap(low1), hidden0, inner0, norms[1], modulate[0], kernels_out[0], entry0, peer0, kernels_in[0]
    )
    _, _, sums0 = norm_step(True, stream0, part, core_swap(send), grad1, norms[0])
    sums = jnp.stack([sums0, sums1, sums2, sums3, sums4, sums5])
    return jnp.sum(loss) / total, (din0, din1, din2), (dout0, dout1), dattn, sums, jnp.stack([dmod0, dmod1])


MESH = pl.DeviceIdType.MESH
ANY = pl.BlockSpec(memory_space=pl.ANY)
SMEM = pl.BlockSpec(memory_space=pltpu.SMEM)
LAYERS = 6
STEPS = 10


def remote(src, dst, send, recv, **where):
    return pltpu.make_async_remote_copy(
        src_ref=src, dst_ref=dst, send_sem=send, recv_sem=recv, device_id=where, device_id_type=MESH
    )


def place():
    return lax.axis_index("dz"), lax.axis_index("dy"), lax.axis_index("hi")


def greet(others):
    barrier = pltpu.get_barrier_semaphore()
    for where in others:
        pl.semaphore_signal(barrier, inc=1, device_id=where, device_id_type=MESH)
    pl.semaphore_wait(barrier, len(others))


def neighbours():
    z, y, x = place()
    others = [{"dz": (z + k) % 4} for k in (1, 2, 3)]
    return others + [{"dy": 1 - y}, {"hi": 1 - x}, {"lo": 1 - lax.axis_index("lo")}]


class Layout:
    def __init__(self, rows, lanes):
        self.rows, self.lanes = rows, lanes

    def block(self, zz, yy):
        return pl.ds(pl.multiple_of((zz * 2 + yy) * self.rows, 32), self.rows)

    def cols(self, xx):
        return pl.ds(pl.multiple_of(xx * self.lanes, 128), self.lanes)


class Gather:
    def __init__(self, layer, shard, full, send, recv, local):
        z, y, x = place()
        rows, lanes = shard.shape
        at = Layout(rows, lanes)
        mine = full.at[at.block(z, y), at.cols(x)]
        self.local = pltpu.make_async_copy(shard, mine, local.at[layer])

        def copy(j, src, dst, **where):
            return remote(src, dst, send.at[layer, j], recv.at[layer, j], **where)

        self.along_z = [copy(k - 1, shard, mine, dz=(z + k) % 4) for k in (1, 2, 3)]
        self.first, self.second = [], []
        for n in range(2):
            part = full.at[at.block(n, y), at.cols(x)]
            self.first.append(copy(3 + n, part, part, dy=1 - y))
            part = full.at[at.block(2 + n, y), at.cols(x)]
            self.first.append(copy(5 + n, part, part, hi=1 - x))
        part = full.at[0 : 4 * rows, at.cols(x)]
        self.second.append(copy(7, part, part, hi=1 - x))
        for n in range(2):
            part = full.at[at.block(2 + n, y), :]
            self.second.append(copy(8 + n, part, part, dy=1 - y))

    def start(self):
        self.local.start()
        for copy in self.along_z:
            copy.start()

    def turn(self):
        self.local.wait()
        for copy in self.along_z:
            copy.wait_recv()
        for copy in self.first:
            copy.start()

    def spread(self):
        for copy in self.first:
            copy.wait_recv()
        for copy in self.second:
            copy.start()

    def ready(self):
        for copy in self.second:
            copy.wait_recv()

    def drain(self):
        for copy in self.along_z + self.first + self.second:
            copy.wait_send()


def add_rows(count, lanes, into, other):
    size = 64 if lanes > 128 else 192

    @pl.loop(0, count // size)
    def _(i):
        at = pl.ds(pl.multiple_of(i * size, 32), size)
        total = into.at[at, :][...].astype(single) + other.at[at, :][...].astype(single)
        into.at[at, :][...] = total.astype(narrow)


class Reduce:
    def __init__(self, layer, grad, bufs, out, send, recv):
        z, y, x = place()
        ra, rb, rc, rd, rz = bufs
        rows, lanes = out.shape
        at = Layout(rows, lanes)
        self.rows, self.lanes, self.out, self.grad, self.bufs = rows, lanes, out, grad, bufs
        self.at, self.here = at, (z, y, x)

        def copy(j, src, dst, **where):
            return remote(src, dst, send.at[layer, j], recv.at[layer, j], **where)

        self.first = [copy(0, grad.at[0 : 4 * rows, at.cols(1 - x)], ra, hi=1 - x)]
        self.second, self.third = [], []
        for n in range(2):
            self.first.append(copy(1 + n, grad.at[at.block(2 + n, 1 - y), :], rb.at[n], dy=1 - y))
        for n in range(2):
            part = grad.at[at.block(n, 1 - y), at.cols(x)]
            self.second.append(copy(3 + n, part, rc.at[n], dy=1 - y))
        for n in range(2):
            part = grad.at[at.block(2 + n, y), at.cols(1 - x)]
            self.second.append(copy(5 + n, part, rd.at[n], hi=1 - x))
        for k in (1, 2, 3):
            zz = (z + k) % 4
            part = grad.at[at.block(zz, y), at.cols(x)]
            self.third.append(copy(6 + k, part, rz.at[k - 1], dz=zz))

    def start(self):
        for copy in self.first:
            copy.start()

    def turn(self):
        (z, y, x), at, (ra, rb, rc, rd, rz) = self.here, self.at, self.bufs
        self.first[0].wait_recv()
        add_rows(4 * self.rows, self.lanes, self.grad.at[0 : 4 * self.rows, at.cols(x)], ra)
        for copy in self.second[:2]:
            copy.start()
        for n in range(2):
            self.first[1 + n].wait_recv()
            add_rows(self.rows, 2 * self.lanes, self.grad.at[at.block(2 + n, y), :], rb.at[n])
            self.second[2 + n].start()

    def spread(self):
        (z, y, x), at, (ra, rb, rc, rd, rz) = self.here, self.at, self.bufs
        for n in range(2):
            self.second[n].wait_recv()
            add_rows(self.rows, self.lanes, self.grad.at[at.block(n, y), at.cols(x)], rc.at[n])
        for n in range(2):
            self.second[2 + n].wait_recv()
            add_rows(self.rows, self.lanes, self.grad.at[at.block(2 + n, y), at.cols(x)], rd.at[n])
        for copy in self.third:
            copy.start()

    def finish(self):
        (z, y, x), at, (ra, rb, rc, rd, rz) = self.here, self.at, self.bufs
        for copy in self.third:
            copy.wait_recv()
        size = 64
        mine = self.grad.at[at.block(z, y), at.cols(x)]

        @pl.loop(0, self.rows // size)
        def _(i):
            part = pl.ds(pl.multiple_of(i * size, 32), size)
            total = mine.at[part, :][...].astype(single)
            for k in range(3):
                total = total + rz.at[k, part, :][...].astype(single)
            self.out.at[part, :][...] = total

    def drain(self):
        for copy in self.first + self.second + self.third:
            copy.wait_send()


class Core:
    def __init__(self, send, recv):
        self.send, self.recv, self.used = send, recv, 0
        self.core = lax.axis_index("lo")

    def take(self, count):
        base = self.used
        self.used += count
        return base

    def copy(self, index, src, dst):
        return remote(src, dst, self.send.at[index], self.recv.at[index], lo=1 - self.core)

    def lanes(self, j):
        return pl.ds(pl.multiple_of((2 * j + self.core) * BLOCK, 128), BLOCK)

    def share(self, full):
        base = self.take(2 * (PIX // CHUNK))

        def copies(i):
            parts = [full.at[rows_of(i), self.lanes(j)] for j in range(2)]
            return [self.copy(base + 2 * i + j, part, part) for j, part in enumerate(parts)]

        def store(i, value):
            for j in range(2):
                full[rows_of(i), self.lanes(j)] = value[:, j * BLOCK : (j + 1) * BLOCK]
            for copy in copies(i):
                copy.start()

        def wait():
            @pl.loop(0, PIX // CHUNK)
            def _(i):
                for copy in copies(i):
                    copy.wait()

        return store, wait

    def combine(self, part, send, recv):
        base = self.take(PIX // CHUNK)

        def one(i):
            return self.copy(base + i, send.at[rows_of(i), :], recv.at[rows_of(i), :])

        def store(i, value):
            own, peer = split_core(value)
            part[rows_of(i), :] = own
            send[rows_of(i), :] = peer.astype(narrow)
            one(i).start()

        def wait():
            @pl.loop(0, PIX // CHUNK)
            def _(i):
                one(i).wait()

        def load(i):
            return part[rows_of(i), :] + recv[rows_of(i), :].astype(single)

        return store, wait, load


class Spill:
    def __init__(self, sems):
        self.sems, self.used, self.open = sems, 0, []

    def start(self, src, dst):
        copy = pltpu.make_async_copy(src, dst, self.sems.at[self.used])
        self.used += 1
        copy.start()
        self.open.append(copy)
        return copy

    def finish(self, copy):
        copy.wait()
        self.open = [other for other in self.open if other is not copy]

    def drain(self):
        for copy in self.open:
            copy.wait()


def forward_kernel(
    total,
    noisy_hbm, noise_hbm, weight_ref, times_ref, labels_ref, norms_own, conv_in, conv_out, attn_weight, time_in, emb_out, emb_proj,
    w0_out, w1_out, w2_out, w3_out, w4_out, w5_out,
    full0_out, full1_out, full2_out, full3_out, x1_out, x2_out, x3_out,
    inner0_out, inner2_out, hidden0_out, hidden2_out, qkv_out, att_out, pg_out, x0_out, log_ref, loss_ref,
    norms_out, mod_ref, wsq_ref, sin_ref, label_ref, pre_ref, embedding_ref,
    w0, w1, w2, w3, w4, w5,
    full0, full1, full2, full3, x1, x2, x3, inner0, inner2, hidden0, hidden2, qkv, att, pg, noise_ref,
    shifted, part, send0, send1, send2, recv0, recv1, recv2, k_ref, vt_ref,
    x0_ref, norms_ref, loss_lanes, norms_flat, msg, s0, s1, s2, s3, s4, s5, p0, p1, p2, p3, m3,
    gsend, grecv, glocal, csend, crecv, xsend, xrecv, esend, erecv, lsem,
):
    x = lax.axis_index("hi")
    spill, core, small = Spill(lsem), Core(csend, crecv), Small(esend, erecv)
    block = pl.ds(pl.multiple_of(x * BLOCK, BLOCK), BLOCK)
    own_x0 = spill.start(noisy_hbm.at[x], x0_ref.at[:, block])
    own_noise = spill.start(noise_hbm.at[x], noise_ref.at[:, block])
    norms_flat[...] = joined_rows(norms_own)
    norms_ref[:, block] = norms_flat[...]
    keep = (sin_ref, label_ref, pre_ref, embedding_ref)
    embed = embed_steps(
        small, times_ref, labels_ref, time_in, emb_out, emb_proj, msg, p0, p1, p2, p3, m3, mod_ref, keep
    )
    greet(all_partners())
    swaps = []
    for n, (src, dst) in enumerate(
        ((noisy_hbm.at[1 - x], x0_ref), (norms_flat, norms_ref), (noise_hbm.at[1 - x], noise_ref))
    ):
        swaps.append(remote(src, dst.at[:, block], xsend.at[n], xrecv.at[n], hi=1 - x))
    gathers = [
        Gather(n, shard, full, gsend, grecv, glocal)
        for n, (shard, full) in enumerate(zip((s0, s1, s2, s3, s4, s5), (w0, w1, w2, w3, w4, w5)))
    ]
    swaps[1].start()
    next(embed)
    swaps[0].start()
    masters = [conv_in.at[0], conv_out.at[0], attn_weight, conv_in.at[1], conv_out.at[1], conv_in.at[2]]
    for master, shard in zip(masters, (s0, s1, s2, s3, s4, s5)):
        shard[...] = master[...].astype(narrow)
    next(embed)
    gathers[0].start()

    def norm_row(n):
        return norms_ref[2 * n : 2 * n + 1, :], norms_ref[2 * n + 1 : 2 * n + 2, :]

    class First:
        def __getitem__(self, at):
            return x0_ref[at].astype(single)

    def entry(x, n, act, full):
        gain, bias = norm_row(n)
        store, wait = core.share(full)
        norm_forward(x, gain, bias, act, store)
        return wait

    def residual(full, w_in, w_out, ready, n, layer, inner, hidden, send, recv):
        shift_full(full, shifted, C)

        def put(i, value):
            inner[rows_of(i), :] = value

        conv_wide(shifted, w_in, put)
        gain, bias = norm_row(n)
        scale, shift = 1.0 + mod_ref[layer, 0:1, :], mod_ref[layer, 1:2, :]

        def keep(i, value):
            hidden[rows_of(i), :] = value

        norm_forward(inner, gain * scale, bias * scale + shift, True, keep)
        shift_full(hidden, shifted, HALF)
        ready()
        store, wait, load = core.combine(part, send, recv)
        conv_tall(shifted, w_out, 1, store)
        return wait, load

    def advance(x_old, load, x_new):
        @pl.loop(0, PIX // CHUNK)
        def _(i):
            x_new[rows_of(i), :] = x_old[rows_of(i), :] + load(i)

    def after(n, copies):
        gathers[n].ready()
        spill.start(copies[0], copies[1])

    next(embed)
    gathers[1].start()
    gathers[2].start()
    spill.finish(own_x0)
    swaps[0].wait_recv()
    swaps[1].wait_recv()
    spill.start(x0_ref, x0_out)
    next(embed)
    for gather in gathers[3:]:
        gather.start()
    wait = entry(First(), 0, True, full0)
    gathers[0].turn()
    masters = [conv_in.at[n] for n in range(3)] + [conv_out.at[n] for n in range(2)]
    masters += [emb_proj.at[n] for n in range(2)] + [attn_weight, time_in, emb_out]
    wsq_ref[...] = scalar_rows([whole(master[...] * master[...]) for master in masters], 16)
    norms_out[...] = norms_ref[...]
    gathers[1].turn()
    gathers[0].spread()
    gathers[2].turn()
    gathers[1].spread()
    next(embed)
    wait()
    spill.start(full0, full0_out)
    after(0, (w0, w0_out))

    def ready1():
        gathers[3].turn()
        gathers[2].spread()
        swaps[2].start()
        after(1, (w1, w1_out))

    wait, load = residual(full0, w0, w1, ready1, 1, 0, inner0, hidden0, send0, recv0)
    spill.start(inner0, inner0_out)
    spill.start(hidden0, hidden0_out)
    wait()
    advance(First(), load, x1)
    spill.start(x1, x1_out)
    wait = entry(x1, 2, False, full1)
    gathers[4].turn()
    gathers[3].spread()
    after(2, (w2, w2_out))
    wait()
    spill.start(full1, full1_out)

    @pl.loop(0, PIX // CHUNK)
    def _(i):
        at = rows_of(i)
        for s in range(2):
            value = dot(full1[at, :], w2[:, s * C : s * C + 3 * BLOCK])
            qkv[at, s * 3 * BLOCK : (s + 1) * 3 * BLOCK] = value.astype(narrow)

    spill.start(qkv, qkv_out)
    attend(qkv, k_ref, vt_ref, log_ref, att)
    spill.start(att, att_out)
    gathers[5].turn()
    gathers[4].spread()
    store, wait, load = core.combine(part, send1, recv1)

    @pl.loop(0, PIX // CHUNK)
    def _(i):
        at = rows_of(i)
        value = dot_t(att[at, 0:BLOCK], w2[:, 3 * BLOCK : C])
        store(i, value + dot_t(att[at, BLOCK:], w2[:, C + 3 * BLOCK :]))

    wait()
    advance(x1, load, x2)
    spill.start(x2, x2_out)
    wait = entry(x2, 3, True, full2)
    after(3, (w3, w3_out))
    wait()
    spill.start(full2, full2_out)

    def ready4():
        gathers[5].spread()
        after(4, (w4, w4_out))

    wait, load = residual(full2, w3, w4, ready4, 4, 1, inner2, hidden2, send2, recv2)
    spill.start(inner2, inner2_out)
    spill.start(hidden2, hidden2_out)
    wait()
    advance(x2, load, x3)
    spill.start(x3, x3_out)
    wait = entry(x3, 5, True, full3)
    after(5, (w5, w5_out))
    wait()
    spill.start(full3, full3_out)
    shift_full(full3, shifted, C)
    spill.finish(own_noise)
    swaps[2].wait_recv()
    loss_lanes[...] = jnp.zeros_like(loss_lanes)

    def store(i, value):
        error = value - noise_ref[rows_of(i), :]
        weight = jnp.where(x == 0, weight_ref[0], weight_ref[1])
        loss_lanes[...] += jnp.sum(weight * error * error, 0, keepdims=True)
        pg[rows_of(i), :] = (2.0 * weight * error / total).astype(narrow)

    conv_wide(shifted, w5, store)
    spill.start(pg, pg_out)
    loss_ref[...] = jnp.broadcast_to(whole(loss_lanes[...]) / total, loss_ref.shape)
    for gather in gathers:
        gather.drain()
    for copy in swaps:
        copy.wait_send()
    spill.drain()


def backward_kernel(
    fulls,
    log_ref, loss_ref, norms_ref, mod_ref, wsq_ref, sin_ref, label_ref, pre_ref, embedding_ref,
    emb_out, emb_proj, norms_own, second,
    in_rows, in_cols, out_rows, out_cols, proj_rows, proj_cols, attn_rows, attn_cols, time_rows, time_cols, eout_rows, eout_cols,
    w0_hbm, w1_hbm, w2_hbm, w3_hbm, w4_hbm, w5_hbm,
    full0_hbm, full1_hbm, full2_hbm, full3_hbm, x1_hbm, x2_hbm, x3_hbm,
    inner0_hbm, inner2_hbm, hidden0_hbm, hidden2_hbm, qkv_hbm, att_hbm, pg_hbm, x0_hbm,
    g0, g1, g2, g3, g4, g5, proj_grad, time_grad, eout_grad, rows_ref, cols_ref, scal_ref, norm_out, second_out, norms_out,
    wa, wb, wattn, d0, d1, d2, d3, d4, d5,
    ra, rb, rc, rd, rz, qa, qb, qc, qd, qz,
    gfull3, gfull2, gfull1, entry, x_ref, x0_ref, inner, hidden, qkv, att, pg,
    shifted, turned, tmp, dh, part, up, send, recv0, recv1, recv2, recv3,
    k_ref, kt_ref, dk_ref, dv_ref, sums_ref, dmod_ref,
    q4, p4, p5, p6, p7, q7, p8, p9, p10, p11, p12,
    rsend, rrecv, csend, crecv, esend, erecv, lsem,
):
    spill, core, small = Spill(lsem), Core(csend, crecv), Small(esend, erecv)
    dmod_ref[...] = jnp.zeros_like(dmod_ref)
    load_w5 = spill.start(w5_hbm, wa)
    load_w4 = spill.start(w4_hbm, wb)
    load_pg = spill.start(pg_hbm, pg)
    load_entry = spill.start(full3_hbm, entry)
    load_x = spill.start(x3_hbm, x_ref)
    load_hidden = spill.start(hidden2_hbm, hidden)
    load_inner = spill.start(inner2_hbm, inner)
    load_qkv = spill.start(qkv_hbm, qkv)
    load_att = spill.start(att_hbm, att)
    load_attn = spill.start(w2_hbm, wattn)
    load_x0 = spill.start(x0_hbm, x0_ref)
    greet(all_partners())
    grads = [d0, d1, d2, d3, d4, d5]
    outs = [g0, g1, g2, g3, g4, g5]
    slots = {0: 0, 1: 1, 3: 2, 4: 3, 5: 4}
    reduces = []
    for n in range(LAYERS):
        bufs = (qa, qb, qc, qd, qz) if n == 2 else tuple(buf.at[slots[n]] for buf in (ra, rb, rc, rd, rz))
        reduces.append(Reduce(n, grads[n], bufs, outs[n], rsend, rrecv))

    keep = (sin_ref, label_ref, pre_ref, embedding_ref)
    embed = embed_back_steps(
        small, dmod_ref, q4, p4, p5, p6, emb_out, emb_proj, keep, proj_grad, eout_grad, time_grad
    )
    matrices = [g0, g3, g5, g1, g4, proj_grad.at[0], proj_grad.at[1], g2, time_grad, eout_grad]
    rows_old = [in_rows[n : n + 1] for n in range(3)] + [out_rows[n : n + 1] for n in range(2)]
    rows_old += [proj_rows[n : n + 1] for n in range(2)] + [attn_rows[...], time_rows[...], eout_rows[...]]
    cols_old = [in_cols[n : n + 1] for n in range(3)] + [out_cols[n : n + 1] for n in range(2)]
    cols_old += [proj_cols[n : n + 1] for n in range(2)] + [attn_cols[...], time_cols[...], eout_cols[...]]
    step = adafactor_steps(
        small, (1, 2, 4, 5, 6, 7, 8, 9), (3, 0), matrices, rows_old, cols_old, fulls, wsq_ref, loss_ref, sums_ref,
        norms_own, second, p7, q7, p8, p9, p10, p11, p12, rows_ref, cols_ref, scal_ref, norm_out, second_out, norms_out,
    )

    def norm_row(n):
        return norms_ref[2 * n : 2 * n + 1, :], norms_ref[2 * n + 1 : 2 * n + 2, :]

    def keep_taps(grad):
        def keep(t, value):
            grad[t * C : (t + 1) * C, :] = value.astype(narrow)

        return keep

    def wide(w, grad, n, recv):
        shift_full(pg, shifted, HALF)
        transpose_into(load_rows(entry), turned)
        kernel_grad(turned, shifted, -1, keep_taps(grad))
        reduces[n].start()
        store, wait, load = core.combine(part, send, recv)
        conv_tall(shifted, w, -1, store)
        return wait, load

    def through_norm(x, load, n, act, first, gfull):
        gain, bias = norm_row(n)
        if gfull is not None:
            share, wait = core.share(gfull)
        else:
            share, wait = None, None

        def store(i, value):
            if share is None:
                return
            if not first:
                value = value + up[rows_of(i), :]
            up[rows_of(i), :] = value
            share(i, value.astype(narrow))

        summed, along = norm_backward(x, load, gain, bias, act, tmp, store)
        sums_ref[n, 0:1, :] = along
        sums_ref[n, 1:2, :] = summed
        return wait

    def residual(gfull, w_out, n_out, n_norm, layer):
        transpose_into(load_rows(gfull), turned)
        shift_full(hidden, shifted, HALF)
        kernel_grad(turned, shifted, 1, keep_taps(grads[n_out]))
        reduces[n_out].start()
        shift_full(gfull, shifted, C)

        def put(i, value):
            dh[rows_of(i), :] = value

        conv_back(shifted, w_out, put)
        gain, bias = norm_row(n_norm)
        scale, shift = 1.0 + mod_ref[layer, 0:1, :], mod_ref[layer, 1:2, :]

        def store(i, value):
            pg[rows_of(i), :] = value.astype(narrow)

        summed, along = norm_backward(inner, load_rows(dh), gain * scale, bias * scale + shift, True, tmp, store)
        sums_ref[n_norm, 0:1, :] = scale * along
        sums_ref[n_norm, 1:2, :] = scale * summed
        dmod_ref[0, layer : layer + 1, :] = gain * along + bias * summed
        dmod_ref[1, layer : layer + 1, :] = summed

    done = spill.finish
    done(load_pg)
    done(load_entry)
    done(load_w5)
    wait, load = wide(wa, d5, 5, recv0)
    load_w3 = spill.start(w3_hbm, wa)
    load_entry = spill.start(full2_hbm, entry)
    done(load_x)
    wait()
    wait = through_norm(x_ref, load, 5, True, True, gfull3)
    load_x = spill.start(x2_hbm, x_ref)
    reduces[5].turn()
    wait()
    done(load_hidden)
    done(load_inner)
    done(load_w4)
    residual(gfull3, wb, 4, 4, 1)
    load_hidden = spill.start(hidden0_hbm, hidden)
    load_inner = spill.start(inner0_hbm, inner)
    load_w1 = spill.start(w1_hbm, wb)
    reduces[5].spread()
    done(load_entry)
    done(load_w3)
    wait, load = wide(wa, d3, 3, recv1)
    load_w0 = spill.start(w0_hbm, wa)
    load_entry = spill.start(full1_hbm, entry)
    reduces[4].turn()
    done(load_x)
    wait()
    wait = through_norm(x_ref, load, 3, True, False, gfull2)
    load_x = spill.start(x1_hbm, x_ref)
    reduces[3].turn()
    reduces[4].spread()
    reduces[5].finish()
    wait()
    done(load_qkv)
    done(load_att)
    done(load_attn)
    transpose_into(load_rows(gfull2), turned)
    for s in range(2):
        lanes = slice(s * BLOCK, (s + 1) * BLOCK)
        d2[:, s * C + 3 * BLOCK : (s + 1) * C] = dot(turned[...], att[:, lanes]).astype(narrow)

        @pl.loop(0, PIX // CHUNK)
        def _(i):
            at = rows_of(i)
            value = dot(gfull2[at, :], wattn[:, s * C + 3 * BLOCK : (s + 1) * C])
            pg[at, lanes] = value.astype(narrow)

    dqkv = [shifted.at[s, 0:PIX, 0 : 3 * BLOCK] for s in range(2)]
    attend_back(qkv, log_ref, pg, k_ref, kt_ref, dk_ref, dv_ref, dqkv)
    done(load_entry)
    transpose_into(load_rows(entry), turned)
    for s in range(2):
        d2[:, s * C : s * C + 3 * BLOCK] = dot(turned[...], dqkv[s][...]).astype(narrow)
    reduces[2].start()
    store, wait, load = core.combine(part, send, recv2)

    @pl.loop(0, PIX // CHUNK)
    def _(i):
        at = rows_of(i)
        value = dot_t(dqkv[0].at[at, :][...], wattn[:, 0 : 3 * BLOCK])
        store(i, value + dot_t(dqkv[1].at[at, :][...], wattn[:, C : C + 3 * BLOCK]))

    load_entry = spill.start(full0_hbm, entry)
    done(load_x)
    wait()
    wait = through_norm(x_ref, load, 2, False, False, gfull1)
    reduces[3].spread()
    reduces[2].turn()
    reduces[4].finish()
    wait()
    done(load_hidden)
    done(load_inner)
    done(load_w1)
    residual(gfull1, wb, 1, 1, 0)
    next(embed)
    reduces[2].spread()
    reduces[3].finish()
    done(load_entry)
    done(load_w0)
    wait, load = wide(wa, d0, 0, recv3)
    next(embed)
    reduces[1].turn()
    reduces[2].finish()
    wait()
    done(load_x0)

    class First:
        def __getitem__(self, at):
            return x0_ref[at].astype(single)

    through_norm(First(), load, 0, True, False, None)
    next(embed)
    reduces[1].spread()
    reduces[0].turn()
    next(embed)
    next(step)
    reduces[0].spread()
    reduces[1].finish()
    reduces[0].finish()
    next(step)
    for reduce in reduces:
        reduce.drain()
    spill.drain()


EXACT = lax.Precision.HIGHEST
IMAGES_HERE = 16


def exact_dot(a, b):
    return jnp.dot(a, b, precision=EXACT, preferred_element_type=single)


def chosen(shape, rule):
    row = lax.broadcasted_iota(jnp.int32, shape, 0)
    column = lax.broadcasted_iota(jnp.int32, shape, 1)
    return jnp.where(rule(row, column), 1.0, 0.0).astype(single)


def odd_even(kind):
    return chosen((HALF, BLOCK), lambda r, c: r == 2 * c + kind)


def even_odd(kind):
    return chosen((BLOCK, HALF), lambda r, c: c == 2 * r + kind)


def contract_rows(a, b):
    return lax.dot_general(a, b, (((0,), (0,)), ((), ())), preferred_element_type=single)


def silu_grad(value):
    gate = sigmoid(value)
    return gate * (1.0 + value * (1.0 - gate))


class Small:
    def __init__(self, send, recv):
        self.send, self.recv, self.used = send, recv, 0
        z, y, x = place()
        core = lax.axis_index("lo")
        self.dp_here, self.chan_here, self.plane_here = 2 * z + y, 2 * x + core, 4 * z + 2 * y + x

    def go(self, count, here, source, target, where):
        copies = []
        for k in range(1, count):
            other = lax.rem(here + k, count)
            sems = self.send.at[self.used], self.recv.at[self.used]
            self.used += 1
            copy = remote(source(other), target.at[here], *sems, **where(other))
            copy.start()
            copies.append(copy)

        def wait():
            for copy in copies:
                copy.wait()

        return wait

    def dp(self, target, source=None):
        source = source or (lambda other: target.at[self.dp_here])
        where = lambda other: {"dz": lax.div(other, 2), "dy": lax.rem(other, 2)}
        return self.go(8, self.dp_here, source, target, where)

    def chan(self, target):
        source = lambda other: target.at[self.chan_here]
        where = lambda other: {"hi": lax.div(other, 2), "lo": lax.rem(other, 2)}
        return self.go(4, self.chan_here, source, target, where)

    def plane(self, target, source):
        where = lambda other: {
            "dz": lax.div(other, 4), "dy": lax.rem(lax.div(other, 2), 2), "hi": lax.rem(other, 2)
        }
        return self.go(16, self.plane_here, source, target, where)


def all_partners():
    z, y, x = place()
    core = lax.axis_index("lo")
    here = 4 * z + 2 * y + x
    others = []
    for k in range(1, 16):
        o = lax.rem(here + k, 16)
        others.append({"dz": lax.div(o, 4), "dy": lax.rem(lax.div(o, 2), 2), "hi": lax.rem(o, 2)})
    return others + [{"lo": 1 - core}, {"hi": 1 - x, "lo": 1 - core}]


def total_of(ref):
    total = ref[0]
    for k in range(1, ref.shape[0]):
        total = total + ref[k]
    return total


def onehot_of(labels, count, first):
    numbers = lax.broadcasted_iota(jnp.int32, (IMAGES_HERE, count), 1) + first
    return jnp.where(labels[:, 0:1] == numbers.astype(single), 1.0, 0.0).astype(narrow)


def sinusoid_rows(times, labels):
    row = lax.broadcasted_iota(jnp.int32, (8, TF), 0)
    lane = lax.broadcasted_iota(jnp.int32, (8, TF), 1)
    half = TF // 2
    frequency = jnp.exp(-math.log(10000.0) * lax.rem(lane, half).astype(single) / half)
    angles = jnp.where(row == 0, times[0], times[1]).astype(single) * frequency
    sin = jnp.where(lane < half, jnp.cos(angles), jnp.sin(angles)).astype(narrow).astype(single)
    label = jnp.where(row == 2, labels[0], labels[1]).astype(single)
    return jnp.where(row < 2, sin, jnp.where(row < 4, label, 0.0))


def embed_steps(small, times, labels, time_in, emb_out, emb_proj, msg, p0, p1, p2, p3, m3, mod_ref, keep):
    sin_ref, label_ref, pre_ref, embedding_ref = keep
    here, chan = small.dp_here, small.chan_here
    rows = time_in.shape[0]
    msg[...] = jnp.zeros_like(msg)
    sent = sinusoid_rows(times, labels)
    for other in range(8):
        msg[other, :, 0:rows] = sent[:, other * rows : (other + 1) * rows]
    p0[here] = msg[here]
    wait = small.dp(p0, lambda other: msg.at[other])
    yield
    wait()
    flat = p0[...].reshape(64, BLOCK)
    sin = exact_dot(chosen((16, 64), lambda r, c: c == 8 * (r // 2) + r % 2), flat)
    label = exact_dot(chosen((16, 64), lambda r, c: c == 8 * (r // 2) + r % 2 + 2), flat)
    sin_ref[...], label_ref[...] = sin, label
    p1[here] = dot(sin[:, 0:rows].astype(narrow), time_in[...].astype(narrow))
    wait = small.dp(p1)
    yield
    wait()
    pre = total_of(p1)
    pre_ref[...] = pre
    hidden = (pre * sigmoid(pre)).astype(narrow)
    width = hidden.shape[1]
    count = emb_out.shape[1] - width
    onehot = onehot_of(label, count, chan * count)
    part = dot_t(hidden, emb_out[:, 0:width].astype(narrow))
    p2[chan] = part + dot_t(onehot, emb_out[:, width:].astype(narrow))
    wait = small.chan(p2)
    yield
    wait()
    embedding = total_of(p2)
    embedding_ref[...] = embedding
    context = (embedding * sigmoid(embedding)).astype(narrow)
    parts = jnp.concatenate([dot(context, emb_proj[n].astype(narrow)) for n in range(2)], 0)
    spread_rows = chosen((128, 32), lambda r, c: (c == 16 * (r % 8) + r // 8) & (r % 8 < 2))
    m3[...] = exact_dot(spread_rows, parts).reshape(16, 8, HALF)
    p3[small.plane_here] = m3[small.plane_here]
    wait = small.plane(p3, lambda other: m3.at[other])
    yield
    wait()
    flat = p3[...].reshape(128, HALF)
    for half in range(2):
        pick = chosen((8, 128), lambda r, c: (c % 8 == r) & ((c // 8) % 2 == half) & (r < 2))
        wide = exact_dot(pick, flat)
        for kind in range(2):
            value = exact_dot(wide, odd_even(kind))
            for n in range(2):
                mod_ref[n, kind : kind + 1, half * BLOCK : (half + 1) * BLOCK] = value[n : n + 1]
    yield


def embed_back_steps(small, dmod, q4, p4, p5, p6, emb_out, emb_proj, keep, proj_grad, out_grad, time_grad):
    sin_ref, label_ref, pre_ref, embedding_ref = keep
    here, chan, plane = small.dp_here, small.chan_here, small.plane_here
    for half in range(2):
        lanes = slice(half * BLOCK, (half + 1) * BLOCK)
        wide = exact_dot(dmod[0][:, lanes], even_odd(0)) + exact_dot(dmod[1][:, lanes], even_odd(1))
        q4[half] = wide.astype(narrow).astype(single)
    p4[plane] = q4[lax.rem(plane, 2)]
    wait = small.plane(p4, lambda other: q4.at[lax.rem(other, 2)])
    yield
    wait()
    flat = p4[...].reshape(128, HALF)
    embedding, pre = embedding_ref[...], pre_ref[...]
    context = (embedding * sigmoid(embedding)).astype(narrow)
    part = None
    for n in range(2):
        grads = exact_dot(chosen((16, 128), lambda r, c: c == 8 * r + n), flat).astype(narrow)
        proj_grad[n] = contract_rows(context, grads)
        more = dot_t(grads, emb_proj[n].astype(narrow))
        part = more if part is None else part + more
    p5[chan] = part
    wait = small.chan(p5)
    yield
    wait()
    low = (total_of(p5) * silu_grad(embedding)).astype(narrow)
    hidden = (pre * sigmoid(pre)).astype(narrow)
    width = hidden.shape[1]
    count = emb_out.shape[1] - width
    p6[here] = dot(low, emb_out[:, 0:width].astype(narrow))
    wait = small.dp(p6)
    out_grad[:, 0:width] = contract_rows(low, hidden)
    out_grad[:, width:] = contract_rows(low, onehot_of(label_ref[...], count, chan * count))
    yield
    wait()
    pre_grad = (total_of(p6) * silu_grad(pre)).astype(narrow)
    time_grad[...] = contract_rows(sin_ref[...].astype(narrow), pre_grad)[0 : time_grad.shape[0]]
    yield


def row_sums(squared):
    return lax.dot_general(
        jnp.ones((8, squared.shape[1]), single), squared, (((1,), (1,)), ((), ())),
        precision=EXACT, preferred_element_type=single,
    )[0:1]


def to_column(row):
    pieces = []
    for start in range(0, row.shape[1], BLOCK):
        part = row[:, start : start + BLOCK]
        n = part.shape[1]
        square = chosen((n, n), lambda r, c: r == c) * part
        pieces.append(jnp.sum(square, 1, keepdims=True))
    return jnp.concatenate(pieces, 0)


def joined_rows(ref):
    return jnp.concatenate([ref[n, k : k + 1, :] for n in range(6) for k in range(2)], 0)


def scalar_rows(values, count, lanes=BLOCK):
    rows = [jnp.broadcast_to(value, (1, lanes)) for value in values]
    return jnp.concatenate(rows + [jnp.zeros((count - len(rows), lanes), single)], 0)


def whole(value):
    return jnp.sum(jnp.sum(value, 1, keepdims=True), 0, keepdims=True)


DECAY = 1.0 - STEP ** (-0.8)
ROW_LANES = 640
COL_LANES = 512


def adafactor_steps(
    small, early, late, grads, rows_old, cols_old, fulls, wsq_ref, loss_ref, sums, norms_own, second,
    p7, q7, p8, p9, p10, p11, p12, rows_ref, cols_ref, scal_ref, norm_out, second_out, norms_out,
):
    here, chan, plane = small.dp_here, small.chan_here, small.plane_here
    x = lax.axis_index("hi")
    count = len(grads)
    for half in range(2):
        lanes = slice(half * BLOCK, (half + 1) * BLOCK)
        rows = [sums[n, k : k + 1, lanes] for n in range(6) for k in range(2)]
        q7[half] = jnp.concatenate(rows + [jnp.zeros((4, BLOCK), single)], 0)
    p7[plane] = q7[x]
    wait_norms = small.plane(p7, lambda other: q7.at[lax.rem(other, 2)])
    p8[chan] = jnp.zeros(p8.shape[1:], single)
    p9[here] = jnp.zeros(p9.shape[1:], single)
    def measure(m):
        value = grads[m][...]
        squared = value * value + tiny_square
        n_rows, n_cols = value.shape
        p8[chan, m : m + 1, 0:n_rows] = row_sums(squared)
        p9[here, m : m + 1, 0:n_cols] = jnp.sum(squared, 0, keepdims=True)
        p8[chan, m : m + 1, 576:] = jnp.broadcast_to(wsq_ref[m : m + 1, 0:1], (1, 64))

    for m in early:
        measure(m)
    yield
    for m in late:
        measure(m)
    p8[chan, count : count + 1, 576:] = jnp.broadcast_to(loss_ref[0:1, 0:1], (1, 64))
    wait_rows = small.chan(p8)
    wait_cols = small.dp(p9)
    wait_rows()
    row_total = total_of(p8)
    rows_new, rows_sum = [], []
    for m, grad in enumerate(grads):
        n_rows = grad.shape[0]
        new = DECAY * rows_old[m] + (1.0 - DECAY) * row_total[m : m + 1, 0:n_rows] / fulls[m][1]
        rows_ref[m : m + 1, 0:n_rows] = new
        rows_new.append(new)
        rows_sum.append(jnp.sum(new, 1, keepdims=True))
    low = lax.broadcasted_iota(jnp.int32, (16, BLOCK), 1) < 64
    p10[here] = jnp.where(low, scalar_rows(rows_sum, 16), row_total[:, 576:577])
    wait_scalars = small.dp(p10)
    wait_cols()
    col_total = total_of(p9)
    cols_new = []
    for m, grad in enumerate(grads):
        n_cols = grad.shape[1]
        new = DECAY * cols_old[m] + (1.0 - DECAY) * col_total[m : m + 1, 0:n_cols] / fulls[m][0]
        cols_ref[m : m + 1, 0:n_cols] = new
        cols_new.append(new)
    wait_norms()
    norm_total = total_of(p7)[0:12]
    own = joined_rows(norms_own)
    norm_out[...] = norm_total
    second_new = DECAY * joined_rows(second) + (1.0 - DECAY) * (norm_total * norm_total + tiny_square)
    second_out[...] = second_new
    norm_update = norm_total * lax.rsqrt(second_new)
    wait_scalars()
    scalars = total_of(p10)
    means, update_sq = [], []
    for m, grad in enumerate(grads):
        mean = scalars[m : m + 1, 0:1] / fulls[m][0]
        means.append(mean)
        update = grad[...] * to_column(lax.rsqrt(rows_new[m] / mean)) * lax.rsqrt(cols_new[m])
        update_sq.append(whole(update * update))
    sq = [jnp.sum(norm_update * norm_update, 1, keepdims=True), jnp.sum(own * own, 1, keepdims=True)]
    wide = jnp.where(lax.broadcasted_iota(jnp.int32, (12, BLOCK), 1) < 64, sq[0], sq[1])
    p11[chan, 0:16] = scalar_rows(update_sq, 16)
    p11[chan, 16:32] = jnp.concatenate([wide, jnp.zeros((4, BLOCK), single)], 0)
    small.chan(p11)()
    over_chan = total_of(p11)
    p12[here] = over_chan[0:16]
    wait = small.dp(p12)
    norm_sq = over_chan[16:28]
    norm_clip = jnp.maximum(1.0, jnp.sqrt(norm_sq[:, 0:1] / float(C)))
    norm_scale = jnp.maximum(floor_scale, jnp.sqrt(norm_sq[:, 64:65] / float(C)))
    norms_out[...] = own - (step_rate * norm_scale / norm_clip) * norm_update
    wait()
    over_all = total_of(p12)
    steps = []
    for m in range(count):
        entries = fulls[m][0] * fulls[m][1]
        clip = jnp.maximum(1.0, jnp.sqrt(over_all[m : m + 1, 0:1] / entries))
        scale = jnp.maximum(floor_scale, jnp.sqrt(scalars[m : m + 1, 64:65] / entries))
        steps.append(step_rate * scale / clip)
    scal_ref[0:16] = scalar_rows(means, 16)
    scal_ref[16:32] = scalar_rows(steps, 16)
    scal_ref[32:40] = jnp.broadcast_to(scalars[count : count + 1, 64:65], (8, BLOCK))
    yield


def finish_kernel(*refs):
    (g0, g1, g2, g3, g4, g5, proj, time, emb, rows, cols, scal, norm, second, norms_new,
     conv_in, conv_out, emb_proj, attn, time_in, emb_out,
     loss, in_g, in_r, in_c, in_w, out_g, out_r, out_c, out_w, proj_g, proj_r, proj_c, proj_w,
     attn_g, attn_r, attn_c, attn_w, time_g, time_r, time_c, time_w, emb_g, emb_r, emb_c, emb_w,
     norm_o, second_o, norms_o) = refs
    loss[...] = scal[32:33, 0:1]
    plan = [
        (0, g0, conv_in.at[0], in_g.at[0], in_r.at[0:1], in_c.at[0:1], in_w.at[0]),
        (1, g3, conv_in.at[1], in_g.at[1], in_r.at[1:2], in_c.at[1:2], in_w.at[1]),
        (2, g5, conv_in.at[2], in_g.at[2], in_r.at[2:3], in_c.at[2:3], in_w.at[2]),
        (3, g1, conv_out.at[0], out_g.at[0], out_r.at[0:1], out_c.at[0:1], out_w.at[0]),
        (4, g4, conv_out.at[1], out_g.at[1], out_r.at[1:2], out_c.at[1:2], out_w.at[1]),
        (5, proj.at[0], emb_proj.at[0], proj_g.at[0], proj_r.at[0:1], proj_c.at[0:1], proj_w.at[0]),
        (6, proj.at[1], emb_proj.at[1], proj_g.at[1], proj_r.at[1:2], proj_c.at[1:2], proj_w.at[1]),
        (7, g2, attn, attn_g, attn_r, attn_c, attn_w),
        (8, time, time_in, time_g, time_r, time_c, time_w),
        (9, emb, emb_out, emb_g, emb_r, emb_c, emb_w),
    ]
    for m, grad, weight, grad_o, rows_o, cols_o, weight_o in plan:
        n_rows, n_cols = grad_o.shape
        row, col = rows[m : m + 1, 0:n_rows], cols[m : m + 1, 0:n_cols]
        rows_o[...] = row
        cols_o[...] = col
        value = grad[...]
        grad_o[...] = value
        mean, step = scal[m : m + 1, 0:1], scal[16 + m : 17 + m, 0:1]
        update = value * to_column(lax.rsqrt(row / mean)) * lax.rsqrt(col)
        weight_o[...] = weight[...] - step * update
    for n in range(6):
        at = slice(2 * n, 2 * n + 2)
        norm_o[n], second_o[n], norms_o[n] = norm[at, :], second[at, :], norms_new[at, :]


def vmem(shape, dtype=single):
    return pltpu.VMEM(shape, dtype)


def semaphores(*shape):
    return pltpu.SemaphoreType.DMA(shape)


TAPS_SHAPE = (9 * C, HALF)
ATTN_SHAPE = (C, 2 * C)
FULL = (PIX, C)
OWN = (PIX, HALF)
QKV = (PIX, 6 * BLOCK)
LOGS = (4, PIX // CHUNK, 1, CHUNK)
WEIGHTS = [TAPS_SHAPE, TAPS_SHAPE, ATTN_SHAPE, TAPS_SHAPE, TAPS_SHAPE, TAPS_SHAPE]


def fused(body, outs, out_specs, in_specs, scratch, args, number, limit, name):
    return pl.pallas_call(
        body,
        out_shape=outs,
        in_specs=in_specs,
        out_specs=out_specs,
        scratch_shapes=scratch,
        compiler_params=pltpu.CompilerParams(
            vmem_limit_bytes=limit * 2**20, collective_id=number, has_side_effects=True
        ),
        name=name,
    )(*args)


def fused_step(
    noisy, noise, timesteps, classes, sample_weight,
    conv_in, conv_out, emb_proj, attn_weight, time_in, emb_out, norms, moments, norm_second,
):
    images = noisy.shape[0] * lax.axis_size("dz") * lax.axis_size("dy")
    total = float(images * PIX * C)
    low_shapes = WEIGHTS + [FULL] * 4
    kept = [struct(s, narrow) for s in low_shapes] + [struct(OWN)] * 5
    kept += [struct(OWN, narrow)] * 2 + [struct(QKV, narrow)] + [struct(OWN, narrow)] * 3
    tail = [LOGS, (8, BLOCK), (12, HALF), (2, 2, HALF), (16, BLOCK), (16, BLOCK), (16, BLOCK), (16, HALF), (16, BLOCK)]
    outs = kept + [struct(s) for s in tail]
    scratch = [vmem(s, narrow) for s in low_shapes] + [vmem(OWN)] * 5
    scratch += [vmem(OWN, narrow)] * 2 + [vmem(QKV, narrow)] + [vmem(OWN, narrow)] * 2 + [vmem(OWN)]
    scratch += [vmem((3, ROWS, C), narrow), vmem(OWN)] + [vmem(OWN, narrow)] * 6
    scratch += [vmem((PIX, BLOCK), narrow), vmem((BLOCK, PIX), narrow)]
    scratch += [vmem(OWN, narrow), vmem((12, HALF)), vmem((1, HALF)), vmem((12, BLOCK)), vmem((8, 8, BLOCK))]
    shard, attn_shard = conv_in.shape[1:], attn_weight.shape
    scratch += [vmem(s, narrow) for s in (shard, shard, attn_shard, shard, shard, shard)]
    scratch += [vmem(s) for s in ((8, 8, BLOCK), (8, 16, HALF), (4, 16, BLOCK), (16, 8, HALF), (16, 8, HALF))]
    scratch += [semaphores(LAYERS, STEPS)] * 2 + [semaphores(LAYERS)]
    scratch += [semaphores(48)] * 2 + [semaphores(3)] * 2 + [semaphores(32)] * 2 + [semaphores(32)]
    pixels = (2, PIX, BLOCK)
    args = [noisy.reshape(pixels), noise.reshape(pixels), sample_weight, timesteps, classes, norms]
    args += [conv_in, conv_out, attn_weight, time_in, emb_out, emb_proj]
    in_specs = [ANY] * 2 + [SMEM] * 3 + [VMEM] * (len(args) - 5)
    body = functools.partial(forward_kernel, total)
    out_specs = [ANY] * len(kept) + [VMEM] * len(tail)
    results = fused(body, outs, out_specs, in_specs, scratch, args, 1, 60, "forward")
    acts, small = results[: len(kept)], results[len(kept) :]

    weights = [conv_in[0], conv_in[1], conv_in[2], conv_out[0], conv_out[1]]
    weights += [emb_proj[0], emb_proj[1], attn_weight, time_in, emb_out]
    dp, chan = lax.axis_size("dz") * lax.axis_size("dy"), lax.axis_size("hi") * lax.axis_size("lo")
    fulls = [(float(w.shape[0] * dp), float(w.shape[1] * chan)) for w in weights]
    shapes = [shard, shard, attn_shard, shard, shard, shard, emb_proj.shape, time_in.shape, emb_out.shape]
    shapes += [(16, ROW_LANES), (16, COL_LANES), (40, BLOCK)] + [(12, BLOCK)] * 3
    outs = [struct(s) for s in shapes]
    scratch = [vmem(TAPS_SHAPE, narrow)] * 2 + [vmem(ATTN_SHAPE, narrow)] + [vmem(s, narrow) for s in WEIGHTS]
    for lead, (rows, lanes) in ((5, shard), (None, attn_shard)):
        parts = [(4 * rows, lanes), (2, rows, 2 * lanes), (2, rows, lanes), (2, rows, lanes), (3, rows, lanes)]
        scratch += [vmem(s if lead is None else (lead, *s), narrow) for s in parts]
    scratch += [vmem(FULL, narrow)] * 4 + [vmem(OWN), vmem(OWN, narrow), vmem(OWN), vmem(OWN, narrow)]
    scratch += [vmem(QKV, narrow), vmem(OWN, narrow), vmem(OWN, narrow)]
    scratch += [vmem((3, ROWS, C), narrow), vmem((C, PIX), narrow)] + [vmem(OWN)] * 4 + [vmem(OWN, narrow)] * 5
    scratch += [vmem((PIX, BLOCK), narrow), vmem((BLOCK, PIX), narrow)] + [vmem((PIX, BLOCK))] * 2
    scratch += [vmem((6, 2, HALF)), vmem((2, 8, HALF))]
    swaps = [(2, 8, HALF), (16, 8, HALF), (4, 16, BLOCK), (8, 16, HALF), (16, 16, BLOCK), (2, 16, BLOCK)]
    swaps += [(4, 16, ROW_LANES), (8, 16, COL_LANES), (8, 16, BLOCK), (4, 32, BLOCK), (8, 16, BLOCK)]
    scratch += [vmem(s) for s in swaps]
    scratch += [semaphores(LAYERS, STEPS)] * 2 + [semaphores(48)] * 2 + [semaphores(80)] * 2 + [semaphores(32)]
    flat = [value.reshape(1, -1) if value.ndim == 1 else value for value in moments]
    args = [*small, emb_out, emb_proj, norms, norm_second, *flat]
    in_specs = [VMEM] * len(args) + [ANY] * len(acts)
    args += acts
    body = functools.partial(backward_kernel, fulls)
    results = fused(body, outs, [VMEM] * len(outs), in_specs, scratch, args, 2, 63, "backward")

    def four(weight, row, col):
        return [struct(weight.shape), struct(row.shape), struct(col.shape), struct(weight.shape)]

    outs = [struct((1, 1))]
    for n, weight in enumerate((conv_in, conv_out, emb_proj, attn_weight, time_in, emb_out)):
        outs += four(weight, flat[2 * n], flat[2 * n + 1])
    outs += [struct(norms.shape)] * 3
    args = [*results, conv_in, conv_out, emb_proj, attn_weight, time_in, emb_out]
    finals = list(call(finish_kernel, outs, [], args, "finish"))
    finals[0] = finals[0].reshape(())
    for n, value in enumerate(moments):
        place_at = 2 + 4 * (n // 2) + n % 2
        finals[place_at] = finals[place_at].reshape(value.shape)
    return tuple(finals)


def pack_flat(members):
    return jnp.concatenate([member.reshape(-1) for member in members])


def unpack_flat(vector, shape_list):
    pieces = []
    offset = 0
    for array_shape in shape_list:
        extent = math.prod(array_shape)
        pieces.append(vector[offset : offset + extent].reshape(array_shape))
        offset += extent
    return pieces


def per_device(
    noisy,
    noise,
    timesteps,
    classes,
    sample_weight,
    conv_in,
    conv_out,
    emb_proj,
    attn_weight,
    time_in,
    emb_out,
    norms,
    conv_in_rows,
    conv_in_cols,
    conv_out_rows,
    conv_out_cols,
    emb_proj_rows,
    emb_proj_cols,
    attn_rows,
    attn_cols,
    time_rows,
    time_cols,
    embout_rows,
    embout_cols,
    norm_second,
):
    rows_here = (conv_in.shape[1], attn_weight.shape[0])
    if lax.axis_size("dz") == 4 and all(rows % 64 == 0 for rows in rows_here):
        moments = [conv_in_rows, conv_in_cols, conv_out_rows, conv_out_cols, emb_proj_rows, emb_proj_cols]
        moments += [attn_rows, attn_cols, time_rows, time_cols, embout_rows, embout_cols]
        return fused_step(
            noisy, noise, timesteps, classes, sample_weight, conv_in, conv_out, emb_proj, attn_weight, time_in,
            emb_out, norms, moments, norm_second,
        )
    masters = [conv_in, conv_out, emb_proj, attn_weight[None], time_in[None], emb_out[None]]
    lowered = [master.astype(narrow) for master in masters]
    modulate, saved = embed_forward(timesteps, classes, lowered[4][0], lowered[5][0], lowered[2])
    norms_wide = join_image(norms, 2)
    shards = [lowered[0][0], lowered[1][0], lowered[3][0], lowered[0][1], lowered[1][1], lowered[0][2]]
    full = [gather_weight(shard) for shard in shards]
    loss_part, din, dout, dattn, sums, dmod = network(
        noisy, noise, sample_weight, (full[0], full[3], full[5]), (full[1], full[4]), full[2], norms_wide, modulate
    )
    reduced_parts = [scatter_grad(part) for part in (din[0], dout[0], dattn, din[1], dout[1], din[2])]
    in0_grad, out0_grad, attn_grad, in1_grad, out1_grad, head_grad = reduced_parts
    proj_grad, time_grad, embout_grad = embed_backward(saved, dmod, lowered[2], lowered[5][0])
    norm_local = lax.psum_scatter(sums, "hi", scatter_dimension=2, tiled=True)
    reduced = [
        jnp.stack([in0_grad, in1_grad, head_grad]),
        jnp.stack([out0_grad, out1_grad]),
        proj_grad,
        attn_grad[None],
        time_grad[None],
        embout_grad[None],
    ]
    decay_rate = 1.0 - STEP ** (-0.8)
    dp_count = lax.axis_size("dz") * lax.axis_size("dy")
    chan_count = lax.axis_size("hi") * lax.axis_size("lo")
    rows_old = [
        conv_in_rows,
        conv_out_rows,
        emb_proj_rows,
        attn_rows[None],
        time_rows[None],
        embout_rows[None],
    ]
    cols_old = [
        conv_in_cols,
        conv_out_cols,
        emb_proj_cols,
        attn_cols[None],
        time_cols[None],
        embout_cols[None],
    ]
    squares = [gradient * gradient + tiny_square for gradient in reduced]
    full_rows = [squared.shape[1] * dp_count for squared in squares]
    full_cols = [squared.shape[2] * chan_count for squared in squares]
    row_parts = [jnp.sum(squared, 2) for squared in squares]
    col_parts = [jnp.sum(squared, 1) for squared in squares]
    row_shapes = [member.shape for member in row_parts]
    col_shapes = [member.shape for member in col_parts]
    norm_width = norm_local.shape[2]
    row_totals = unpack_flat(lax.psum(pack_flat(row_parts), ("hi", "lo")), row_shapes)
    rows_new = [
        decay_rate * rows_old[position]
        + (1.0 - decay_rate) * row_totals[position] / full_cols[position]
        for position in range(6)
    ]
    row_sums_local = [jnp.sum(member, 1) for member in rows_new]
    col_vector, norm_total = lax.psum((pack_flat(col_parts + row_sums_local), norm_local), DP)
    col_pieces = unpack_flat(col_vector, col_shapes + [(member.shape[0],) for member in rows_new])
    col_totals = col_pieces[:6]
    row_means = [col_pieces[6 + position] / full_rows[position] for position in range(6)]
    cols_new = [
        decay_rate * cols_old[position]
        + (1.0 - decay_rate) * col_totals[position] / full_rows[position]
        for position in range(6)
    ]
    updates = [
        reduced[position]
        * lax.rsqrt(rows_new[position] / row_means[position][:, None])[:, :, None]
        * lax.rsqrt(cols_new[position])[:, None, :]
        for position in range(6)
    ]
    second_new = decay_rate * norm_second + (1.0 - decay_rate) * (
        norm_total * norm_total + tiny_square
    )
    norm_update = norm_total * lax.rsqrt(second_new)
    update_squares = pack_flat([jnp.sum(member * member, (1, 2)) for member in updates])
    weight_squares = pack_flat([jnp.sum(master * master, (1, 2)) for master in masters])
    norm_update_sq = jnp.sum(norm_update * norm_update, 2) / dp_count
    norm_weight_sq = jnp.sum(norms * norms, 2) / dp_count
    update_total, weight_total, norm_update_total, norm_weight_total, loss = lax.psum(
        (update_squares, weight_squares, norm_update_sq, norm_weight_sq, loss_part), ("dz", "dy", "hi", "lo")
    )
    layer_shapes = [(member.shape[0],) for member in masters]
    update_sums = unpack_flat(update_total, layer_shapes)
    weight_sums = unpack_flat(weight_total, layer_shapes)
    results = [loss]
    for position in range(6):
        entries = float(full_rows[position] * full_cols[position])
        clip_factor = jnp.maximum(1.0, jnp.sqrt(update_sums[position] / entries))
        scale_factor = jnp.maximum(floor_scale, jnp.sqrt(weight_sums[position] / entries))
        weight_new = (
            masters[position]
            - (step_rate * scale_factor / clip_factor)[:, None, None] * updates[position]
        )
        if position >= 3:
            results += [
                reduced[position][0],
                rows_new[position][0],
                cols_new[position][0],
                weight_new[0],
            ]
        else:
            results += [reduced[position], rows_new[position], cols_new[position], weight_new]
    norm_entries = float(norm_width * chan_count)
    norm_clip = jnp.maximum(1.0, jnp.sqrt(norm_update_total / norm_entries))
    norm_scale = jnp.maximum(floor_scale, jnp.sqrt(norm_weight_total / norm_entries))
    norms_new = norms - (step_rate * norm_scale / norm_clip)[:, :, None] * norm_update
    results += [norm_total, second_new, norms_new]
    return (
        results[0],
        results[1],
        results[2],
        results[3],
        results[4],
        results[5],
        results[6],
        results[7],
        results[8],
        results[9],
        results[10],
        results[11],
        results[12],
        results[13],
        results[14],
        results[15],
        results[16],
        results[17],
        results[18],
        results[19],
        results[20],
        results[21],
        results[22],
        results[23],
        results[24],
        results[25],
        results[26],
        results[27],
    )


CHAN = ("hi", "lo")


def solution(mesh):
    dp, chan = mesh.shape["dp"], mesh.shape["chan"]
    mesh = Mesh(mesh.devices.reshape(dp // 2, 2, 2, chan // 2), DP + CHAN)
    in_specs = (
        P(DP, None, None, CHAN),
        P(DP, None, None, CHAN),
        P(DP),
        P(DP),
        P(DP),
        P(None, DP, CHAN),
        P(None, DP, CHAN),
        P(None, DP, CHAN),
        P(DP, CHAN),
        P(DP, CHAN),
        P(DP, CHAN),
        P(None, None, CHAN),
        P(None, DP),
        P(None, CHAN),
        P(None, DP),
        P(None, CHAN),
        P(None, DP),
        P(None, CHAN),
        P(DP),
        P(CHAN),
        P(DP),
        P(CHAN),
        P(DP),
        P(CHAN),
        P(None, None, CHAN),
    )
    out_specs = (
        P(),
        P(None, DP, CHAN),
        P(None, DP),
        P(None, CHAN),
        P(None, DP, CHAN),
        P(None, DP, CHAN),
        P(None, DP),
        P(None, CHAN),
        P(None, DP, CHAN),
        P(None, DP, CHAN),
        P(None, DP),
        P(None, CHAN),
        P(None, DP, CHAN),
        P(DP, CHAN),
        P(DP),
        P(CHAN),
        P(DP, CHAN),
        P(DP, CHAN),
        P(DP),
        P(CHAN),
        P(DP, CHAN),
        P(DP, CHAN),
        P(DP),
        P(CHAN),
        P(DP, CHAN),
        P(None, None, CHAN),
        P(None, None, CHAN),
        P(None, None, CHAN),
    )
    return jax.shard_map(
        per_device, mesh=mesh, in_specs=in_specs, out_specs=out_specs, check_vma=False
    )
```

```python
import functools
import math

import jax
import jax.numpy as jnp
from jax import lax
from jax.experimental import pallas as pl
from jax.experimental.pallas import tpu as pltpu
from jax.sharding import Mesh
from jax.sharding import PartitionSpec as P

C = 512
HEADS = 8
GROUPS = 32
TF = 256
STEP = 10
SIDE = 32
PIX = 1024
HALF = 256
BLOCK = 128
PAD = SIDE
ROWS = PIX + 2 * PAD
CHUNK = 256

single = jnp.float32
narrow = jnp.bfloat16
step_rate = 0.5
floor_scale = 0.001
tiny_square = 1e-30
norm_eps = 1e-05

TAPS = [(t // 3 - 1, t % 3 - 1) for t in range(9)]


def dot(a, b):
    return jnp.dot(a, b, preferred_element_type=single)


def dot_t(a, b):
    return lax.dot_general(a, b, (((1,), (1,)), ((), ())), preferred_element_type=single)


def group_sum(row):
    lane = lax.broadcasted_iota(jnp.int32, (HALF, HALF), 0)
    other = lax.broadcasted_iota(jnp.int32, (HALF, HALF), 1)
    size = C // GROUPS
    ones = jnp.where(lane // size == other // size, 1.0, 0.0).astype(single)
    tall = jnp.broadcast_to(row, (8, HALF))
    return jnp.dot(tall, ones, precision=lax.Precision.HIGHEST, preferred_element_type=single)[0:1]


def loop_sum(count, make):
    zeros = make(None)

    def body(i, carried):
        return [old + new for old, new in zip(carried, make(i))]

    return lax.fori_loop(0, count, body, [jnp.zeros((1, HALF), single)] * zeros)


def rows_of(i, size=CHUNK, offset=0):
    return pl.ds(pl.multiple_of(offset + i * size, 32), size)


def stats(x_ref):
    members = float(PIX * (C // GROUPS))

    def first(i):
        if i is None:
            return 1
        return [jnp.sum(x_ref[rows_of(i), :], 0, keepdims=True)]

    (total,) = loop_sum(PIX // CHUNK, first)
    mean = group_sum(total) / members

    def second(i):
        if i is None:
            return 1
        center = x_ref[rows_of(i), :] - mean
        return [jnp.sum(center * center, 0, keepdims=True)]

    (square,) = loop_sum(PIX // CHUNK, second)
    rstd = lax.rsqrt(group_sum(square) / members + norm_eps)
    return mean, rstd


def sigmoid(v):
    return 1.0 / (1.0 + jnp.exp(-v))


def norm_forward(x_ref, gain, bias, act, store):
    mean, rstd = stats(x_ref)

    @pl.loop(0, PIX // CHUNK)
    def _(i):
        value = (x_ref[rows_of(i), :] - mean) * rstd * gain + bias
        if act:
            value = value * sigmoid(value)
        store(i, value.astype(narrow))


def norm_backward(x_ref, load_grad, gain, bias, act, tmp_ref, store, wait=None):
    mean, rstd = stats(x_ref)
    members = float(PIX * (C // GROUPS))
    if wait is not None:
        wait()

    def first(i):
        if i is None:
            return 2
        hat = (x_ref[rows_of(i), :] - mean) * rstd
        grad = load_grad(i)
        if act:
            mixed = hat * gain + bias
            gate = sigmoid(mixed)
            grad = grad * gate * (1.0 + mixed * (1.0 - gate))
        tmp_ref[rows_of(i), :] = grad
        return [jnp.sum(grad, 0, keepdims=True), jnp.sum(grad * hat, 0, keepdims=True)]

    total, along = loop_sum(PIX // CHUNK, first)
    mean_grad = group_sum(gain * total) / members
    mean_along = group_sum(gain * along) / members

    @pl.loop(0, PIX // CHUNK)
    def _(i):
        hat = (x_ref[rows_of(i), :] - mean) * rstd
        store(i, rstd * (tmp_ref[rows_of(i), :] * gain - mean_grad - hat * mean_along))

    return total, along


def shifts(load, s_ref, width):
    for b in range(3):
        s_ref[b, 0:PAD, 0:width] = jnp.zeros((PAD, width), narrow)
        s_ref[b, PAD + PIX : ROWS, 0:width] = jnp.zeros((PAD, width), narrow)
    size = 128

    @pl.loop(0, PIX // size)
    def _(i):
        value = load(i, size)
        wide = value.astype(single)
        across = lax.broadcasted_iota(jnp.int32, wide.shape, 0) % SIDE
        left = jnp.where(across > 0, pltpu.roll(wide, 1, 0), 0.0)
        right = jnp.where(across < SIDE - 1, pltpu.roll(wide, size - 1, 0), 0.0)
        at = rows_of(i, size, PAD)
        s_ref[0, at, 0:width] = left.astype(narrow)
        s_ref[1, at, 0:width] = value
        s_ref[2, at, 0:width] = right.astype(narrow)


def tap_rows(s_ref, t, sign, i, size, width):
    a, b = TAPS[t]
    return s_ref[sign * b + 1, rows_of(i, size, PAD + sign * a * SIDE), 0:width]


def split_core(value):
    core = lax.axis_index("lo")
    b0, b1, b2, b3 = [value[:, k * BLOCK : (k + 1) * BLOCK] for k in range(4)]
    even, odd = jnp.concatenate([b0, b2], 1), jnp.concatenate([b1, b3], 1)
    first = core == 0
    return jnp.where(first, even, odd), jnp.where(first, odd, even)


def join_core(own_ref, peer_ref, full_ref):
    core = lax.axis_index("lo")

    @pl.loop(0, PIX // CHUNK)
    def _(i):
        at = rows_of(i)
        own, peer = own_ref[at, :].astype(single), peer_ref[at, :].astype(single)
        even = jnp.where(core == 0, own, peer).astype(narrow)
        odd = jnp.where(core == 0, peer, own).astype(narrow)
        full_ref[at, 0:BLOCK] = even[:, 0:BLOCK]
        full_ref[at, BLOCK : 2 * BLOCK] = odd[:, 0:BLOCK]
        full_ref[at, 2 * BLOCK : 3 * BLOCK] = even[:, BLOCK:]
        full_ref[at, 3 * BLOCK :] = odd[:, BLOCK:]


def conv_wide(s_ref, w_ref, store):
    @pl.loop(0, PIX // CHUNK)
    def _(i):
        total = None
        for t in range(9):
            part = dot(tap_rows(s_ref, t, 1, i, CHUNK, C), w_ref[t * C : (t + 1) * C, :])
            total = part if total is None else total + part
        store(i, total)


def conv_tall(s_ref, w_ref, sign, store):
    @pl.loop(0, PIX // CHUNK)
    def _(i):
        total = None
        for t in range(9):
            part = dot_t(tap_rows(s_ref, t, sign, i, CHUNK, HALF), w_ref[t * C : (t + 1) * C, :])
            total = part if total is None else total + part
        store(i, total)


def conv_back(s_ref, w_ref, store):
    @pl.loop(0, PIX // CHUNK)
    def _(i):
        total = None
        for t in range(9):
            part = dot(tap_rows(s_ref, t, -1, i, CHUNK, C), w_ref[t * C : (t + 1) * C, :])
            total = part if total is None else total + part
        store(i, total)


def transpose_into(load, t_ref):
    for i in range(PIX // CHUNK):
        t_ref[:, i * CHUNK : (i + 1) * CHUNK] = jnp.transpose(load(i).astype(single)).astype(narrow)


def kernel_grad(t_ref, s_ref, sign, store):
    for t in range(9):
        a, b = TAPS[t]
        start = PAD + sign * a * SIDE
        store(t, dot(t_ref[...], s_ref[sign * b + 1, start : start + PIX, 0:HALF]))


def low_lanes(shape):
    return lax.broadcasted_iota(jnp.int32, shape, 1) < BLOCK // 2


def swap_halves(value):
    half = BLOCK // 2
    return jnp.concatenate([value[:, half:], value[:, :half]], 1)


def mask_half(value, upper):
    low = low_lanes(value.shape)
    return jnp.where(low != upper, value.astype(single), 0.0).astype(narrow)


def head_parts(qkv_ref, s, h):
    base = 3 * BLOCK * s
    b0, b1, b2 = [slice(base + k * BLOCK, base + (k + 1) * BLOCK) for k in range(3)]
    return (b0, b0, b1) if h == 0 else (b1, b2, b2)


SCALE = (C // HEADS) ** (-0.5)


def attend(qkv_ref, k_ref, vt_ref, log_ref, out_ref, between=None):
    for s in range(2):
        for h in range(2):
            q_at, k_at, v_at = head_parts(qkv_ref, s, h)
            k_ref[...] = swap_halves(qkv_ref[:, k_at])
            vt_ref[...] = jnp.transpose(qkv_ref[:, v_at].astype(single)).astype(narrow)

            @pl.loop(0, PIX // CHUNK)
            def _(i):
                query = mask_half(qkv_ref[rows_of(i), q_at], h == 1)
                scores = dot_t(k_ref[...], query) * SCALE
                top = jnp.max(scores, 0, keepdims=True)
                exponent = jnp.exp(scores - top)
                total = jnp.sum(exponent, 0, keepdims=True)
                mixed = dot(vt_ref[...], exponent.astype(narrow)) / total
                log_ref[2 * s + h, i] = top + jnp.log(total)
                turned = jnp.transpose(mixed)
                at = rows_of(i)
                lanes = slice(s * BLOCK, (s + 1) * BLOCK)
                if h == 0:
                    out_ref[at, lanes] = turned.astype(narrow)
                else:
                    kept = out_ref[at, lanes].astype(single)
                    out_ref[at, lanes] = jnp.where(low_lanes(turned.shape), kept, turned).astype(narrow)

            if between is not None:
                between(2 * s + h + 1)


def attend_back(qkv_ref, log_ref, grad_ref, k_ref, kt_ref, dk_ref, dv_ref, dqkv, between=None):
    for s in range(2):
        lanes = slice(s * BLOCK, (s + 1) * BLOCK)
        for h in range(2):
            q_at, k_at, v_at = head_parts(qkv_ref, s, h)
            q_to, k_to, v_to = head_parts(None, 0, h)
            grad_to = dqkv[s]
            k_ref[...] = swap_halves(qkv_ref[:, k_at])
            kt_ref[...] = jnp.transpose(k_ref[...].astype(single)).astype(narrow)
            dk_ref[...] = jnp.zeros_like(dk_ref)
            dv_ref[...] = jnp.zeros_like(dv_ref)

            @pl.loop(0, PIX // CHUNK)
            def _(i):
                at = rows_of(i)
                query = mask_half(qkv_ref[at, q_at], h == 1)
                grad = mask_half(grad_ref[at, lanes], h == 1)
                weights = jnp.exp(dot_t(k_ref[...], query) * SCALE - log_ref[2 * s + h, i])
                dv_ref[...] += dot(weights.astype(narrow), grad)
                dweights = dot_t(qkv_ref[:, v_at], grad)
                inner = jnp.sum(weights * dweights, 0, keepdims=True)
                dscores = (weights * (dweights - inner) * SCALE).astype(narrow)
                dk_ref[...] += dot(dscores, query)
                turned = jnp.transpose(dot(kt_ref[...], dscores))
                kept = grad_to[at, q_to].astype(single)
                low = low_lanes(turned.shape)
                if h == 0:
                    grad_to[at, q_to] = turned.astype(narrow)
                else:
                    grad_to[at, q_to] = jnp.where(low, kept, turned).astype(narrow)

            low = low_lanes((PIX, BLOCK))
            dk = swap_halves(dk_ref[...])
            if h == 0:
                grad_to[:, k_to] = jnp.where(low, grad_to[:, k_to].astype(single), dk).astype(narrow)
                grad_to[:, v_to] = dv_ref[...].astype(narrow)
            else:
                grad_to[:, k_to] = jnp.where(low, dk, dv_ref[...]).astype(narrow)
            if between is not None:
                between(2 * s + h + 1)


VMEM = pl.BlockSpec(memory_space=pltpu.VMEM)


def call(body, outs, scratch, args, name):
    return pl.pallas_call(
        body,
        out_shape=outs,
        in_specs=[VMEM] * len(args),
        out_specs=[VMEM] * len(outs),
        scratch_shapes=scratch,
        compiler_params=pltpu.CompilerParams(vmem_limit_bytes=56 * 2**20),
        name=name,
    )(*args)


def struct(shape, dtype=single):
    return jax.ShapeDtypeStruct(shape, dtype)


def entry_kernel(act, x_ref, own_ref, recv_ref, norm_ref, stream_ref, entry_ref):
    @pl.loop(0, PIX // CHUNK)
    def _(i):
        at = rows_of(i)
        stream_ref[at, :] = x_ref[at, :] + (own_ref[at, :] + recv_ref[at, :].astype(single))

    def store(i, value):
        entry_ref[rows_of(i), :] = value

    norm_forward(stream_ref, norm_ref[0:1, :], norm_ref[1:2, :], act, store)


def first_kernel(x_ref, norm_ref, stream_ref, entry_ref):
    @pl.loop(0, PIX // CHUNK)
    def _(i):
        at = rows_of(i)
        stream_ref[at, :] = x_ref[at, :].astype(single)

    def store(i, value):
        entry_ref[rows_of(i), :] = value

    norm_forward(stream_ref, norm_ref[0:1, :], norm_ref[1:2, :], True, store)


def mid_rows(norm_ref, mod_ref):
    gain, bias = norm_ref[0:1, :], norm_ref[1:2, :]
    scale, shift = 1.0 + mod_ref[0:1, :], mod_ref[1:2, :]
    return gain, bias, scale, shift


def put_split(own_ref, peer_ref):
    def store(i, value):
        own, peer = split_core(value)
        own_ref[rows_of(i), :] = own
        peer_ref[rows_of(i), :] = peer.astype(narrow)

    return store


def shift_full(full_ref, s_ref, width):
    shifts(lambda i, size: full_ref[rows_of(i, size), :], s_ref, width)


def res_kernel(own_ref, peer_ref, win_ref, wout_ref, norm_ref, mod_ref, inner_ref, hidden_ref, part_ref, send_ref, full_ref, s_ref):
    join_core(own_ref, peer_ref, full_ref)
    shift_full(full_ref, s_ref, C)

    def put(i, value):
        inner_ref[rows_of(i), :] = value

    conv_wide(s_ref, win_ref, put)
    gain, bias, scale, shift = mid_rows(norm_ref, mod_ref)

    def store(i, value):
        hidden_ref[rows_of(i), :] = value

    norm_forward(inner_ref, gain * scale, bias * scale + shift, True, store)
    shift_full(hidden_ref, s_ref, HALF)
    conv_tall(s_ref, wout_ref, 1, put_split(part_ref, send_ref))


def attn_kernel(own_ref, peer_ref, w_ref, qkv_ref, log_ref, out_ref, part_ref, send_ref, full_ref, k_ref, vt_ref):
    join_core(own_ref, peer_ref, full_ref)

    @pl.loop(0, PIX // CHUNK)
    def _(i):
        at = rows_of(i)
        for s in range(2):
            value = dot(full_ref[at, :], w_ref[:, s * C : s * C + 3 * BLOCK])
            qkv_ref[at, s * 3 * BLOCK : (s + 1) * 3 * BLOCK] = value.astype(narrow)

    attend(qkv_ref, k_ref, vt_ref, log_ref, out_ref)
    store = put_split(part_ref, send_ref)

    @pl.loop(0, PIX // CHUNK)
    def _(i):
        at = rows_of(i)
        value = dot_t(out_ref[at, 0:BLOCK], w_ref[:, 3 * BLOCK : C])
        store(i, value + dot_t(out_ref[at, BLOCK:], w_ref[:, C + 3 * BLOCK :]))


def load_rows(ref):
    return lambda i: ref[rows_of(i), :]


def head_kernel(total, own_ref, peer_ref, w_ref, noise_ref, weight_ref, loss_ref, dw_ref, part_ref, send_ref, full_ref, s_ref, t_ref, grad_ref):
    join_core(own_ref, peer_ref, full_ref)
    shift_full(full_ref, s_ref, C)
    loss_ref[...] = jnp.zeros_like(loss_ref)

    def store(i, value):
        error = value - noise_ref[rows_of(i), :]
        weight = weight_ref[0:1, :]
        loss_ref[...] += jnp.sum(weight * error * error, 0, keepdims=True)
        grad_ref[rows_of(i), :] = (2.0 * weight * error / total).astype(narrow)

    conv_wide(s_ref, w_ref, store)
    wide_back(full_ref, w_ref, grad_ref, dw_ref, part_ref, send_ref, s_ref, t_ref)


def wide_back(full_ref, w_ref, grad_ref, dw_ref, part_ref, send_ref, s_ref, t_ref):
    shift_full(grad_ref, s_ref, HALF)
    transpose_into(load_rows(full_ref), t_ref)

    def keep(t, value):
        dw_ref[t * C : (t + 1) * C, :] = value.astype(narrow)

    kernel_grad(t_ref, s_ref, -1, keep)
    conv_tall(s_ref, w_ref, -1, put_split(part_ref, send_ref))


def normback_kernel(act, x_ref, part_ref, recv_ref, up_ref, norm_ref, dx_ref, low_ref, sums_ref, tmp_ref):
    def load(i):
        return part_ref[rows_of(i), :] + recv_ref[rows_of(i), :].astype(single)

    def store(i, value):
        value = value + up_ref[rows_of(i), :]
        dx_ref[rows_of(i), :] = value
        low_ref[rows_of(i), :] = value.astype(narrow)

    total, along = norm_backward(x_ref, load, norm_ref[0:1, :], norm_ref[1:2, :], act, tmp_ref, store)
    sums_ref[0:1, :] = along
    sums_ref[1:2, :] = total


def resback_kernel(
    gown_ref, gpeer_ref, hidden_ref, inner_ref, norm_ref, mod_ref, wout_ref, own_ref, peer_ref, win_ref,
    dout_ref, din_ref, part_ref, send_ref, sums_ref, dmod_ref,
    full_ref, s_ref, t_ref, dh_ref, tmp_ref, grad_ref,
):
    join_core(gown_ref, gpeer_ref, full_ref)
    transpose_into(load_rows(full_ref), t_ref)
    shift_full(hidden_ref, s_ref, HALF)

    def keep(t, value):
        dout_ref[t * C : (t + 1) * C, :] = value.astype(narrow)

    kernel_grad(t_ref, s_ref, 1, keep)
    shift_full(full_ref, s_ref, C)

    def put(i, value):
        dh_ref[rows_of(i), :] = value

    conv_back(s_ref, wout_ref, put)
    gain, bias, scale, shift = mid_rows(norm_ref, mod_ref)

    def store(i, value):
        grad_ref[rows_of(i), :] = value.astype(narrow)

    total, along = norm_backward(
        inner_ref, load_rows(dh_ref), gain * scale, bias * scale + shift, True, tmp_ref, store
    )
    sums_ref[0:1, :] = scale * along
    sums_ref[1:2, :] = scale * total
    dmod_ref[0:1, :] = gain * along + bias * total
    dmod_ref[1:2, :] = total
    join_core(own_ref, peer_ref, full_ref)
    wide_back(full_ref, win_ref, grad_ref, din_ref, part_ref, send_ref, s_ref, t_ref)


def attnback_kernel(
    gown_ref, gpeer_ref, qkv_ref, log_ref, out_ref, w_ref, own_ref, peer_ref,
    dw_ref, part_ref, send_ref,
    full_ref, t_ref, grad_ref, k_ref, kt_ref, dk_ref, dv_ref, dqkv_ref,
):
    join_core(gown_ref, gpeer_ref, full_ref)
    transpose_into(load_rows(full_ref), t_ref)
    for s in range(2):
        lanes = slice(s * BLOCK, (s + 1) * BLOCK)
        dw_ref[:, s * C + 3 * BLOCK : (s + 1) * C] = dot(t_ref[...], out_ref[:, lanes]).astype(narrow)

        @pl.loop(0, PIX // CHUNK)
        def _(i):
            at = rows_of(i)
            value = dot(full_ref[at, :], w_ref[:, s * C + 3 * BLOCK : (s + 1) * C])
            grad_ref[at, lanes] = value.astype(narrow)

    dqkv = [dqkv_ref.at[:, s * 3 * BLOCK : (s + 1) * 3 * BLOCK] for s in range(2)]
    attend_back(qkv_ref, log_ref, grad_ref, k_ref, kt_ref, dk_ref, dv_ref, dqkv)
    join_core(own_ref, peer_ref, full_ref)
    transpose_into(load_rows(full_ref), t_ref)
    for s in range(2):
        lanes = slice(s * 3 * BLOCK, (s + 1) * 3 * BLOCK)
        dw_ref[:, s * C : s * C + 3 * BLOCK] = dot(t_ref[...], dqkv_ref[:, lanes]).astype(narrow)
    store = put_split(part_ref, send_ref)

    @pl.loop(0, PIX // CHUNK)
    def _(i):
        at = rows_of(i)
        value = dot_t(dqkv_ref[at, 0 : 3 * BLOCK], w_ref[:, 0 : 3 * BLOCK])
        store(i, value + dot_t(dqkv_ref[at, 3 * BLOCK :], w_ref[:, C : C + 3 * BLOCK]))


HALF_F32 = struct((PIX, HALF))
HALF_LOW = struct((PIX, HALF), narrow)
FULL_LOW = pltpu.VMEM((PIX, C), narrow)
SHIFTED = pltpu.VMEM((3, ROWS, C), narrow)
TURNED = pltpu.VMEM((C, PIX), narrow)
SWAP = [(0, 1), (1, 0)]


def core_swap(value):
    return lax.ppermute(value, "lo", SWAP)


def image_swap(value):
    return lax.ppermute(value, "hi", SWAP)


DP = ("dz", "dy")


def pick_image(value):
    hi = lax.axis_index("hi")
    kept = jnp.where(hi == 0, value[0], value[1])
    came = image_swap(jnp.where(hi == 0, value[1], value[0]))
    return jnp.where(hi == 0, jnp.concatenate([kept, came], 1), jnp.concatenate([came, kept], 1))


def join_image(value, axis):
    hi = lax.axis_index("hi")
    came = image_swap(value)
    return jnp.where(
        hi == 0, jnp.concatenate([value, came], axis), jnp.concatenate([came, value], axis)
    )


def gather_weight(shard):
    rows = lax.all_gather(shard, DP, axis=0, tiled=True)
    return lax.all_gather(rows, "hi", axis=1, tiled=True)


def scatter_grad(value):
    cols = lax.psum_scatter(value, "hi", scatter_dimension=1, tiled=True)
    return lax.psum_scatter(cols, DP, scatter_dimension=0, tiled=True).astype(single)


def chan_index():
    return lax.axis_index("hi") * 2 + lax.axis_index("lo")


def sinusoid_of(timesteps):
    half_count = TF // 2
    frequency = jnp.exp(-math.log(10000.0) * jnp.arange(half_count, dtype=single) / half_count)
    angles = timesteps.astype(single)[:, None] * frequency[None, :]
    return jnp.concatenate([jnp.cos(angles), jnp.sin(angles)], 1).astype(narrow)


def embed_forward(timesteps, classes, time_in, emb_out, emb_proj):
    times = lax.all_gather(timesteps, DP, axis=0, tiled=True)
    labels = lax.all_gather(classes, DP, axis=0, tiled=True)
    rows = time_in.shape[0]
    place = lax.axis_index(DP) * rows
    sinusoid = lax.dynamic_slice_in_dim(sinusoid_of(times), place, rows, 1)
    pre = lax.psum(dot(sinusoid, time_in), DP)
    hidden = jax.nn.silu(pre).astype(narrow)
    class_here = emb_out.shape[1] - hidden.shape[1]
    numbers = chan_index() * class_here + jnp.arange(class_here)
    onehot = (labels[:, None] == numbers[None, :]).astype(narrow)
    joined = jnp.concatenate([hidden, onehot], 1)
    embedding = lax.psum(dot_t(joined, emb_out), ("hi", "lo"))
    context = jax.nn.silu(embedding).astype(narrow)
    parts = jnp.einsum("be,lej->blj", context, emb_proj, preferred_element_type=single)
    mine = lax.psum_scatter(parts, DP, scatter_dimension=0, tiled=True)
    hi = lax.axis_index("hi")
    kept = jnp.where(hi == 0, mine[0], mine[1])
    came = image_swap(jnp.where(hi == 0, mine[1], mine[0]))
    wide = jnp.where(hi == 0, jnp.concatenate([kept, came], 1), jnp.concatenate([came, kept], 1))
    modulate = jnp.swapaxes(wide.reshape(2, HALF, 2), 1, 2)
    return modulate, (sinusoid, pre, joined, embedding, context)


def embed_backward(saved, dmod, emb_proj, emb_out):
    sinusoid, pre, joined, embedding, context = saved
    flat = jnp.swapaxes(dmod, 1, 2).reshape(2, 2 * HALF).astype(narrow)
    hi = lax.axis_index("hi")
    width = flat.shape[1] // 2
    kept = jnp.where(hi == 0, flat[:, :width], flat[:, width:])
    came = image_swap(jnp.where(hi == 0, flat[:, width:], flat[:, :width]))
    both = jnp.where(hi == 0, jnp.stack([kept, came]), jnp.stack([came, kept]))
    grads = lax.all_gather(both, DP, axis=0, tiled=True)
    proj_grad = jnp.einsum("be,blj->lej", context, grads, preferred_element_type=single)
    part = jnp.einsum("blj,lej->be", grads, emb_proj, preferred_element_type=single)
    context_grad = lax.psum(part, ("hi", "lo"))
    _, pullback = jax.vjp(jax.nn.silu, embedding)
    (embed_grad,) = pullback(context_grad)
    embed_low = embed_grad.astype(narrow)
    out_grad = jnp.einsum("be,bj->ej", embed_low, joined, preferred_element_type=single)
    joined_grad = lax.psum(dot(embed_low, emb_out[:, : pre.shape[1]]), DP)
    _, pullback = jax.vjp(jax.nn.silu, pre)
    (pre_grad,) = pullback(joined_grad)
    time_grad = jnp.einsum("bt,be->te", sinusoid, pre_grad.astype(narrow), preferred_element_type=single)
    return proj_grad, time_grad, out_grad


def res_forward(own, peer, win, wout, norm, mod):
    outs = [HALF_F32, HALF_LOW, HALF_F32, HALF_LOW]
    return call(res_kernel, outs, [FULL_LOW, SHIFTED], [own, peer, win, wout, norm, mod], "res_forward")


def res_backward(gown, gpeer, hidden, inner, norm, mod, wout, own, peer, win):
    taps = struct((9 * C, HALF), narrow)
    outs = [taps, taps, HALF_F32, HALF_LOW, struct((2, HALF)), struct((2, HALF))]
    scratch = [FULL_LOW, SHIFTED, TURNED, pltpu.VMEM((PIX, HALF), single), pltpu.VMEM((PIX, HALF), single), pltpu.VMEM((PIX, HALF), narrow)]
    return call(resback_kernel, outs, scratch, [gown, gpeer, hidden, inner, norm, mod, wout, own, peer, win], "res_backward")


def norm_step(act, x, part, recv, up, norm):
    outs = [HALF_F32, HALF_LOW, struct((2, HALF))]
    body = functools.partial(normback_kernel, act)
    return call(body, outs, [pltpu.VMEM((PIX, HALF), single)], [x, part, recv, up, norm], "norm_backward")


def entry_step(act, x, part, recv, norm):
    return call(functools.partial(entry_kernel, act), [HALF_F32, HALF_LOW], [], [x, part, recv, norm], "entry")


def network(noisy, noise, sample_weight, kernels_in, kernels_out, attn, norms, modulate):
    images = noisy.shape[0] * lax.axis_size("dz") * lax.axis_size("dy")
    total = float(images * PIX * C)
    x0 = pick_image(noisy.reshape(2, PIX, BLOCK))
    target = pick_image(noise.reshape(2, PIX, BLOCK))
    weight = jnp.where(lax.axis_index("hi") == 0, sample_weight[0], sample_weight[1])
    weight = jnp.broadcast_to(weight, (8, HALF))
    stream0, entry0 = call(first_kernel, [HALF_F32, HALF_LOW], [], [x0, norms[0]], "entry")
    peer0 = core_swap(entry0)
    inner0, hidden0, part, send = res_forward(entry0, peer0, kernels_in[0], kernels_out[0], norms[1], modulate[0])
    stream1, entry1 = entry_step(False, stream0, part, core_swap(send), norms[2])
    peer1 = core_swap(entry1)
    outs = [struct((PIX, 6 * BLOCK), narrow), struct((4, PIX // CHUNK, 1, CHUNK)), HALF_LOW, HALF_F32, HALF_LOW]
    scratch = [FULL_LOW, pltpu.VMEM((PIX, BLOCK), narrow), pltpu.VMEM((BLOCK, PIX), narrow)]
    qkv, log, attended, part, send = call(attn_kernel, outs, scratch, [entry1, peer1, attn], "attention")
    stream2, entry2 = entry_step(True, stream1, part, core_swap(send), norms[3])
    peer2 = core_swap(entry2)
    inner2, hidden2, part, send = res_forward(entry2, peer2, kernels_in[1], kernels_out[1], norms[4], modulate[1])
    stream3, entry3 = entry_step(True, stream2, part, core_swap(send), norms[5])
    peer3 = core_swap(entry3)
    taps = struct((9 * C, HALF), narrow)
    outs = [struct((1, HALF)), taps, HALF_F32, HALF_LOW]
    scratch = [FULL_LOW, SHIFTED, TURNED, pltpu.VMEM((PIX, HALF), narrow)]
    args = [entry3, peer3, kernels_in[2], target, weight]
    loss, din2, part, send = call(functools.partial(head_kernel, total), outs, scratch, args, "head")
    zero = jnp.zeros((PIX, HALF), single)
    grad3, low3, sums5 = norm_step(True, stream3, part, core_swap(send), zero, norms[5])
    dout1, din1, part, send, sums4, dmod1 = res_backward(
        low3, core_swap(low3), hidden2, inner2, norms[4], modulate[1], kernels_out[1], entry2, peer2, kernels_in[1]
    )
    grad2, low2, sums3 = norm_step(True, stream2, part, core_swap(send), grad3, norms[3])
    outs = [struct((C, 2 * C), narrow), HALF_F32, HALF_LOW]
    scratch = [
        FULL_LOW, TURNED, pltpu.VMEM((PIX, HALF), narrow), pltpu.VMEM((PIX, BLOCK), narrow), pltpu.VMEM((BLOCK, PIX), narrow),
        pltpu.VMEM((PIX, BLOCK), single), pltpu.VMEM((PIX, BLOCK), single), pltpu.VMEM((PIX, 6 * BLOCK), narrow),
    ]
    args = [low2, core_swap(low2), qkv, log, attended, attn, entry1, peer1]
    dattn, part, send = call(attnback_kernel, outs, scratch, args, "attention_backward")
    grad1, low1, sums2 = norm_step(False, stream1, part, core_swap(send), grad2, norms[2])
    dout0, din0, part, send, sums1, dmod0 = res_backward(
        low1, core_swap(low1), hidden0, inner0, norms[1], modulate[0], kernels_out[0], entry0, peer0, kernels_in[0]
    )
    _, _, sums0 = norm_step(True, stream0, part, core_swap(send), grad1, norms[0])
    sums = jnp.stack([sums0, sums1, sums2, sums3, sums4, sums5])
    return jnp.sum(loss) / total, (din0, din1, din2), (dout0, dout1), dattn, sums, jnp.stack([dmod0, dmod1])


MESH = pl.DeviceIdType.MESH
ANY = pl.BlockSpec(memory_space=pl.ANY)
SMEM = pl.BlockSpec(memory_space=pltpu.SMEM)
LAYERS = 6
REDUCES = 8
LANDINGS = 5 * REDUCES
STEPS = 13


def remote(src, dst, send, recv, **where):
    return pltpu.make_async_remote_copy(
        src_ref=src, dst_ref=dst, send_sem=send, recv_sem=recv, device_id=where, device_id_type=MESH
    )


def place():
    return lax.axis_index("dz"), lax.axis_index("dy"), lax.axis_index("hi")


def greet(others):
    barrier = pltpu.get_barrier_semaphore()
    for where in others:
        pl.semaphore_signal(barrier, inc=1, device_id=where, device_id_type=MESH)
    pl.semaphore_wait(barrier, len(others))


def neighbours():
    z, y, x = place()
    others = [{"dz": (z + k) % 4} for k in (1, 2, 3)]
    return others + [{"dy": 1 - y}, {"hi": 1 - x}, {"lo": 1 - lax.axis_index("lo")}]


class Layout:
    def __init__(self, rows, lanes):
        self.rows, self.lanes = rows, lanes

    def block(self, zz, yy):
        return pl.ds(pl.multiple_of((zz * 2 + yy) * self.rows, 32), self.rows)

    def cols(self, xx):
        return pl.ds(pl.multiple_of(xx * self.lanes, 128), self.lanes)


class Gather:
    def __init__(self, layer, shard, full, send, recv, local):
        z, y, x = place()
        rows, lanes = shard.shape
        at = Layout(rows, lanes)
        mine = full.at[at.block(z, y), at.cols(x)]
        self.local = pltpu.make_async_copy(shard, mine, local.at[layer])

        def copy(j, src, dst, **where):
            return remote(src, dst, send.at[layer, j], recv.at[layer, j], **where)

        self.along_z = [copy(k - 1, shard, mine, dz=(z + k) % 4) for k in (1, 2, 3)]
        self.first, self.second = [], []
        for n in range(2):
            part = full.at[at.block(n, y), at.cols(x)]
            self.first.append(copy(3 + n, part, part, dy=1 - y))
            part = full.at[at.block(2 + n, y), at.cols(x)]
            self.first.append(copy(5 + n, part, part, hi=1 - x))
        part = full.at[0 : 4 * rows, at.cols(x)]
        self.second.append(copy(7, part, part, hi=1 - x))
        for n in range(2):
            part = full.at[at.block(2 + n, y), :]
            self.second.append(copy(8 + n, part, part, dy=1 - y))

    def start(self):
        self.local.start()
        for copy in self.along_z:
            copy.start()

    def turn(self):
        self.local.wait()
        for copy in self.along_z:
            copy.wait_recv()
        for copy in self.first:
            copy.start()

    def spread(self):
        for copy in self.first:
            copy.wait_recv()
        for copy in self.second:
            copy.start()

    def ready(self):
        for copy in self.second:
            copy.wait_recv()

    def drain(self):
        for copy in self.along_z + self.first + self.second:
            copy.wait_send()


def add_rows(count, lanes, into, other):
    size = next(n for n in (192, 144, 96, 64, 48, 32) if count % n == 0 and n * lanes <= 32768)

    @pl.loop(0, count // size)
    def _(i):
        at = pl.ds(pl.multiple_of(i * size, 16), size)
        into.at[at, :][...] = into.at[at, :][...] + other.at[at, :][...]


class Reduce:
    buffers = 5

    def __init__(self, layer, grad, bufs, out, low, count, send, recv):
        z, y, x = place()
        ra, rb, rc, rd, rz = bufs
        rows, lanes = out.shape
        at = Layout(rows, lanes)
        self.lanes, self.out, self.bufs, self.low, self.count = lanes, out, bufs, low, count

        def copy(j, src, dst, **where):
            return remote(src, dst, send.at[layer, j], recv.at[layer, j], **where)

        def part(zz, yy, xx=None):
            cut = pl.ds(pl.multiple_of((zz * 2 + yy) * rows + low, 32), count)
            return grad.at[cut, :] if xx is None else grad.at[cut, at.cols(xx)]

        self.part, self.here = part, (z, y, x)
        self.first = []
        for k in range(4):
            self.first.append(copy(k, part(k // 2, k % 2, 1 - x), ra.at[k], hi=1 - x))
        for n in range(2):
            self.first.append(copy(4 + n, part(2 + n, 1 - y), rb.at[n], dy=1 - y))
        self.second, self.third = [], []
        for n in range(2):
            self.second.append(copy(6 + n, part(n, 1 - y, x), rc.at[n], dy=1 - y))
        for n in range(2):
            self.second.append(copy(8 + n, part(2 + n, y, 1 - x), rd.at[n], hi=1 - x))
        for k in (1, 2, 3):
            zz = (z + k) % 4
            self.third.append(copy(9 + k, part(zz, y, x), rz.at[k - 1], dz=zz))

    def start(self):
        for copy in self.first:
            copy.start()

    def turn(self):
        (z, y, x), (ra, rb, rc, rd, rz) = self.here, self.bufs
        for k in range(4):
            self.first[k].wait_recv()
            add_rows(self.count, self.lanes, self.part(k // 2, k % 2, x), ra.at[k])
        for copy in self.second[:2]:
            copy.start()
        for n in range(2):
            self.first[4 + n].wait_recv()
            add_rows(self.count, 2 * self.lanes, self.part(2 + n, y), rb.at[n])
            self.second[2 + n].start()

    def spread(self):
        (z, y, x), (ra, rb, rc, rd, rz) = self.here, self.bufs
        for n in range(2):
            self.second[n].wait_recv()
            add_rows(self.count, self.lanes, self.part(n, y, x), rc.at[n])
        for n in range(2):
            self.second[2 + n].wait_recv()
            add_rows(self.count, self.lanes, self.part(2 + n, y, x), rd.at[n])
        for copy in self.third:
            copy.start()

    def finish(self):
        (z, y, x), (ra, rb, rc, rd, rz) = self.here, self.bufs
        for copy in self.third:
            copy.wait_recv()
        size = 32
        mine = self.part(z, y, x)

        @pl.loop(0, self.count // size)
        def _(i):
            part = pl.ds(pl.multiple_of(i * size, 32), size)
            total = mine.at[part, :][...].astype(single)
            for k in range(3):
                total = total + rz.at[k, part, :][...].astype(single)
            self.out.at[pl.ds(pl.multiple_of(self.low + i * size, 32), size), :][...] = total

    def drain(self):
        for copy in self.first + self.second + self.third:
            copy.wait_send()


def reduce_plan(outs):
    rows = [out.shape[0] for out in outs]
    plan = [("5", 5, 0, rows[5]), ("3", 3, 0, rows[3]), ("4", 4, 0, rows[4]), ("2", 2, 0, rows[2])]
    for n in (1, 0):
        half = rows[n] // 2
        plan += [(f"{n}a", n, 0, half), (f"{n}b", n, half, half)]
    return plan


class LateGather:
    def __init__(self, layer, shard, full, send, recv, local):
        z, y, x = place()
        rows, lanes = shard.shape
        half = rows // 2
        at = Layout(rows, lanes)
        mine = full.at[at.block(z, y), at.cols(x)]
        self.local = pltpu.make_async_copy(shard, mine, local.at[layer])

        def copy(j, src, dst, **where):
            return remote(src, dst, send.at[layer, j], recv.at[layer, j], **where)

        def part(yy, k):
            return pl.ds(pl.multiple_of((z * 2 + yy) * rows + k * half, 32), half)

        self.first = [
            copy(0, shard.at[0:half, :], full.at[part(y, 0), at.cols(x)], hi=1 - x),
            copy(1, shard.at[half:, :], full.at[part(y, 1), at.cols(x)], dy=1 - y),
        ]
        self.second = [copy(2, full.at[part(y, 0), :], full.at[part(y, 0), :], dy=1 - y)]
        for yy in range(2):
            block = full.at[part(yy, 1), at.cols(x)]
            self.second.append(copy(3 + yy, block, block, hi=1 - x))
        layer_rows = full.at[pl.ds(pl.multiple_of(z * 2 * rows, 32), 2 * rows), :]
        self.third = [copy(4 + k, layer_rows, layer_rows, dz=(z + k) % 4) for k in (1, 2, 3)]

    def start(self):
        self.local.start()
        for copy in self.first:
            copy.start()

    def turn(self):
        self.local.wait()
        for copy in self.first:
            copy.wait_recv()
        for copy in self.second:
            copy.start()

    def spread(self):
        for copy in self.second:
            copy.wait_recv()
        for copy in self.third:
            copy.start()

    def ready(self):
        for copy in self.third:
            copy.wait_recv()

    def drain(self):
        for copy in self.first + self.second + self.third:
            copy.wait_send()


class EarlyReduce:
    buffers = 5

    def __init__(self, layer, grad, bufs, out, low, count, send, recv):
        z, y, x = place()
        rz, ra, rb, rc, rd = bufs
        rows, lanes = out.shape
        half = rows // 2
        at = Layout(rows, lanes)
        self.out, self.grad, self.bufs, self.lanes, self.half, self.rows = out, grad, bufs, lanes, half, rows

        def copy(j, src, dst, **where):
            return remote(src, dst, send.at[layer, j], recv.at[layer, j], **where)

        def layer_rows(zz):
            return pl.ds(pl.multiple_of(zz * 2 * rows, 32), 2 * rows)

        def part(yy, k):
            return pl.ds(pl.multiple_of((z * 2 + yy) * rows + k * half, 32), half)

        self.mine, self.part, self.cols, self.here = grad.at[layer_rows(z), :], part, at.cols, (z, y, x)
        self.first = [copy(k - 1, grad.at[layer_rows((z + k) % 4), :], rz.at[k - 1], dz=(z + k) % 4) for k in (1, 2, 3)]
        self.second = [copy(3, grad.at[part(1 - y, 0), :], ra, dy=1 - y)]
        for yy in range(2):
            self.second.append(copy(4 + yy, grad.at[part(yy, 1), at.cols(1 - x)], rb.at[yy], hi=1 - x))
        self.third = [
            copy(6, grad.at[part(y, 0), at.cols(1 - x)], rc, hi=1 - x),
            copy(7, grad.at[part(1 - y, 1), at.cols(x)], rd, dy=1 - y),
        ]

    def start(self):
        for copy in self.first:
            copy.start()

    def turn(self):
        rz = self.bufs[0]
        for k, copy in enumerate(self.first):
            copy.wait_recv()
            add_rows(2 * self.rows, 2 * self.lanes, self.mine, rz.at[k])
        for copy in self.second:
            copy.start()

    def spread(self):
        (z, y, x), (rz, ra, rb, rc, rd) = self.here, self.bufs
        self.second[0].wait_recv()
        add_rows(self.half, 2 * self.lanes, self.grad.at[self.part(y, 0), :], ra)
        self.third[0].start()
        for yy in range(2):
            self.second[1 + yy].wait_recv()
            add_rows(self.half, self.lanes, self.grad.at[self.part(yy, 1), self.cols(x)], rb.at[yy])
        self.third[1].start()

    def finish(self):
        (z, y, x), (rz, ra, rb, rc, rd) = self.here, self.bufs
        for copy in self.third:
            copy.wait_recv()
        size = 96
        for k, came in enumerate((rc, rd)):
            mine = self.grad.at[self.part(y, k), self.cols(x)]

            @pl.loop(0, self.half // size)
            def _(i):
                part = pl.ds(pl.multiple_of(i * size, 32), size)
                total = mine.at[part, :][...].astype(single) + came.at[part, :][...].astype(single)
                self.out.at[pl.ds(pl.multiple_of(k * self.half + i * size, 32), size), :][...] = total

    def drain(self):
        for copy in self.first + self.second + self.third:
            copy.wait_send()


class Core:
    def __init__(self, send, recv):
        self.send, self.recv, self.used = send, recv, 0
        self.core = lax.axis_index("lo")

    def take(self, count):
        base = self.used
        self.used += count
        return base

    def copy(self, index, src, dst):
        return remote(src, dst, self.send.at[index], self.recv.at[index], lo=1 - self.core)

    def lanes(self, j):
        return pl.ds(pl.multiple_of((2 * j + self.core) * BLOCK, 128), BLOCK)

    def share(self, full):
        base = self.take(2 * (PIX // CHUNK))

        def copies(i):
            parts = [full.at[rows_of(i), self.lanes(j)] for j in range(2)]
            return [self.copy(base + 2 * i + j, part, part) for j, part in enumerate(parts)]

        def store(i, value):
            for j in range(2):
                full[rows_of(i), self.lanes(j)] = value[:, j * BLOCK : (j + 1) * BLOCK]
            for copy in copies(i):
                copy.start()

        def wait():
            @pl.loop(0, PIX // CHUNK)
            def _(i):
                for copy in copies(i):
                    copy.wait()

        return store, wait

    def combine(self, part, send, recv):
        base = self.take(PIX // CHUNK)

        def one(i):
            return self.copy(base + i, send.at[rows_of(i), :], recv.at[rows_of(i), :])

        def store(i, value):
            own, peer = split_core(value)
            part[rows_of(i), :] = own
            send[rows_of(i), :] = peer.astype(narrow)
            one(i).start()

        def wait():
            @pl.loop(0, PIX // CHUNK)
            def _(i):
                one(i).wait()

        def load(i):
            return part[rows_of(i), :] + recv[rows_of(i), :].astype(single)

        return store, wait, load


def step_kernel(
    fulls, total,
    noisy_hbm, noise_hbm, weight_ref, times_ref, labels_ref, norms_own, second,
    conv_in, conv_out, attn_weight, time_in, emb_out, emb_proj,
    in_rows, in_cols, out_rows, out_cols, proj_rows, proj_cols, attn_rows, attn_cols, time_rows, time_cols, eout_rows, eout_cols,
    g0, g1, g2, g3, g4, g5, proj_grad, time_grad, eout_grad, rows_ref, cols_ref, scal_ref, norm_out, second_out, norms_out,
    w0, w1, w2, w3, w4, w5, d1, full0, full1, full2, full3,
    *refs,
):
    landing = refs[:LANDINGS]
    (
    x1, x2, x3, inner0, inner2, noise_ref, part, tmp, dh, up,
    hidden0, hidden2, att, pg, x0_ref, send, recv, qkv,
    shifted, turned, k_ref, kt_ref, dk_ref, dv_ref, log_ref,
    norms_ref, mod_ref, loss_lanes, norms_flat, sums_ref, dmod_ref, wsq_ref, sin_ref, label_ref, pre_ref, embedding_ref,
    s0, s1, s2, s3, s4, s5,
    msg, p0, p1, p2, p3, m3, q4, p4, p5, p6, p7, q7, p8, p9, p10, p11, p12, p13,
    gsend, grecv, glocal, rsend, rrecv, csend, crecv, xsend, xrecv, esend, erecv, lsem,
    ) = refs[LANDINGS:]
    x = lax.axis_index("hi")
    core, small = Core(csend, crecv), Small(esend, erecv)
    block = pl.ds(pl.multiple_of(x * BLOCK, BLOCK), BLOCK)
    own_x0 = pltpu.make_async_copy(noisy_hbm.at[x], x0_ref.at[:, block], lsem.at[0])
    own_noise = pltpu.make_async_copy(noise_hbm.at[x], noise_ref.at[:, block], lsem.at[1])
    own_x0.start()
    own_noise.start()
    norms_flat[...] = joined_rows(norms_own)
    norms_ref[:, block] = norms_flat[...]
    dmod_ref[...] = jnp.zeros_like(dmod_ref)
    loss_lanes[...] = jnp.zeros_like(loss_lanes)
    keep = (sin_ref, label_ref, pre_ref, embedding_ref)
    embed = embed_steps(
        small, times_ref, labels_ref, time_in, emb_out, emb_proj, msg, p0, p1, p2, p3, m3, mod_ref, keep
    )
    shards, full_weights = (s0, s1, s2, s3, s4, s5), (w0, w1, w2, w3, w4, w5)
    gathers = []
    for n, (shard, full) in enumerate(zip(shards, full_weights)):
        kind = LateGather if n == 5 else Gather
        gathers.append(kind(n, shard, full, gsend, grecv, glocal))
    outs, grads = (g0, g1, g2, g3, g4, g5), (w1, d1, w2, w3, w4, w5)
    reduces, used = {}, 0
    for number, (name, n, low, count) in enumerate(reduce_plan(outs)):
        kind = EarlyReduce if n == 5 else Reduce
        bufs = landing[used : used + kind.buffers]
        used += kind.buffers
        reduces[name] = kind(number, grads[n], bufs, outs[n], low, count, rsend, rrecv)
    matrices = [g0, g3, g5, g1, g4, proj_grad.at[0], proj_grad.at[1], g2, time_grad, eout_grad]
    rows_old = [in_rows[n : n + 1] for n in range(3)] + [out_rows[n : n + 1] for n in range(2)]
    rows_old += [proj_rows[n : n + 1] for n in range(2)] + [attn_rows[...], time_rows[...], eout_rows[...]]
    cols_old = [in_cols[n : n + 1] for n in range(3)] + [out_cols[n : n + 1] for n in range(2)]
    cols_old += [proj_cols[n : n + 1] for n in range(2)] + [attn_cols[...], time_cols[...], eout_cols[...]]
    step = adafactor_steps(
        small, (1, 2, 4, 5, 6, 7, 8, 9), (0, 3), matrices, rows_old, cols_old, fulls, wsq_ref, loss_lanes, sums_ref,
        norms_own, second, p7, q7, p8, p9, p10, p11, p12, p13, rows_ref, cols_ref, scal_ref, norm_out, second_out, norms_out,
    )
    embed_end = embed_back_steps(
        small, dmod_ref, q4, p4, p5, p6, emb_out, emb_proj, keep, proj_grad, eout_grad, time_grad
    )

    def norm_row(n):
        return norms_ref[2 * n : 2 * n + 1, :], norms_ref[2 * n + 1 : 2 * n + 2, :]

    def keep_taps(grad):
        def store(t, value):
            grad[t * C : (t + 1) * C, :] = value.astype(narrow)

        return store

    class First:
        def __getitem__(self, at):
            return x0_ref[at].astype(single)

    def entry(x, n, act, full):
        gain, bias = norm_row(n)
        store, wait = core.share(full)
        norm_forward(x, gain, bias, act, store)
        return wait

    def middle(n, layer):
        gain, bias = norm_row(n)
        scale, shift = 1.0 + mod_ref[layer, 0:1, :], mod_ref[layer, 1:2, :]
        return gain, bias, scale, gain * scale, bias * scale + shift

    def first_half(full, w, n, layer, inner, hidden):
        shift_full(full, shifted, C)

        def put(i, value):
            inner[rows_of(i), :] = value

        conv_wide(shifted, w, put)
        _, _, _, gain, bias = middle(n, layer)

        def store(i, value):
            hidden[rows_of(i), :] = value

        norm_forward(inner, gain, bias, True, store)
        shift_full(hidden, shifted, HALF)

    def second_half(w):
        store, wait, load = core.combine(part, send, recv)
        conv_tall(shifted, w, 1, store)
        return wait, load

    def advance(x_old, load, x_new):
        @pl.loop(0, PIX // CHUNK)
        def _(i):
            x_new[rows_of(i), :] = x_old[rows_of(i), :] + load(i)

    greet(all_partners())
    swaps = []
    for n, (src, dst) in enumerate(
        ((norms_flat, norms_ref), (noisy_hbm.at[1 - x], x0_ref), (noise_hbm.at[1 - x], noise_ref))
    ):
        swaps.append(remote(src, dst.at[:, block], xsend.at[n], xrecv.at[n], hi=1 - x))
    swaps[0].start()
    next(embed)
    masters = [conv_in.at[0], conv_out.at[0], attn_weight, conv_in.at[1], conv_out.at[1], conv_in.at[2]]
    s0[...] = masters[0][...].astype(narrow)
    gathers[0].start()
    s5[...] = masters[5][...].astype(narrow)
    gathers[5].start()
    swaps[1].start()
    for n in range(1, 5):
        shards[n][...] = masters[n][...].astype(narrow)
    next(embed)
    gathers[1].start()
    gathers[5].turn()
    own_x0.wait()
    own_noise.wait()
    swaps[0].wait_recv()
    swaps[1].wait_recv()
    wait_entry = entry(First(), 0, True, full0)
    next(embed)
    gathers[0].turn()
    next(embed)
    for n in (2, 3, 4):
        gathers[n].start()
    gathers[5].spread()
    masters = [conv_in.at[n] for n in range(3)] + [conv_out.at[n] for n in range(2)]
    masters += [emb_proj.at[n] for n in range(2)] + [attn_weight, time_in, emb_out]
    wsq_ref[...] = scalar_rows([whole(master[...] * master[...]) for master in masters], 16)
    gathers[0].spread()
    gathers[1].turn()
    next(embed)
    wait_entry()
    gathers[0].ready()
    first_half(full0, w0, 1, 0, inner0, hidden0)
    gathers[2].turn()
    gathers[1].spread()
    gathers[3].turn()
    gathers[2].spread()
    gathers[1].ready()
    wait, load = second_half(w1)
    wait()
    advance(First(), load, x1)
    wait_entry = entry(x1, 2, False, full1)
    gathers[4].turn()
    gathers[3].spread()
    gathers[2].ready()
    wait_entry()

    @pl.loop(0, PIX // CHUNK)
    def _(i):
        at = rows_of(i)
        for s in range(2):
            value = dot(full1[at, :], w2[:, s * C : s * C + 3 * BLOCK])
            qkv[at, s * 3 * BLOCK : (s + 1) * 3 * BLOCK] = value.astype(narrow)

    def between(done):
        if done == 2:
            gathers[4].spread()
            swaps[2].start()

    attend(qkv, k_ref, kt_ref, log_ref, att, between)
    store, wait, load = core.combine(part, send, recv)

    @pl.loop(0, PIX // CHUNK)
    def _(i):
        at = rows_of(i)
        value = dot_t(att[at, 0:BLOCK], w2[:, 3 * BLOCK : C])
        store(i, value + dot_t(att[at, BLOCK:], w2[:, C + 3 * BLOCK :]))

    wait()
    advance(x1, load, x2)
    wait_entry = entry(x2, 3, True, full2)
    gathers[3].ready()
    wait_entry()
    first_half(full2, w3, 4, 1, inner2, hidden2)
    gathers[4].ready()
    wait, load = second_half(w4)
    wait()
    advance(x2, load, x3)
    wait_entry = entry(x3, 5, True, full3)
    for n in range(5):
        gathers[n].drain()
    wait_entry()
    shift_full(full3, shifted, C)
    transpose_into(load_rows(full3), turned)
    gathers[5].ready()
    gathers[5].drain()
    for copy in swaps:
        copy.wait_send()
    swaps[2].wait_recv()

    def store(i, value):
        error = value - noise_ref[rows_of(i), :]
        weight = jnp.where(x == 0, weight_ref[0], weight_ref[1])
        loss_lanes[0:1, :] += jnp.sum(weight * error * error, 0, keepdims=True)
        pg[rows_of(i), :] = (2.0 * weight * error / total).astype(narrow)

    conv_wide(shifted, w5, store)
    loss_lanes[...] = jnp.broadcast_to(whole(loss_lanes[0:1, :]) / total, loss_lanes.shape)

    def start(n):
        for name, reduce in reduces.items():
            if int(name[0]) == n:
                reduce.start()

    def wide(w, n):
        store, wait, load = core.combine(part, send, recv)
        conv_tall(shifted, w, -1, store)
        if n != 0:
            kernel_grad(turned, shifted, -1, keep_taps(grads[n]))
            start(n)
        return wait, load

    def through_norm(x, wait, load, n, act, first, full):
        gain, bias = norm_row(n)
        share, shared = core.share(full) if full is not None else (None, None)

        def store(i, value):
            if share is None:
                return
            if not first:
                value = value + up[rows_of(i), :]
            up[rows_of(i), :] = value
            share(i, value.astype(narrow))

        summed, along = norm_backward(x, load, gain, bias, act, tmp, store, wait)
        sums_ref[n, 0:1, :] = along
        sums_ref[n, 1:2, :] = summed
        return shared

    def out_grad(full, hidden, n):
        transpose_into(load_rows(full), turned)
        shift_full(hidden, shifted, HALF)
        kernel_grad(turned, shifted, 1, keep_taps(grads[n]))
        start(n)

    def back_half(full, w, n, layer, inner, between=None):
        shift_full(full, shifted, C)

        def put(i, value):
            dh[rows_of(i), :] = value

        conv_back(shifted, w, put)
        if between is not None:
            between()
        gain, bias, scale, gain_all, bias_all = middle(n, layer)

        def store(i, value):
            pg[rows_of(i), :] = value.astype(narrow)

        summed, along = norm_backward(inner, load_rows(dh), gain_all, bias_all, True, tmp, store)
        sums_ref[n, 0:1, :] = scale * along
        sums_ref[n, 1:2, :] = scale * summed
        dmod_ref[0, layer : layer + 1, :] = gain * along + bias * summed
        dmod_ref[1, layer : layer + 1, :] = summed

    shift_full(pg, shifted, HALF)
    wait, load = wide(w5, 5)
    shared = through_norm(x3, wait, load, 5, True, True, full3)
    shared()
    back_half(full3, w4, 4, 1, inner2)
    transpose_into(load_rows(full2), turned)
    shift_full(pg, shifted, HALF)
    wait, load = wide(w3, 3)
    shared = through_norm(x2, wait, load, 3, True, False, full2)
    out_grad(full3, hidden2, 4)
    shared()
    for s in range(2):
        lanes = slice(s * BLOCK, (s + 1) * BLOCK)

        @pl.loop(0, PIX // CHUNK)
        def _(i):
            at = rows_of(i)
            value = dot(full2[at, :], w2[:, s * C + 3 * BLOCK : (s + 1) * C])
            pg[at, lanes] = value.astype(narrow)

    transpose_into(load_rows(full2), turned)
    for s in range(2):
        lanes = slice(s * BLOCK, (s + 1) * BLOCK)
        w2[:, s * C + 3 * BLOCK : (s + 1) * C] = dot(turned[...], att[:, lanes]).astype(narrow)

    def between(done):
        if done == 2:
            reduces["3"].turn()
        if done == 4:
            reduces["4"].turn()

    dqkv = [shifted.at[s, 0:PIX, 0 : 3 * BLOCK] for s in range(2)]
    attend_back(qkv, log_ref, pg, k_ref, kt_ref, dk_ref, dv_ref, dqkv, between)
    transpose_into(load_rows(full1), turned)
    store, wait, load = core.combine(part, send, recv)

    @pl.loop(0, PIX // CHUNK)
    def _(i):
        at = rows_of(i)
        value = dot_t(dqkv[0].at[at, :][...], w2[:, 0 : 3 * BLOCK])
        store(i, value + dot_t(dqkv[1].at[at, :][...], w2[:, C : C + 3 * BLOCK]))

    for s in range(2):
        w2[:, s * C : s * C + 3 * BLOCK] = dot(turned[...], dqkv[s][...]).astype(narrow)
    start(2)
    shared = through_norm(x1, wait, load, 2, False, False, full1)
    reduces["3"].spread()
    shared()
    out_grad(full1, hidden0, 1)

    def between():
        reduces["5"].turn()
        reduces["4"].spread()

    back_half(full1, w1, 1, 0, inner0, between)
    next(embed_end)
    transpose_into(load_rows(full0), turned)
    shift_full(pg, shifted, HALF)
    reduces["2"].turn()
    kernel_grad(turned, shifted, -1, keep_taps(grads[0]))
    reduces["0a"].start()
    wait, load = wide(w0, 0)
    reduces["1a"].turn()
    reduces["0b"].start()
    through_norm(First(), wait, load, 0, True, False, None)
    reduces["5"].spread()
    reduces["3"].finish()
    reduces["1b"].turn()
    reduces["4"].finish()
    next(embed_end)
    reduces["2"].spread()
    reduces["0a"].turn()
    next(embed_end)
    reduces["1a"].spread()
    reduces["5"].finish()
    reduces["0b"].turn()
    next(embed_end)
    reduces["2"].finish()
    next(step)
    reduces["1b"].spread()
    reduces["0a"].spread()
    reduces["0b"].spread()
    next(step)
    reduces["1a"].finish()
    reduces["1b"].finish()
    reduces["0a"].finish()
    reduces["0b"].finish()
    next(step)
    for reduce in reduces.values():
        reduce.drain()


EXACT = lax.Precision.HIGHEST
IMAGES_HERE = 16


def exact_dot(a, b):
    return jnp.dot(a, b, precision=EXACT, preferred_element_type=single)


def chosen(shape, rule):
    row = lax.broadcasted_iota(jnp.int32, shape, 0)
    column = lax.broadcasted_iota(jnp.int32, shape, 1)
    return jnp.where(rule(row, column), 1.0, 0.0).astype(single)


def odd_even(kind):
    return chosen((HALF, BLOCK), lambda r, c: r == 2 * c + kind)


def even_odd(kind):
    return chosen((BLOCK, HALF), lambda r, c: c == 2 * r + kind)


def contract_rows(a, b):
    return lax.dot_general(a, b, (((0,), (0,)), ((), ())), preferred_element_type=single)


def silu_grad(value):
    gate = sigmoid(value)
    return gate * (1.0 + value * (1.0 - gate))


class Small:
    def __init__(self, send, recv):
        self.send, self.recv, self.used = send, recv, 0
        z, y, x = place()
        core = lax.axis_index("lo")
        self.dp_here, self.chan_here, self.plane_here = 2 * z + y, 2 * x + core, 4 * z + 2 * y + x

    def go(self, count, here, source, target, where):
        copies = []
        for k in range(1, count):
            other = lax.rem(here + k, count)
            sems = self.send.at[self.used], self.recv.at[self.used]
            self.used += 1
            copy = remote(source(other), target.at[here], *sems, **where(other))
            copy.start()
            copies.append(copy)

        def wait():
            for copy in copies:
                copy.wait()

        return wait

    def dp(self, target, source=None):
        source = source or (lambda other: target.at[self.dp_here])
        where = lambda other: {"dz": lax.div(other, 2), "dy": lax.rem(other, 2)}
        return self.go(8, self.dp_here, source, target, where)

    def chan(self, target):
        source = lambda other: target.at[self.chan_here]
        where = lambda other: {"hi": lax.div(other, 2), "lo": lax.rem(other, 2)}
        return self.go(4, self.chan_here, source, target, where)

    def plane(self, target, source):
        where = lambda other: {
            "dz": lax.div(other, 4), "dy": lax.rem(lax.div(other, 2), 2), "hi": lax.rem(other, 2)
        }
        return self.go(16, self.plane_here, source, target, where)


def all_partners():
    z, y, x = place()
    core = lax.axis_index("lo")
    here = 4 * z + 2 * y + x
    others = []
    for k in range(1, 16):
        o = lax.rem(here + k, 16)
        others.append({"dz": lax.div(o, 4), "dy": lax.rem(lax.div(o, 2), 2), "hi": lax.rem(o, 2)})
    return others + [{"lo": 1 - core}, {"hi": 1 - x, "lo": 1 - core}]


def total_of(ref):
    total = ref[0]
    for k in range(1, ref.shape[0]):
        total = total + ref[k]
    return total


def onehot_of(labels, count, first):
    numbers = lax.broadcasted_iota(jnp.int32, (IMAGES_HERE, count), 1) + first
    return jnp.where(labels[:, 0:1] == numbers.astype(single), 1.0, 0.0).astype(narrow)


def sinusoid_rows(times, labels):
    row = lax.broadcasted_iota(jnp.int32, (8, TF), 0)
    lane = lax.broadcasted_iota(jnp.int32, (8, TF), 1)
    half = TF // 2
    frequency = jnp.exp(-math.log(10000.0) * lax.rem(lane, half).astype(single) / half)
    angles = jnp.where(row == 0, times[0], times[1]).astype(single) * frequency
    sin = jnp.where(lane < half, jnp.cos(angles), jnp.sin(angles)).astype(narrow).astype(single)
    label = jnp.where(row == 2, labels[0], labels[1]).astype(single)
    return jnp.where(row < 2, sin, jnp.where(row < 4, label, 0.0))


def embed_steps(small, times, labels, time_in, emb_out, emb_proj, msg, p0, p1, p2, p3, m3, mod_ref, keep):
    sin_ref, label_ref, pre_ref, embedding_ref = keep
    here, chan = small.dp_here, small.chan_here
    rows = time_in.shape[0]
    msg[...] = jnp.zeros_like(msg)
    sent = sinusoid_rows(times, labels)
    for other in range(8):
        msg[other, :, 0:rows] = sent[:, other * rows : (other + 1) * rows]
    p0[here] = msg[here]
    wait = small.dp(p0, lambda other: msg.at[other])
    yield
    wait()
    flat = p0[...].reshape(64, BLOCK)
    sin = exact_dot(chosen((16, 64), lambda r, c: c == 8 * (r // 2) + r % 2), flat)
    label = exact_dot(chosen((16, 64), lambda r, c: c == 8 * (r // 2) + r % 2 + 2), flat)
    sin_ref[...], label_ref[...] = sin, label
    p1[here] = dot(sin[:, 0:rows].astype(narrow), time_in[...].astype(narrow))
    wait = small.dp(p1)
    yield
    wait()
    pre = total_of(p1)
    pre_ref[...] = pre
    hidden = (pre * sigmoid(pre)).astype(narrow)
    width = hidden.shape[1]
    count = emb_out.shape[1] - width
    onehot = onehot_of(label, count, chan * count)
    part = dot_t(hidden, emb_out[:, 0:width].astype(narrow))
    p2[chan] = part + dot_t(onehot, emb_out[:, width:].astype(narrow))
    wait = small.chan(p2)
    yield
    wait()
    embedding = total_of(p2)
    embedding_ref[...] = embedding
    context = (embedding * sigmoid(embedding)).astype(narrow)
    parts = jnp.concatenate([dot(context, emb_proj[n].astype(narrow)) for n in range(2)], 0)
    spread_rows = chosen((128, 32), lambda r, c: (c == 16 * (r % 8) + r // 8) & (r % 8 < 2))
    m3[...] = exact_dot(spread_rows, parts).reshape(16, 8, HALF)
    p3[small.plane_here] = m3[small.plane_here]
    wait = small.plane(p3, lambda other: m3.at[other])
    yield
    wait()
    flat = p3[...].reshape(128, HALF)
    for half in range(2):
        pick = chosen((8, 128), lambda r, c: (c % 8 == r) & ((c // 8) % 2 == half) & (r < 2))
        wide = exact_dot(pick, flat)
        for kind in range(2):
            value = exact_dot(wide, odd_even(kind))
            for n in range(2):
                mod_ref[n, kind : kind + 1, half * BLOCK : (half + 1) * BLOCK] = value[n : n + 1]
    yield


def embed_back_steps(small, dmod, q4, p4, p5, p6, emb_out, emb_proj, keep, proj_grad, out_grad, time_grad):
    sin_ref, label_ref, pre_ref, embedding_ref = keep
    here, chan, plane = small.dp_here, small.chan_here, small.plane_here
    for half in range(2):
        lanes = slice(half * BLOCK, (half + 1) * BLOCK)
        wide = exact_dot(dmod[0][:, lanes], even_odd(0)) + exact_dot(dmod[1][:, lanes], even_odd(1))
        q4[half] = wide.astype(narrow).astype(single)
    p4[plane] = q4[lax.rem(plane, 2)]
    wait = small.plane(p4, lambda other: q4.at[lax.rem(other, 2)])
    yield
    wait()
    flat = p4[...].reshape(128, HALF)
    embedding, pre = embedding_ref[...], pre_ref[...]
    context = (embedding * sigmoid(embedding)).astype(narrow)
    part = None
    for n in range(2):
        grads = exact_dot(chosen((16, 128), lambda r, c: c == 8 * r + n), flat).astype(narrow)
        proj_grad[n] = contract_rows(context, grads)
        more = dot_t(grads, emb_proj[n].astype(narrow))
        part = more if part is None else part + more
    p5[chan] = part
    wait = small.chan(p5)
    yield
    wait()
    low = (total_of(p5) * silu_grad(embedding)).astype(narrow)
    hidden = (pre * sigmoid(pre)).astype(narrow)
    width = hidden.shape[1]
    count = emb_out.shape[1] - width
    p6[here] = dot(low, emb_out[:, 0:width].astype(narrow))
    wait = small.dp(p6)
    out_grad[:, 0:width] = contract_rows(low, hidden)
    out_grad[:, width:] = contract_rows(low, onehot_of(label_ref[...], count, chan * count))
    yield
    wait()
    pre_grad = (total_of(p6) * silu_grad(pre)).astype(narrow)
    time_grad[...] = contract_rows(sin_ref[...].astype(narrow), pre_grad)[0 : time_grad.shape[0]]
    yield


def to_row(column):
    pieces = []
    for start in range(0, column.shape[0], BLOCK):
        part = column[start : start + BLOCK]
        n = part.shape[0]
        pieces.append(jnp.sum(chosen((n, n), lambda r, c: r == c) * part, 0, keepdims=True))
    return jnp.concatenate(pieces, 1)


def to_column(row):
    pieces = []
    for start in range(0, row.shape[1], BLOCK):
        part = row[:, start : start + BLOCK]
        n = part.shape[1]
        square = chosen((n, n), lambda r, c: r == c) * part
        pieces.append(jnp.sum(square, 1, keepdims=True))
    return jnp.concatenate(pieces, 0)


def joined_rows(ref):
    return jnp.concatenate([ref[n, k : k + 1, :] for n in range(6) for k in range(2)], 0)


def scalar_rows(values, count, lanes=BLOCK):
    rows = [jnp.broadcast_to(value, (1, lanes)) for value in values]
    return jnp.concatenate(rows + [jnp.zeros((count - len(rows), lanes), single)], 0)


def whole(value):
    return jnp.sum(jnp.sum(value, 1, keepdims=True), 0, keepdims=True)


DECAY = 1.0 - STEP ** (-0.8)
ROW_LANES = 640
COL_LANES = 512


def adafactor_steps(
    small, early, late, grads, rows_old, cols_old, fulls, wsq_ref, loss_ref, sums, norms_own, second,
    p7, q7, p8, p9, p10, p11, p12, p13, rows_ref, cols_ref, scal_ref, norm_out, second_out, norms_out,
):
    here, chan, plane = small.dp_here, small.chan_here, small.plane_here
    x = lax.axis_index("hi")
    count = len(grads)
    for half in range(2):
        lanes = slice(half * BLOCK, (half + 1) * BLOCK)
        rows = [sums[n, k : k + 1, lanes] for n in range(6) for k in range(2)]
        q7[half] = jnp.concatenate(rows + [jnp.zeros((4, BLOCK), single)], 0)
    p7[plane] = q7[x]
    wait_norms = small.plane(p7, lambda other: q7.at[lax.rem(other, 2)])
    update_sq, row_sum = {}, {}

    def measure(some, row_buf, col_buf):
        row_buf[chan] = jnp.zeros(row_buf.shape[1:], single)
        col_buf[here] = jnp.zeros(col_buf.shape[1:], single)
        for k, m in enumerate(some):
            value = grads[m][...]
            squared = value * value + tiny_square
            n_rows, n_cols = value.shape
            row_buf[chan, k : k + 1, 0:n_rows] = to_row(jnp.sum(squared, 1, keepdims=True))
            col_buf[here, k : k + 1, 0:n_cols] = jnp.sum(squared, 0, keepdims=True)
        return small.chan(row_buf), small.dp(col_buf)

    def moments(some, row_buf, col_buf, waits):
        for wait in waits:
            wait()
        row_total, col_total = total_of(row_buf), total_of(col_buf)
        for k, m in enumerate(some):
            n_rows, n_cols = grads[m].shape
            row = DECAY * rows_old[m] + (1.0 - DECAY) * row_total[k : k + 1, 0:n_rows] / fulls[m][1]
            col = DECAY * cols_old[m] + (1.0 - DECAY) * col_total[k : k + 1, 0:n_cols] / fulls[m][0]
            rows_ref[m : m + 1, 0:n_rows] = row
            cols_ref[m : m + 1, 0:n_cols] = col
            row_sum[m] = jnp.sum(row, 1, keepdims=True)
            update = grads[m][...] * to_column(lax.rsqrt(row)) * lax.rsqrt(col)
            update_sq[m] = whole(update * update)

    waits = measure(early, p8, p9)
    yield
    moments(early, p8, p9, waits)
    wait_norms()
    norm_total = total_of(p7)[0:12]
    own = joined_rows(norms_own)
    norm_out[...] = norm_total
    second_new = DECAY * joined_rows(second) + (1.0 - DECAY) * (norm_total * norm_total + tiny_square)
    second_out[...] = second_new
    norm_update = norm_total * lax.rsqrt(second_new)
    sq = [jnp.sum(norm_update * norm_update, 1, keepdims=True), jnp.sum(own * own, 1, keepdims=True)]
    wide = jnp.where(lax.broadcasted_iota(jnp.int32, (12, BLOCK), 1) < 64, sq[0], sq[1])
    yield
    moments(late, p10, p11, measure(late, p10, p11))
    lane = lax.broadcasted_iota(jnp.int32, (16, BLOCK), 1)
    sums_here = scalar_rows([update_sq[m] for m in range(count)], 16)
    row = lax.broadcasted_iota(jnp.int32, (16, BLOCK), 0)
    weights = jnp.where(row == count, loss_ref[0:1, 0:1], wsq_ref[:, 0:1])
    p12[chan, 0:16] = jnp.where(lane < 32, sums_here, weights)
    p12[chan, 16:32] = jnp.concatenate([wide, jnp.zeros((4, BLOCK), single)], 0)
    small.chan(p12)()
    over_chan = total_of(p12)
    p13[here] = jnp.where(lane < 64, over_chan[0:16], scalar_rows([row_sum[m] for m in range(count)], 16))
    wait = small.dp(p13)
    norm_sq = over_chan[16:28]
    norm_clip = jnp.maximum(1.0, jnp.sqrt(norm_sq[:, 0:1] / float(C)))
    norm_scale = jnp.maximum(floor_scale, jnp.sqrt(norm_sq[:, 64:65] / float(C)))
    norms_out[...] = own - (step_rate * norm_scale / norm_clip) * norm_update
    wait()
    over_all = total_of(p13)
    means, steps = [], []
    for m in range(count):
        entries = fulls[m][0] * fulls[m][1]
        mean = over_all[m : m + 1, 64:65] / fulls[m][0]
        clip = jnp.maximum(1.0, jnp.sqrt(mean * over_all[m : m + 1, 0:1] / entries))
        scale = jnp.maximum(floor_scale, jnp.sqrt(over_all[m : m + 1, 32:33] / entries))
        means.append(mean)
        steps.append(step_rate * scale / clip)
    scal_ref[0:16] = scalar_rows(means, 16)
    scal_ref[16:32] = scalar_rows(steps, 16)
    scal_ref[32:40] = jnp.broadcast_to(over_all[count : count + 1, 32:33], (8, BLOCK))
    yield


def finish_kernel(*refs):
    (g0, g1, g2, g3, g4, g5, proj, time, emb, rows, cols, scal, norm, second, norms_new,
     conv_in, conv_out, emb_proj, attn, time_in, emb_out,
     loss, in_g, in_r, in_c, in_w, out_g, out_r, out_c, out_w, proj_g, proj_r, proj_c, proj_w,
     attn_g, attn_r, attn_c, attn_w, time_g, time_r, time_c, time_w, emb_g, emb_r, emb_c, emb_w,
     norm_o, second_o, norms_o) = refs
    loss[...] = scal[32:33, 0:1]
    plan = [
        (0, g0, conv_in.at[0], in_g.at[0], in_r.at[0:1], in_c.at[0:1], in_w.at[0]),
        (1, g3, conv_in.at[1], in_g.at[1], in_r.at[1:2], in_c.at[1:2], in_w.at[1]),
        (2, g5, conv_in.at[2], in_g.at[2], in_r.at[2:3], in_c.at[2:3], in_w.at[2]),
        (3, g1, conv_out.at[0], out_g.at[0], out_r.at[0:1], out_c.at[0:1], out_w.at[0]),
        (4, g4, conv_out.at[1], out_g.at[1], out_r.at[1:2], out_c.at[1:2], out_w.at[1]),
        (5, proj.at[0], emb_proj.at[0], proj_g.at[0], proj_r.at[0:1], proj_c.at[0:1], proj_w.at[0]),
        (6, proj.at[1], emb_proj.at[1], proj_g.at[1], proj_r.at[1:2], proj_c.at[1:2], proj_w.at[1]),
        (7, g2, attn, attn_g, attn_r, attn_c, attn_w),
        (8, time, time_in, time_g, time_r, time_c, time_w),
        (9, emb, emb_out, emb_g, emb_r, emb_c, emb_w),
    ]
    for m, grad, weight, grad_o, rows_o, cols_o, weight_o in plan:
        n_rows, n_cols = grad_o.shape
        row, col = rows[m : m + 1, 0:n_rows], cols[m : m + 1, 0:n_cols]
        rows_o[...] = row
        cols_o[...] = col
        value = grad[...]
        grad_o[...] = value
        mean, step = scal[m : m + 1, 0:1], scal[16 + m : 17 + m, 0:1]
        update = value * to_column(lax.rsqrt(row / mean)) * lax.rsqrt(col)
        weight_o[...] = weight[...] - step * update
    for n in range(6):
        at = slice(2 * n, 2 * n + 2)
        norm_o[n], second_o[n], norms_o[n] = norm[at, :], second[at, :], norms_new[at, :]


def vmem(shape, dtype=single):
    return pltpu.VMEM(shape, dtype)


def semaphores(*shape):
    return pltpu.SemaphoreType.DMA(shape)


TAPS_SHAPE = (9 * C, HALF)
ATTN_SHAPE = (C, 2 * C)
FULL = (PIX, C)
OWN = (PIX, HALF)
QKV = (PIX, 6 * BLOCK)
LOGS = (4, PIX // CHUNK, 1, CHUNK)
WEIGHTS = [TAPS_SHAPE, TAPS_SHAPE, ATTN_SHAPE, TAPS_SHAPE, TAPS_SHAPE, TAPS_SHAPE]


def fused(body, outs, out_specs, in_specs, scratch, args, number, limit, name):
    return pl.pallas_call(
        body,
        out_shape=outs,
        in_specs=in_specs,
        out_specs=out_specs,
        scratch_shapes=scratch,
        compiler_params=pltpu.CompilerParams(
            vmem_limit_bytes=limit * 2**20, collective_id=number, has_side_effects=True
        ),
        name=name,
    )(*args)


def fused_step(
    noisy, noise, timesteps, classes, sample_weight,
    conv_in, conv_out, emb_proj, attn_weight, time_in, emb_out, norms, moments, norm_second,
):
    images = noisy.shape[0] * lax.axis_size("dz") * lax.axis_size("dy")
    total = float(images * PIX * C)
    weights = [conv_in[0], conv_in[1], conv_in[2], conv_out[0], conv_out[1]]
    weights += [emb_proj[0], emb_proj[1], attn_weight, time_in, emb_out]
    dp, chan = lax.axis_size("dz") * lax.axis_size("dy"), lax.axis_size("hi") * lax.axis_size("lo")
    fulls = [(float(w.shape[0] * dp), float(w.shape[1] * chan)) for w in weights]
    shard, attn_shard = conv_in.shape[1:], attn_weight.shape
    shard_shapes = [shard, shard, attn_shard, shard, shard, shard]
    shapes = shard_shapes + [emb_proj.shape, time_in.shape, emb_out.shape]
    shapes += [(16, ROW_LANES), (16, COL_LANES), (40, BLOCK)] + [(12, BLOCK)] * 3
    outs = [struct(s) for s in shapes]

    low = WEIGHTS + [TAPS_SHAPE] + [FULL] * 4
    for _, layer, _, count in reduce_plan([struct(s) for s in shard_shapes]):
        rows, lanes = shard_shapes[layer]
        if layer == 5:
            half = rows // 2
            low += [(3, 2 * rows, 2 * lanes), (half, 2 * lanes), (2, half, lanes), (half, lanes), (half, lanes)]
        else:
            low += [(4, count, lanes), (2, count, 2 * lanes), (2, count, lanes), (2, count, lanes), (3, count, lanes)]
    scratch = [vmem(s, narrow) for s in low] + [vmem(OWN)] * 10
    scratch += [vmem(OWN, narrow)] * 7 + [vmem(QKV, narrow), vmem((3, ROWS, C), narrow), vmem((C, PIX), narrow)]
    scratch += [vmem((PIX, BLOCK), narrow), vmem((BLOCK, PIX), narrow), vmem((PIX, BLOCK)), vmem((PIX, BLOCK))]
    small = [LOGS, (12, HALF), (2, 2, HALF), (8, HALF), (12, BLOCK), (6, 2, HALF), (2, 8, HALF)]
    small += [(16, BLOCK), (16, BLOCK), (16, BLOCK), (16, HALF), (16, BLOCK)]
    scratch += [vmem(s) for s in small] + [vmem(s, narrow) for s in shard_shapes]
    swaps = [(8, 8, BLOCK), (8, 8, BLOCK), (8, 16, HALF), (4, 16, BLOCK), (16, 8, HALF), (16, 8, HALF)]
    swaps += [(2, 8, HALF), (16, 8, HALF), (4, 16, BLOCK), (8, 16, HALF), (16, 16, BLOCK), (2, 16, BLOCK)]
    swaps += [(4, 16, ROW_LANES), (8, 16, COL_LANES), (4, 8, ROW_LANES), (8, 8, BLOCK), (4, 32, BLOCK), (8, 16, BLOCK)]
    scratch += [vmem(s) for s in swaps]
    scratch += [semaphores(LAYERS, 10)] * 2 + [semaphores(LAYERS)] + [semaphores(REDUCES, STEPS)] * 2
    scratch += [semaphores(96)] * 2 + [semaphores(3)] * 2 + [semaphores(128)] * 2 + [semaphores(2)]
    flat = [value.reshape(1, -1) if value.ndim == 1 else value for value in moments]
    pixels = (2, PIX, BLOCK)
    args = [noisy.reshape(pixels), noise.reshape(pixels), sample_weight, timesteps, classes, norms, norm_second]
    args += [conv_in, conv_out, attn_weight, time_in, emb_out, emb_proj, *flat]
    in_specs = [ANY] * 2 + [SMEM] * 3 + [VMEM] * (len(args) - 5)
    body = functools.partial(step_kernel, fulls, total)
    results = fused(body, outs, [VMEM] * len(outs), in_specs, scratch, args, 1, 63, "step")

    def four(weight, row, col):
        return [struct(weight.shape), struct(row.shape), struct(col.shape), struct(weight.shape)]

    outs = [struct((1, 1))]
    for n, weight in enumerate((conv_in, conv_out, emb_proj, attn_weight, time_in, emb_out)):
        outs += four(weight, flat[2 * n], flat[2 * n + 1])
    outs += [struct(norms.shape)] * 3
    args = [*results, conv_in, conv_out, emb_proj, attn_weight, time_in, emb_out]
    finals = list(call(finish_kernel, outs, [], args, "finish"))
    finals[0] = finals[0].reshape(())
    for n, value in enumerate(moments):
        place_at = 2 + 4 * (n // 2) + n % 2
        finals[place_at] = finals[place_at].reshape(value.shape)
    return tuple(finals)


def pack_flat(members):
    return jnp.concatenate([member.reshape(-1) for member in members])


def unpack_flat(vector, shape_list):
    pieces = []
    offset = 0
    for array_shape in shape_list:
        extent = math.prod(array_shape)
        pieces.append(vector[offset : offset + extent].reshape(array_shape))
        offset += extent
    return pieces


def per_device(
    noisy,
    noise,
    timesteps,
    classes,
    sample_weight,
    conv_in,
    conv_out,
    emb_proj,
    attn_weight,
    time_in,
    emb_out,
    norms,
    conv_in_rows,
    conv_in_cols,
    conv_out_rows,
    conv_out_cols,
    emb_proj_rows,
    emb_proj_cols,
    attn_rows,
    attn_cols,
    time_rows,
    time_cols,
    embout_rows,
    embout_cols,
    norm_second,
):
    rows_here = (conv_in.shape[1], attn_weight.shape[0])
    if lax.axis_size("dz") == 4 and all(rows % 64 == 0 for rows in rows_here):
        moments = [conv_in_rows, conv_in_cols, conv_out_rows, conv_out_cols, emb_proj_rows, emb_proj_cols]
        moments += [attn_rows, attn_cols, time_rows, time_cols, embout_rows, embout_cols]
        return fused_step(
            noisy, noise, timesteps, classes, sample_weight, conv_in, conv_out, emb_proj, attn_weight, time_in,
            emb_out, norms, moments, norm_second,
        )
    masters = [conv_in, conv_out, emb_proj, attn_weight[None], time_in[None], emb_out[None]]
    lowered = [master.astype(narrow) for master in masters]
    modulate, saved = embed_forward(timesteps, classes, lowered[4][0], lowered[5][0], lowered[2])
    norms_wide = join_image(norms, 2)
    shards = [lowered[0][0], lowered[1][0], lowered[3][0], lowered[0][1], lowered[1][1], lowered[0][2]]
    full = [gather_weight(shard) for shard in shards]
    loss_part, din, dout, dattn, sums, dmod = network(
        noisy, noise, sample_weight, (full[0], full[3], full[5]), (full[1], full[4]), full[2], norms_wide, modulate
    )
    reduced_parts = [scatter_grad(part) for part in (din[0], dout[0], dattn, din[1], dout[1], din[2])]
    in0_grad, out0_grad, attn_grad, in1_grad, out1_grad, head_grad = reduced_parts
    proj_grad, time_grad, embout_grad = embed_backward(saved, dmod, lowered[2], lowered[5][0])
    norm_local = lax.psum_scatter(sums, "hi", scatter_dimension=2, tiled=True)
    reduced = [
        jnp.stack([in0_grad, in1_grad, head_grad]),
        jnp.stack([out0_grad, out1_grad]),
        proj_grad,
        attn_grad[None],
        time_grad[None],
        embout_grad[None],
    ]
    decay_rate = 1.0 - STEP ** (-0.8)
    dp_count = lax.axis_size("dz") * lax.axis_size("dy")
    chan_count = lax.axis_size("hi") * lax.axis_size("lo")
    rows_old = [
        conv_in_rows,
        conv_out_rows,
        emb_proj_rows,
        attn_rows[None],
        time_rows[None],
        embout_rows[None],
    ]
    cols_old = [
        conv_in_cols,
        conv_out_cols,
        emb_proj_cols,
        attn_cols[None],
        time_cols[None],
        embout_cols[None],
    ]
    squares = [gradient * gradient + tiny_square for gradient in reduced]
    full_rows = [squared.shape[1] * dp_count for squared in squares]
    full_cols = [squared.shape[2] * chan_count for squared in squares]
    row_parts = [jnp.sum(squared, 2) for squared in squares]
    col_parts = [jnp.sum(squared, 1) for squared in squares]
    row_shapes = [member.shape for member in row_parts]
    col_shapes = [member.shape for member in col_parts]
    norm_width = norm_local.shape[2]
    row_totals = unpack_flat(lax.psum(pack_flat(row_parts), ("hi", "lo")), row_shapes)
    rows_new = [
        decay_rate * rows_old[position]
        + (1.0 - decay_rate) * row_totals[position] / full_cols[position]
        for position in range(6)
    ]
    row_sums_local = [jnp.sum(member, 1) for member in rows_new]
    col_vector, norm_total = lax.psum((pack_flat(col_parts + row_sums_local), norm_local), DP)
    col_pieces = unpack_flat(col_vector, col_shapes + [(member.shape[0],) for member in rows_new])
    col_totals = col_pieces[:6]
    row_means = [col_pieces[6 + position] / full_rows[position] for position in range(6)]
    cols_new = [
        decay_rate * cols_old[position]
        + (1.0 - decay_rate) * col_totals[position] / full_rows[position]
        for position in range(6)
    ]
    updates = [
        reduced[position]
        * lax.rsqrt(rows_new[position] / row_means[position][:, None])[:, :, None]
        * lax.rsqrt(cols_new[position])[:, None, :]
        for position in range(6)
    ]
    second_new = decay_rate * norm_second + (1.0 - decay_rate) * (
        norm_total * norm_total + tiny_square
    )
    norm_update = norm_total * lax.rsqrt(second_new)
    update_squares = pack_flat([jnp.sum(member * member, (1, 2)) for member in updates])
    weight_squares = pack_flat([jnp.sum(master * master, (1, 2)) for master in masters])
    norm_update_sq = jnp.sum(norm_update * norm_update, 2) / dp_count
    norm_weight_sq = jnp.sum(norms * norms, 2) / dp_count
    update_total, weight_total, norm_update_total, norm_weight_total, loss = lax.psum(
        (update_squares, weight_squares, norm_update_sq, norm_weight_sq, loss_part), ("dz", "dy", "hi", "lo")
    )
    layer_shapes = [(member.shape[0],) for member in masters]
    update_sums = unpack_flat(update_total, layer_shapes)
    weight_sums = unpack_flat(weight_total, layer_shapes)
    results = [loss]
    for position in range(6):
        entries = float(full_rows[position] * full_cols[position])
        clip_factor = jnp.maximum(1.0, jnp.sqrt(update_sums[position] / entries))
        scale_factor = jnp.maximum(floor_scale, jnp.sqrt(weight_sums[position] / entries))
        weight_new = (
            masters[position]
            - (step_rate * scale_factor / clip_factor)[:, None, None] * updates[position]
        )
        if position >= 3:
            results += [
                reduced[position][0],
                rows_new[position][0],
                cols_new[position][0],
                weight_new[0],
            ]
        else:
            results += [reduced[position], rows_new[position], cols_new[position], weight_new]
    norm_entries = float(norm_width * chan_count)
    norm_clip = jnp.maximum(1.0, jnp.sqrt(norm_update_total / norm_entries))
    norm_scale = jnp.maximum(floor_scale, jnp.sqrt(norm_weight_total / norm_entries))
    norms_new = norms - (step_rate * norm_scale / norm_clip)[:, :, None] * norm_update
    results += [norm_total, second_new, norms_new]
    return (
        results[0],
        results[1],
        results[2],
        results[3],
        results[4],
        results[5],
        results[6],
        results[7],
        results[8],
        results[9],
        results[10],
        results[11],
        results[12],
        results[13],
        results[14],
        results[15],
        results[16],
        results[17],
        results[18],
        results[19],
        results[20],
        results[21],
        results[22],
        results[23],
        results[24],
        results[25],
        results[26],
        results[27],
    )


CHAN = ("hi", "lo")


def solution(mesh):
    dp, chan = mesh.shape["dp"], mesh.shape["chan"]
    mesh = Mesh(mesh.devices.reshape(dp // 2, 2, 2, chan // 2), DP + CHAN)
    in_specs = (
        P(DP, None, None, CHAN),
        P(DP, None, None, CHAN),
        P(DP),
        P(DP),
        P(DP),
        P(None, DP, CHAN),
        P(None, DP, CHAN),
        P(None, DP, CHAN),
        P(DP, CHAN),
        P(DP, CHAN),
        P(DP, CHAN),
        P(None, None, CHAN),
        P(None, DP),
        P(None, CHAN),
        P(None, DP),
        P(None, CHAN),
        P(None, DP),
        P(None, CHAN),
        P(DP),
        P(CHAN),
        P(DP),
        P(CHAN),
        P(DP),
        P(CHAN),
        P(None, None, CHAN),
    )
    out_specs = (
        P(),
        P(None, DP, CHAN),
        P(None, DP),
        P(None, CHAN),
        P(None, DP, CHAN),
        P(None, DP, CHAN),
        P(None, DP),
        P(None, CHAN),
        P(None, DP, CHAN),
        P(None, DP, CHAN),
        P(None, DP),
        P(None, CHAN),
        P(None, DP, CHAN),
        P(DP, CHAN),
        P(DP),
        P(CHAN),
        P(DP, CHAN),
        P(DP, CHAN),
        P(DP),
        P(CHAN),
        P(DP, CHAN),
        P(DP, CHAN),
        P(DP),
        P(CHAN),
        P(DP, CHAN),
        P(None, None, CHAN),
        P(None, None, CHAN),
        P(None, None, CHAN),
    )
    return jax.shard_map(
        per_device, mesh=mesh, in_specs=in_specs, out_specs=out_specs, check_vma=False
    )
```

```python
import functools
import math

import jax
import jax.numpy as jnp
from jax import lax
from jax.experimental import pallas as pl
from jax.experimental.pallas import tpu as pltpu
from jax.sharding import Mesh
from jax.sharding import PartitionSpec as P

C = 512
HEADS = 8
GROUPS = 32
TF = 256
STEP = 10
SIDE = 32
PIX = 1024
HALF = 256
BLOCK = 128
PAD = SIDE
ROWS = PIX + 2 * PAD
CHUNK = 256

single = jnp.float32
narrow = jnp.bfloat16
step_rate = 0.5
floor_scale = 0.001
tiny_square = 1e-30
norm_eps = 1e-05

TAPS = [(t // 3 - 1, t % 3 - 1) for t in range(9)]


def dot(a, b):
    return jnp.dot(a, b, preferred_element_type=single)


def dot_t(a, b):
    return lax.dot_general(a, b, (((1,), (1,)), ((), ())), preferred_element_type=single)


def group_sum(row):
    lane = lax.broadcasted_iota(jnp.int32, (HALF, HALF), 0)
    other = lax.broadcasted_iota(jnp.int32, (HALF, HALF), 1)
    size = C // GROUPS
    ones = jnp.where(lane // size == other // size, 1.0, 0.0).astype(single)
    tall = jnp.broadcast_to(row, (8, HALF))
    return jnp.dot(tall, ones, precision=lax.Precision.HIGHEST, preferred_element_type=single)[0:1]


def loop_sum(count, make):
    zeros = make(None)

    def body(i, carried):
        return [old + new for old, new in zip(carried, make(i))]

    return lax.fori_loop(0, count, body, [jnp.zeros((1, HALF), single)] * zeros, unroll=NORM_UNROLL)


def rows_of(i, size=CHUNK, offset=0):
    return pl.ds(pl.multiple_of(offset + i * size, 32), size)


def stats(x_ref):
    members = float(PIX * (C // GROUPS))

    def first(i):
        if i is None:
            return 1
        return [jnp.sum(x_ref[rows_of(i), :], 0, keepdims=True)]

    (total,) = loop_sum(PIX // CHUNK, first)
    mean = group_sum(total) / members

    def second(i):
        if i is None:
            return 1
        center = x_ref[rows_of(i), :] - mean
        return [jnp.sum(center * center, 0, keepdims=True)]

    (square,) = loop_sum(PIX // CHUNK, second)
    rstd = lax.rsqrt(group_sum(square) / members + norm_eps)
    return mean, rstd


def sigmoid(v):
    return 1.0 / (1.0 + jnp.exp(-v))


def norm_forward(x_ref, gain, bias, act, store):
    mean, rstd = stats(x_ref)

    @pl.loop(0, PIX // CHUNK, unroll=NORM_UNROLL)
    def _(i):
        value = (x_ref[rows_of(i), :] - mean) * rstd * gain + bias
        if act:
            value = value * sigmoid(value)
        store(i, value.astype(narrow))


def norm_backward(x_ref, load_grad, gain, bias, act, tmp_ref, store, wait=None):
    mean, rstd = stats(x_ref)
    members = float(PIX * (C // GROUPS))
    if wait is not None:
        wait()

    def first(i):
        if i is None:
            return 2
        hat = (x_ref[rows_of(i), :] - mean) * rstd
        grad = load_grad(i)
        if act:
            mixed = hat * gain + bias
            gate = sigmoid(mixed)
            grad = grad * gate * (1.0 + mixed * (1.0 - gate))
        tmp_ref[rows_of(i), :] = grad
        return [jnp.sum(grad, 0, keepdims=True), jnp.sum(grad * hat, 0, keepdims=True)]

    total, along = loop_sum(PIX // CHUNK, first)
    mean_grad = group_sum(gain * total) / members
    mean_along = group_sum(gain * along) / members

    @pl.loop(0, PIX // CHUNK, unroll=NORM_UNROLL)
    def _(i):
        hat = (x_ref[rows_of(i), :] - mean) * rstd
        store(i, rstd * (tmp_ref[rows_of(i), :] * gain - mean_grad - hat * mean_along))

    return total, along


def shifts(load, s_ref, width):
    for b in range(3):
        s_ref[b, 0:PAD, 0:width] = jnp.zeros((PAD, width), narrow)
        s_ref[b, PAD + PIX : ROWS, 0:width] = jnp.zeros((PAD, width), narrow)
    size = 128

    @pl.loop(0, PIX // size)
    def _(i):
        value = load(i, size)
        wide = value.astype(single)
        across = lax.broadcasted_iota(jnp.int32, wide.shape, 0) % SIDE
        left = jnp.where(across > 0, pltpu.roll(wide, 1, 0), 0.0)
        right = jnp.where(across < SIDE - 1, pltpu.roll(wide, size - 1, 0), 0.0)
        at = rows_of(i, size, PAD)
        s_ref[0, at, 0:width] = left.astype(narrow)
        s_ref[1, at, 0:width] = value
        s_ref[2, at, 0:width] = right.astype(narrow)


def tap_rows(s_ref, t, sign, i, size, width):
    a, b = TAPS[t]
    return s_ref[sign * b + 1, rows_of(i, size, PAD + sign * a * SIDE), 0:width]


def split_core(value):
    core = lax.axis_index("lo")
    b0, b1, b2, b3 = [value[:, k * BLOCK : (k + 1) * BLOCK] for k in range(4)]
    even, odd = jnp.concatenate([b0, b2], 1), jnp.concatenate([b1, b3], 1)
    first = core == 0
    return jnp.where(first, even, odd), jnp.where(first, odd, even)


def join_core(own_ref, peer_ref, full_ref):
    core = lax.axis_index("lo")

    @pl.loop(0, PIX // CHUNK)
    def _(i):
        at = rows_of(i)
        own, peer = own_ref[at, :].astype(single), peer_ref[at, :].astype(single)
        even = jnp.where(core == 0, own, peer).astype(narrow)
        odd = jnp.where(core == 0, peer, own).astype(narrow)
        full_ref[at, 0:BLOCK] = even[:, 0:BLOCK]
        full_ref[at, BLOCK : 2 * BLOCK] = odd[:, 0:BLOCK]
        full_ref[at, 2 * BLOCK : 3 * BLOCK] = even[:, BLOCK:]
        full_ref[at, 3 * BLOCK :] = odd[:, BLOCK:]


def conv_wide(s_ref, w_ref, store):
    @pl.loop(0, PIX // CHUNK, unroll=CONV_UNROLL)
    def _(i):
        total = None
        for t in range(9):
            part = dot(tap_rows(s_ref, t, 1, i, CHUNK, C), w_ref[t * C : (t + 1) * C, :])
            total = part if total is None else total + part
        store(i, total)


def conv_tall(s_ref, w_ref, sign, store):
    @pl.loop(0, PIX // CHUNK, unroll=CONV_UNROLL)
    def _(i):
        total = None
        for t in range(9):
            part = dot_t(tap_rows(s_ref, t, sign, i, CHUNK, HALF), w_ref[t * C : (t + 1) * C, :])
            total = part if total is None else total + part
        store(i, total)


def conv_back(s_ref, w_ref, store):
    @pl.loop(0, PIX // CHUNK, unroll=CONV_UNROLL)
    def _(i):
        total = None
        for t in range(9):
            part = dot(tap_rows(s_ref, t, -1, i, CHUNK, C), w_ref[t * C : (t + 1) * C, :])
            total = part if total is None else total + part
        store(i, total)


def transpose_into(load, t_ref):
    for i in range(PIX // CHUNK):
        t_ref[:, i * CHUNK : (i + 1) * CHUNK] = jnp.transpose(load(i).astype(single)).astype(narrow)


def kernel_grad(t_ref, s_ref, sign, store):
    for t in range(9):
        a, b = TAPS[t]
        start = PAD + sign * a * SIDE
        store(t, dot(t_ref[...], s_ref[sign * b + 1, start : start + PIX, 0:HALF]))


def low_lanes(shape):
    return lax.broadcasted_iota(jnp.int32, shape, 1) < BLOCK // 2


def swap_halves(value):
    half = BLOCK // 2
    return jnp.concatenate([value[:, half:], value[:, :half]], 1)


def mask_half(value, upper, scale=1.0):
    low = low_lanes(value.shape)
    return jnp.where(low != upper, value.astype(single) * scale, 0.0).astype(narrow)


def head_parts(qkv_ref, s, h):
    base = 3 * BLOCK * s
    b0, b1, b2 = [slice(base + k * BLOCK, base + (k + 1) * BLOCK) for k in range(3)]
    return (b0, b0, b1) if h == 0 else (b1, b2, b2)


SCALE = (C // HEADS) ** (-0.5)
UNROLL = 4
CONV_UNROLL = 4
NORM_UNROLL = 4


def attend(qkv_ref, k_ref, vt_ref, log_ref, out_ref, between=None):
    for s in range(2):
        for h in range(2):
            q_at, k_at, v_at = head_parts(qkv_ref, s, h)
            k_ref[...] = swap_halves(qkv_ref[:, k_at])
            vt_ref[...] = jnp.transpose(qkv_ref[:, v_at].astype(single)).astype(narrow)

            @pl.loop(0, PIX // CHUNK)
            def _(i):
                query = mask_half(qkv_ref[rows_of(i), q_at], h == 1, SCALE)
                scores = dot_t(k_ref[...], query)
                top = jnp.max(scores, 0, keepdims=True)
                exponent = jnp.exp(scores - top)
                total = jnp.sum(exponent, 0, keepdims=True)
                mixed = dot(vt_ref[...], exponent.astype(narrow)) / total
                log_ref[2 * s + h, i] = top + jnp.log(total)
                turned = jnp.transpose(mixed)
                at = rows_of(i)
                lanes = slice(s * BLOCK, (s + 1) * BLOCK)
                if h == 0:
                    out_ref[at, lanes] = turned.astype(narrow)
                else:
                    kept = out_ref[at, lanes].astype(single)
                    out_ref[at, lanes] = jnp.where(low_lanes(turned.shape), kept, turned).astype(narrow)

            if between is not None:
                between(2 * s + h + 1)


def attend_back(qkv_ref, log_ref, grad_ref, k_ref, kt_ref, dk_ref, dv_ref, dqkv, between=None):
    for s in range(2):
        lanes = slice(s * BLOCK, (s + 1) * BLOCK)
        for h in range(2):
            q_at, k_at, v_at = head_parts(qkv_ref, s, h)
            q_to, k_to, v_to = head_parts(None, 0, h)
            grad_to = dqkv[s]
            k_ref[...] = swap_halves(qkv_ref[:, k_at])
            kt_ref[...] = jnp.transpose(k_ref[...].astype(single)).astype(narrow)
            dk_ref[...] = jnp.zeros_like(dk_ref)
            dv_ref[...] = jnp.zeros_like(dv_ref)

            @pl.loop(0, PIX // CHUNK, unroll=UNROLL)
            def _(i):
                at = rows_of(i)
                query = mask_half(qkv_ref[at, q_at], h == 1, SCALE)
                grad = mask_half(grad_ref[at, lanes], h == 1)
                weights = jnp.exp(dot_t(k_ref[...], query) - log_ref[2 * s + h, i])
                dv_ref[...] += dot(weights.astype(narrow), grad)
                dweights = dot_t(qkv_ref[:, v_at], grad)
                inner = jnp.sum(weights * dweights, 0, keepdims=True)
                dscores = (weights * (dweights - inner)).astype(narrow)
                dk_ref[...] += dot(dscores, query)
                turned = jnp.transpose(dot(kt_ref[...], dscores) * SCALE)
                kept = grad_to[at, q_to].astype(single)
                low = low_lanes(turned.shape)
                if h == 0:
                    grad_to[at, q_to] = turned.astype(narrow)
                else:
                    grad_to[at, q_to] = jnp.where(low, kept, turned).astype(narrow)

            low = low_lanes((PIX, BLOCK))
            dk = swap_halves(dk_ref[...])
            if h == 0:
                grad_to[:, k_to] = jnp.where(low, grad_to[:, k_to].astype(single), dk).astype(narrow)
                grad_to[:, v_to] = dv_ref[...].astype(narrow)
            else:
                grad_to[:, k_to] = jnp.where(low, dk, dv_ref[...]).astype(narrow)
            if between is not None:
                between(2 * s + h + 1)


VMEM = pl.BlockSpec(memory_space=pltpu.VMEM)


def call(body, outs, scratch, args, name):
    return pl.pallas_call(
        body,
        out_shape=outs,
        in_specs=[VMEM] * len(args),
        out_specs=[VMEM] * len(outs),
        scratch_shapes=scratch,
        compiler_params=pltpu.CompilerParams(vmem_limit_bytes=56 * 2**20),
        name=name,
    )(*args)


def struct(shape, dtype=single):
    return jax.ShapeDtypeStruct(shape, dtype)


def entry_kernel(act, x_ref, own_ref, recv_ref, norm_ref, stream_ref, entry_ref):
    @pl.loop(0, PIX // CHUNK)
    def _(i):
        at = rows_of(i)
        stream_ref[at, :] = x_ref[at, :] + (own_ref[at, :] + recv_ref[at, :].astype(single))

    def store(i, value):
        entry_ref[rows_of(i), :] = value

    norm_forward(stream_ref, norm_ref[0:1, :], norm_ref[1:2, :], act, store)


def first_kernel(x_ref, norm_ref, stream_ref, entry_ref):
    @pl.loop(0, PIX // CHUNK)
    def _(i):
        at = rows_of(i)
        stream_ref[at, :] = x_ref[at, :].astype(single)

    def store(i, value):
        entry_ref[rows_of(i), :] = value

    norm_forward(stream_ref, norm_ref[0:1, :], norm_ref[1:2, :], True, store)


def mid_rows(norm_ref, mod_ref):
    gain, bias = norm_ref[0:1, :], norm_ref[1:2, :]
    scale, shift = 1.0 + mod_ref[0:1, :], mod_ref[1:2, :]
    return gain, bias, scale, shift


def put_split(own_ref, peer_ref):
    def store(i, value):
        own, peer = split_core(value)
        own_ref[rows_of(i), :] = own
        peer_ref[rows_of(i), :] = peer.astype(narrow)

    return store


def shift_full(full_ref, s_ref, width):
    shifts(lambda i, size: full_ref[rows_of(i, size), :], s_ref, width)


def res_kernel(own_ref, peer_ref, win_ref, wout_ref, norm_ref, mod_ref, inner_ref, hidden_ref, part_ref, send_ref, full_ref, s_ref):
    join_core(own_ref, peer_ref, full_ref)
    shift_full(full_ref, s_ref, C)

    def put(i, value):
        inner_ref[rows_of(i), :] = value

    conv_wide(s_ref, win_ref, put)
    gain, bias, scale, shift = mid_rows(norm_ref, mod_ref)

    def store(i, value):
        hidden_ref[rows_of(i), :] = value

    norm_forward(inner_ref, gain * scale, bias * scale + shift, True, store)
    shift_full(hidden_ref, s_ref, HALF)
    conv_tall(s_ref, wout_ref, 1, put_split(part_ref, send_ref))


def attn_kernel(own_ref, peer_ref, w_ref, qkv_ref, log_ref, out_ref, part_ref, send_ref, full_ref, k_ref, vt_ref):
    join_core(own_ref, peer_ref, full_ref)

    @pl.loop(0, PIX // CHUNK)
    def _(i):
        at = rows_of(i)
        for s in range(2):
            value = dot(full_ref[at, :], w_ref[:, s * C : s * C + 3 * BLOCK])
            qkv_ref[at, s * 3 * BLOCK : (s + 1) * 3 * BLOCK] = value.astype(narrow)

    attend(qkv_ref, k_ref, vt_ref, log_ref, out_ref)
    store = put_split(part_ref, send_ref)

    @pl.loop(0, PIX // CHUNK)
    def _(i):
        at = rows_of(i)
        value = dot_t(out_ref[at, 0:BLOCK], w_ref[:, 3 * BLOCK : C])
        store(i, value + dot_t(out_ref[at, BLOCK:], w_ref[:, C + 3 * BLOCK :]))


def load_rows(ref):
    return lambda i: ref[rows_of(i), :]


def head_kernel(total, own_ref, peer_ref, w_ref, noise_ref, weight_ref, loss_ref, dw_ref, part_ref, send_ref, full_ref, s_ref, t_ref, grad_ref):
    join_core(own_ref, peer_ref, full_ref)
    shift_full(full_ref, s_ref, C)
    loss_ref[...] = jnp.zeros_like(loss_ref)

    def store(i, value):
        error = value - noise_ref[rows_of(i), :]
        weight = weight_ref[0:1, :]
        loss_ref[...] += jnp.sum(weight * error * error, 0, keepdims=True)
        grad_ref[rows_of(i), :] = (2.0 * weight * error / total).astype(narrow)

    conv_wide(s_ref, w_ref, store)
    wide_back(full_ref, w_ref, grad_ref, dw_ref, part_ref, send_ref, s_ref, t_ref)


def wide_back(full_ref, w_ref, grad_ref, dw_ref, part_ref, send_ref, s_ref, t_ref):
    shift_full(grad_ref, s_ref, HALF)
    transpose_into(load_rows(full_ref), t_ref)

    def keep(t, value):
        dw_ref[t * C : (t + 1) * C, :] = value.astype(narrow)

    kernel_grad(t_ref, s_ref, -1, keep)
    conv_tall(s_ref, w_ref, -1, put_split(part_ref, send_ref))


def normback_kernel(act, x_ref, part_ref, recv_ref, up_ref, norm_ref, dx_ref, low_ref, sums_ref, tmp_ref):
    def load(i):
        return part_ref[rows_of(i), :] + recv_ref[rows_of(i), :].astype(single)

    def store(i, value):
        value = value + up_ref[rows_of(i), :]
        dx_ref[rows_of(i), :] = value
        low_ref[rows_of(i), :] = value.astype(narrow)

    total, along = norm_backward(x_ref, load, norm_ref[0:1, :], norm_ref[1:2, :], act, tmp_ref, store)
    sums_ref[0:1, :] = along
    sums_ref[1:2, :] = total


def resback_kernel(
    gown_ref, gpeer_ref, hidden_ref, inner_ref, norm_ref, mod_ref, wout_ref, own_ref, peer_ref, win_ref,
    dout_ref, din_ref, part_ref, send_ref, sums_ref, dmod_ref,
    full_ref, s_ref, t_ref, dh_ref, tmp_ref, grad_ref,
):
    join_core(gown_ref, gpeer_ref, full_ref)
    transpose_into(load_rows(full_ref), t_ref)
    shift_full(hidden_ref, s_ref, HALF)

    def keep(t, value):
        dout_ref[t * C : (t + 1) * C, :] = value.astype(narrow)

    kernel_grad(t_ref, s_ref, 1, keep)
    shift_full(full_ref, s_ref, C)

    def put(i, value):
        dh_ref[rows_of(i), :] = value

    conv_back(s_ref, wout_ref, put)
    gain, bias, scale, shift = mid_rows(norm_ref, mod_ref)

    def store(i, value):
        grad_ref[rows_of(i), :] = value.astype(narrow)

    total, along = norm_backward(
        inner_ref, load_rows(dh_ref), gain * scale, bias * scale + shift, True, tmp_ref, store
    )
    sums_ref[0:1, :] = scale * along
    sums_ref[1:2, :] = scale * total
    dmod_ref[0:1, :] = gain * along + bias * total
    dmod_ref[1:2, :] = total
    join_core(own_ref, peer_ref, full_ref)
    wide_back(full_ref, win_ref, grad_ref, din_ref, part_ref, send_ref, s_ref, t_ref)


def attnback_kernel(
    gown_ref, gpeer_ref, qkv_ref, log_ref, out_ref, w_ref, own_ref, peer_ref,
    dw_ref, part_ref, send_ref,
    full_ref, t_ref, grad_ref, k_ref, kt_ref, dk_ref, dv_ref, dqkv_ref,
):
    join_core(gown_ref, gpeer_ref, full_ref)
    transpose_into(load_rows(full_ref), t_ref)
    for s in range(2):
        lanes = slice(s * BLOCK, (s + 1) * BLOCK)
        dw_ref[:, s * C + 3 * BLOCK : (s + 1) * C] = dot(t_ref[...], out_ref[:, lanes]).astype(narrow)

        @pl.loop(0, PIX // CHUNK)
        def _(i):
            at = rows_of(i)
            value = dot(full_ref[at, :], w_ref[:, s * C + 3 * BLOCK : (s + 1) * C])
            grad_ref[at, lanes] = value.astype(narrow)

    dqkv = [dqkv_ref.at[:, s * 3 * BLOCK : (s + 1) * 3 * BLOCK] for s in range(2)]
    attend_back(qkv_ref, log_ref, grad_ref, k_ref, kt_ref, dk_ref, dv_ref, dqkv)
    join_core(own_ref, peer_ref, full_ref)
    transpose_into(load_rows(full_ref), t_ref)
    for s in range(2):
        lanes = slice(s * 3 * BLOCK, (s + 1) * 3 * BLOCK)
        dw_ref[:, s * C : s * C + 3 * BLOCK] = dot(t_ref[...], dqkv_ref[:, lanes]).astype(narrow)
    store = put_split(part_ref, send_ref)

    @pl.loop(0, PIX // CHUNK)
    def _(i):
        at = rows_of(i)
        value = dot_t(dqkv_ref[at, 0 : 3 * BLOCK], w_ref[:, 0 : 3 * BLOCK])
        store(i, value + dot_t(dqkv_ref[at, 3 * BLOCK :], w_ref[:, C : C + 3 * BLOCK]))


HALF_F32 = struct((PIX, HALF))
HALF_LOW = struct((PIX, HALF), narrow)
FULL_LOW = pltpu.VMEM((PIX, C), narrow)
SHIFTED = pltpu.VMEM((3, ROWS, C), narrow)
TURNED = pltpu.VMEM((C, PIX), narrow)
SWAP = [(0, 1), (1, 0)]


def core_swap(value):
    return lax.ppermute(value, "lo", SWAP)


def image_swap(value):
    return lax.ppermute(value, "hi", SWAP)


DP = ("dz", "dy")


def pick_image(value):
    hi = lax.axis_index("hi")
    kept = jnp.where(hi == 0, value[0], value[1])
    came = image_swap(jnp.where(hi == 0, value[1], value[0]))
    return jnp.where(hi == 0, jnp.concatenate([kept, came], 1), jnp.concatenate([came, kept], 1))


def join_image(value, axis):
    hi = lax.axis_index("hi")
    came = image_swap(value)
    return jnp.where(
        hi == 0, jnp.concatenate([value, came], axis), jnp.concatenate([came, value], axis)
    )


def gather_weight(shard):
    rows = lax.all_gather(shard, DP, axis=0, tiled=True)
    return lax.all_gather(rows, "hi", axis=1, tiled=True)


def scatter_grad(value):
    cols = lax.psum_scatter(value, "hi", scatter_dimension=1, tiled=True)
    return lax.psum_scatter(cols, DP, scatter_dimension=0, tiled=True).astype(single)


def chan_index():
    return lax.axis_index("hi") * 2 + lax.axis_index("lo")


def sinusoid_of(timesteps):
    half_count = TF // 2
    frequency = jnp.exp(-math.log(10000.0) * jnp.arange(half_count, dtype=single) / half_count)
    angles = timesteps.astype(single)[:, None] * frequency[None, :]
    return jnp.concatenate([jnp.cos(angles), jnp.sin(angles)], 1).astype(narrow)


def embed_forward(timesteps, classes, time_in, emb_out, emb_proj):
    times = lax.all_gather(timesteps, DP, axis=0, tiled=True)
    labels = lax.all_gather(classes, DP, axis=0, tiled=True)
    rows = time_in.shape[0]
    place = lax.axis_index(DP) * rows
    sinusoid = lax.dynamic_slice_in_dim(sinusoid_of(times), place, rows, 1)
    pre = lax.psum(dot(sinusoid, time_in), DP)
    hidden = jax.nn.silu(pre).astype(narrow)
    class_here = emb_out.shape[1] - hidden.shape[1]
    numbers = chan_index() * class_here + jnp.arange(class_here)
    onehot = (labels[:, None] == numbers[None, :]).astype(narrow)
    joined = jnp.concatenate([hidden, onehot], 1)
    embedding = lax.psum(dot_t(joined, emb_out), ("hi", "lo"))
    context = jax.nn.silu(embedding).astype(narrow)
    parts = jnp.einsum("be,lej->blj", context, emb_proj, preferred_element_type=single)
    mine = lax.psum_scatter(parts, DP, scatter_dimension=0, tiled=True)
    hi = lax.axis_index("hi")
    kept = jnp.where(hi == 0, mine[0], mine[1])
    came = image_swap(jnp.where(hi == 0, mine[1], mine[0]))
    wide = jnp.where(hi == 0, jnp.concatenate([kept, came], 1), jnp.concatenate([came, kept], 1))
    modulate = jnp.swapaxes(wide.reshape(2, HALF, 2), 1, 2)
    return modulate, (sinusoid, pre, joined, embedding, context)


def embed_backward(saved, dmod, emb_proj, emb_out):
    sinusoid, pre, joined, embedding, context = saved
    flat = jnp.swapaxes(dmod, 1, 2).reshape(2, 2 * HALF).astype(narrow)
    hi = lax.axis_index("hi")
    width = flat.shape[1] // 2
    kept = jnp.where(hi == 0, flat[:, :width], flat[:, width:])
    came = image_swap(jnp.where(hi == 0, flat[:, width:], flat[:, :width]))
    both = jnp.where(hi == 0, jnp.stack([kept, came]), jnp.stack([came, kept]))
    grads = lax.all_gather(both, DP, axis=0, tiled=True)
    proj_grad = jnp.einsum("be,blj->lej", context, grads, preferred_element_type=single)
    part = jnp.einsum("blj,lej->be", grads, emb_proj, preferred_element_type=single)
    context_grad = lax.psum(part, ("hi", "lo"))
    _, pullback = jax.vjp(jax.nn.silu, embedding)
    (embed_grad,) = pullback(context_grad)
    embed_low = embed_grad.astype(narrow)
    out_grad = jnp.einsum("be,bj->ej", embed_low, joined, preferred_element_type=single)
    joined_grad = lax.psum(dot(embed_low, emb_out[:, : pre.shape[1]]), DP)
    _, pullback = jax.vjp(jax.nn.silu, pre)
    (pre_grad,) = pullback(joined_grad)
    time_grad = jnp.einsum("bt,be->te", sinusoid, pre_grad.astype(narrow), preferred_element_type=single)
    return proj_grad, time_grad, out_grad


def res_forward(own, peer, win, wout, norm, mod):
    outs = [HALF_F32, HALF_LOW, HALF_F32, HALF_LOW]
    return call(res_kernel, outs, [FULL_LOW, SHIFTED], [own, peer, win, wout, norm, mod], "res_forward")


def res_backward(gown, gpeer, hidden, inner, norm, mod, wout, own, peer, win):
    taps = struct((9 * C, HALF), narrow)
    outs = [taps, taps, HALF_F32, HALF_LOW, struct((2, HALF)), struct((2, HALF))]
    scratch = [FULL_LOW, SHIFTED, TURNED, pltpu.VMEM((PIX, HALF), single), pltpu.VMEM((PIX, HALF), single), pltpu.VMEM((PIX, HALF), narrow)]
    return call(resback_kernel, outs, scratch, [gown, gpeer, hidden, inner, norm, mod, wout, own, peer, win], "res_backward")


def norm_step(act, x, part, recv, up, norm):
    outs = [HALF_F32, HALF_LOW, struct((2, HALF))]
    body = functools.partial(normback_kernel, act)
    return call(body, outs, [pltpu.VMEM((PIX, HALF), single)], [x, part, recv, up, norm], "norm_backward")


def entry_step(act, x, part, recv, norm):
    return call(functools.partial(entry_kernel, act), [HALF_F32, HALF_LOW], [], [x, part, recv, norm], "entry")


def network(noisy, noise, sample_weight, kernels_in, kernels_out, attn, norms, modulate):
    images = noisy.shape[0] * lax.axis_size("dz") * lax.axis_size("dy")
    total = float(images * PIX * C)
    x0 = pick_image(noisy.reshape(2, PIX, BLOCK))
    target = pick_image(noise.reshape(2, PIX, BLOCK))
    weight = jnp.where(lax.axis_index("hi") == 0, sample_weight[0], sample_weight[1])
    weight = jnp.broadcast_to(weight, (8, HALF))
    stream0, entry0 = call(first_kernel, [HALF_F32, HALF_LOW], [], [x0, norms[0]], "entry")
    peer0 = core_swap(entry0)
    inner0, hidden0, part, send = res_forward(entry0, peer0, kernels_in[0], kernels_out[0], norms[1], modulate[0])
    stream1, entry1 = entry_step(False, stream0, part, core_swap(send), norms[2])
    peer1 = core_swap(entry1)
    outs = [struct((PIX, 6 * BLOCK), narrow), struct((4, PIX // CHUNK, 1, CHUNK)), HALF_LOW, HALF_F32, HALF_LOW]
    scratch = [FULL_LOW, pltpu.VMEM((PIX, BLOCK), narrow), pltpu.VMEM((BLOCK, PIX), narrow)]
    qkv, log, attended, part, send = call(attn_kernel, outs, scratch, [entry1, peer1, attn], "attention")
    stream2, entry2 = entry_step(True, stream1, part, core_swap(send), norms[3])
    peer2 = core_swap(entry2)
    inner2, hidden2, part, send = res_forward(entry2, peer2, kernels_in[1], kernels_out[1], norms[4], modulate[1])
    stream3, entry3 = entry_step(True, stream2, part, core_swap(send), norms[5])
    peer3 = core_swap(entry3)
    taps = struct((9 * C, HALF), narrow)
    outs = [struct((1, HALF)), taps, HALF_F32, HALF_LOW]
    scratch = [FULL_LOW, SHIFTED, TURNED, pltpu.VMEM((PIX, HALF), narrow)]
    args = [entry3, peer3, kernels_in[2], target, weight]
    loss, din2, part, send = call(functools.partial(head_kernel, total), outs, scratch, args, "head")
    zero = jnp.zeros((PIX, HALF), single)
    grad3, low3, sums5 = norm_step(True, stream3, part, core_swap(send), zero, norms[5])
    dout1, din1, part, send, sums4, dmod1 = res_backward(
        low3, core_swap(low3), hidden2, inner2, norms[4], modulate[1], kernels_out[1], entry2, peer2, kernels_in[1]
    )
    grad2, low2, sums3 = norm_step(True, stream2, part, core_swap(send), grad3, norms[3])
    outs = [struct((C, 2 * C), narrow), HALF_F32, HALF_LOW]
    scratch = [
        FULL_LOW, TURNED, pltpu.VMEM((PIX, HALF), narrow), pltpu.VMEM((PIX, BLOCK), narrow), pltpu.VMEM((BLOCK, PIX), narrow),
        pltpu.VMEM((PIX, BLOCK), single), pltpu.VMEM((PIX, BLOCK), single), pltpu.VMEM((PIX, 6 * BLOCK), narrow),
    ]
    args = [low2, core_swap(low2), qkv, log, attended, attn, entry1, peer1]
    dattn, part, send = call(attnback_kernel, outs, scratch, args, "attention_backward")
    grad1, low1, sums2 = norm_step(False, stream1, part, core_swap(send), grad2, norms[2])
    dout0, din0, part, send, sums1, dmod0 = res_backward(
        low1, core_swap(low1), hidden0, inner0, norms[1], modulate[0], kernels_out[0], entry0, peer0, kernels_in[0]
    )
    _, _, sums0 = norm_step(True, stream0, part, core_swap(send), grad1, norms[0])
    sums = jnp.stack([sums0, sums1, sums2, sums3, sums4, sums5])
    return jnp.sum(loss) / total, (din0, din1, din2), (dout0, dout1), dattn, sums, jnp.stack([dmod0, dmod1])


MESH = pl.DeviceIdType.MESH
ANY = pl.BlockSpec(memory_space=pl.ANY)
SMEM = pl.BlockSpec(memory_space=pltpu.SMEM)
LAYERS = 6
REDUCES = 8
EARLY = ("5", "1b")
LANDINGS = 5 * REDUCES
STEPS = 16


def remote(src, dst, send, recv, **where):
    return pltpu.make_async_remote_copy(
        src_ref=src, dst_ref=dst, send_sem=send, recv_sem=recv, device_id=where, device_id_type=MESH
    )


def place():
    return lax.axis_index("dz"), lax.axis_index("dy"), lax.axis_index("hi")


def greet(others):
    barrier = pltpu.get_barrier_semaphore()
    for where in others:
        pl.semaphore_signal(barrier, inc=1, device_id=where, device_id_type=MESH)
    pl.semaphore_wait(barrier, len(others))


def neighbours():
    z, y, x = place()
    others = [{"dz": (z + k) % 4} for k in (1, 2, 3)]
    return others + [{"dy": 1 - y}, {"hi": 1 - x}, {"lo": 1 - lax.axis_index("lo")}]


class Layout:
    def __init__(self, rows, lanes):
        self.rows, self.lanes = rows, lanes

    def block(self, zz, yy):
        return pl.ds(pl.multiple_of((zz * 2 + yy) * self.rows, 32), self.rows)

    def cols(self, xx):
        return pl.ds(pl.multiple_of(xx * self.lanes, 128), self.lanes)


class AlongZ:
    def __init__(self, own, region, send, recv):
        z, _, _ = place()
        self.z, self.sends, self.waits = z, [], []
        for j, d in enumerate((2, -2, 1, -1)):
            allowed = z + d < 4 if d > 0 else z + d >= 0
            self.sends.append((allowed, remote(own, region(z), send(j), recv(z), dz=z + d)))
        self.relays = []
        for here, source, target in ((2, 0, 3), (1, 3, 0)):
            part = region(source)
            self.relays.append((z == here, remote(part, part, send(4), recv(source), dz=target)))
        for source in range(4):
            relayed = {0: z == 2, 3: z == 1}.get(source)
            wanted = z != source if relayed is None else (z != source) & jnp.logical_not(relayed)
            part = region(source)
            self.waits.append((wanted, remote(part, part, send(0), recv(source), dz=z)))

    def start(self):
        for allowed, copy in self.sends:
            pl.when(allowed)(copy.start)

    def pass_on(self):
        for here, copy in self.relays:

            def go(copy=copy):
                copy.wait_recv()
                copy.start()

            pl.when(here)(go)

    def wait(self):
        for wanted, copy in self.waits:
            pl.when(wanted)(copy.wait_recv)

    def drain(self):
        for allowed, copy in self.sends + self.relays:
            pl.when(allowed)(copy.wait_send)


class SumAlongZ:
    def __init__(self, block, slots, rows, lanes, send, recv):
        z, _, _ = place()
        self.z, self.block, self.slots, self.rows, self.lanes = z, block, slots, rows, lanes
        self.send, self.recv = send, recv
        self.outer = (z == 0) | (z == 3)
        self.sends, self.relays = [], []

        def copy(j, target, slot, to):
            return remote(block(target), slots.at[slot], send(j), recv(slot), dz=to)

        for here, j, target, slot, to in (
            (0, 0, 3, 1, 1), (0, 1, 2, 0, 2), (0, 2, 1, 0, 1),
            (3, 0, 0, 2, 2), (3, 1, 1, 3, 1), (3, 2, 2, 3, 2),
            (1, 0, 0, 1, 0), (1, 1, 2, 1, 2),
            (2, 0, 1, 2, 1), (2, 1, 3, 2, 3),
        ):
            self.sends.append((z == here, copy(j, target, slot, to)))
        for here, target in ((1, 3), (2, 0)):
            self.relays.append((here, z == here, target, copy(3, target, here, target)))

    def start(self):
        for here, copy in self.sends:
            pl.when(here)(copy.start)

    def pass_on(self):
        for number, here, target, copy in self.relays:

            def go(number=number, target=target, copy=copy):
                copy.wait_recv()
                add_rows(self.rows, self.lanes, self.block(target), self.slots.at[number])
                copy.start()

            pl.when(here)(go)

    def collect(self, add):
        def take(sources):
            def go():
                for source in sources:
                    waiting = self.slots.at[source]
                    remote(waiting, waiting, self.send(0), self.recv(source), dz=self.z).wait_recv()
                add([self.slots.at[source] for source in sources])

            return go

        pl.when(self.outer)(take((1, 2)))
        pl.when(self.z == 1)(take((0, 2, 3)))
        pl.when(self.z == 2)(take((0, 1, 3)))

    def drain(self):
        for here, copy in self.sends:
            pl.when(here)(copy.wait_send)
        for _, here, _, copy in self.relays:
            pl.when(here)(copy.wait_send)


class Gather:
    def __init__(self, layer, shard, full, send, recv, local):
        z, y, x = place()
        rows, lanes = shard.shape
        at = Layout(rows, lanes)
        mine = full.at[at.block(z, y), at.cols(x)]
        self.local = pltpu.make_async_copy(shard, mine, local.at[layer])

        def copy(j, src, dst, **where):
            return remote(src, dst, send.at[layer, j], recv.at[layer, j], **where)

        region = lambda zz: full.at[at.block(zz, y), at.cols(x)]
        self.along_z = AlongZ(shard, region, lambda j: send.at[layer, 7 + j], lambda j: recv.at[layer, 7 + j])
        self.first, self.second = [], []
        for n in range(2):
            part = full.at[at.block(n, y), at.cols(x)]
            self.first.append(copy(n, part, part, dy=1 - y))
            part = full.at[at.block(2 + n, y), at.cols(x)]
            self.first.append(copy(2 + n, part, part, hi=1 - x))
        part = full.at[0 : 4 * rows, at.cols(x)]
        self.second.append(copy(4, part, part, hi=1 - x))
        for n in range(2):
            part = full.at[at.block(2 + n, y), :]
            self.second.append(copy(5 + n, part, part, dy=1 - y))

    def start(self):
        self.local.start()
        self.along_z.start()

    def pass_on(self):
        self.along_z.pass_on()

    def turn(self):
        self.local.wait()
        self.along_z.wait()
        for copy in self.first:
            copy.start()

    def spread(self):
        for copy in self.first:
            copy.wait_recv()
        for copy in self.second:
            copy.start()

    def ready(self):
        for copy in self.second:
            copy.wait_recv()

    def drain(self):
        self.along_z.drain()
        for copy in self.first + self.second:
            copy.wait_send()


def add_rows(count, lanes, into, other):
    size = next(n for n in (192, 144, 96, 64, 48, 32) if count % n == 0 and n * lanes <= 32768)

    @pl.loop(0, count // size)
    def _(i):
        at = pl.ds(pl.multiple_of(i * size, 16), size)
        into.at[at, :][...] = into.at[at, :][...] + other.at[at, :][...]


class Reduce:
    buffers = 5

    def __init__(self, layer, grad, bufs, out, low, count, send, recv):
        z, y, x = place()
        ra, rb, rc, rd, rz = bufs
        rows, lanes = out.shape
        at = Layout(rows, lanes)
        self.lanes, self.out, self.bufs, self.low, self.count = lanes, out, bufs, low, count

        def copy(j, src, dst, **where):
            return remote(src, dst, send.at[layer, j], recv.at[layer, j], **where)

        def part(zz, yy, xx=None):
            cut = pl.ds(pl.multiple_of((zz * 2 + yy) * rows + low, 32), count)
            return grad.at[cut, :] if xx is None else grad.at[cut, at.cols(xx)]

        self.part, self.here = part, (z, y, x)
        self.first = []
        for k in range(4):
            self.first.append(copy(k, part(k // 2, k % 2, 1 - x), ra.at[k], hi=1 - x))
        for n in range(2):
            self.first.append(copy(4 + n, part(2 + n, 1 - y), rb.at[n], dy=1 - y))
        self.second = []
        for n in range(2):
            self.second.append(copy(6 + n, part(n, 1 - y, x), rc.at[n], dy=1 - y))
        for n in range(2):
            self.second.append(copy(8 + n, part(2 + n, y, 1 - x), rd.at[n], hi=1 - x))
        self.third = SumAlongZ(
            lambda zz: part(zz, y, x), rz, count, lanes, lambda j: send.at[layer, 10 + j], lambda j: recv.at[layer, 10 + j]
        )

    def start(self):
        for copy in self.first:
            copy.start()

    def turn(self):
        (z, y, x), (ra, rb, rc, rd, rz) = self.here, self.bufs
        for k in range(4):
            self.first[k].wait_recv()
            add_rows(self.count, self.lanes, self.part(k // 2, k % 2, x), ra.at[k])
        for copy in self.second[:2]:
            copy.start()
        for n in range(2):
            self.first[4 + n].wait_recv()
            add_rows(self.count, 2 * self.lanes, self.part(2 + n, y), rb.at[n])
            self.second[2 + n].start()

    def spread(self):
        (z, y, x), (ra, rb, rc, rd, rz) = self.here, self.bufs
        for n in range(2):
            self.second[n].wait_recv()
            add_rows(self.count, self.lanes, self.part(n, y, x), rc.at[n])
        for n in range(2):
            self.second[2 + n].wait_recv()
            add_rows(self.count, self.lanes, self.part(2 + n, y, x), rd.at[n])
        self.third.start()

    def pass_on(self):
        self.third.pass_on()

    def finish(self):
        z, y, x = self.here
        size = 32
        mine = self.part(z, y, x)

        def add(sources):
            @pl.loop(0, self.count // size)
            def _(i):
                part = pl.ds(pl.multiple_of(i * size, 32), size)
                total = mine.at[part, :][...].astype(single)
                for source in sources:
                    total = total + source.at[part, :][...].astype(single)
                self.out.at[pl.ds(pl.multiple_of(self.low + i * size, 32), size), :][...] = total

        self.third.collect(add)

    def drain(self):
        self.third.drain()
        for copy in self.first + self.second:
            copy.wait_send()


def reduce_plan(outs):
    rows = [out.shape[0] for out in outs]
    plan = [(str(n), n, 0, rows[n]) for n in (5, 4, 3, 2)]
    for n in (1, 0):
        half = rows[n] // 2
        plan += [(f"{n}a", n, 0, half), (f"{n}b", n, half, half)]
    return plan


class LateGather:
    def __init__(self, layer, shard, full, send, recv, local):
        z, y, x = place()
        rows, lanes = shard.shape
        half = rows // 2
        at = Layout(rows, lanes)
        mine = full.at[at.block(z, y), at.cols(x)]
        self.local = pltpu.make_async_copy(shard, mine, local.at[layer])

        def copy(j, src, dst, **where):
            return remote(src, dst, send.at[layer, j], recv.at[layer, j], **where)

        def part(yy, k):
            return pl.ds(pl.multiple_of((z * 2 + yy) * rows + k * half, 32), half)

        self.first = [
            copy(0, shard.at[0:half, :], full.at[part(y, 0), at.cols(x)], hi=1 - x),
            copy(1, shard.at[half:, :], full.at[part(y, 1), at.cols(x)], dy=1 - y),
        ]
        self.second = [copy(2, full.at[part(y, 0), :], full.at[part(y, 0), :], dy=1 - y)]
        for yy in range(2):
            block = full.at[part(yy, 1), at.cols(x)]
            self.second.append(copy(3 + yy, block, block, hi=1 - x))
        self.third = []
        for k in range(4):
            region = lambda zz, k=k: full.at[pl.ds(pl.multiple_of(zz * 2 * rows + k * half, 32), half), :]
            sems = [lambda j, k=k, ref=ref: ref.at[layer, 7 + 5 * k + j] for ref in (send, recv)]
            self.third.append(AlongZ(region(z), region, *sems))

    def start(self):
        self.local.start()
        for copy in self.first:
            copy.start()

    def turn(self):
        self.local.wait()
        for copy in self.first:
            copy.wait_recv()
        for copy in self.second:
            copy.start()

    def spread(self, k):
        if k == 0:
            for copy in self.second:
                copy.wait_recv()
        self.third[k].start()

    def pass_on(self, k):
        self.third[k].pass_on()

    def ready(self):
        for chunk in self.third:
            chunk.wait()

    def drain(self):
        for chunk in self.third:
            chunk.drain()
        for copy in self.first + self.second:
            copy.wait_send()


class EarlyReduce:
    buffers = 5

    def __init__(self, layer, grad, bufs, out, low, count, send, recv):
        z, y, x = place()
        rz, ra, rb, rc, rd = bufs
        rows, lanes = out.shape
        half = count // 2
        at = Layout(rows, lanes)
        self.out, self.grad, self.bufs, self.lanes, self.half = out, grad, bufs, lanes, half
        self.low, self.count = low, count

        def copy(j, src, dst, **where):
            return remote(src, dst, send.at[layer, j], recv.at[layer, j], **where)

        def part(yy, k):
            return pl.ds(pl.multiple_of((z * 2 + yy) * rows + low + k * half, 16), half)

        self.part, self.cols, self.here, self.first = part, at.cols, (z, y, x), []
        for yy in range(2):

            def block(zz, yy=yy):
                return grad.at[pl.ds(pl.multiple_of((zz * 2 + yy) * rows + low, 32), count), :]

            sems = [lambda j, yy=yy, ref=ref: ref.at[layer, 8 + 4 * yy + j] for ref in (send, recv)]
            self.first.append(SumAlongZ(block, rz.at[yy], count, 2 * lanes, *sems))
        self.second = [copy(3, grad.at[part(1 - y, 0), :], ra, dy=1 - y)]
        for yy in range(2):
            self.second.append(copy(4 + yy, grad.at[part(yy, 1), at.cols(1 - x)], rb.at[yy], hi=1 - x))
        self.third = [
            copy(6, grad.at[part(y, 0), at.cols(1 - x)], rc, hi=1 - x),
            copy(7, grad.at[part(1 - y, 1), at.cols(x)], rd, dy=1 - y),
        ]

    def start(self):
        for chunk in self.first:
            chunk.start()

    def pass_on(self):
        for chunk in self.first:
            chunk.pass_on()

    def turn(self):
        z = self.here[0]
        for chunk in self.first:

            def add(sources, chunk=chunk):
                for source in sources:
                    add_rows(self.count, 2 * self.lanes, chunk.block(z), source)

            chunk.collect(add)
        for copy in self.second:
            copy.start()

    def spread(self):
        (z, y, x), (rz, ra, rb, rc, rd) = self.here, self.bufs
        self.second[0].wait_recv()
        add_rows(self.half, 2 * self.lanes, self.grad.at[self.part(y, 0), :], ra)
        self.third[0].start()
        for yy in range(2):
            self.second[1 + yy].wait_recv()
            add_rows(self.half, self.lanes, self.grad.at[self.part(yy, 1), self.cols(x)], rb.at[yy])
        self.third[1].start()

    def finish(self):
        (z, y, x), (rz, ra, rb, rc, rd) = self.here, self.bufs
        for copy in self.third:
            copy.wait_recv()
        size = 48
        for k, came in enumerate((rc, rd)):
            mine = self.grad.at[self.part(y, k), self.cols(x)]

            @pl.loop(0, self.half // size)
            def _(i):
                part = pl.ds(pl.multiple_of(i * size, 16), size)
                total = mine.at[part, :][...].astype(single) + came.at[part, :][...].astype(single)
                self.out.at[pl.ds(pl.multiple_of(self.low + k * self.half + i * size, 16), size), :][...] = total

    def drain(self):
        for chunk in self.first:
            chunk.drain()
        for copy in self.second + self.third:
            copy.wait_send()


class Core:
    def __init__(self, send, recv):
        self.send, self.recv, self.used = send, recv, 0
        self.core = lax.axis_index("lo")

    def take(self, count):
        base = self.used
        self.used += count
        return base

    def copy(self, index, src, dst):
        return remote(src, dst, self.send.at[index], self.recv.at[index], lo=1 - self.core)

    def lanes(self, j):
        return pl.ds(pl.multiple_of((2 * j + self.core) * BLOCK, 128), BLOCK)

    def share(self, full):
        base = self.take(2 * (PIX // CHUNK))

        def copies(i):
            parts = [full.at[rows_of(i), self.lanes(j)] for j in range(2)]
            return [self.copy(base + 2 * i + j, part, part) for j, part in enumerate(parts)]

        def store(i, value):
            for j in range(2):
                full[rows_of(i), self.lanes(j)] = value[:, j * BLOCK : (j + 1) * BLOCK]
            for copy in copies(i):
                copy.start()

        def wait():
            @pl.loop(0, PIX // CHUNK)
            def _(i):
                for copy in copies(i):
                    copy.wait()

        return store, wait

    def combine(self, part, send, recv):
        base = self.take(PIX // CHUNK)

        def one(i):
            return self.copy(base + i, send.at[rows_of(i), :], recv.at[rows_of(i), :])

        def store(i, value):
            own, peer = split_core(value)
            part[rows_of(i), :] = own
            send[rows_of(i), :] = peer.astype(narrow)
            one(i).start()

        def wait():
            @pl.loop(0, PIX // CHUNK)
            def _(i):
                one(i).wait()

        def load(i):
            return part[rows_of(i), :] + recv[rows_of(i), :].astype(single)

        return store, wait, load


def step_kernel(
    fulls, total,
    noisy_hbm, noise_hbm, weight_ref, times_ref, labels_ref, norms_own, second,
    conv_in, conv_out, attn_weight, time_in, emb_out, emb_proj,
    in_rows, in_cols, out_rows, out_cols, proj_rows, proj_cols, attn_rows, attn_cols, time_rows, time_cols, eout_rows, eout_cols,
    g0, g1, g2, g3, g4, g5, proj_grad, time_grad, eout_grad, rows_ref, cols_ref, scal_ref, norm_out, second_out, norms_out,
    w0, w1, w2, w3, w4, w5, d1, full0, full1, full2, full3,
    *refs,
):
    landing = refs[:LANDINGS]
    (
    x1, x2, x3, inner0, inner2, noise_ref, part, tmp, dh, up,
    hidden0, hidden2, att, pg, x0_ref, send, recv, qkv,
    shifted, turned, k_ref, kt_ref, dk_ref, dv_ref, log_ref,
    norms_ref, mod_ref, loss_lanes, norms_flat, sums_ref, dmod_ref, wsq_ref, sin_ref, label_ref, pre_ref, embedding_ref,
    s0, s1, s2, s3, s4, s5, noise_send, noise_recv,
    msg, p0, p1, p2, p3, m3, q4, p4, p5, p6, p7, q7, p8, p9, p10, p11, p12, p13,
    gsend, grecv, glocal, rsend, rrecv, csend, crecv, xsend, xrecv, esend, erecv, lsem,
    ) = refs[LANDINGS:]
    x = lax.axis_index("hi")
    core, small = Core(csend, crecv), Small(esend, erecv)
    block = pl.ds(pl.multiple_of(x * BLOCK, BLOCK), BLOCK)
    own_x0 = pltpu.make_async_copy(noisy_hbm.at[x], x0_ref.at[:, block], lsem.at[0])
    own_noise = pltpu.make_async_copy(noise_hbm.at[x], noise_ref.at[:, block], lsem.at[1])
    other_noise = pltpu.make_async_copy(noise_hbm.at[1 - x], dk_ref, lsem.at[2])
    own_x0.start()
    own_noise.start()
    other_noise.start()
    norms_flat[...] = joined_rows(norms_own)
    norms_ref[:, block] = norms_flat[...]
    dmod_ref[...] = jnp.zeros_like(dmod_ref)
    loss_lanes[...] = jnp.zeros_like(loss_lanes)
    keep = (sin_ref, label_ref, pre_ref, embedding_ref)
    embed = embed_steps(
        small, times_ref, labels_ref, time_in, emb_out, emb_proj, msg, p0, p1, p2, p3, m3, mod_ref, keep
    )
    shards, full_weights = (s0, s1, s2, s3, s4, s5), (w0, w1, w2, w3, w4, w5)
    gathers = []
    for n, (shard, full) in enumerate(zip(shards, full_weights)):
        kind = LateGather if n == 5 else Gather
        gathers.append(kind(n, shard, full, gsend, grecv, glocal))
    outs, grads = (g0, g1, g2, g3, g4, g5), (w1, w4, w2, w3, d1, w5)
    reduces, used = {}, 0
    for number, (name, n, low, count) in enumerate(reduce_plan(outs)):
        kind = EarlyReduce if name in EARLY else Reduce
        bufs = landing[used : used + kind.buffers]
        used += kind.buffers
        reduces[name] = kind(number, grads[n], bufs, outs[n], low, count, rsend, rrecv)
    matrices = [g0, g3, g5, g1, g4, proj_grad.at[0], proj_grad.at[1], g2, time_grad, eout_grad]
    rows_old = [in_rows[n : n + 1] for n in range(3)] + [out_rows[n : n + 1] for n in range(2)]
    rows_old += [proj_rows[n : n + 1] for n in range(2)] + [attn_rows[...], time_rows[...], eout_rows[...]]
    cols_old = [in_cols[n : n + 1] for n in range(3)] + [out_cols[n : n + 1] for n in range(2)]
    cols_old += [proj_cols[n : n + 1] for n in range(2)] + [attn_cols[...], time_cols[...], eout_cols[...]]
    step = adafactor_steps(
        small, (1, 2, 4, 5, 6, 7, 8, 9), (0, 3), matrices, rows_old, cols_old, fulls, wsq_ref, loss_lanes, sums_ref,
        norms_own, second, p7, q7, p8, p9, p10, p11, p12, p13, rows_ref, cols_ref, scal_ref, norm_out, second_out, norms_out,
    )
    embed_end = embed_back_steps(
        small, dmod_ref, q4, p4, p5, p6, emb_out, emb_proj, keep, proj_grad, eout_grad, time_grad
    )

    def norm_row(n):
        return norms_ref[2 * n : 2 * n + 1, :], norms_ref[2 * n + 1 : 2 * n + 2, :]

    def keep_taps(grad):
        def store(t, value):
            grad[t * C : (t + 1) * C, :] = value.astype(narrow)

        return store

    class First:
        def __getitem__(self, at):
            return x0_ref[at].astype(single)

    def entry(x, n, act, full):
        gain, bias = norm_row(n)
        store, wait = core.share(full)
        norm_forward(x, gain, bias, act, store)
        return wait

    def middle(n, layer):
        gain, bias = norm_row(n)
        scale, shift = 1.0 + mod_ref[layer, 0:1, :], mod_ref[layer, 1:2, :]
        return gain, bias, scale, gain * scale, bias * scale + shift

    def first_half(full, w, n, layer, inner, hidden, between=None):
        shift_full(full, shifted, C)

        def put(i, value):
            inner[rows_of(i), :] = value

        conv_wide(shifted, w, put)
        if between is not None:
            between()
        _, _, _, gain, bias = middle(n, layer)

        def store(i, value):
            hidden[rows_of(i), :] = value

        norm_forward(inner, gain, bias, True, store)
        shift_full(hidden, shifted, HALF)

    def second_half(w):
        store, wait, load = core.combine(part, send, recv)
        conv_tall(shifted, w, 1, store)
        return wait, load

    def advance(x_old, load, x_new):
        @pl.loop(0, PIX // CHUNK)
        def _(i):
            x_new[rows_of(i), :] = x_old[rows_of(i), :] + load(i)

    greet(all_partners())
    swaps = []
    for n, (src, dst) in enumerate(
        ((norms_flat, norms_ref.at[:, block]), (noisy_hbm.at[1 - x], x0_ref.at[:, block]), (noise_send, noise_recv))
    ):
        swaps.append(remote(src, dst, xsend.at[n], xrecv.at[n], hi=1 - x))
    swaps[0].start()
    next(embed)
    masters = [conv_in.at[0], conv_out.at[0], attn_weight, conv_in.at[1], conv_out.at[1], conv_in.at[2]]
    s0[...] = masters[0][...].astype(narrow)
    gathers[0].start()
    s5[...] = masters[5][...].astype(narrow)
    gathers[5].start()
    swaps[1].start()
    for n in range(1, 5):
        shards[n][...] = masters[n][...].astype(narrow)
    next(embed)
    gathers[5].turn()
    gathers[0].pass_on()
    gathers[1].start()
    gathers[0].turn()
    next(embed)
    gathers[0].spread()
    gathers[2].start()
    own_x0.wait()
    swaps[0].wait_recv()
    swaps[1].wait_recv()
    wait_entry = entry(First(), 0, True, full0)
    gathers[1].pass_on()
    gathers[1].turn()
    next(embed)
    gathers[3].start()
    masters = [conv_in.at[n] for n in range(3)] + [conv_out.at[n] for n in range(2)]
    masters += [emb_proj.at[n] for n in range(2)] + [attn_weight, time_in, emb_out]
    wsq_ref[...] = scalar_rows([whole(master[...] * master[...]) for master in masters], 16)
    own_noise.wait()
    other_noise.wait()
    noise_send[...] = dk_ref[...].astype(narrow)
    gathers[2].pass_on()
    gathers[2].turn()
    wait_entry()
    gathers[0].ready()

    def between():
        gathers[4].start()
        gathers[3].pass_on()
        next(embed)
        gathers[1].spread()
        gathers[3].turn()
        gathers[2].spread()

    first_half(full0, w0, 1, 0, inner0, hidden0, between)
    gathers[4].pass_on()
    gathers[5].spread(0)
    gathers[4].turn()
    gathers[1].ready()
    wait, load = second_half(w1)
    wait()
    advance(First(), load, x1)
    wait_entry = entry(x1, 2, False, full1)
    gathers[5].pass_on(0)
    gathers[5].spread(1)
    gathers[3].spread()
    gathers[5].spread(2)
    gathers[2].ready()
    wait_entry()

    @pl.loop(0, PIX // CHUNK)
    def _(i):
        at = rows_of(i)
        for s in range(2):
            value = dot(full1[at, :], w2[:, s * C : s * C + 3 * BLOCK])
            qkv[at, s * 3 * BLOCK : (s + 1) * 3 * BLOCK] = value.astype(narrow)

    def between(done):
        if done == 1:
            gathers[4].spread()
            gathers[5].pass_on(1)
            gathers[5].spread(3)
            swaps[2].start()
        if done == 3:
            gathers[5].pass_on(2)
        if done == 4:
            gathers[5].pass_on(3)

    attend(qkv, k_ref, kt_ref, log_ref, att, between)
    store, wait, load = core.combine(part, send, recv)

    @pl.loop(0, PIX // CHUNK)
    def _(i):
        at = rows_of(i)
        value = dot_t(att[at, 0:BLOCK], w2[:, 3 * BLOCK : C])
        store(i, value + dot_t(att[at, BLOCK:], w2[:, C + 3 * BLOCK :]))

    wait()
    advance(x1, load, x2)
    wait_entry = entry(x2, 3, True, full2)
    gathers[3].ready()
    wait_entry()
    first_half(full2, w3, 4, 1, inner2, hidden2)
    gathers[4].ready()
    wait, load = second_half(w4)
    wait()
    advance(x2, load, x3)
    wait_entry = entry(x3, 5, True, full3)
    for n in range(5):
        gathers[n].drain()
    wait_entry()
    shift_full(full3, shifted, C)
    transpose_into(load_rows(full3), turned)
    gathers[5].ready()
    gathers[5].drain()
    for copy in swaps:
        copy.wait_send()
    swaps[2].wait_recv()
    noise_ref[:, pl.ds(pl.multiple_of((1 - x) * BLOCK, BLOCK), BLOCK)] = noise_recv[...].astype(single)

    def store(i, value):
        error = value - noise_ref[rows_of(i), :]
        weight = jnp.where(x == 0, weight_ref[0], weight_ref[1])
        loss_lanes[0:1, :] += jnp.sum(weight * error * error, 0, keepdims=True)
        pg[rows_of(i), :] = (2.0 * weight * error / total).astype(narrow)

    conv_wide(shifted, w5, store)
    loss_lanes[...] = jnp.broadcast_to(whole(loss_lanes[0:1, :]) / total, loss_lanes.shape)

    def start(n):
        for name, reduce in reduces.items():
            if int(name[0]) == n:
                reduce.start()

    def wide(w, n):
        store, wait, load = core.combine(part, send, recv)
        conv_tall(shifted, w, -1, store)
        if n != 0:
            kernel_grad(turned, shifted, -1, keep_taps(grads[n]))
            start(n)
        return wait, load

    def through_norm(x, wait, load, n, act, first, full):
        gain, bias = norm_row(n)
        share, shared = core.share(full) if full is not None else (None, None)

        def store(i, value):
            if share is None:
                return
            if not first:
                value = value + up[rows_of(i), :]
            up[rows_of(i), :] = value
            share(i, value.astype(narrow))

        summed, along = norm_backward(x, load, gain, bias, act, tmp, store, wait)
        sums_ref[n, 0:1, :] = along
        sums_ref[n, 1:2, :] = summed
        return shared

    def out_grad(full, hidden, n):
        transpose_into(load_rows(full), turned)
        shift_full(hidden, shifted, HALF)
        kernel_grad(turned, shifted, 1, keep_taps(grads[n]))

    def back_half(full, w, n, layer, inner, between=None):
        shift_full(full, shifted, C)

        def put(i, value):
            dh[rows_of(i), :] = value

        conv_back(shifted, w, put)
        if between is not None:
            between()
        gain, bias, scale, gain_all, bias_all = middle(n, layer)

        def store(i, value):
            pg[rows_of(i), :] = value.astype(narrow)

        summed, along = norm_backward(inner, load_rows(dh), gain_all, bias_all, True, tmp, store)
        sums_ref[n, 0:1, :] = scale * along
        sums_ref[n, 1:2, :] = scale * summed
        dmod_ref[0, layer : layer + 1, :] = gain * along + bias * summed
        dmod_ref[1, layer : layer + 1, :] = summed

    shift_full(pg, shifted, HALF)
    wait, load = wide(w5, 5)
    shared = through_norm(x3, wait, load, 5, True, True, full3)
    shared()
    out_grad(full3, hidden2, 4)
    start(4)
    back_half(full3, w4, 4, 1, inner2)
    transpose_into(load_rows(full2), turned)
    shift_full(pg, shifted, HALF)
    wait, load = wide(w3, 3)
    shared = through_norm(x2, wait, load, 3, True, False, full2)
    reduces["5"].pass_on()
    reduces["4"].turn()
    shared()
    for s in range(2):
        lanes = slice(s * BLOCK, (s + 1) * BLOCK)

        @pl.loop(0, PIX // CHUNK)
        def _(i):
            at = rows_of(i)
            value = dot(full2[at, :], w2[:, s * C + 3 * BLOCK : (s + 1) * C])
            pg[at, lanes] = value.astype(narrow)

    transpose_into(load_rows(full2), turned)
    for s in range(2):
        lanes = slice(s * BLOCK, (s + 1) * BLOCK)
        w2[:, s * C + 3 * BLOCK : (s + 1) * C] = dot(turned[...], att[:, lanes]).astype(narrow)

    def between(done):
        if done == 2:
            reduces["3"].turn()
        if done == 3:
            reduces["4"].spread()
        if done == 4:
            reduces["5"].turn()
            reduces["3"].spread()

    dqkv = [shifted.at[s, 0:PIX, 0 : 3 * BLOCK] for s in range(2)]
    attend_back(qkv, log_ref, pg, k_ref, kt_ref, dk_ref, dv_ref, dqkv, between)
    transpose_into(load_rows(full1), turned)
    store, wait, load = core.combine(part, send, recv)

    @pl.loop(0, PIX // CHUNK)
    def _(i):
        at = rows_of(i)
        value = dot_t(dqkv[0].at[at, :][...], w2[:, 0 : 3 * BLOCK])
        store(i, value + dot_t(dqkv[1].at[at, :][...], w2[:, C : C + 3 * BLOCK]))

    for s in range(2):
        w2[:, s * C : s * C + 3 * BLOCK] = dot(turned[...], dqkv[s][...]).astype(narrow)
    start(2)
    shared = through_norm(x1, wait, load, 2, False, False, full1)
    reduces["4"].pass_on()
    reduces["5"].spread()
    shared()

    def between():
        reduces["3"].pass_on()
        reduces["2"].turn()

    back_half(full1, w1, 1, 0, inner0, between)
    next(embed_end)
    out_grad(full1, hidden0, 1)
    reduces["2"].spread()
    next(embed_end)
    reduces["1a"].start()
    transpose_into(load_rows(full0), turned)
    shift_full(pg, shifted, HALF)
    kernel_grad(turned, shifted, -1, keep_taps(grads[0]))
    next(embed_end)
    reduces["1b"].start()
    reduces["0a"].start()
    wait, load = wide(w0, 0)
    reduces["1a"].turn()
    reduces["0b"].start()
    next(embed_end)
    reduces["2"].pass_on()
    reduces["4"].finish()
    through_norm(First(), wait, load, 0, True, False, None)
    reduces["1b"].pass_on()
    reduces["3"].finish()
    reduces["5"].finish()
    reduces["0a"].turn()
    reduces["1a"].spread()
    reduces["2"].finish()
    reduces["1b"].turn()
    reduces["0b"].turn()
    reduces["0a"].spread()
    reduces["1a"].pass_on()
    reduces["1b"].spread()
    next(step)
    reduces["0b"].spread()
    reduces["0a"].pass_on()
    reduces["1a"].finish()
    next(step)
    reduces["0b"].pass_on()
    reduces["1b"].finish()
    reduces["0a"].finish()
    reduces["0b"].finish()
    next(step)
    for reduce in reduces.values():
        reduce.drain()


EXACT = lax.Precision.HIGHEST
IMAGES_HERE = 16


def exact_dot(a, b):
    return jnp.dot(a, b, precision=EXACT, preferred_element_type=single)


def chosen(shape, rule):
    row = lax.broadcasted_iota(jnp.int32, shape, 0)
    column = lax.broadcasted_iota(jnp.int32, shape, 1)
    return jnp.where(rule(row, column), 1.0, 0.0).astype(single)


def odd_even(kind):
    return chosen((HALF, BLOCK), lambda r, c: r == 2 * c + kind)


def even_odd(kind):
    return chosen((BLOCK, HALF), lambda r, c: c == 2 * r + kind)


def contract_rows(a, b):
    return lax.dot_general(a, b, (((0,), (0,)), ((), ())), preferred_element_type=single)


def silu_grad(value):
    gate = sigmoid(value)
    return gate * (1.0 + value * (1.0 - gate))


class Small:
    def __init__(self, send, recv):
        self.send, self.recv, self.used = send, recv, 0
        z, y, x = place()
        core = lax.axis_index("lo")
        self.dp_here, self.chan_here, self.plane_here = 2 * z + y, 2 * x + core, 4 * z + 2 * y + x

    def go(self, count, here, source, target, where):
        copies = []
        for k in range(1, count):
            other = lax.rem(here + k, count)
            sems = self.send.at[self.used], self.recv.at[self.used]
            self.used += 1
            copy = remote(source(other), target.at[here], *sems, **where(other))
            copy.start()
            copies.append(copy)

        def wait():
            for copy in copies:
                copy.wait()

        return wait

    def dp(self, target, source=None):
        source = source or (lambda other: target.at[self.dp_here])
        where = lambda other: {"dz": lax.div(other, 2), "dy": lax.rem(other, 2)}
        return self.go(8, self.dp_here, source, target, where)

    def chan(self, target):
        source = lambda other: target.at[self.chan_here]
        where = lambda other: {"hi": lax.div(other, 2), "lo": lax.rem(other, 2)}
        return self.go(4, self.chan_here, source, target, where)

    def plane(self, target, source):
        where = lambda other: {
            "dz": lax.div(other, 4), "dy": lax.rem(lax.div(other, 2), 2), "hi": lax.rem(other, 2)
        }
        return self.go(16, self.plane_here, source, target, where)


def all_partners():
    z, y, x = place()
    core = lax.axis_index("lo")
    here = 4 * z + 2 * y + x
    others = []
    for k in range(1, 16):
        o = lax.rem(here + k, 16)
        others.append({"dz": lax.div(o, 4), "dy": lax.rem(lax.div(o, 2), 2), "hi": lax.rem(o, 2)})
    return others + [{"lo": 1 - core}, {"hi": 1 - x, "lo": 1 - core}]


def total_of(ref):
    total = ref[0]
    for k in range(1, ref.shape[0]):
        total = total + ref[k]
    return total


def onehot_of(labels, count, first):
    numbers = lax.broadcasted_iota(jnp.int32, (IMAGES_HERE, count), 1) + first
    return jnp.where(labels[:, 0:1] == numbers.astype(single), 1.0, 0.0).astype(narrow)


def sinusoid_rows(times, labels):
    row = lax.broadcasted_iota(jnp.int32, (8, TF), 0)
    lane = lax.broadcasted_iota(jnp.int32, (8, TF), 1)
    half = TF // 2
    frequency = jnp.exp(-math.log(10000.0) * lax.rem(lane, half).astype(single) / half)
    angles = jnp.where(row == 0, times[0], times[1]).astype(single) * frequency
    sin = jnp.where(lane < half, jnp.cos(angles), jnp.sin(angles)).astype(narrow).astype(single)
    label = jnp.where(row == 2, labels[0], labels[1]).astype(single)
    return jnp.where(row < 2, sin, jnp.where(row < 4, label, 0.0))


def embed_steps(small, times, labels, time_in, emb_out, emb_proj, msg, p0, p1, p2, p3, m3, mod_ref, keep):
    sin_ref, label_ref, pre_ref, embedding_ref = keep
    here, chan = small.dp_here, small.chan_here
    rows = time_in.shape[0]
    msg[...] = jnp.zeros_like(msg)
    sent = sinusoid_rows(times, labels)
    for other in range(8):
        msg[other, :, 0:rows] = sent[:, other * rows : (other + 1) * rows]
    p0[here] = msg[here]
    wait = small.dp(p0, lambda other: msg.at[other])
    yield
    wait()
    flat = p0[...].reshape(64, BLOCK)
    sin = exact_dot(chosen((16, 64), lambda r, c: c == 8 * (r // 2) + r % 2), flat)
    label = exact_dot(chosen((16, 64), lambda r, c: c == 8 * (r // 2) + r % 2 + 2), flat)
    sin_ref[...], label_ref[...] = sin, label
    p1[here] = dot(sin[:, 0:rows].astype(narrow), time_in[...].astype(narrow))
    wait = small.dp(p1)
    yield
    wait()
    pre = total_of(p1)
    pre_ref[...] = pre
    hidden = (pre * sigmoid(pre)).astype(narrow)
    width = hidden.shape[1]
    count = emb_out.shape[1] - width
    onehot = onehot_of(label, count, chan * count)
    part = dot_t(hidden, emb_out[:, 0:width].astype(narrow))
    p2[chan] = part + dot_t(onehot, emb_out[:, width:].astype(narrow))
    wait = small.chan(p2)
    yield
    wait()
    embedding = total_of(p2)
    embedding_ref[...] = embedding
    context = (embedding * sigmoid(embedding)).astype(narrow)
    parts = jnp.concatenate([dot(context, emb_proj[n].astype(narrow)) for n in range(2)], 0)
    spread_rows = chosen((128, 32), lambda r, c: (c == 16 * (r % 8) + r // 8) & (r % 8 < 2))
    m3[...] = exact_dot(spread_rows, parts).reshape(16, 8, HALF)
    p3[small.plane_here] = m3[small.plane_here]
    wait = small.plane(p3, lambda other: m3.at[other])
    yield
    wait()
    flat = p3[...].reshape(128, HALF)
    for half in range(2):
        pick = chosen((8, 128), lambda r, c: (c % 8 == r) & ((c // 8) % 2 == half) & (r < 2))
        wide = exact_dot(pick, flat)
        for kind in range(2):
            value = exact_dot(wide, odd_even(kind))
            for n in range(2):
                mod_ref[n, kind : kind + 1, half * BLOCK : (half + 1) * BLOCK] = value[n : n + 1]
    yield


def embed_back_steps(small, dmod, q4, p4, p5, p6, emb_out, emb_proj, keep, proj_grad, out_grad, time_grad):
    sin_ref, label_ref, pre_ref, embedding_ref = keep
    here, chan, plane = small.dp_here, small.chan_here, small.plane_here
    for half in range(2):
        lanes = slice(half * BLOCK, (half + 1) * BLOCK)
        wide = exact_dot(dmod[0][:, lanes], even_odd(0)) + exact_dot(dmod[1][:, lanes], even_odd(1))
        q4[half] = wide.astype(narrow).astype(single)
    p4[plane] = q4[lax.rem(plane, 2)]
    wait = small.plane(p4, lambda other: q4.at[lax.rem(other, 2)])
    yield
    wait()
    flat = p4[...].reshape(128, HALF)
    embedding, pre = embedding_ref[...], pre_ref[...]
    context = (embedding * sigmoid(embedding)).astype(narrow)
    part = None
    for n in range(2):
        grads = exact_dot(chosen((16, 128), lambda r, c: c == 8 * r + n), flat).astype(narrow)
        proj_grad[n] = contract_rows(context, grads)
        more = dot_t(grads, emb_proj[n].astype(narrow))
        part = more if part is None else part + more
    p5[chan] = part
    wait = small.chan(p5)
    yield
    wait()
    low = (total_of(p5) * silu_grad(embedding)).astype(narrow)
    hidden = (pre * sigmoid(pre)).astype(narrow)
    width = hidden.shape[1]
    count = emb_out.shape[1] - width
    p6[here] = dot(low, emb_out[:, 0:width].astype(narrow))
    wait = small.dp(p6)
    out_grad[:, 0:width] = contract_rows(low, hidden)
    out_grad[:, width:] = contract_rows(low, onehot_of(label_ref[...], count, chan * count))
    yield
    wait()
    pre_grad = (total_of(p6) * silu_grad(pre)).astype(narrow)
    time_grad[...] = contract_rows(sin_ref[...].astype(narrow), pre_grad)[0 : time_grad.shape[0]]
    yield


def to_row(column):
    pieces = []
    for start in range(0, column.shape[0], BLOCK):
        part = column[start : start + BLOCK]
        n = part.shape[0]
        pieces.append(jnp.sum(chosen((n, n), lambda r, c: r == c) * part, 0, keepdims=True))
    return jnp.concatenate(pieces, 1)


def to_column(row):
    pieces = []
    for start in range(0, row.shape[1], BLOCK):
        part = row[:, start : start + BLOCK]
        n = part.shape[1]
        square = chosen((n, n), lambda r, c: r == c) * part
        pieces.append(jnp.sum(square, 1, keepdims=True))
    return jnp.concatenate(pieces, 0)


def joined_rows(ref):
    return jnp.concatenate([ref[n, k : k + 1, :] for n in range(6) for k in range(2)], 0)


def scalar_rows(values, count, lanes=BLOCK):
    rows = [jnp.broadcast_to(value, (1, lanes)) for value in values]
    return jnp.concatenate(rows + [jnp.zeros((count - len(rows), lanes), single)], 0)


def whole(value):
    return jnp.sum(jnp.sum(value, 1, keepdims=True), 0, keepdims=True)


DECAY = 1.0 - STEP ** (-0.8)
ROW_LANES = 640
COL_LANES = 512


def adafactor_steps(
    small, early, late, grads, rows_old, cols_old, fulls, wsq_ref, loss_ref, sums, norms_own, second,
    p7, q7, p8, p9, p10, p11, p12, p13, rows_ref, cols_ref, scal_ref, norm_out, second_out, norms_out,
):
    here, chan, plane = small.dp_here, small.chan_here, small.plane_here
    x = lax.axis_index("hi")
    count = len(grads)
    for half in range(2):
        lanes = slice(half * BLOCK, (half + 1) * BLOCK)
        rows = [sums[n, k : k + 1, lanes] for n in range(6) for k in range(2)]
        q7[half] = jnp.concatenate(rows + [jnp.zeros((4, BLOCK), single)], 0)
    p7[plane] = q7[x]
    wait_norms = small.plane(p7, lambda other: q7.at[lax.rem(other, 2)])
    update_sq, row_sum = {}, {}

    def measure(some, row_buf, col_buf):
        row_buf[chan] = jnp.zeros(row_buf.shape[1:], single)
        col_buf[here] = jnp.zeros(col_buf.shape[1:], single)
        for k, m in enumerate(some):
            value = grads[m][...]
            squared = value * value + tiny_square
            n_rows, n_cols = value.shape
            row_buf[chan, k : k + 1, 0:n_rows] = to_row(jnp.sum(squared, 1, keepdims=True))
            col_buf[here, k : k + 1, 0:n_cols] = jnp.sum(squared, 0, keepdims=True)
        return small.chan(row_buf), small.dp(col_buf)

    def moments(some, row_buf, col_buf, waits):
        for wait in waits:
            wait()
        row_total, col_total = total_of(row_buf), total_of(col_buf)
        for k, m in enumerate(some):
            n_rows, n_cols = grads[m].shape
            row = DECAY * rows_old[m] + (1.0 - DECAY) * row_total[k : k + 1, 0:n_rows] / fulls[m][1]
            col = DECAY * cols_old[m] + (1.0 - DECAY) * col_total[k : k + 1, 0:n_cols] / fulls[m][0]
            rows_ref[m : m + 1, 0:n_rows] = row
            cols_ref[m : m + 1, 0:n_cols] = col
            row_sum[m] = jnp.sum(row, 1, keepdims=True)
            update = grads[m][...] * to_column(lax.rsqrt(row)) * lax.rsqrt(col)
            update_sq[m] = whole(update * update)

    waits = measure(early, p8, p9)
    yield
    moments(early, p8, p9, waits)
    wait_norms()
    norm_total = total_of(p7)[0:12]
    own = joined_rows(norms_own)
    norm_out[...] = norm_total
    second_new = DECAY * joined_rows(second) + (1.0 - DECAY) * (norm_total * norm_total + tiny_square)
    second_out[...] = second_new
    norm_update = norm_total * lax.rsqrt(second_new)
    sq = [jnp.sum(norm_update * norm_update, 1, keepdims=True), jnp.sum(own * own, 1, keepdims=True)]
    wide = jnp.where(lax.broadcasted_iota(jnp.int32, (12, BLOCK), 1) < 64, sq[0], sq[1])
    yield
    moments(late, p10, p11, measure(late, p10, p11))
    lane = lax.broadcasted_iota(jnp.int32, (16, BLOCK), 1)
    sums_here = scalar_rows([update_sq[m] for m in range(count)], 16)
    row = lax.broadcasted_iota(jnp.int32, (16, BLOCK), 0)
    weights = jnp.where(row == count, loss_ref[0:1, 0:1], wsq_ref[:, 0:1])
    p12[chan, 0:16] = jnp.where(lane < 32, sums_here, weights)
    p12[chan, 16:32] = jnp.concatenate([wide, jnp.zeros((4, BLOCK), single)], 0)
    small.chan(p12)()
    over_chan = total_of(p12)
    p13[here] = jnp.where(lane < 64, over_chan[0:16], scalar_rows([row_sum[m] for m in range(count)], 16))
    wait = small.dp(p13)
    norm_sq = over_chan[16:28]
    norm_clip = jnp.maximum(1.0, jnp.sqrt(norm_sq[:, 0:1] / float(C)))
    norm_scale = jnp.maximum(floor_scale, jnp.sqrt(norm_sq[:, 64:65] / float(C)))
    norms_out[...] = own - (step_rate * norm_scale / norm_clip) * norm_update
    wait()
    over_all = total_of(p13)
    means, steps = [], []
    for m in range(count):
        entries = fulls[m][0] * fulls[m][1]
        mean = over_all[m : m + 1, 64:65] / fulls[m][0]
        clip = jnp.maximum(1.0, jnp.sqrt(mean * over_all[m : m + 1, 0:1] / entries))
        scale = jnp.maximum(floor_scale, jnp.sqrt(over_all[m : m + 1, 32:33] / entries))
        means.append(mean)
        steps.append(step_rate * scale / clip)
    scal_ref[0:16] = scalar_rows(means, 16)
    scal_ref[16:32] = scalar_rows(steps, 16)
    scal_ref[32:40] = jnp.broadcast_to(over_all[count : count + 1, 32:33], (8, BLOCK))
    yield


def finish_kernel(*refs):
    (g0, g1, g2, g3, g4, g5, proj, time, emb, rows, cols, scal, norm, second, norms_new,
     conv_in, conv_out, emb_proj, attn, time_in, emb_out,
     loss, in_g, in_r, in_c, in_w, out_g, out_r, out_c, out_w, proj_g, proj_r, proj_c, proj_w,
     attn_g, attn_r, attn_c, attn_w, time_g, time_r, time_c, time_w, emb_g, emb_r, emb_c, emb_w,
     norm_o, second_o, norms_o) = refs
    loss[...] = scal[32:33, 0:1]
    plan = [
        (0, g0, conv_in.at[0], in_g.at[0], in_r.at[0:1], in_c.at[0:1], in_w.at[0]),
        (1, g3, conv_in.at[1], in_g.at[1], in_r.at[1:2], in_c.at[1:2], in_w.at[1]),
        (2, g5, conv_in.at[2], in_g.at[2], in_r.at[2:3], in_c.at[2:3], in_w.at[2]),
        (3, g1, conv_out.at[0], out_g.at[0], out_r.at[0:1], out_c.at[0:1], out_w.at[0]),
        (4, g4, conv_out.at[1], out_g.at[1], out_r.at[1:2], out_c.at[1:2], out_w.at[1]),
        (5, proj.at[0], emb_proj.at[0], proj_g.at[0], proj_r.at[0:1], proj_c.at[0:1], proj_w.at[0]),
        (6, proj.at[1], emb_proj.at[1], proj_g.at[1], proj_r.at[1:2], proj_c.at[1:2], proj_w.at[1]),
        (7, g2, attn, attn_g, attn_r, attn_c, attn_w),
        (8, time, time_in, time_g, time_r, time_c, time_w),
        (9, emb, emb_out, emb_g, emb_r, emb_c, emb_w),
    ]
    for m, grad, weight, grad_o, rows_o, cols_o, weight_o in plan:
        n_rows, n_cols = grad_o.shape
        row, col = rows[m : m + 1, 0:n_rows], cols[m : m + 1, 0:n_cols]
        rows_o[...] = row
        cols_o[...] = col
        value = grad[...]
        grad_o[...] = value
        mean, step = scal[m : m + 1, 0:1], scal[16 + m : 17 + m, 0:1]
        update = value * to_column(lax.rsqrt(row / mean)) * lax.rsqrt(col)
        weight_o[...] = weight[...] - step * update
    for n in range(6):
        at = slice(2 * n, 2 * n + 2)
        norm_o[n], second_o[n], norms_o[n] = norm[at, :], second[at, :], norms_new[at, :]


def vmem(shape, dtype=single):
    return pltpu.VMEM(shape, dtype)


def semaphores(*shape):
    return pltpu.SemaphoreType.DMA(shape)


TAPS_SHAPE = (9 * C, HALF)
ATTN_SHAPE = (C, 2 * C)
FULL = (PIX, C)
OWN = (PIX, HALF)
QKV = (PIX, 6 * BLOCK)
LOGS = (4, PIX // CHUNK, 1, CHUNK)
WEIGHTS = [TAPS_SHAPE, TAPS_SHAPE, ATTN_SHAPE, TAPS_SHAPE, TAPS_SHAPE, TAPS_SHAPE]


def fused(body, outs, out_specs, in_specs, scratch, args, number, limit, name):
    return pl.pallas_call(
        body,
        out_shape=outs,
        in_specs=in_specs,
        out_specs=out_specs,
        scratch_shapes=scratch,
        compiler_params=pltpu.CompilerParams(
            vmem_limit_bytes=limit * 2**20, collective_id=number, has_side_effects=True
        ),
        name=name,
    )(*args)


def fused_step(
    noisy, noise, timesteps, classes, sample_weight,
    conv_in, conv_out, emb_proj, attn_weight, time_in, emb_out, norms, moments, norm_second,
):
    images = noisy.shape[0] * lax.axis_size("dz") * lax.axis_size("dy")
    total = float(images * PIX * C)
    weights = [conv_in[0], conv_in[1], conv_in[2], conv_out[0], conv_out[1]]
    weights += [emb_proj[0], emb_proj[1], attn_weight, time_in, emb_out]
    dp, chan = lax.axis_size("dz") * lax.axis_size("dy"), lax.axis_size("hi") * lax.axis_size("lo")
    fulls = [(float(w.shape[0] * dp), float(w.shape[1] * chan)) for w in weights]
    shard, attn_shard = conv_in.shape[1:], attn_weight.shape
    shard_shapes = [shard, shard, attn_shard, shard, shard, shard]
    shapes = shard_shapes + [emb_proj.shape, time_in.shape, emb_out.shape]
    shapes += [(16, ROW_LANES), (16, COL_LANES), (40, BLOCK)] + [(12, BLOCK)] * 3
    outs = [struct(s) for s in shapes]

    low = WEIGHTS + [TAPS_SHAPE] + [FULL] * 4
    for name, layer, _, count in reduce_plan([struct(s) for s in shard_shapes]):
        rows, lanes = shard_shapes[layer]
        if name in EARLY:
            half = count // 2
            low += [(2, 4, count, 2 * lanes), (half, 2 * lanes), (2, half, lanes), (half, lanes), (half, lanes)]
        else:
            low += [(4, count, lanes), (2, count, 2 * lanes), (2, count, lanes), (2, count, lanes), (4, count, lanes)]
    scratch = [vmem(s, narrow) for s in low] + [vmem(OWN)] * 10
    scratch += [vmem(OWN, narrow)] * 7 + [vmem(QKV, narrow), vmem((3, ROWS, C), narrow), vmem((C, PIX), narrow)]
    scratch += [vmem((PIX, BLOCK), narrow), vmem((BLOCK, PIX), narrow), vmem((PIX, BLOCK)), vmem((PIX, BLOCK))]
    small = [LOGS, (12, HALF), (2, 2, HALF), (8, HALF), (12, BLOCK), (6, 2, HALF), (2, 8, HALF)]
    small += [(16, BLOCK), (16, BLOCK), (16, BLOCK), (16, HALF), (16, BLOCK)]
    scratch += [vmem(s) for s in small] + [vmem(s, narrow) for s in shard_shapes + [(PIX, BLOCK)] * 2]
    swaps = [(8, 8, BLOCK), (8, 8, BLOCK), (8, 16, HALF), (4, 16, BLOCK), (16, 8, HALF), (16, 8, HALF)]
    swaps += [(2, 8, HALF), (16, 8, HALF), (4, 16, BLOCK), (8, 16, HALF), (16, 16, BLOCK), (2, 16, BLOCK)]
    swaps += [(4, 8, ROW_LANES), (8, 8, COL_LANES), (4, 8, ROW_LANES), (8, 8, BLOCK), (4, 32, BLOCK), (8, 16, BLOCK)]
    scratch += [vmem(s) for s in swaps]
    scratch += [semaphores(LAYERS, 28)] * 2 + [semaphores(LAYERS)] + [semaphores(REDUCES, STEPS)] * 2
    scratch += [semaphores(96)] * 2 + [semaphores(3)] * 2 + [semaphores(128)] * 2 + [semaphores(3)]
    flat = [value.reshape(1, -1) if value.ndim == 1 else value for value in moments]
    pixels = (2, PIX, BLOCK)
    args = [noisy.reshape(pixels), noise.reshape(pixels), sample_weight, timesteps, classes, norms, norm_second]
    args += [conv_in, conv_out, attn_weight, time_in, emb_out, emb_proj, *flat]
    in_specs = [ANY] * 2 + [SMEM] * 3 + [VMEM] * (len(args) - 5)
    body = functools.partial(step_kernel, fulls, total)
    results = fused(body, outs, [VMEM] * len(outs), in_specs, scratch, args, 1, 63, "step")

    def four(weight, row, col):
        return [struct(weight.shape), struct(row.shape), struct(col.shape), struct(weight.shape)]

    outs = [struct((1, 1))]
    for n, weight in enumerate((conv_in, conv_out, emb_proj, attn_weight, time_in, emb_out)):
        outs += four(weight, flat[2 * n], flat[2 * n + 1])
    outs += [struct(norms.shape)] * 3
    args = [*results, conv_in, conv_out, emb_proj, attn_weight, time_in, emb_out]
    finals = list(call(finish_kernel, outs, [], args, "finish"))
    finals[0] = finals[0].reshape(())
    for n, value in enumerate(moments):
        place_at = 2 + 4 * (n // 2) + n % 2
        finals[place_at] = finals[place_at].reshape(value.shape)
    return tuple(finals)


def pack_flat(members):
    return jnp.concatenate([member.reshape(-1) for member in members])


def unpack_flat(vector, shape_list):
    pieces = []
    offset = 0
    for array_shape in shape_list:
        extent = math.prod(array_shape)
        pieces.append(vector[offset : offset + extent].reshape(array_shape))
        offset += extent
    return pieces


def per_device(
    noisy,
    noise,
    timesteps,
    classes,
    sample_weight,
    conv_in,
    conv_out,
    emb_proj,
    attn_weight,
    time_in,
    emb_out,
    norms,
    conv_in_rows,
    conv_in_cols,
    conv_out_rows,
    conv_out_cols,
    emb_proj_rows,
    emb_proj_cols,
    attn_rows,
    attn_cols,
    time_rows,
    time_cols,
    embout_rows,
    embout_cols,
    norm_second,
):
    rows_here = (conv_in.shape[1], attn_weight.shape[0])
    if lax.axis_size("dz") == 4 and all(rows % 64 == 0 for rows in rows_here):
        moments = [conv_in_rows, conv_in_cols, conv_out_rows, conv_out_cols, emb_proj_rows, emb_proj_cols]
        moments += [attn_rows, attn_cols, time_rows, time_cols, embout_rows, embout_cols]
        return fused_step(
            noisy, noise, timesteps, classes, sample_weight, conv_in, conv_out, emb_proj, attn_weight, time_in,
            emb_out, norms, moments, norm_second,
        )
    masters = [conv_in, conv_out, emb_proj, attn_weight[None], time_in[None], emb_out[None]]
    lowered = [master.astype(narrow) for master in masters]
    modulate, saved = embed_forward(timesteps, classes, lowered[4][0], lowered[5][0], lowered[2])
    norms_wide = join_image(norms, 2)
    shards = [lowered[0][0], lowered[1][0], lowered[3][0], lowered[0][1], lowered[1][1], lowered[0][2]]
    full = [gather_weight(shard) for shard in shards]
    loss_part, din, dout, dattn, sums, dmod = network(
        noisy, noise, sample_weight, (full[0], full[3], full[5]), (full[1], full[4]), full[2], norms_wide, modulate
    )
    reduced_parts = [scatter_grad(part) for part in (din[0], dout[0], dattn, din[1], dout[1], din[2])]
    in0_grad, out0_grad, attn_grad, in1_grad, out1_grad, head_grad = reduced_parts
    proj_grad, time_grad, embout_grad = embed_backward(saved, dmod, lowered[2], lowered[5][0])
    norm_local = lax.psum_scatter(sums, "hi", scatter_dimension=2, tiled=True)
    reduced = [
        jnp.stack([in0_grad, in1_grad, head_grad]),
        jnp.stack([out0_grad, out1_grad]),
        proj_grad,
        attn_grad[None],
        time_grad[None],
        embout_grad[None],
    ]
    decay_rate = 1.0 - STEP ** (-0.8)
    dp_count = lax.axis_size("dz") * lax.axis_size("dy")
    chan_count = lax.axis_size("hi") * lax.axis_size("lo")
    rows_old = [
        conv_in_rows,
        conv_out_rows,
        emb_proj_rows,
        attn_rows[None],
        time_rows[None],
        embout_rows[None],
    ]
    cols_old = [
        conv_in_cols,
        conv_out_cols,
        emb_proj_cols,
        attn_cols[None],
        time_cols[None],
        embout_cols[None],
    ]
    squares = [gradient * gradient + tiny_square for gradient in reduced]
    full_rows = [squared.shape[1] * dp_count for squared in squares]
    full_cols = [squared.shape[2] * chan_count for squared in squares]
    row_parts = [jnp.sum(squared, 2) for squared in squares]
    col_parts = [jnp.sum(squared, 1) for squared in squares]
    row_shapes = [member.shape for member in row_parts]
    col_shapes = [member.shape for member in col_parts]
    norm_width = norm_local.shape[2]
    row_totals = unpack_flat(lax.psum(pack_flat(row_parts), ("hi", "lo")), row_shapes)
    rows_new = [
        decay_rate * rows_old[position]
        + (1.0 - decay_rate) * row_totals[position] / full_cols[position]
        for position in range(6)
    ]
    row_sums_local = [jnp.sum(member, 1) for member in rows_new]
    col_vector, norm_total = lax.psum((pack_flat(col_parts + row_sums_local), norm_local), DP)
    col_pieces = unpack_flat(col_vector, col_shapes + [(member.shape[0],) for member in rows_new])
    col_totals = col_pieces[:6]
    row_means = [col_pieces[6 + position] / full_rows[position] for position in range(6)]
    cols_new = [
        decay_rate * cols_old[position]
        + (1.0 - decay_rate) * col_totals[position] / full_rows[position]
        for position in range(6)
    ]
    updates = [
        reduced[position]
        * lax.rsqrt(rows_new[position] / row_means[position][:, None])[:, :, None]
        * lax.rsqrt(cols_new[position])[:, None, :]
        for position in range(6)
    ]
    second_new = decay_rate * norm_second + (1.0 - decay_rate) * (
        norm_total * norm_total + tiny_square
    )
    norm_update = norm_total * lax.rsqrt(second_new)
    update_squares = pack_flat([jnp.sum(member * member, (1, 2)) for member in updates])
    weight_squares = pack_flat([jnp.sum(master * master, (1, 2)) for master in masters])
    norm_update_sq = jnp.sum(norm_update * norm_update, 2) / dp_count
    norm_weight_sq = jnp.sum(norms * norms, 2) / dp_count
    update_total, weight_total, norm_update_total, norm_weight_total, loss = lax.psum(
        (update_squares, weight_squares, norm_update_sq, norm_weight_sq, loss_part), ("dz", "dy", "hi", "lo")
    )
    layer_shapes = [(member.shape[0],) for member in masters]
    update_sums = unpack_flat(update_total, layer_shapes)
    weight_sums = unpack_flat(weight_total, layer_shapes)
    results = [loss]
    for position in range(6):
        entries = float(full_rows[position] * full_cols[position])
        clip_factor = jnp.maximum(1.0, jnp.sqrt(update_sums[position] / entries))
        scale_factor = jnp.maximum(floor_scale, jnp.sqrt(weight_sums[position] / entries))
        weight_new = (
            masters[position]
            - (step_rate * scale_factor / clip_factor)[:, None, None] * updates[position]
        )
        if position >= 3:
            results += [
                reduced[position][0],
                rows_new[position][0],
                cols_new[position][0],
                weight_new[0],
            ]
        else:
            results += [reduced[position], rows_new[position], cols_new[position], weight_new]
    norm_entries = float(norm_width * chan_count)
    norm_clip = jnp.maximum(1.0, jnp.sqrt(norm_update_total / norm_entries))
    norm_scale = jnp.maximum(floor_scale, jnp.sqrt(norm_weight_total / norm_entries))
    norms_new = norms - (step_rate * norm_scale / norm_clip)[:, :, None] * norm_update
    results += [norm_total, second_new, norms_new]
    return (
        results[0],
        results[1],
        results[2],
        results[3],
        results[4],
        results[5],
        results[6],
        results[7],
        results[8],
        results[9],
        results[10],
        results[11],
        results[12],
        results[13],
        results[14],
        results[15],
        results[16],
        results[17],
        results[18],
        results[19],
        results[20],
        results[21],
        results[22],
        results[23],
        results[24],
        results[25],
        results[26],
        results[27],
    )


CHAN = ("hi", "lo")


def solution(mesh):
    dp, chan = mesh.shape["dp"], mesh.shape["chan"]
    mesh = Mesh(mesh.devices.reshape(dp // 2, 2, 2, chan // 2), DP + CHAN)
    in_specs = (
        P(DP, None, None, CHAN),
        P(DP, None, None, CHAN),
        P(DP),
        P(DP),
        P(DP),
        P(None, DP, CHAN),
        P(None, DP, CHAN),
        P(None, DP, CHAN),
        P(DP, CHAN),
        P(DP, CHAN),
        P(DP, CHAN),
        P(None, None, CHAN),
        P(None, DP),
        P(None, CHAN),
        P(None, DP),
        P(None, CHAN),
        P(None, DP),
        P(None, CHAN),
        P(DP),
        P(CHAN),
        P(DP),
        P(CHAN),
        P(DP),
        P(CHAN),
        P(None, None, CHAN),
    )
    out_specs = (
        P(),
        P(None, DP, CHAN),
        P(None, DP),
        P(None, CHAN),
        P(None, DP, CHAN),
        P(None, DP, CHAN),
        P(None, DP),
        P(None, CHAN),
        P(None, DP, CHAN),
        P(None, DP, CHAN),
        P(None, DP),
        P(None, CHAN),
        P(None, DP, CHAN),
        P(DP, CHAN),
        P(DP),
        P(CHAN),
        P(DP, CHAN),
        P(DP, CHAN),
        P(DP),
        P(CHAN),
        P(DP, CHAN),
        P(DP, CHAN),
        P(DP),
        P(CHAN),
        P(DP, CHAN),
        P(None, None, CHAN),
        P(None, None, CHAN),
        P(None, None, CHAN),
    )
    return jax.shard_map(
        per_device, mesh=mesh, in_specs=in_specs, out_specs=out_specs, check_vma=False
    )
```

```python
import functools
import math

import jax
import jax.numpy as jnp
from jax import lax
from jax.experimental import pallas as pl
from jax.experimental.pallas import tpu as pltpu
from jax.sharding import Mesh
from jax.sharding import PartitionSpec as P

C = 512
HEADS = 8
GROUPS = 32
TF = 256
STEP = 10
SIDE = 32
PIX = 1024
HALF = 256
BLOCK = 128
PAD = SIDE
ROWS = PIX + 2 * PAD
CHUNK = 256

single = jnp.float32
narrow = jnp.bfloat16
step_rate = 0.5
floor_scale = 0.001
tiny_square = 1e-30
norm_eps = 1e-05

TAPS = [(t // 3 - 1, t % 3 - 1) for t in range(9)]


def dot(a, b):
    return jnp.dot(a, b, preferred_element_type=single)


def dot_t(a, b):
    return lax.dot_general(a, b, (((1,), (1,)), ((), ())), preferred_element_type=single)


def group_sum(row):
    lane = lax.broadcasted_iota(jnp.int32, (HALF, HALF), 0)
    other = lax.broadcasted_iota(jnp.int32, (HALF, HALF), 1)
    size = C // GROUPS
    ones = jnp.where(lane // size == other // size, 1.0, 0.0).astype(single)
    tall = jnp.broadcast_to(row, (8, HALF))
    return jnp.dot(tall, ones, precision=lax.Precision.HIGHEST, preferred_element_type=single)[0:1]


def loop_sum(count, make):
    zeros = make(None)

    def body(i, carried):
        return [old + new for old, new in zip(carried, make(i))]

    return lax.fori_loop(0, count, body, [jnp.zeros((1, HALF), single)] * zeros, unroll=NORM_UNROLL)


def rows_of(i, size=CHUNK, offset=0):
    return pl.ds(pl.multiple_of(offset + i * size, 32), size)


def stats(x_ref):
    members = float(PIX * (C // GROUPS))

    def first(i):
        if i is None:
            return 1
        return [jnp.sum(x_ref[rows_of(i), :], 0, keepdims=True)]

    (total,) = loop_sum(PIX // CHUNK, first)
    mean = group_sum(total) / members

    def second(i):
        if i is None:
            return 1
        center = x_ref[rows_of(i), :] - mean
        return [jnp.sum(center * center, 0, keepdims=True)]

    (square,) = loop_sum(PIX // CHUNK, second)
    rstd = lax.rsqrt(group_sum(square) / members + norm_eps)
    return mean, rstd


def sigmoid(v):
    return 1.0 / (1.0 + jnp.exp(-v))


def norm_forward(x_ref, gain, bias, act, store):
    mean, rstd = stats(x_ref)

    @pl.loop(0, PIX // CHUNK, unroll=NORM_UNROLL)
    def _(i):
        value = (x_ref[rows_of(i), :] - mean) * rstd * gain + bias
        if act:
            value = value * sigmoid(value)
        store(i, value.astype(narrow))


def norm_backward(x_ref, load_grad, gain, bias, act, tmp_ref, store, wait=None):
    mean, rstd = stats(x_ref)
    members = float(PIX * (C // GROUPS))
    if wait is not None:
        wait()

    def first(i):
        if i is None:
            return 2
        hat = (x_ref[rows_of(i), :] - mean) * rstd
        grad = load_grad(i)
        if act:
            mixed = hat * gain + bias
            gate = sigmoid(mixed)
            grad = grad * gate * (1.0 + mixed * (1.0 - gate))
        tmp_ref[rows_of(i), :] = grad
        return [jnp.sum(grad, 0, keepdims=True), jnp.sum(grad * hat, 0, keepdims=True)]

    total, along = loop_sum(PIX // CHUNK, first)
    mean_grad = group_sum(gain * total) / members
    mean_along = group_sum(gain * along) / members

    @pl.loop(0, PIX // CHUNK, unroll=NORM_UNROLL)
    def _(i):
        hat = (x_ref[rows_of(i), :] - mean) * rstd
        store(i, rstd * (tmp_ref[rows_of(i), :] * gain - mean_grad - hat * mean_along))

    return total, along


def shifts(load, s_ref, width):
    for b in range(3):
        s_ref[b, 0:PAD, 0:width] = jnp.zeros((PAD, width), narrow)
        s_ref[b, PAD + PIX : ROWS, 0:width] = jnp.zeros((PAD, width), narrow)
    size = 128

    @pl.loop(0, PIX // size)
    def _(i):
        value = load(i, size)
        wide = value.astype(single)
        across = lax.broadcasted_iota(jnp.int32, wide.shape, 0) % SIDE
        left = jnp.where(across > 0, pltpu.roll(wide, 1, 0), 0.0)
        right = jnp.where(across < SIDE - 1, pltpu.roll(wide, size - 1, 0), 0.0)
        at = rows_of(i, size, PAD)
        s_ref[0, at, 0:width] = left.astype(narrow)
        s_ref[1, at, 0:width] = value
        s_ref[2, at, 0:width] = right.astype(narrow)


def tap_rows(s_ref, t, sign, i, size, width):
    a, b = TAPS[t]
    return s_ref[sign * b + 1, rows_of(i, size, PAD + sign * a * SIDE), 0:width]


def split_core(value):
    core = lax.axis_index("lo")
    b0, b1, b2, b3 = [value[:, k * BLOCK : (k + 1) * BLOCK] for k in range(4)]
    even, odd = jnp.concatenate([b0, b2], 1), jnp.concatenate([b1, b3], 1)
    first = core == 0
    return jnp.where(first, even, odd), jnp.where(first, odd, even)


def join_core(own_ref, peer_ref, full_ref):
    core = lax.axis_index("lo")

    @pl.loop(0, PIX // CHUNK)
    def _(i):
        at = rows_of(i)
        own, peer = own_ref[at, :].astype(single), peer_ref[at, :].astype(single)
        even = jnp.where(core == 0, own, peer).astype(narrow)
        odd = jnp.where(core == 0, peer, own).astype(narrow)
        full_ref[at, 0:BLOCK] = even[:, 0:BLOCK]
        full_ref[at, BLOCK : 2 * BLOCK] = odd[:, 0:BLOCK]
        full_ref[at, 2 * BLOCK : 3 * BLOCK] = even[:, BLOCK:]
        full_ref[at, 3 * BLOCK :] = odd[:, BLOCK:]


def conv_wide(s_ref, w_ref, store):
    @pl.loop(0, PIX // CHUNK, unroll=CONV_UNROLL)
    def _(i):
        total = None
        for t in range(9):
            part = dot(tap_rows(s_ref, t, 1, i, CHUNK, C), w_ref[t * C : (t + 1) * C, :])
            total = part if total is None else total + part
        store(i, total)


def conv_tall(s_ref, w_ref, sign, store):
    @pl.loop(0, PIX // CHUNK, unroll=CONV_UNROLL)
    def _(i):
        total = None
        for t in range(9):
            part = dot_t(tap_rows(s_ref, t, sign, i, CHUNK, HALF), w_ref[t * C : (t + 1) * C, :])
            total = part if total is None else total + part
        store(i, total)


def conv_back(s_ref, w_ref, store):
    @pl.loop(0, PIX // CHUNK, unroll=CONV_UNROLL)
    def _(i):
        total = None
        for t in range(9):
            part = dot(tap_rows(s_ref, t, -1, i, CHUNK, C), w_ref[t * C : (t + 1) * C, :])
            total = part if total is None else total + part
        store(i, total)


def transpose_into(load, t_ref):
    for i in range(PIX // CHUNK):
        t_ref[:, i * CHUNK : (i + 1) * CHUNK] = jnp.transpose(load(i).astype(single)).astype(narrow)


def kernel_grad(t_ref, s_ref, sign, store):
    for t in range(9):
        a, b = TAPS[t]
        start = PAD + sign * a * SIDE
        store(t, dot(t_ref[...], s_ref[sign * b + 1, start : start + PIX, 0:HALF]))


def low_lanes(shape):
    return lax.broadcasted_iota(jnp.int32, shape, 1) < BLOCK // 2


def swap_halves(value):
    half = BLOCK // 2
    return jnp.concatenate([value[:, half:], value[:, :half]], 1)


def mask_half(value, upper, scale=1.0):
    low = low_lanes(value.shape)
    return jnp.where(low != upper, value.astype(single) * scale, 0.0).astype(narrow)


def head_parts(qkv_ref, s, h):
    base = 3 * BLOCK * s
    b0, b1, b2 = [slice(base + k * BLOCK, base + (k + 1) * BLOCK) for k in range(3)]
    return (b0, b0, b1) if h == 0 else (b1, b2, b2)


SCALE = (C // HEADS) ** (-0.5)
UNROLL = 4
CONV_UNROLL = 4
NORM_UNROLL = 4


def attend(qkv_ref, k_ref, vt_ref, log_ref, out_ref, between=None):
    for s in range(2):
        for h in range(2):
            q_at, k_at, v_at = head_parts(qkv_ref, s, h)
            k_ref[...] = swap_halves(qkv_ref[:, k_at])
            vt_ref[...] = jnp.transpose(qkv_ref[:, v_at].astype(single)).astype(narrow)

            @pl.loop(0, PIX // CHUNK)
            def _(i):
                query = mask_half(qkv_ref[rows_of(i), q_at], h == 1, SCALE)
                scores = dot_t(k_ref[...], query)
                top = jnp.max(scores, 0, keepdims=True)
                exponent = jnp.exp(scores - top)
                total = jnp.sum(exponent, 0, keepdims=True)
                mixed = dot(vt_ref[...], exponent.astype(narrow)) / total
                log_ref[2 * s + h, i] = top + jnp.log(total)
                turned = jnp.transpose(mixed)
                at = rows_of(i)
                lanes = slice(s * BLOCK, (s + 1) * BLOCK)
                if h == 0:
                    out_ref[at, lanes] = turned.astype(narrow)
                else:
                    kept = out_ref[at, lanes].astype(single)
                    out_ref[at, lanes] = jnp.where(low_lanes(turned.shape), kept, turned).astype(narrow)

            if between is not None:
                between(2 * s + h + 1)


def attend_back(qkv_ref, log_ref, grad_ref, k_ref, kt_ref, dk_ref, dv_ref, dqkv, between=None):
    for s in range(2):
        lanes = slice(s * BLOCK, (s + 1) * BLOCK)
        for h in range(2):
            q_at, k_at, v_at = head_parts(qkv_ref, s, h)
            q_to, k_to, v_to = head_parts(None, 0, h)
            grad_to = dqkv[s]
            k_ref[...] = swap_halves(qkv_ref[:, k_at])
            kt_ref[...] = jnp.transpose(k_ref[...].astype(single)).astype(narrow)
            dk_ref[...] = jnp.zeros_like(dk_ref)
            dv_ref[...] = jnp.zeros_like(dv_ref)

            @pl.loop(0, PIX // CHUNK, unroll=UNROLL)
            def _(i):
                at = rows_of(i)
                query = mask_half(qkv_ref[at, q_at], h == 1, SCALE)
                grad = mask_half(grad_ref[at, lanes], h == 1)
                weights = jnp.exp(dot_t(k_ref[...], query) - log_ref[2 * s + h, i])
                dv_ref[...] += dot(weights.astype(narrow), grad)
                dweights = dot_t(qkv_ref[:, v_at], grad)
                inner = jnp.sum(weights * dweights, 0, keepdims=True)
                dscores = (weights * (dweights - inner)).astype(narrow)
                dk_ref[...] += dot(dscores, query)
                turned = jnp.transpose(dot(kt_ref[...], dscores) * SCALE)
                kept = grad_to[at, q_to].astype(single)
                low = low_lanes(turned.shape)
                if h == 0:
                    grad_to[at, q_to] = turned.astype(narrow)
                else:
                    grad_to[at, q_to] = jnp.where(low, kept, turned).astype(narrow)

            low = low_lanes((PIX, BLOCK))
            dk = swap_halves(dk_ref[...])
            if h == 0:
                grad_to[:, k_to] = jnp.where(low, grad_to[:, k_to].astype(single), dk).astype(narrow)
                grad_to[:, v_to] = dv_ref[...].astype(narrow)
            else:
                grad_to[:, k_to] = jnp.where(low, dk, dv_ref[...]).astype(narrow)
            if between is not None:
                between(2 * s + h + 1)


VMEM = pl.BlockSpec(memory_space=pltpu.VMEM)


def call(body, outs, scratch, args, name):
    return pl.pallas_call(
        body,
        out_shape=outs,
        in_specs=[VMEM] * len(args),
        out_specs=[VMEM] * len(outs),
        scratch_shapes=scratch,
        compiler_params=pltpu.CompilerParams(vmem_limit_bytes=56 * 2**20),
        name=name,
    )(*args)


def struct(shape, dtype=single):
    return jax.ShapeDtypeStruct(shape, dtype)


def entry_kernel(act, x_ref, own_ref, recv_ref, norm_ref, stream_ref, entry_ref):
    @pl.loop(0, PIX // CHUNK)
    def _(i):
        at = rows_of(i)
        stream_ref[at, :] = x_ref[at, :] + (own_ref[at, :] + recv_ref[at, :].astype(single))

    def store(i, value):
        entry_ref[rows_of(i), :] = value

    norm_forward(stream_ref, norm_ref[0:1, :], norm_ref[1:2, :], act, store)


def first_kernel(x_ref, norm_ref, stream_ref, entry_ref):
    @pl.loop(0, PIX // CHUNK)
    def _(i):
        at = rows_of(i)
        stream_ref[at, :] = x_ref[at, :].astype(single)

    def store(i, value):
        entry_ref[rows_of(i), :] = value

    norm_forward(stream_ref, norm_ref[0:1, :], norm_ref[1:2, :], True, store)


def mid_rows(norm_ref, mod_ref):
    gain, bias = norm_ref[0:1, :], norm_ref[1:2, :]
    scale, shift = 1.0 + mod_ref[0:1, :], mod_ref[1:2, :]
    return gain, bias, scale, shift


def put_split(own_ref, peer_ref):
    def store(i, value):
        own, peer = split_core(value)
        own_ref[rows_of(i), :] = own
        peer_ref[rows_of(i), :] = peer.astype(narrow)

    return store


def shift_full(full_ref, s_ref, width):
    shifts(lambda i, size: full_ref[rows_of(i, size), :], s_ref, width)


def res_kernel(own_ref, peer_ref, win_ref, wout_ref, norm_ref, mod_ref, inner_ref, hidden_ref, part_ref, send_ref, full_ref, s_ref):
    join_core(own_ref, peer_ref, full_ref)
    shift_full(full_ref, s_ref, C)

    def put(i, value):
        inner_ref[rows_of(i), :] = value

    conv_wide(s_ref, win_ref, put)
    gain, bias, scale, shift = mid_rows(norm_ref, mod_ref)

    def store(i, value):
        hidden_ref[rows_of(i), :] = value

    norm_forward(inner_ref, gain * scale, bias * scale + shift, True, store)
    shift_full(hidden_ref, s_ref, HALF)
    conv_tall(s_ref, wout_ref, 1, put_split(part_ref, send_ref))


def attn_kernel(own_ref, peer_ref, w_ref, qkv_ref, log_ref, out_ref, part_ref, send_ref, full_ref, k_ref, vt_ref):
    join_core(own_ref, peer_ref, full_ref)

    @pl.loop(0, PIX // CHUNK)
    def _(i):
        at = rows_of(i)
        for s in range(2):
            value = dot(full_ref[at, :], w_ref[:, s * C : s * C + 3 * BLOCK])
            qkv_ref[at, s * 3 * BLOCK : (s + 1) * 3 * BLOCK] = value.astype(narrow)

    attend(qkv_ref, k_ref, vt_ref, log_ref, out_ref)
    store = put_split(part_ref, send_ref)

    @pl.loop(0, PIX // CHUNK)
    def _(i):
        at = rows_of(i)
        value = dot_t(out_ref[at, 0:BLOCK], w_ref[:, 3 * BLOCK : C])
        store(i, value + dot_t(out_ref[at, BLOCK:], w_ref[:, C + 3 * BLOCK :]))


def load_rows(ref):
    return lambda i: ref[rows_of(i), :]


def head_kernel(total, own_ref, peer_ref, w_ref, noise_ref, weight_ref, loss_ref, dw_ref, part_ref, send_ref, full_ref, s_ref, t_ref, grad_ref):
    join_core(own_ref, peer_ref, full_ref)
    shift_full(full_ref, s_ref, C)
    loss_ref[...] = jnp.zeros_like(loss_ref)

    def store(i, value):
        error = value - noise_ref[rows_of(i), :]
        weight = weight_ref[0:1, :]
        loss_ref[...] += jnp.sum(weight * error * error, 0, keepdims=True)
        grad_ref[rows_of(i), :] = (2.0 * weight * error / total).astype(narrow)

    conv_wide(s_ref, w_ref, store)
    wide_back(full_ref, w_ref, grad_ref, dw_ref, part_ref, send_ref, s_ref, t_ref)


def wide_back(full_ref, w_ref, grad_ref, dw_ref, part_ref, send_ref, s_ref, t_ref):
    shift_full(grad_ref, s_ref, HALF)
    transpose_into(load_rows(full_ref), t_ref)

    def keep(t, value):
        dw_ref[t * C : (t + 1) * C, :] = value.astype(narrow)

    kernel_grad(t_ref, s_ref, -1, keep)
    conv_tall(s_ref, w_ref, -1, put_split(part_ref, send_ref))


def normback_kernel(act, x_ref, part_ref, recv_ref, up_ref, norm_ref, dx_ref, low_ref, sums_ref, tmp_ref):
    def load(i):
        return part_ref[rows_of(i), :] + recv_ref[rows_of(i), :].astype(single)

    def store(i, value):
        value = value + up_ref[rows_of(i), :]
        dx_ref[rows_of(i), :] = value
        low_ref[rows_of(i), :] = value.astype(narrow)

    total, along = norm_backward(x_ref, load, norm_ref[0:1, :], norm_ref[1:2, :], act, tmp_ref, store)
    sums_ref[0:1, :] = along
    sums_ref[1:2, :] = total


def resback_kernel(
    gown_ref, gpeer_ref, hidden_ref, inner_ref, norm_ref, mod_ref, wout_ref, own_ref, peer_ref, win_ref,
    dout_ref, din_ref, part_ref, send_ref, sums_ref, dmod_ref,
    full_ref, s_ref, t_ref, dh_ref, tmp_ref, grad_ref,
):
    join_core(gown_ref, gpeer_ref, full_ref)
    transpose_into(load_rows(full_ref), t_ref)
    shift_full(hidden_ref, s_ref, HALF)

    def keep(t, value):
        dout_ref[t * C : (t + 1) * C, :] = value.astype(narrow)

    kernel_grad(t_ref, s_ref, 1, keep)
    shift_full(full_ref, s_ref, C)

    def put(i, value):
        dh_ref[rows_of(i), :] = value

    conv_back(s_ref, wout_ref, put)
    gain, bias, scale, shift = mid_rows(norm_ref, mod_ref)

    def store(i, value):
        grad_ref[rows_of(i), :] = value.astype(narrow)

    total, along = norm_backward(
        inner_ref, load_rows(dh_ref), gain * scale, bias * scale + shift, True, tmp_ref, store
    )
    sums_ref[0:1, :] = scale * along
    sums_ref[1:2, :] = scale * total
    dmod_ref[0:1, :] = gain * along + bias * total
    dmod_ref[1:2, :] = total
    join_core(own_ref, peer_ref, full_ref)
    wide_back(full_ref, win_ref, grad_ref, din_ref, part_ref, send_ref, s_ref, t_ref)


def attnback_kernel(
    gown_ref, gpeer_ref, qkv_ref, log_ref, out_ref, w_ref, own_ref, peer_ref,
    dw_ref, part_ref, send_ref,
    full_ref, t_ref, grad_ref, k_ref, kt_ref, dk_ref, dv_ref, dqkv_ref,
):
    join_core(gown_ref, gpeer_ref, full_ref)
    transpose_into(load_rows(full_ref), t_ref)
    for s in range(2):
        lanes = slice(s * BLOCK, (s + 1) * BLOCK)
        dw_ref[:, s * C + 3 * BLOCK : (s + 1) * C] = dot(t_ref[...], out_ref[:, lanes]).astype(narrow)

        @pl.loop(0, PIX // CHUNK)
        def _(i):
            at = rows_of(i)
            value = dot(full_ref[at, :], w_ref[:, s * C + 3 * BLOCK : (s + 1) * C])
            grad_ref[at, lanes] = value.astype(narrow)

    dqkv = [dqkv_ref.at[:, s * 3 * BLOCK : (s + 1) * 3 * BLOCK] for s in range(2)]
    attend_back(qkv_ref, log_ref, grad_ref, k_ref, kt_ref, dk_ref, dv_ref, dqkv)
    join_core(own_ref, peer_ref, full_ref)
    transpose_into(load_rows(full_ref), t_ref)
    for s in range(2):
        lanes = slice(s * 3 * BLOCK, (s + 1) * 3 * BLOCK)
        dw_ref[:, s * C : s * C + 3 * BLOCK] = dot(t_ref[...], dqkv_ref[:, lanes]).astype(narrow)
    store = put_split(part_ref, send_ref)

    @pl.loop(0, PIX // CHUNK)
    def _(i):
        at = rows_of(i)
        value = dot_t(dqkv_ref[at, 0 : 3 * BLOCK], w_ref[:, 0 : 3 * BLOCK])
        store(i, value + dot_t(dqkv_ref[at, 3 * BLOCK :], w_ref[:, C : C + 3 * BLOCK]))


HALF_F32 = struct((PIX, HALF))
HALF_LOW = struct((PIX, HALF), narrow)
FULL_LOW = pltpu.VMEM((PIX, C), narrow)
SHIFTED = pltpu.VMEM((3, ROWS, C), narrow)
TURNED = pltpu.VMEM((C, PIX), narrow)
SWAP = [(0, 1), (1, 0)]


def core_swap(value):
    return lax.ppermute(value, "lo", SWAP)


def image_swap(value):
    return lax.ppermute(value, "hi", SWAP)


DP = ("dz", "dy")


def pick_image(value):
    hi = lax.axis_index("hi")
    kept = jnp.where(hi == 0, value[0], value[1])
    came = image_swap(jnp.where(hi == 0, value[1], value[0]))
    return jnp.where(hi == 0, jnp.concatenate([kept, came], 1), jnp.concatenate([came, kept], 1))


def join_image(value, axis):
    hi = lax.axis_index("hi")
    came = image_swap(value)
    return jnp.where(
        hi == 0, jnp.concatenate([value, came], axis), jnp.concatenate([came, value], axis)
    )


def gather_weight(shard):
    rows = lax.all_gather(shard, DP, axis=0, tiled=True)
    return lax.all_gather(rows, "hi", axis=1, tiled=True)


def scatter_grad(value):
    cols = lax.psum_scatter(value, "hi", scatter_dimension=1, tiled=True)
    return lax.psum_scatter(cols, DP, scatter_dimension=0, tiled=True).astype(single)


def chan_index():
    return lax.axis_index("hi") * 2 + lax.axis_index("lo")


def sinusoid_of(timesteps):
    half_count = TF // 2
    frequency = jnp.exp(-math.log(10000.0) * jnp.arange(half_count, dtype=single) / half_count)
    angles = timesteps.astype(single)[:, None] * frequency[None, :]
    return jnp.concatenate([jnp.cos(angles), jnp.sin(angles)], 1).astype(narrow)


def embed_forward(timesteps, classes, time_in, emb_out, emb_proj):
    times = lax.all_gather(timesteps, DP, axis=0, tiled=True)
    labels = lax.all_gather(classes, DP, axis=0, tiled=True)
    rows = time_in.shape[0]
    place = lax.axis_index(DP) * rows
    sinusoid = lax.dynamic_slice_in_dim(sinusoid_of(times), place, rows, 1)
    pre = lax.psum(dot(sinusoid, time_in), DP)
    hidden = jax.nn.silu(pre).astype(narrow)
    class_here = emb_out.shape[1] - hidden.shape[1]
    numbers = chan_index() * class_here + jnp.arange(class_here)
    onehot = (labels[:, None] == numbers[None, :]).astype(narrow)
    joined = jnp.concatenate([hidden, onehot], 1)
    embedding = lax.psum(dot_t(joined, emb_out), ("hi", "lo"))
    context = jax.nn.silu(embedding).astype(narrow)
    parts = jnp.einsum("be,lej->blj", context, emb_proj, preferred_element_type=single)
    mine = lax.psum_scatter(parts, DP, scatter_dimension=0, tiled=True)
    hi = lax.axis_index("hi")
    kept = jnp.where(hi == 0, mine[0], mine[1])
    came = image_swap(jnp.where(hi == 0, mine[1], mine[0]))
    wide = jnp.where(hi == 0, jnp.concatenate([kept, came], 1), jnp.concatenate([came, kept], 1))
    modulate = jnp.swapaxes(wide.reshape(2, HALF, 2), 1, 2)
    return modulate, (sinusoid, pre, joined, embedding, context)


def embed_backward(saved, dmod, emb_proj, emb_out):
    sinusoid, pre, joined, embedding, context = saved
    flat = jnp.swapaxes(dmod, 1, 2).reshape(2, 2 * HALF).astype(narrow)
    hi = lax.axis_index("hi")
    width = flat.shape[1] // 2
    kept = jnp.where(hi == 0, flat[:, :width], flat[:, width:])
    came = image_swap(jnp.where(hi == 0, flat[:, width:], flat[:, :width]))
    both = jnp.where(hi == 0, jnp.stack([kept, came]), jnp.stack([came, kept]))
    grads = lax.all_gather(both, DP, axis=0, tiled=True)
    proj_grad = jnp.einsum("be,blj->lej", context, grads, preferred_element_type=single)
    part = jnp.einsum("blj,lej->be", grads, emb_proj, preferred_element_type=single)
    context_grad = lax.psum(part, ("hi", "lo"))
    _, pullback = jax.vjp(jax.nn.silu, embedding)
    (embed_grad,) = pullback(context_grad)
    embed_low = embed_grad.astype(narrow)
    out_grad = jnp.einsum("be,bj->ej", embed_low, joined, preferred_element_type=single)
    joined_grad = lax.psum(dot(embed_low, emb_out[:, : pre.shape[1]]), DP)
    _, pullback = jax.vjp(jax.nn.silu, pre)
    (pre_grad,) = pullback(joined_grad)
    time_grad = jnp.einsum("bt,be->te", sinusoid, pre_grad.astype(narrow), preferred_element_type=single)
    return proj_grad, time_grad, out_grad


def res_forward(own, peer, win, wout, norm, mod):
    outs = [HALF_F32, HALF_LOW, HALF_F32, HALF_LOW]
    return call(res_kernel, outs, [FULL_LOW, SHIFTED], [own, peer, win, wout, norm, mod], "res_forward")


def res_backward(gown, gpeer, hidden, inner, norm, mod, wout, own, peer, win):
    taps = struct((9 * C, HALF), narrow)
    outs = [taps, taps, HALF_F32, HALF_LOW, struct((2, HALF)), struct((2, HALF))]
    scratch = [FULL_LOW, SHIFTED, TURNED, pltpu.VMEM((PIX, HALF), single), pltpu.VMEM((PIX, HALF), single), pltpu.VMEM((PIX, HALF), narrow)]
    return call(resback_kernel, outs, scratch, [gown, gpeer, hidden, inner, norm, mod, wout, own, peer, win], "res_backward")


def norm_step(act, x, part, recv, up, norm):
    outs = [HALF_F32, HALF_LOW, struct((2, HALF))]
    body = functools.partial(normback_kernel, act)
    return call(body, outs, [pltpu.VMEM((PIX, HALF), single)], [x, part, recv, up, norm], "norm_backward")


def entry_step(act, x, part, recv, norm):
    return call(functools.partial(entry_kernel, act), [HALF_F32, HALF_LOW], [], [x, part, recv, norm], "entry")


def network(noisy, noise, sample_weight, kernels_in, kernels_out, attn, norms, modulate):
    images = noisy.shape[0] * lax.axis_size("dz") * lax.axis_size("dy")
    total = float(images * PIX * C)
    x0 = pick_image(noisy.reshape(2, PIX, BLOCK))
    target = pick_image(noise.reshape(2, PIX, BLOCK))
    weight = jnp.where(lax.axis_index("hi") == 0, sample_weight[0], sample_weight[1])
    weight = jnp.broadcast_to(weight, (8, HALF))
    stream0, entry0 = call(first_kernel, [HALF_F32, HALF_LOW], [], [x0, norms[0]], "entry")
    peer0 = core_swap(entry0)
    inner0, hidden0, part, send = res_forward(entry0, peer0, kernels_in[0], kernels_out[0], norms[1], modulate[0])
    stream1, entry1 = entry_step(False, stream0, part, core_swap(send), norms[2])
    peer1 = core_swap(entry1)
    outs = [struct((PIX, 6 * BLOCK), narrow), struct((4, PIX // CHUNK, 1, CHUNK)), HALF_LOW, HALF_F32, HALF_LOW]
    scratch = [FULL_LOW, pltpu.VMEM((PIX, BLOCK), narrow), pltpu.VMEM((BLOCK, PIX), narrow)]
    qkv, log, attended, part, send = call(attn_kernel, outs, scratch, [entry1, peer1, attn], "attention")
    stream2, entry2 = entry_step(True, stream1, part, core_swap(send), norms[3])
    peer2 = core_swap(entry2)
    inner2, hidden2, part, send = res_forward(entry2, peer2, kernels_in[1], kernels_out[1], norms[4], modulate[1])
    stream3, entry3 = entry_step(True, stream2, part, core_swap(send), norms[5])
    peer3 = core_swap(entry3)
    taps = struct((9 * C, HALF), narrow)
    outs = [struct((1, HALF)), taps, HALF_F32, HALF_LOW]
    scratch = [FULL_LOW, SHIFTED, TURNED, pltpu.VMEM((PIX, HALF), narrow)]
    args = [entry3, peer3, kernels_in[2], target, weight]
    loss, din2, part, send = call(functools.partial(head_kernel, total), outs, scratch, args, "head")
    zero = jnp.zeros((PIX, HALF), single)
    grad3, low3, sums5 = norm_step(True, stream3, part, core_swap(send), zero, norms[5])
    dout1, din1, part, send, sums4, dmod1 = res_backward(
        low3, core_swap(low3), hidden2, inner2, norms[4], modulate[1], kernels_out[1], entry2, peer2, kernels_in[1]
    )
    grad2, low2, sums3 = norm_step(True, stream2, part, core_swap(send), grad3, norms[3])
    outs = [struct((C, 2 * C), narrow), HALF_F32, HALF_LOW]
    scratch = [
        FULL_LOW, TURNED, pltpu.VMEM((PIX, HALF), narrow), pltpu.VMEM((PIX, BLOCK), narrow), pltpu.VMEM((BLOCK, PIX), narrow),
        pltpu.VMEM((PIX, BLOCK), single), pltpu.VMEM((PIX, BLOCK), single), pltpu.VMEM((PIX, 6 * BLOCK), narrow),
    ]
    args = [low2, core_swap(low2), qkv, log, attended, attn, entry1, peer1]
    dattn, part, send = call(attnback_kernel, outs, scratch, args, "attention_backward")
    grad1, low1, sums2 = norm_step(False, stream1, part, core_swap(send), grad2, norms[2])
    dout0, din0, part, send, sums1, dmod0 = res_backward(
        low1, core_swap(low1), hidden0, inner0, norms[1], modulate[0], kernels_out[0], entry0, peer0, kernels_in[0]
    )
    _, _, sums0 = norm_step(True, stream0, part, core_swap(send), grad1, norms[0])
    sums = jnp.stack([sums0, sums1, sums2, sums3, sums4, sums5])
    return jnp.sum(loss) / total, (din0, din1, din2), (dout0, dout1), dattn, sums, jnp.stack([dmod0, dmod1])


MESH = pl.DeviceIdType.MESH
ANY = pl.BlockSpec(memory_space=pl.ANY)
SMEM = pl.BlockSpec(memory_space=pltpu.SMEM)
LAYERS = 6
REDUCES = 8
EARLY = ("5", "1b")
LANDINGS = 5 * REDUCES
STEPS = 16


def remote(src, dst, send, recv, **where):
    return pltpu.make_async_remote_copy(
        src_ref=src, dst_ref=dst, send_sem=send, recv_sem=recv, device_id=where, device_id_type=MESH
    )


def place():
    return lax.axis_index("dz"), lax.axis_index("dy"), lax.axis_index("hi")


def greet(others):
    barrier = pltpu.get_barrier_semaphore()
    for where in others:
        pl.semaphore_signal(barrier, inc=1, device_id=where, device_id_type=MESH)
    return lambda: pl.semaphore_wait(barrier, len(others))


def neighbours():
    z, y, x = place()
    others = [{"dz": (z + k) % 4} for k in (1, 2, 3)]
    return others + [{"dy": 1 - y}, {"hi": 1 - x}, {"lo": 1 - lax.axis_index("lo")}]


class Layout:
    def __init__(self, rows, lanes):
        self.rows, self.lanes = rows, lanes

    def block(self, zz, yy):
        return pl.ds(pl.multiple_of((zz * 2 + yy) * self.rows, 32), self.rows)

    def cols(self, xx):
        return pl.ds(pl.multiple_of(xx * self.lanes, 128), self.lanes)


class AlongZ:
    def __init__(self, own, region, send, recv):
        z, _, _ = place()
        self.z, self.sends, self.waits = z, [], []
        for j, d in enumerate((2, -2, 1, -1)):
            allowed = z + d < 4 if d > 0 else z + d >= 0
            self.sends.append((allowed, remote(own, region(z), send(j), recv(z), dz=z + d)))
        self.relays = []
        for here, source, target in ((2, 0, 3), (1, 3, 0)):
            part = region(source)
            self.relays.append((z == here, remote(part, part, send(4), recv(source), dz=target)))
        for source in range(4):
            relayed = {0: z == 2, 3: z == 1}.get(source)
            wanted = z != source if relayed is None else (z != source) & jnp.logical_not(relayed)
            part = region(source)
            self.waits.append((wanted, remote(part, part, send(0), recv(source), dz=z)))

    def start(self):
        for allowed, copy in self.sends:
            pl.when(allowed)(copy.start)

    def pass_on(self):
        for here, copy in self.relays:

            def go(copy=copy):
                copy.wait_recv()
                copy.start()

            pl.when(here)(go)

    def wait(self):
        for wanted, copy in self.waits:
            pl.when(wanted)(copy.wait_recv)

    def drain(self):
        for allowed, copy in self.sends + self.relays:
            pl.when(allowed)(copy.wait_send)


class SumAlongZ:
    def __init__(self, block, slots, rows, lanes, send, recv):
        z, _, _ = place()
        self.z, self.block, self.slots, self.rows, self.lanes = z, block, slots, rows, lanes
        self.send, self.recv = send, recv
        self.outer = (z == 0) | (z == 3)
        self.sends, self.relays = [], []

        def copy(j, target, slot, to):
            return remote(block(target), slots.at[slot], send(j), recv(slot), dz=to)

        for here, j, target, slot, to in (
            (0, 0, 3, 1, 1), (0, 1, 2, 0, 2), (0, 2, 1, 0, 1),
            (3, 0, 0, 2, 2), (3, 1, 1, 3, 1), (3, 2, 2, 3, 2),
            (1, 0, 0, 1, 0), (1, 1, 2, 1, 2),
            (2, 0, 1, 2, 1), (2, 1, 3, 2, 3),
        ):
            self.sends.append((z == here, copy(j, target, slot, to)))
        for here, target in ((1, 3), (2, 0)):
            self.relays.append((here, z == here, target, copy(3, target, here, target)))

    def start(self):
        for here, copy in self.sends:
            pl.when(here)(copy.start)

    def pass_on(self):
        for number, here, target, copy in self.relays:

            def go(number=number, target=target, copy=copy):
                copy.wait_recv()
                add_rows(self.rows, self.lanes, self.block(target), self.slots.at[number])
                copy.start()

            pl.when(here)(go)

    def collect(self, add):
        def take(sources):
            def go():
                for source in sources:
                    waiting = self.slots.at[source]
                    remote(waiting, waiting, self.send(0), self.recv(source), dz=self.z).wait_recv()
                add([self.slots.at[source] for source in sources])

            return go

        pl.when(self.outer)(take((1, 2)))
        pl.when(self.z == 1)(take((0, 2, 3)))
        pl.when(self.z == 2)(take((0, 1, 3)))

    def drain(self):
        for here, copy in self.sends:
            pl.when(here)(copy.wait_send)
        for _, here, _, copy in self.relays:
            pl.when(here)(copy.wait_send)


class Gather:
    def __init__(self, layer, shard, full, send, recv, local):
        z, y, x = place()
        rows, lanes = shard.shape
        at = Layout(rows, lanes)
        mine = full.at[at.block(z, y), at.cols(x)]
        self.local = pltpu.make_async_copy(shard, mine, local.at[layer])

        def copy(j, src, dst, **where):
            return remote(src, dst, send.at[layer, j], recv.at[layer, j], **where)

        region = lambda zz: full.at[at.block(zz, y), at.cols(x)]
        self.along_z = AlongZ(shard, region, lambda j: send.at[layer, 7 + j], lambda j: recv.at[layer, 7 + j])
        self.first, self.second = [], []
        for n in range(2):
            part = full.at[at.block(n, y), at.cols(x)]
            self.first.append(copy(n, part, part, dy=1 - y))
            part = full.at[at.block(2 + n, y), at.cols(x)]
            self.first.append(copy(2 + n, part, part, hi=1 - x))
        part = full.at[0 : 4 * rows, at.cols(x)]
        self.second.append(copy(4, part, part, hi=1 - x))
        for n in range(2):
            part = full.at[at.block(2 + n, y), :]
            self.second.append(copy(5 + n, part, part, dy=1 - y))

    def start(self):
        self.local.start()
        self.along_z.start()

    def pass_on(self):
        self.along_z.pass_on()

    def turn(self):
        self.local.wait()
        self.along_z.wait()
        for copy in self.first:
            copy.start()

    def spread(self):
        for copy in self.first:
            copy.wait_recv()
        for copy in self.second:
            copy.start()

    def ready(self):
        for copy in self.second:
            copy.wait_recv()

    def drain(self):
        self.along_z.drain()
        for copy in self.first + self.second:
            copy.wait_send()


def add_rows(count, lanes, into, other):
    size = next(n for n in (192, 144, 96, 64, 48, 32) if count % n == 0 and n * lanes <= 32768)

    @pl.loop(0, count // size)
    def _(i):
        at = pl.ds(pl.multiple_of(i * size, 16), size)
        into.at[at, :][...] = into.at[at, :][...] + other.at[at, :][...]


class Reduce:
    buffers = 5

    def __init__(self, layer, grad, bufs, out, low, count, send, recv):
        z, y, x = place()
        ra, rb, rc, rd, rz = bufs
        rows, lanes = out.shape
        at = Layout(rows, lanes)
        self.lanes, self.out, self.bufs, self.low, self.count = lanes, out, bufs, low, count

        def copy(j, src, dst, **where):
            return remote(src, dst, send.at[layer, j], recv.at[layer, j], **where)

        def part(zz, yy, xx=None):
            cut = pl.ds(pl.multiple_of((zz * 2 + yy) * rows + low, 32), count)
            return grad.at[cut, :] if xx is None else grad.at[cut, at.cols(xx)]

        self.part, self.here = part, (z, y, x)
        self.first = []
        for k in range(4):
            self.first.append(copy(k, part(k // 2, k % 2, 1 - x), ra.at[k], hi=1 - x))
        for n in range(2):
            self.first.append(copy(4 + n, part(2 + n, 1 - y), rb.at[n], dy=1 - y))
        self.second = []
        for n in range(2):
            self.second.append(copy(6 + n, part(n, 1 - y, x), rc.at[n], dy=1 - y))
        for n in range(2):
            self.second.append(copy(8 + n, part(2 + n, y, 1 - x), rd.at[n], hi=1 - x))
        self.third = SumAlongZ(
            lambda zz: part(zz, y, x), rz, count, lanes, lambda j: send.at[layer, 10 + j], lambda j: recv.at[layer, 10 + j]
        )

    def start(self):
        for copy in self.first:
            copy.start()

    def turn(self):
        (z, y, x), (ra, rb, rc, rd, rz) = self.here, self.bufs
        for k in range(4):
            self.first[k].wait_recv()
            add_rows(self.count, self.lanes, self.part(k // 2, k % 2, x), ra.at[k])
        for copy in self.second[:2]:
            copy.start()
        for n in range(2):
            self.first[4 + n].wait_recv()
            add_rows(self.count, 2 * self.lanes, self.part(2 + n, y), rb.at[n])
            self.second[2 + n].start()

    def spread(self):
        (z, y, x), (ra, rb, rc, rd, rz) = self.here, self.bufs
        for n in range(2):
            self.second[n].wait_recv()
            add_rows(self.count, self.lanes, self.part(n, y, x), rc.at[n])
        for n in range(2):
            self.second[2 + n].wait_recv()
            add_rows(self.count, self.lanes, self.part(2 + n, y, x), rd.at[n])
        self.third.start()

    def pass_on(self):
        self.third.pass_on()

    def finish(self):
        z, y, x = self.here
        size = 32
        mine = self.part(z, y, x)

        def add(sources):
            @pl.loop(0, self.count // size)
            def _(i):
                part = pl.ds(pl.multiple_of(i * size, 32), size)
                total = mine.at[part, :][...].astype(single)
                for source in sources:
                    total = total + source.at[part, :][...].astype(single)
                self.out.at[pl.ds(pl.multiple_of(self.low + i * size, 32), size), :][...] = total

        self.third.collect(add)

    def drain(self):
        self.third.drain()
        for copy in self.first + self.second:
            copy.wait_send()


def reduce_plan(outs):
    rows = [out.shape[0] for out in outs]
    plan = [(str(n), n, 0, rows[n]) for n in (5, 4, 3, 2)]
    for n in (1, 0):
        half = rows[n] // 2
        plan += [(f"{n}a", n, 0, half), (f"{n}b", n, half, half)]
    return plan


class LateGather:
    def __init__(self, layer, shard, full, send, recv, local):
        z, y, x = place()
        rows, lanes = shard.shape
        half = rows // 2
        at = Layout(rows, lanes)
        mine = full.at[at.block(z, y), at.cols(x)]
        self.local = pltpu.make_async_copy(shard, mine, local.at[layer])

        def copy(j, src, dst, **where):
            return remote(src, dst, send.at[layer, j], recv.at[layer, j], **where)

        def part(yy, k):
            return pl.ds(pl.multiple_of((z * 2 + yy) * rows + k * half, 32), half)

        self.first = [
            copy(0, shard.at[0:half, :], full.at[part(y, 0), at.cols(x)], hi=1 - x),
            copy(1, shard.at[half:, :], full.at[part(y, 1), at.cols(x)], dy=1 - y),
        ]
        self.second = [copy(2, full.at[part(y, 0), :], full.at[part(y, 0), :], dy=1 - y)]
        for yy in range(2):
            block = full.at[part(yy, 1), at.cols(x)]
            self.second.append(copy(3 + yy, block, block, hi=1 - x))
        self.third = []
        for k in range(4):
            region = lambda zz, k=k: full.at[pl.ds(pl.multiple_of(zz * 2 * rows + k * half, 32), half), :]
            sems = [lambda j, k=k, ref=ref: ref.at[layer, 7 + 5 * k + j] for ref in (send, recv)]
            self.third.append(AlongZ(region(z), region, *sems))

    def start(self):
        self.local.start()
        for copy in self.first:
            copy.start()

    def turn(self):
        self.local.wait()
        for copy in self.first:
            copy.wait_recv()
        for copy in self.second:
            copy.start()

    def spread(self, k):
        if k == 0:
            for copy in self.second:
                copy.wait_recv()
        self.third[k].start()

    def pass_on(self, k):
        self.third[k].pass_on()

    def ready(self):
        for chunk in self.third:
            chunk.wait()

    def drain(self):
        for chunk in self.third:
            chunk.drain()
        for copy in self.first + self.second:
            copy.wait_send()


class EarlyReduce:
    buffers = 5

    def __init__(self, layer, grad, bufs, out, low, count, send, recv):
        z, y, x = place()
        rz, ra, rb, rc, rd = bufs
        rows, lanes = out.shape
        half = count // 2
        at = Layout(rows, lanes)
        self.out, self.grad, self.bufs, self.lanes, self.half = out, grad, bufs, lanes, half
        self.low, self.count = low, count

        def copy(j, src, dst, **where):
            return remote(src, dst, send.at[layer, j], recv.at[layer, j], **where)

        def part(yy, k):
            return pl.ds(pl.multiple_of((z * 2 + yy) * rows + low + k * half, 16), half)

        self.part, self.cols, self.here, self.first = part, at.cols, (z, y, x), []
        for yy in range(2):

            def block(zz, yy=yy):
                return grad.at[pl.ds(pl.multiple_of((zz * 2 + yy) * rows + low, 32), count), :]

            sems = [lambda j, yy=yy, ref=ref: ref.at[layer, 8 + 4 * yy + j] for ref in (send, recv)]
            self.first.append(SumAlongZ(block, rz.at[yy], count, 2 * lanes, *sems))
        self.second = [copy(3, grad.at[part(1 - y, 0), :], ra, dy=1 - y)]
        for yy in range(2):
            self.second.append(copy(4 + yy, grad.at[part(yy, 1), at.cols(1 - x)], rb.at[yy], hi=1 - x))
        self.third = [
            copy(6, grad.at[part(y, 0), at.cols(1 - x)], rc, hi=1 - x),
            copy(7, grad.at[part(1 - y, 1), at.cols(x)], rd, dy=1 - y),
        ]

    def start(self):
        for chunk in self.first:
            chunk.start()

    def pass_on(self):
        for chunk in self.first:
            chunk.pass_on()

    def turn(self):
        z = self.here[0]
        for chunk in self.first:

            def add(sources, chunk=chunk):
                for source in sources:
                    add_rows(self.count, 2 * self.lanes, chunk.block(z), source)

            chunk.collect(add)
        for copy in self.second:
            copy.start()

    def spread(self):
        (z, y, x), (rz, ra, rb, rc, rd) = self.here, self.bufs
        self.second[0].wait_recv()
        add_rows(self.half, 2 * self.lanes, self.grad.at[self.part(y, 0), :], ra)
        self.third[0].start()
        for yy in range(2):
            self.second[1 + yy].wait_recv()
            add_rows(self.half, self.lanes, self.grad.at[self.part(yy, 1), self.cols(x)], rb.at[yy])
        self.third[1].start()

    def finish(self):
        (z, y, x), (rz, ra, rb, rc, rd) = self.here, self.bufs
        for copy in self.third:
            copy.wait_recv()
        size = 48
        for k, came in enumerate((rc, rd)):
            mine = self.grad.at[self.part(y, k), self.cols(x)]

            @pl.loop(0, self.half // size)
            def _(i):
                part = pl.ds(pl.multiple_of(i * size, 16), size)
                total = mine.at[part, :][...].astype(single) + came.at[part, :][...].astype(single)
                self.out.at[pl.ds(pl.multiple_of(self.low + k * self.half + i * size, 16), size), :][...] = total

    def drain(self):
        for chunk in self.first:
            chunk.drain()
        for copy in self.second + self.third:
            copy.wait_send()


class Core:
    def __init__(self, send, recv):
        self.send, self.recv, self.used = send, recv, 0
        self.core = lax.axis_index("lo")

    def take(self, count):
        base = self.used
        self.used += count
        return base

    def copy(self, index, src, dst):
        return remote(src, dst, self.send.at[index], self.recv.at[index], lo=1 - self.core)

    def lanes(self, j):
        return pl.ds(pl.multiple_of((2 * j + self.core) * BLOCK, 128), BLOCK)

    def share(self, full):
        base = self.take(2 * (PIX // CHUNK))

        def copies(i):
            parts = [full.at[rows_of(i), self.lanes(j)] for j in range(2)]
            return [self.copy(base + 2 * i + j, part, part) for j, part in enumerate(parts)]

        def store(i, value):
            for j in range(2):
                full[rows_of(i), self.lanes(j)] = value[:, j * BLOCK : (j + 1) * BLOCK]
            for copy in copies(i):
                copy.start()

        def wait():
            @pl.loop(0, PIX // CHUNK)
            def _(i):
                for copy in copies(i):
                    copy.wait()

        return store, wait

    def combine(self, part, send, recv):
        base = self.take(PIX // CHUNK)

        def one(i):
            return self.copy(base + i, send.at[rows_of(i), :], recv.at[rows_of(i), :])

        def store(i, value):
            own, peer = split_core(value)
            part[rows_of(i), :] = own
            send[rows_of(i), :] = peer.astype(narrow)
            one(i).start()

        def wait():
            @pl.loop(0, PIX // CHUNK)
            def _(i):
                one(i).wait()

        def load(i):
            return part[rows_of(i), :] + recv[rows_of(i), :].astype(single)

        return store, wait, load


def step_kernel(
    fulls, total,
    noisy_hbm, noise_hbm, weight_ref, times_ref, labels_ref, norms_own, second,
    conv_in, conv_out, attn_weight, time_in, emb_out, emb_proj,
    in_rows, in_cols, out_rows, out_cols, proj_rows, proj_cols, attn_rows, attn_cols, time_rows, time_cols, eout_rows, eout_cols,
    g0, g1, g2, g3, g4, g5, proj_grad, time_grad, eout_grad, rows_ref, cols_ref, scal_ref, norm_out, second_out, norms_out,
    w0, w1, w2, w3, w4, w5, d1, full0, full1, full2, full3,
    *refs,
):
    landing = refs[:LANDINGS]
    (
    x1, x2, x3, inner0, inner2, noise_ref, part, tmp, dh, up,
    hidden0, hidden2, att, pg, x0_ref, send, recv, qkv,
    shifted, turned, k_ref, kt_ref, dk_ref, dv_ref, log_ref,
    norms_ref, mod_ref, loss_lanes, norms_flat, sums_ref, dmod_ref, wsq_ref, sin_ref, label_ref, pre_ref, embedding_ref,
    s0, s1, s2, s3, s4, s5, noise_send, noise_recv,
    msg, p0, p1, p2, p3, m3, q4, p4, p5, p6, p7, q7, p8, p9, p10, p11, p12, p13,
    gsend, grecv, glocal, rsend, rrecv, csend, crecv, xsend, xrecv, esend, erecv, lsem,
    ) = refs[LANDINGS:]
    x = lax.axis_index("hi")
    met = greet(all_partners())
    core, small = Core(csend, crecv), Small(esend, erecv)
    block = pl.ds(pl.multiple_of(x * BLOCK, BLOCK), BLOCK)
    own_x0 = pltpu.make_async_copy(noisy_hbm.at[x], x0_ref.at[:, block], lsem.at[0])
    own_noise = pltpu.make_async_copy(noise_hbm.at[x], noise_ref.at[:, block], lsem.at[1])
    other_noise = pltpu.make_async_copy(noise_hbm.at[1 - x], dk_ref, lsem.at[2])
    own_x0.start()
    own_noise.start()
    other_noise.start()
    norms_flat[...] = joined_rows(norms_own)
    norms_ref[:, block] = norms_flat[...]
    dmod_ref[...] = jnp.zeros_like(dmod_ref)
    loss_lanes[...] = jnp.zeros_like(loss_lanes)
    keep = (sin_ref, label_ref, pre_ref, embedding_ref)
    embed = embed_steps(
        small, times_ref, labels_ref, time_in, emb_out, emb_proj, msg, p0, p1, p2, p3, m3, mod_ref, keep
    )
    shards, full_weights = (s0, s1, s2, s3, s4, s5), (w0, w1, w2, w3, w4, w5)
    gathers = []
    for n, (shard, full) in enumerate(zip(shards, full_weights)):
        kind = LateGather if n == 5 else Gather
        gathers.append(kind(n, shard, full, gsend, grecv, glocal))
    outs, grads = (g0, g1, g2, g3, g4, g5), (w1, w4, w2, w3, d1, w5)
    reduces, used = {}, 0
    for number, (name, n, low, count) in enumerate(reduce_plan(outs)):
        kind = EarlyReduce if name in EARLY else Reduce
        bufs = landing[used : used + kind.buffers]
        used += kind.buffers
        reduces[name] = kind(number, grads[n], bufs, outs[n], low, count, rsend, rrecv)
    matrices = [g0, g3, g5, g1, g4, proj_grad.at[0], proj_grad.at[1], g2, time_grad, eout_grad]
    rows_old = [in_rows[n : n + 1] for n in range(3)] + [out_rows[n : n + 1] for n in range(2)]
    rows_old += [proj_rows[n : n + 1] for n in range(2)] + [attn_rows[...], time_rows[...], eout_rows[...]]
    cols_old = [in_cols[n : n + 1] for n in range(3)] + [out_cols[n : n + 1] for n in range(2)]
    cols_old += [proj_cols[n : n + 1] for n in range(2)] + [attn_cols[...], time_cols[...], eout_cols[...]]
    step = adafactor_steps(
        small, (1, 2, 4, 5, 6, 7, 8, 9), (0, 3), matrices, rows_old, cols_old, fulls, wsq_ref, loss_lanes, sums_ref,
        norms_own, second, p7, q7, p8, p9, p10, p11, p12, p13, rows_ref, cols_ref, scal_ref, norm_out, second_out, norms_out,
    )
    embed_end = embed_back_steps(
        small, dmod_ref, q4, p4, p5, p6, emb_out, emb_proj, keep, proj_grad, eout_grad, time_grad
    )

    def norm_row(n):
        return norms_ref[2 * n : 2 * n + 1, :], norms_ref[2 * n + 1 : 2 * n + 2, :]

    def keep_taps(grad):
        def store(t, value):
            grad[t * C : (t + 1) * C, :] = value.astype(narrow)

        return store

    class First:
        def __getitem__(self, at):
            return x0_ref[at].astype(single)

    def entry(x, n, act, full):
        gain, bias = norm_row(n)
        store, wait = core.share(full)
        norm_forward(x, gain, bias, act, store)
        return wait

    def middle(n, layer):
        gain, bias = norm_row(n)
        scale, shift = 1.0 + mod_ref[layer, 0:1, :], mod_ref[layer, 1:2, :]
        return gain, bias, scale, gain * scale, bias * scale + shift

    def first_half(full, w, n, layer, inner, hidden, between=None):
        shift_full(full, shifted, C)

        def put(i, value):
            inner[rows_of(i), :] = value

        conv_wide(shifted, w, put)
        if between is not None:
            between()
        _, _, _, gain, bias = middle(n, layer)

        def store(i, value):
            hidden[rows_of(i), :] = value

        norm_forward(inner, gain, bias, True, store)
        shift_full(hidden, shifted, HALF)

    def second_half(w):
        store, wait, load = core.combine(part, send, recv)
        conv_tall(shifted, w, 1, store)
        return wait, load

    def advance(x_old, load, x_new):
        @pl.loop(0, PIX // CHUNK)
        def _(i):
            x_new[rows_of(i), :] = x_old[rows_of(i), :] + load(i)

    masters = [conv_in.at[0], conv_out.at[0], attn_weight, conv_in.at[1], conv_out.at[1], conv_in.at[2]]
    for master, shard in zip(masters, shards):
        shard[...] = master[...].astype(narrow)
    next(embed)
    masters = [conv_in.at[n] for n in range(3)] + [conv_out.at[n] for n in range(2)]
    masters += [emb_proj.at[n] for n in range(2)] + [attn_weight, time_in, emb_out]
    wsq_ref[...] = scalar_rows([whole(master[...] * master[...]) for master in masters], 16)
    met()
    swaps = []
    for n, (src, dst) in enumerate(
        ((norms_flat, norms_ref.at[:, block]), (noisy_hbm.at[1 - x], x0_ref.at[:, block]), (noise_send, noise_recv))
    ):
        swaps.append(remote(src, dst, xsend.at[n], xrecv.at[n], hi=1 - x))
    next(embed)
    gathers[0].start()
    swaps[0].start()
    gathers[5].start()
    swaps[1].start()
    next(embed)
    gathers[5].turn()
    gathers[0].pass_on()
    gathers[1].start()
    gathers[0].turn()
    next(embed)
    gathers[0].spread()
    gathers[2].start()
    own_x0.wait()
    swaps[0].wait_recv()
    swaps[1].wait_recv()
    wait_entry = entry(First(), 0, True, full0)
    gathers[1].pass_on()
    gathers[1].turn()
    next(embed)
    gathers[3].start()
    own_noise.wait()
    other_noise.wait()
    noise_send[...] = dk_ref[...].astype(narrow)
    gathers[2].pass_on()
    gathers[2].turn()
    wait_entry()
    gathers[0].ready()

    def between():
        gathers[4].start()
        gathers[3].pass_on()
        next(embed)
        gathers[1].spread()
        gathers[3].turn()
        gathers[2].spread()

    first_half(full0, w0, 1, 0, inner0, hidden0, between)
    gathers[4].pass_on()
    gathers[5].spread(0)
    gathers[4].turn()
    gathers[1].ready()
    wait, load = second_half(w1)
    wait()
    advance(First(), load, x1)
    wait_entry = entry(x1, 2, False, full1)
    gathers[5].pass_on(0)
    gathers[5].spread(1)
    gathers[3].spread()
    gathers[5].spread(2)
    gathers[2].ready()
    wait_entry()

    @pl.loop(0, PIX // CHUNK)
    def _(i):
        at = rows_of(i)
        for s in range(2):
            value = dot(full1[at, :], w2[:, s * C : s * C + 3 * BLOCK])
            qkv[at, s * 3 * BLOCK : (s + 1) * 3 * BLOCK] = value.astype(narrow)

    def between(done):
        if done == 1:
            gathers[4].spread()
            gathers[5].pass_on(1)
            gathers[5].spread(3)
            swaps[2].start()
        if done == 3:
            gathers[5].pass_on(2)
        if done == 4:
            gathers[5].pass_on(3)

    attend(qkv, k_ref, kt_ref, log_ref, att, between)
    store, wait, load = core.combine(part, send, recv)

    @pl.loop(0, PIX // CHUNK)
    def _(i):
        at = rows_of(i)
        value = dot_t(att[at, 0:BLOCK], w2[:, 3 * BLOCK : C])
        store(i, value + dot_t(att[at, BLOCK:], w2[:, C + 3 * BLOCK :]))

    wait()
    advance(x1, load, x2)
    wait_entry = entry(x2, 3, True, full2)
    gathers[3].ready()
    wait_entry()
    first_half(full2, w3, 4, 1, inner2, hidden2)
    gathers[4].ready()
    wait, load = second_half(w4)
    wait()
    advance(x2, load, x3)
    wait_entry = entry(x3, 5, True, full3)
    for n in range(5):
        gathers[n].drain()
    wait_entry()
    shift_full(full3, shifted, C)
    transpose_into(load_rows(full3), turned)
    gathers[5].ready()
    gathers[5].drain()
    for copy in swaps:
        copy.wait_send()
    swaps[2].wait_recv()
    noise_ref[:, pl.ds(pl.multiple_of((1 - x) * BLOCK, BLOCK), BLOCK)] = noise_recv[...].astype(single)

    def store(i, value):
        error = value - noise_ref[rows_of(i), :]
        weight = jnp.where(x == 0, weight_ref[0], weight_ref[1])
        loss_lanes[0:1, :] += jnp.sum(weight * error * error, 0, keepdims=True)
        pg[rows_of(i), :] = (2.0 * weight * error / total).astype(narrow)

    conv_wide(shifted, w5, store)
    loss_lanes[...] = jnp.broadcast_to(whole(loss_lanes[0:1, :]) / total, loss_lanes.shape)

    def start(n):
        for name, reduce in reduces.items():
            if int(name[0]) == n:
                reduce.start()

    def wide(w, n):
        store, wait, load = core.combine(part, send, recv)
        conv_tall(shifted, w, -1, store)
        if n != 0:
            kernel_grad(turned, shifted, -1, keep_taps(grads[n]))
            start(n)
        return wait, load

    def through_norm(x, wait, load, n, act, first, full):
        gain, bias = norm_row(n)
        share, shared = core.share(full) if full is not None else (None, None)

        def store(i, value):
            if share is None:
                return
            if not first:
                value = value + up[rows_of(i), :]
            up[rows_of(i), :] = value
            share(i, value.astype(narrow))

        summed, along = norm_backward(x, load, gain, bias, act, tmp, store, wait)
        sums_ref[n, 0:1, :] = along
        sums_ref[n, 1:2, :] = summed
        return shared

    def out_grad(full, hidden, n):
        transpose_into(load_rows(full), turned)
        shift_full(hidden, shifted, HALF)
        kernel_grad(turned, shifted, 1, keep_taps(grads[n]))

    def back_half(full, w, n, layer, inner, between=None):
        shift_full(full, shifted, C)

        def put(i, value):
            dh[rows_of(i), :] = value

        conv_back(shifted, w, put)
        if between is not None:
            between()
        gain, bias, scale, gain_all, bias_all = middle(n, layer)

        def store(i, value):
            pg[rows_of(i), :] = value.astype(narrow)

        summed, along = norm_backward(inner, load_rows(dh), gain_all, bias_all, True, tmp, store)
        sums_ref[n, 0:1, :] = scale * along
        sums_ref[n, 1:2, :] = scale * summed
        dmod_ref[0, layer : layer + 1, :] = gain * along + bias * summed
        dmod_ref[1, layer : layer + 1, :] = summed

    shift_full(pg, shifted, HALF)
    wait, load = wide(w5, 5)
    shared = through_norm(x3, wait, load, 5, True, True, full3)
    shared()
    out_grad(full3, hidden2, 4)
    start(4)
    back_half(full3, w4, 4, 1, inner2)
    transpose_into(load_rows(full2), turned)
    shift_full(pg, shifted, HALF)
    wait, load = wide(w3, 3)
    shared = through_norm(x2, wait, load, 3, True, False, full2)
    reduces["5"].pass_on()
    reduces["4"].turn()
    shared()
    for s in range(2):
        lanes = slice(s * BLOCK, (s + 1) * BLOCK)

        @pl.loop(0, PIX // CHUNK)
        def _(i):
            at = rows_of(i)
            value = dot(full2[at, :], w2[:, s * C + 3 * BLOCK : (s + 1) * C])
            pg[at, lanes] = value.astype(narrow)

    transpose_into(load_rows(full2), turned)
    for s in range(2):
        lanes = slice(s * BLOCK, (s + 1) * BLOCK)
        w2[:, s * C + 3 * BLOCK : (s + 1) * C] = dot(turned[...], att[:, lanes]).astype(narrow)

    def between(done):
        if done == 2:
            reduces["3"].turn()
        if done == 3:
            reduces["4"].spread()
        if done == 4:
            reduces["5"].turn()
            reduces["3"].spread()

    dqkv = [shifted.at[s, 0:PIX, 0 : 3 * BLOCK] for s in range(2)]
    attend_back(qkv, log_ref, pg, k_ref, kt_ref, dk_ref, dv_ref, dqkv, between)
    transpose_into(load_rows(full1), turned)
    store, wait, load = core.combine(part, send, recv)

    @pl.loop(0, PIX // CHUNK)
    def _(i):
        at = rows_of(i)
        value = dot_t(dqkv[0].at[at, :][...], w2[:, 0 : 3 * BLOCK])
        store(i, value + dot_t(dqkv[1].at[at, :][...], w2[:, C : C + 3 * BLOCK]))

    for s in range(2):
        w2[:, s * C : s * C + 3 * BLOCK] = dot(turned[...], dqkv[s][...]).astype(narrow)
    start(2)
    shared = through_norm(x1, wait, load, 2, False, False, full1)
    reduces["4"].pass_on()
    reduces["5"].spread()
    shared()

    def between():
        reduces["3"].pass_on()
        reduces["2"].turn()

    back_half(full1, w1, 1, 0, inner0, between)
    next(embed_end)
    out_grad(full1, hidden0, 1)
    reduces["2"].spread()
    next(embed_end)
    reduces["1a"].start()
    transpose_into(load_rows(full0), turned)
    shift_full(pg, shifted, HALF)
    kernel_grad(turned, shifted, -1, keep_taps(grads[0]))
    next(embed_end)
    reduces["1b"].start()
    reduces["0a"].start()
    wait, load = wide(w0, 0)
    reduces["1a"].turn()
    reduces["0b"].start()
    next(embed_end)
    reduces["2"].pass_on()
    reduces["4"].finish()
    through_norm(First(), wait, load, 0, True, False, None)
    reduces["1b"].pass_on()
    reduces["3"].finish()
    reduces["5"].finish()
    reduces["0a"].turn()
    reduces["1a"].spread()
    reduces["2"].finish()
    reduces["1b"].turn()
    reduces["0b"].turn()
    reduces["0a"].spread()
    reduces["1a"].pass_on()
    reduces["1b"].spread()
    next(step)
    reduces["0b"].spread()
    reduces["0a"].pass_on()
    reduces["1a"].finish()
    next(step)
    reduces["0b"].pass_on()
    reduces["1b"].finish()
    reduces["0a"].finish()
    reduces["0b"].finish()
    next(step)
    for reduce in reduces.values():
        reduce.drain()


EXACT = lax.Precision.HIGHEST
IMAGES_HERE = 16


def exact_dot(a, b):
    return jnp.dot(a, b, precision=EXACT, preferred_element_type=single)


def chosen(shape, rule):
    row = lax.broadcasted_iota(jnp.int32, shape, 0)
    column = lax.broadcasted_iota(jnp.int32, shape, 1)
    return jnp.where(rule(row, column), 1.0, 0.0).astype(single)


def odd_even(kind):
    return chosen((HALF, BLOCK), lambda r, c: r == 2 * c + kind)


def even_odd(kind):
    return chosen((BLOCK, HALF), lambda r, c: c == 2 * r + kind)


def contract_rows(a, b):
    return lax.dot_general(a, b, (((0,), (0,)), ((), ())), preferred_element_type=single)


def silu_grad(value):
    gate = sigmoid(value)
    return gate * (1.0 + value * (1.0 - gate))


class Small:
    def __init__(self, send, recv):
        self.send, self.recv, self.used = send, recv, 0
        z, y, x = place()
        core = lax.axis_index("lo")
        self.dp_here, self.chan_here, self.plane_here = 2 * z + y, 2 * x + core, 4 * z + 2 * y + x

    def go(self, count, here, source, target, where):
        copies = []
        for k in range(1, count):
            other = lax.rem(here + k, count)
            sems = self.send.at[self.used], self.recv.at[self.used]
            self.used += 1
            copy = remote(source(other), target.at[here], *sems, **where(other))
            copy.start()
            copies.append(copy)

        def wait():
            for copy in copies:
                copy.wait()

        return wait

    def dp(self, target, source=None):
        source = source or (lambda other: target.at[self.dp_here])
        where = lambda other: {"dz": lax.div(other, 2), "dy": lax.rem(other, 2)}
        return self.go(8, self.dp_here, source, target, where)

    def chan(self, target):
        source = lambda other: target.at[self.chan_here]
        where = lambda other: {"hi": lax.div(other, 2), "lo": lax.rem(other, 2)}
        return self.go(4, self.chan_here, source, target, where)

    def plane(self, target, source):
        where = lambda other: {
            "dz": lax.div(other, 4), "dy": lax.rem(lax.div(other, 2), 2), "hi": lax.rem(other, 2)
        }
        return self.go(16, self.plane_here, source, target, where)


def all_partners():
    z, y, x = place()
    core = lax.axis_index("lo")
    here = 4 * z + 2 * y + x
    others = []
    for k in range(1, 16):
        o = lax.rem(here + k, 16)
        others.append({"dz": lax.div(o, 4), "dy": lax.rem(lax.div(o, 2), 2), "hi": lax.rem(o, 2)})
    return others + [{"lo": 1 - core}, {"hi": 1 - x, "lo": 1 - core}]


def total_of(ref):
    total = ref[0]
    for k in range(1, ref.shape[0]):
        total = total + ref[k]
    return total


def onehot_of(labels, count, first):
    numbers = lax.broadcasted_iota(jnp.int32, (IMAGES_HERE, count), 1) + first
    return jnp.where(labels[:, 0:1] == numbers.astype(single), 1.0, 0.0).astype(narrow)


def sinusoid_rows(times, labels):
    row = lax.broadcasted_iota(jnp.int32, (8, TF), 0)
    lane = lax.broadcasted_iota(jnp.int32, (8, TF), 1)
    half = TF // 2
    frequency = jnp.exp(-math.log(10000.0) * lax.rem(lane, half).astype(single) / half)
    angles = jnp.where(row == 0, times[0], times[1]).astype(single) * frequency
    sin = jnp.where(lane < half, jnp.cos(angles), jnp.sin(angles)).astype(narrow).astype(single)
    label = jnp.where(row == 2, labels[0], labels[1]).astype(single)
    return jnp.where(row < 2, sin, jnp.where(row < 4, label, 0.0))


def embed_steps(small, times, labels, time_in, emb_out, emb_proj, msg, p0, p1, p2, p3, m3, mod_ref, keep):
    sin_ref, label_ref, pre_ref, embedding_ref = keep
    here, chan = small.dp_here, small.chan_here
    rows = time_in.shape[0]
    msg[...] = jnp.zeros_like(msg)
    sent = sinusoid_rows(times, labels)
    for other in range(8):
        msg[other, :, 0:rows] = sent[:, other * rows : (other + 1) * rows]
    p0[here] = msg[here]
    yield
    wait = small.dp(p0, lambda other: msg.at[other])
    yield
    wait()
    flat = p0[...].reshape(64, BLOCK)
    sin = exact_dot(chosen((16, 64), lambda r, c: c == 8 * (r // 2) + r % 2), flat)
    label = exact_dot(chosen((16, 64), lambda r, c: c == 8 * (r // 2) + r % 2 + 2), flat)
    sin_ref[...], label_ref[...] = sin, label
    p1[here] = dot(sin[:, 0:rows].astype(narrow), time_in[...].astype(narrow))
    wait = small.dp(p1)
    yield
    wait()
    pre = total_of(p1)
    pre_ref[...] = pre
    hidden = (pre * sigmoid(pre)).astype(narrow)
    width = hidden.shape[1]
    count = emb_out.shape[1] - width
    onehot = onehot_of(label, count, chan * count)
    part = dot_t(hidden, emb_out[:, 0:width].astype(narrow))
    p2[chan] = part + dot_t(onehot, emb_out[:, width:].astype(narrow))
    wait = small.chan(p2)
    yield
    wait()
    embedding = total_of(p2)
    embedding_ref[...] = embedding
    context = (embedding * sigmoid(embedding)).astype(narrow)
    parts = jnp.concatenate([dot(context, emb_proj[n].astype(narrow)) for n in range(2)], 0)
    spread_rows = chosen((128, 32), lambda r, c: (c == 16 * (r % 8) + r // 8) & (r % 8 < 2))
    m3[...] = exact_dot(spread_rows, parts).reshape(16, 8, HALF)
    p3[small.plane_here] = m3[small.plane_here]
    wait = small.plane(p3, lambda other: m3.at[other])
    yield
    wait()
    flat = p3[...].reshape(128, HALF)
    for half in range(2):
        pick = chosen((8, 128), lambda r, c: (c % 8 == r) & ((c // 8) % 2 == half) & (r < 2))
        wide = exact_dot(pick, flat)
        for kind in range(2):
            value = exact_dot(wide, odd_even(kind))
            for n in range(2):
                mod_ref[n, kind : kind + 1, half * BLOCK : (half + 1) * BLOCK] = value[n : n + 1]
    yield


def embed_back_steps(small, dmod, q4, p4, p5, p6, emb_out, emb_proj, keep, proj_grad, out_grad, time_grad):
    sin_ref, label_ref, pre_ref, embedding_ref = keep
    here, chan, plane = small.dp_here, small.chan_here, small.plane_here
    for half in range(2):
        lanes = slice(half * BLOCK, (half + 1) * BLOCK)
        wide = exact_dot(dmod[0][:, lanes], even_odd(0)) + exact_dot(dmod[1][:, lanes], even_odd(1))
        q4[half] = wide.astype(narrow).astype(single)
    p4[plane] = q4[lax.rem(plane, 2)]
    wait = small.plane(p4, lambda other: q4.at[lax.rem(other, 2)])
    yield
    wait()
    flat = p4[...].reshape(128, HALF)
    embedding, pre = embedding_ref[...], pre_ref[...]
    context = (embedding * sigmoid(embedding)).astype(narrow)
    part = None
    for n in range(2):
        grads = exact_dot(chosen((16, 128), lambda r, c: c == 8 * r + n), flat).astype(narrow)
        proj_grad[n] = contract_rows(context, grads)
        more = dot_t(grads, emb_proj[n].astype(narrow))
        part = more if part is None else part + more
    p5[chan] = part
    wait = small.chan(p5)
    yield
    wait()
    low = (total_of(p5) * silu_grad(embedding)).astype(narrow)
    hidden = (pre * sigmoid(pre)).astype(narrow)
    width = hidden.shape[1]
    count = emb_out.shape[1] - width
    p6[here] = dot(low, emb_out[:, 0:width].astype(narrow))
    wait = small.dp(p6)
    out_grad[:, 0:width] = contract_rows(low, hidden)
    out_grad[:, width:] = contract_rows(low, onehot_of(label_ref[...], count, chan * count))
    yield
    wait()
    pre_grad = (total_of(p6) * silu_grad(pre)).astype(narrow)
    time_grad[...] = contract_rows(sin_ref[...].astype(narrow), pre_grad)[0 : time_grad.shape[0]]
    yield


def to_row(column):
    pieces = []
    for start in range(0, column.shape[0], BLOCK):
        part = column[start : start + BLOCK]
        n = part.shape[0]
        pieces.append(jnp.sum(chosen((n, n), lambda r, c: r == c) * part, 0, keepdims=True))
    return jnp.concatenate(pieces, 1)


def to_column(row):
    pieces = []
    for start in range(0, row.shape[1], BLOCK):
        part = row[:, start : start + BLOCK]
        n = part.shape[1]
        square = chosen((n, n), lambda r, c: r == c) * part
        pieces.append(jnp.sum(square, 1, keepdims=True))
    return jnp.concatenate(pieces, 0)


def joined_rows(ref):
    return jnp.concatenate([ref[n, k : k + 1, :] for n in range(6) for k in range(2)], 0)


def scalar_rows(values, count, lanes=BLOCK):
    rows = [jnp.broadcast_to(value, (1, lanes)) for value in values]
    return jnp.concatenate(rows + [jnp.zeros((count - len(rows), lanes), single)], 0)


def whole(value):
    return jnp.sum(jnp.sum(value, 1, keepdims=True), 0, keepdims=True)


DECAY = 1.0 - STEP ** (-0.8)
ROW_LANES = 640
COL_LANES = 512


def adafactor_steps(
    small, early, late, grads, rows_old, cols_old, fulls, wsq_ref, loss_ref, sums, norms_own, second,
    p7, q7, p8, p9, p10, p11, p12, p13, rows_ref, cols_ref, scal_ref, norm_out, second_out, norms_out,
):
    here, chan, plane = small.dp_here, small.chan_here, small.plane_here
    x = lax.axis_index("hi")
    count = len(grads)
    for half in range(2):
        lanes = slice(half * BLOCK, (half + 1) * BLOCK)
        rows = [sums[n, k : k + 1, lanes] for n in range(6) for k in range(2)]
        q7[half] = jnp.concatenate(rows + [jnp.zeros((4, BLOCK), single)], 0)
    p7[plane] = q7[x]
    wait_norms = small.plane(p7, lambda other: q7.at[lax.rem(other, 2)])
    update_sq, row_sum = {}, {}

    def measure(some, row_buf, col_buf):
        row_buf[chan] = jnp.zeros(row_buf.shape[1:], single)
        col_buf[here] = jnp.zeros(col_buf.shape[1:], single)
        for k, m in enumerate(some):
            value = grads[m][...]
            squared = value * value + tiny_square
            n_rows, n_cols = value.shape
            row_buf[chan, k : k + 1, 0:n_rows] = to_row(jnp.sum(squared, 1, keepdims=True))
            col_buf[here, k : k + 1, 0:n_cols] = jnp.sum(squared, 0, keepdims=True)
        return small.chan(row_buf), small.dp(col_buf)

    def moments(some, row_buf, col_buf, waits):
        for wait in waits:
            wait()
        row_total, col_total = total_of(row_buf), total_of(col_buf)
        for k, m in enumerate(some):
            n_rows, n_cols = grads[m].shape
            row = DECAY * rows_old[m] + (1.0 - DECAY) * row_total[k : k + 1, 0:n_rows] / fulls[m][1]
            col = DECAY * cols_old[m] + (1.0 - DECAY) * col_total[k : k + 1, 0:n_cols] / fulls[m][0]
            rows_ref[m : m + 1, 0:n_rows] = row
            cols_ref[m : m + 1, 0:n_cols] = col
            row_sum[m] = jnp.sum(row, 1, keepdims=True)
            update = grads[m][...] * to_column(lax.rsqrt(row)) * lax.rsqrt(col)
            update_sq[m] = whole(update * update)

    waits = measure(early, p8, p9)
    yield
    moments(early, p8, p9, waits)
    wait_norms()
    norm_total = total_of(p7)[0:12]
    own = joined_rows(norms_own)
    norm_out[...] = norm_total
    second_new = DECAY * joined_rows(second) + (1.0 - DECAY) * (norm_total * norm_total + tiny_square)
    second_out[...] = second_new
    norm_update = norm_total * lax.rsqrt(second_new)
    sq = [jnp.sum(norm_update * norm_update, 1, keepdims=True), jnp.sum(own * own, 1, keepdims=True)]
    wide = jnp.where(lax.broadcasted_iota(jnp.int32, (12, BLOCK), 1) < 64, sq[0], sq[1])
    yield
    moments(late, p10, p11, measure(late, p10, p11))
    lane = lax.broadcasted_iota(jnp.int32, (16, BLOCK), 1)
    sums_here = scalar_rows([update_sq[m] for m in range(count)], 16)
    row = lax.broadcasted_iota(jnp.int32, (16, BLOCK), 0)
    weights = jnp.where(row == count, loss_ref[0:1, 0:1], wsq_ref[:, 0:1])
    p12[chan, 0:16] = jnp.where(lane < 32, sums_here, weights)
    p12[chan, 16:32] = jnp.concatenate([wide, jnp.zeros((4, BLOCK), single)], 0)
    small.chan(p12)()
    over_chan = total_of(p12)
    p13[here] = jnp.where(lane < 64, over_chan[0:16], scalar_rows([row_sum[m] for m in range(count)], 16))
    wait = small.dp(p13)
    norm_sq = over_chan[16:28]
    norm_clip = jnp.maximum(1.0, jnp.sqrt(norm_sq[:, 0:1] / float(C)))
    norm_scale = jnp.maximum(floor_scale, jnp.sqrt(norm_sq[:, 64:65] / float(C)))
    norms_out[...] = own - (step_rate * norm_scale / norm_clip) * norm_update
    wait()
    over_all = total_of(p13)
    means, steps = [], []
    for m in range(count):
        entries = fulls[m][0] * fulls[m][1]
        mean = over_all[m : m + 1, 64:65] / fulls[m][0]
        clip = jnp.maximum(1.0, jnp.sqrt(mean * over_all[m : m + 1, 0:1] / entries))
        scale = jnp.maximum(floor_scale, jnp.sqrt(over_all[m : m + 1, 32:33] / entries))
        means.append(mean)
        steps.append(step_rate * scale / clip)
    scal_ref[0:16] = scalar_rows(means, 16)
    scal_ref[16:32] = scalar_rows(steps, 16)
    scal_ref[32:40] = jnp.broadcast_to(over_all[count : count + 1, 32:33], (8, BLOCK))
    yield


def finish_kernel(*refs):
    (g0, g1, g2, g3, g4, g5, proj, time, emb, rows, cols, scal, norm, second, norms_new,
     conv_in, conv_out, emb_proj, attn, time_in, emb_out,
     loss, in_g, in_r, in_c, in_w, out_g, out_r, out_c, out_w, proj_g, proj_r, proj_c, proj_w,
     attn_g, attn_r, attn_c, attn_w, time_g, time_r, time_c, time_w, emb_g, emb_r, emb_c, emb_w,
     norm_o, second_o, norms_o) = refs
    loss[...] = scal[32:33, 0:1]
    plan = [
        (0, g0, conv_in.at[0], in_g.at[0], in_r.at[0:1], in_c.at[0:1], in_w.at[0]),
        (1, g3, conv_in.at[1], in_g.at[1], in_r.at[1:2], in_c.at[1:2], in_w.at[1]),
        (2, g5, conv_in.at[2], in_g.at[2], in_r.at[2:3], in_c.at[2:3], in_w.at[2]),
        (3, g1, conv_out.at[0], out_g.at[0], out_r.at[0:1], out_c.at[0:1], out_w.at[0]),
        (4, g4, conv_out.at[1], out_g.at[1], out_r.at[1:2], out_c.at[1:2], out_w.at[1]),
        (5, proj.at[0], emb_proj.at[0], proj_g.at[0], proj_r.at[0:1], proj_c.at[0:1], proj_w.at[0]),
        (6, proj.at[1], emb_proj.at[1], proj_g.at[1], proj_r.at[1:2], proj_c.at[1:2], proj_w.at[1]),
        (7, g2, attn, attn_g, attn_r, attn_c, attn_w),
        (8, time, time_in, time_g, time_r, time_c, time_w),
        (9, emb, emb_out, emb_g, emb_r, emb_c, emb_w),
    ]
    for m, grad, weight, grad_o, rows_o, cols_o, weight_o in plan:
        n_rows, n_cols = grad_o.shape
        row, col = rows[m : m + 1, 0:n_rows], cols[m : m + 1, 0:n_cols]
        rows_o[...] = row
        cols_o[...] = col
        value = grad[...]
        grad_o[...] = value
        mean, step = scal[m : m + 1, 0:1], scal[16 + m : 17 + m, 0:1]
        update = value * to_column(lax.rsqrt(row / mean)) * lax.rsqrt(col)
        weight_o[...] = weight[...] - step * update
    for n in range(6):
        at = slice(2 * n, 2 * n + 2)
        norm_o[n], second_o[n], norms_o[n] = norm[at, :], second[at, :], norms_new[at, :]


def vmem(shape, dtype=single):
    return pltpu.VMEM(shape, dtype)


def semaphores(*shape):
    return pltpu.SemaphoreType.DMA(shape)


TAPS_SHAPE = (9 * C, HALF)
ATTN_SHAPE = (C, 2 * C)
FULL = (PIX, C)
OWN = (PIX, HALF)
QKV = (PIX, 6 * BLOCK)
LOGS = (4, PIX // CHUNK, 1, CHUNK)
WEIGHTS = [TAPS_SHAPE, TAPS_SHAPE, ATTN_SHAPE, TAPS_SHAPE, TAPS_SHAPE, TAPS_SHAPE]


def fused(body, outs, out_specs, in_specs, scratch, args, number, limit, name):
    return pl.pallas_call(
        body,
        out_shape=outs,
        in_specs=in_specs,
        out_specs=out_specs,
        scratch_shapes=scratch,
        compiler_params=pltpu.CompilerParams(
            vmem_limit_bytes=limit * 2**20, collective_id=number, has_side_effects=True
        ),
        name=name,
    )(*args)


def fused_step(
    noisy, noise, timesteps, classes, sample_weight,
    conv_in, conv_out, emb_proj, attn_weight, time_in, emb_out, norms, moments, norm_second,
):
    images = noisy.shape[0] * lax.axis_size("dz") * lax.axis_size("dy")
    total = float(images * PIX * C)
    weights = [conv_in[0], conv_in[1], conv_in[2], conv_out[0], conv_out[1]]
    weights += [emb_proj[0], emb_proj[1], attn_weight, time_in, emb_out]
    dp, chan = lax.axis_size("dz") * lax.axis_size("dy"), lax.axis_size("hi") * lax.axis_size("lo")
    fulls = [(float(w.shape[0] * dp), float(w.shape[1] * chan)) for w in weights]
    shard, attn_shard = conv_in.shape[1:], attn_weight.shape
    shard_shapes = [shard, shard, attn_shard, shard, shard, shard]
    shapes = shard_shapes + [emb_proj.shape, time_in.shape, emb_out.shape]
    shapes += [(16, ROW_LANES), (16, COL_LANES), (40, BLOCK)] + [(12, BLOCK)] * 3
    outs = [struct(s) for s in shapes]

    low = WEIGHTS + [TAPS_SHAPE] + [FULL] * 4
    for name, layer, _, count in reduce_plan([struct(s) for s in shard_shapes]):
        rows, lanes = shard_shapes[layer]
        if name in EARLY:
            half = count // 2
            low += [(2, 4, count, 2 * lanes), (half, 2 * lanes), (2, half, lanes), (half, lanes), (half, lanes)]
        else:
            low += [(4, count, lanes), (2, count, 2 * lanes), (2, count, lanes), (2, count, lanes), (4, count, lanes)]
    scratch = [vmem(s, narrow) for s in low] + [vmem(OWN)] * 10
    scratch += [vmem(OWN, narrow)] * 7 + [vmem(QKV, narrow), vmem((3, ROWS, C), narrow), vmem((C, PIX), narrow)]
    scratch += [vmem((PIX, BLOCK), narrow), vmem((BLOCK, PIX), narrow), vmem((PIX, BLOCK)), vmem((PIX, BLOCK))]
    small = [LOGS, (12, HALF), (2, 2, HALF), (8, HALF), (12, BLOCK), (6, 2, HALF), (2, 8, HALF)]
    small += [(16, BLOCK), (16, BLOCK), (16, BLOCK), (16, HALF), (16, BLOCK)]
    scratch += [vmem(s) for s in small] + [vmem(s, narrow) for s in shard_shapes + [(PIX, BLOCK)] * 2]
    swaps = [(8, 8, BLOCK), (8, 8, BLOCK), (8, 16, HALF), (4, 16, BLOCK), (16, 8, HALF), (16, 8, HALF)]
    swaps += [(2, 8, HALF), (16, 8, HALF), (4, 16, BLOCK), (8, 16, HALF), (16, 16, BLOCK), (2, 16, BLOCK)]
    swaps += [(4, 8, ROW_LANES), (8, 8, COL_LANES), (4, 8, ROW_LANES), (8, 8, BLOCK), (4, 32, BLOCK), (8, 16, BLOCK)]
    scratch += [vmem(s) for s in swaps]
    scratch += [semaphores(LAYERS, 28)] * 2 + [semaphores(LAYERS)] + [semaphores(REDUCES, STEPS)] * 2
    scratch += [semaphores(96)] * 2 + [semaphores(3)] * 2 + [semaphores(128)] * 2 + [semaphores(3)]
    flat = [value.reshape(1, -1) if value.ndim == 1 else value for value in moments]
    pixels = (2, PIX, BLOCK)
    args = [noisy.reshape(pixels), noise.reshape(pixels), sample_weight, timesteps, classes, norms, norm_second]
    args += [conv_in, conv_out, attn_weight, time_in, emb_out, emb_proj, *flat]
    in_specs = [ANY] * 2 + [SMEM] * 3 + [VMEM] * (len(args) - 5)
    body = functools.partial(step_kernel, fulls, total)
    results = fused(body, outs, [VMEM] * len(outs), in_specs, scratch, args, 1, 63, "step")

    def four(weight, row, col):
        return [struct(weight.shape), struct(row.shape), struct(col.shape), struct(weight.shape)]

    outs = [struct((1, 1))]
    for n, weight in enumerate((conv_in, conv_out, emb_proj, attn_weight, time_in, emb_out)):
        outs += four(weight, flat[2 * n], flat[2 * n + 1])
    outs += [struct(norms.shape)] * 3
    args = [*results, conv_in, conv_out, emb_proj, attn_weight, time_in, emb_out]
    finals = list(call(finish_kernel, outs, [], args, "finish"))
    finals[0] = finals[0].reshape(())
    for n, value in enumerate(moments):
        place_at = 2 + 4 * (n // 2) + n % 2
        finals[place_at] = finals[place_at].reshape(value.shape)
    return tuple(finals)


def pack_flat(members):
    return jnp.concatenate([member.reshape(-1) for member in members])


def unpack_flat(vector, shape_list):
    pieces = []
    offset = 0
    for array_shape in shape_list:
        extent = math.prod(array_shape)
        pieces.append(vector[offset : offset + extent].reshape(array_shape))
        offset += extent
    return pieces


def per_device(
    noisy,
    noise,
    timesteps,
    classes,
    sample_weight,
    conv_in,
    conv_out,
    emb_proj,
    attn_weight,
    time_in,
    emb_out,
    norms,
    conv_in_rows,
    conv_in_cols,
    conv_out_rows,
    conv_out_cols,
    emb_proj_rows,
    emb_proj_cols,
    attn_rows,
    attn_cols,
    time_rows,
    time_cols,
    embout_rows,
    embout_cols,
    norm_second,
):
    rows_here = (conv_in.shape[1], attn_weight.shape[0])
    if lax.axis_size("dz") == 4 and all(rows % 64 == 0 for rows in rows_here):
        moments = [conv_in_rows, conv_in_cols, conv_out_rows, conv_out_cols, emb_proj_rows, emb_proj_cols]
        moments += [attn_rows, attn_cols, time_rows, time_cols, embout_rows, embout_cols]
        return fused_step(
            noisy, noise, timesteps, classes, sample_weight, conv_in, conv_out, emb_proj, attn_weight, time_in,
            emb_out, norms, moments, norm_second,
        )
    masters = [conv_in, conv_out, emb_proj, attn_weight[None], time_in[None], emb_out[None]]
    lowered = [master.astype(narrow) for master in masters]
    modulate, saved = embed_forward(timesteps, classes, lowered[4][0], lowered[5][0], lowered[2])
    norms_wide = join_image(norms, 2)
    shards = [lowered[0][0], lowered[1][0], lowered[3][0], lowered[0][1], lowered[1][1], lowered[0][2]]
    full = [gather_weight(shard) for shard in shards]
    loss_part, din, dout, dattn, sums, dmod = network(
        noisy, noise, sample_weight, (full[0], full[3], full[5]), (full[1], full[4]), full[2], norms_wide, modulate
    )
    reduced_parts = [scatter_grad(part) for part in (din[0], dout[0], dattn, din[1], dout[1], din[2])]
    in0_grad, out0_grad, attn_grad, in1_grad, out1_grad, head_grad = reduced_parts
    proj_grad, time_grad, embout_grad = embed_backward(saved, dmod, lowered[2], lowered[5][0])
    norm_local = lax.psum_scatter(sums, "hi", scatter_dimension=2, tiled=True)
    reduced = [
        jnp.stack([in0_grad, in1_grad, head_grad]),
        jnp.stack([out0_grad, out1_grad]),
        proj_grad,
        attn_grad[None],
        time_grad[None],
        embout_grad[None],
    ]
    decay_rate = 1.0 - STEP ** (-0.8)
    dp_count = lax.axis_size("dz") * lax.axis_size("dy")
    chan_count = lax.axis_size("hi") * lax.axis_size("lo")
    rows_old = [
        conv_in_rows,
        conv_out_rows,
        emb_proj_rows,
        attn_rows[None],
        time_rows[None],
        embout_rows[None],
    ]
    cols_old = [
        conv_in_cols,
        conv_out_cols,
        emb_proj_cols,
        attn_cols[None],
        time_cols[None],
        embout_cols[None],
    ]
    squares = [gradient * gradient + tiny_square for gradient in reduced]
    full_rows = [squared.shape[1] * dp_count for squared in squares]
    full_cols = [squared.shape[2] * chan_count for squared in squares]
    row_parts = [jnp.sum(squared, 2) for squared in squares]
    col_parts = [jnp.sum(squared, 1) for squared in squares]
    row_shapes = [member.shape for member in row_parts]
    col_shapes = [member.shape for member in col_parts]
    norm_width = norm_local.shape[2]
    row_totals = unpack_flat(lax.psum(pack_flat(row_parts), ("hi", "lo")), row_shapes)
    rows_new = [
        decay_rate * rows_old[position]
        + (1.0 - decay_rate) * row_totals[position] / full_cols[position]
        for position in range(6)
    ]
    row_sums_local = [jnp.sum(member, 1) for member in rows_new]
    col_vector, norm_total = lax.psum((pack_flat(col_parts + row_sums_local), norm_local), DP)
    col_pieces = unpack_flat(col_vector, col_shapes + [(member.shape[0],) for member in rows_new])
    col_totals = col_pieces[:6]
    row_means = [col_pieces[6 + position] / full_rows[position] for position in range(6)]
    cols_new = [
        decay_rate * cols_old[position]
        + (1.0 - decay_rate) * col_totals[position] / full_rows[position]
        for position in range(6)
    ]
    updates = [
        reduced[position]
        * lax.rsqrt(rows_new[position] / row_means[position][:, None])[:, :, None]
        * lax.rsqrt(cols_new[position])[:, None, :]
        for position in range(6)
    ]
    second_new = decay_rate * norm_second + (1.0 - decay_rate) * (
        norm_total * norm_total + tiny_square
    )
    norm_update = norm_total * lax.rsqrt(second_new)
    update_squares = pack_flat([jnp.sum(member * member, (1, 2)) for member in updates])
    weight_squares = pack_flat([jnp.sum(master * master, (1, 2)) for master in masters])
    norm_update_sq = jnp.sum(norm_update * norm_update, 2) / dp_count
    norm_weight_sq = jnp.sum(norms * norms, 2) / dp_count
    update_total, weight_total, norm_update_total, norm_weight_total, loss = lax.psum(
        (update_squares, weight_squares, norm_update_sq, norm_weight_sq, loss_part), ("dz", "dy", "hi", "lo")
    )
    layer_shapes = [(member.shape[0],) for member in masters]
    update_sums = unpack_flat(update_total, layer_shapes)
    weight_sums = unpack_flat(weight_total, layer_shapes)
    results = [loss]
    for position in range(6):
        entries = float(full_rows[position] * full_cols[position])
        clip_factor = jnp.maximum(1.0, jnp.sqrt(update_sums[position] / entries))
        scale_factor = jnp.maximum(floor_scale, jnp.sqrt(weight_sums[position] / entries))
        weight_new = (
            masters[position]
            - (step_rate * scale_factor / clip_factor)[:, None, None] * updates[position]
        )
        if position >= 3:
            results += [
                reduced[position][0],
                rows_new[position][0],
                cols_new[position][0],
                weight_new[0],
            ]
        else:
            results += [reduced[position], rows_new[position], cols_new[position], weight_new]
    norm_entries = float(norm_width * chan_count)
    norm_clip = jnp.maximum(1.0, jnp.sqrt(norm_update_total / norm_entries))
    norm_scale = jnp.maximum(floor_scale, jnp.sqrt(norm_weight_total / norm_entries))
    norms_new = norms - (step_rate * norm_scale / norm_clip)[:, :, None] * norm_update
    results += [norm_total, second_new, norms_new]
    return (
        results[0],
        results[1],
        results[2],
        results[3],
        results[4],
        results[5],
        results[6],
        results[7],
        results[8],
        results[9],
        results[10],
        results[11],
        results[12],
        results[13],
        results[14],
        results[15],
        results[16],
        results[17],
        results[18],
        results[19],
        results[20],
        results[21],
        results[22],
        results[23],
        results[24],
        results[25],
        results[26],
        results[27],
    )


CHAN = ("hi", "lo")


def solution(mesh):
    dp, chan = mesh.shape["dp"], mesh.shape["chan"]
    mesh = Mesh(mesh.devices.reshape(dp // 2, 2, 2, chan // 2), DP + CHAN)
    in_specs = (
        P(DP, None, None, CHAN),
        P(DP, None, None, CHAN),
        P(DP),
        P(DP),
        P(DP),
        P(None, DP, CHAN),
        P(None, DP, CHAN),
        P(None, DP, CHAN),
        P(DP, CHAN),
        P(DP, CHAN),
        P(DP, CHAN),
        P(None, None, CHAN),
        P(None, DP),
        P(None, CHAN),
        P(None, DP),
        P(None, CHAN),
        P(None, DP),
        P(None, CHAN),
        P(DP),
        P(CHAN),
        P(DP),
        P(CHAN),
        P(DP),
        P(CHAN),
        P(None, None, CHAN),
    )
    out_specs = (
        P(),
        P(None, DP, CHAN),
        P(None, DP),
        P(None, CHAN),
        P(None, DP, CHAN),
        P(None, DP, CHAN),
        P(None, DP),
        P(None, CHAN),
        P(None, DP, CHAN),
        P(None, DP, CHAN),
        P(None, DP),
        P(None, CHAN),
        P(None, DP, CHAN),
        P(DP, CHAN),
        P(DP),
        P(CHAN),
        P(DP, CHAN),
        P(DP, CHAN),
        P(DP),
        P(CHAN),
        P(DP, CHAN),
        P(DP, CHAN),
        P(DP),
        P(CHAN),
        P(DP, CHAN),
        P(None, None, CHAN),
        P(None, None, CHAN),
        P(None, None, CHAN),
    )
    return jax.shard_map(
        per_device, mesh=mesh, in_specs=in_specs, out_specs=out_specs, check_vma=False
    )
```
